32 devices in a mesh: grp: 4 (over y, core), gy: 2 (over x), gx: 4 (over z).
Axes of the slice: x: 2, y: 2, z: 4, core: 2. Of those that a mesh axis runs over, the one named last changes fastest.
Arguments:
- design: float32 [8, 16, 512], P('grp', 'gy', 'gx'), may hold values from 0 to 1
- populations: float32 [19, 8, 16, 512], P(None, 'grp', 'gy', 'gx'), may hold values from 0.02 to 0.1
- cotangent: float32 [19, 8, 16, 512], P(None, 'grp', 'gy', 'gx'), may hold values from -150 to 150
- wall_mask: int32 [8, 16, 512], P('grp', 'gy', 'gx'), may hold values 0 or 1
- inlet_mask: int32 [8, 16, 512], P('grp', 'gy', 'gx'), may hold values 0 or 1
- beta_step: int32 [], replicated, may hold values from 0 to 64
Outputs:
- final_populations: float32 [19, 8, 16, 512], P(None, 'grp', 'gy', 'gx')
- design_grad: float32 [8, 16, 512], P('grp', 'gy', 'gx')
The draws below stay inside these ranges and needn't reach their ends.
All inputs are finite; a program needn't handle non-finite values. No bound on the sum of `wall_mask` or of `inlet_mask` on one device may be relied on, other than what follows from the above.
Results may differ from the reference program's by a relative error of at most 0.0003.
Values sent between devices are 32-bit elements; how exact they have to be, the bound alone decides.
No kernel may reach another device: no remote copies, remote signals or barrier semaphores. Data moves between devices by JAX's collectives and lax.ppermute only.
A program may use at most 64 MiB of HBM per device.

```python
import jax
import jax.numpy as jnp
import numpy as np
from jax import lax

STEPS = 4
BISECT = 30
NZ = 8
NY = 16
NX = 512


def with_ends(drawn, stream_key, least, high):
    index_at = [jax.random.randint(jax.random.fold_in(stream_key, axis), (), 0, length) for axis, length in enumerate(drawn.shape)]
    longest = drawn.shape.index(max(drawn.shape))
    neighbour = index_at[:longest] + [(index_at[longest] + 1) % drawn.shape[longest]] + index_at[longest + 1:]
    return drawn.at[tuple(index_at)].set(least).at[tuple(neighbour)].set(high)


def shard_levels(stream_key, dims, cuts, low, largest):
    loudness, own = 1.0, jax.random.fold_in(stream_key, 6)
    for position, shards_of in cuts:
        heights = jnp.exp(jax.random.uniform(jax.random.fold_in(own, position), (shards_of,), jnp.float32, low / len(cuts), largest / len(cuts)))
        loudness = loudness * jnp.repeat(heights, dims[position] // shards_of).reshape([-1 if axis == position else 1 for axis in range(len(dims))])
    return loudness


def gaussian(rng, extent, width, limit, shards=(), kind=jnp.bfloat16):
    gain = shard_levels(rng, extent, shards, -0.22, 0.18) if shards else 1.0
    values = jax.random.normal(rng, extent, jnp.float32) * width * gain
    return jnp.minimum(jnp.maximum(values, -limit), limit).astype(kind)


def setup_inputs(seed: int = 0) -> dict:
    key_of = jax.random.split(jax.random.key(seed), 7)
    design = jnp.clip(1.0 * jax.random.uniform(key_of[0], (NZ, NY, NX), jnp.float32) ** shard_levels(key_of[0], (NZ, NY, NX), ((0, 4), (1, 2), (2, 4)), -0.2, 0.2), 0.0, 1.0)
    populations = jnp.clip(0.02 + 0.08 * jax.random.uniform(key_of[1], (19, NZ, NY, NX), jnp.float32) ** shard_levels(key_of[1], (19, NZ, NY, NX), ((1, 4), (2, 2), (3, 4)), -0.2, 0.2), 0.02, 0.1)
    cotangent = gaussian(key_of[2], (19, NZ, NY, NX), 25.0, 150.0, ((1, 4), (2, 2), (3, 4)), jnp.float32)
    wall_mask = with_ends((jax.random.randint(key_of[3], (NZ, NY, NX), 0, 6) < 1).astype(jnp.int32), jax.random.fold_in(key_of[3], 1), 0, 1)
    inlet_mask = with_ends((jax.random.randint(key_of[4], (NZ, NY, NX), 0, 20) < 1).astype(jnp.int32), jax.random.fold_in(key_of[4], 1), 0, 1)
    beta_step = jax.random.randint(key_of[5], (), 0, 65).astype(jnp.int32)
    return dict(design=design, populations=populations, cotangent=cotangent, wall_mask=wall_mask, inlet_mask=inlet_mask, beta_step=beta_step)


velocities = np.array([[0, 0, 0], [1, 0, 0], [-1, 0, 0], [0, 1, 0], [0, -1, 0], [0, 0, 1], [0, 0, -1], [1, 1, 0], [-1, -1, 0], [1, -1, 0], [-1, 1, 0], [1, 0, 1], [-1, 0, -1], [1, 0, -1], [-1, 0, 1], [0, 1, 1], [0, -1, -1], [0, 1, -1], [0, -1, 1]])
opposite = [0, 2, 1, 4, 3, 6, 5, 8, 7, 10, 9, 12, 11, 14, 13, 16, 15, 18, 17]
lattice_weights = [1.0 / 3.0] + [1.0 / 18.0] * 6 + [1.0 / 36.0] * 12
relax_rate = 0.8
inlet_speed = 0.05
alpha_most = 8.0
penalty_shape = 0.1
fluid_share = 0.4

def equilibrium(density, speed_z, speed_y, speed_x):
    square = speed_z * speed_z + speed_y * speed_y + speed_x * speed_x
    comps = []
    for i in range(19):
        along = float(velocities[i][0]) * speed_z + float(velocities[i][1]) * speed_y + float(velocities[i][2]) * speed_x
        comps.append(lattice_weights[i] * density * (1.0 + 3.0 * along + 4.5 * along * along - 1.5 * square))
    return jnp.stack(comps)

def moment(popul, axis):
    total = jnp.zeros(popul.shape[1:], popul.dtype)
    for i in range(1, 19):
        if velocities[i][axis] != 0:
            total = total + float(velocities[i][axis]) * popul[i]
    return total

def collide(popul, alpha, wall_mask, inlet_mask):
    density = lax.optimization_barrier(jnp.sum(popul, axis=0))
    scale = density * (1.0 + alpha)
    feq = equilibrium(density, moment(popul, 0) / scale, moment(popul, 1) / scale, moment(popul, 2) / scale)
    post = popul + relax_rate * (feq - popul)
    bounce = jnp.stack([popul[opposite[i]] for i in range(19)])
    inlet_values = []
    for i in range(19):
        along = float(velocities[i][0]) * inlet_speed
        inlet_values.append(lattice_weights[i] * (1.0 + 3.0 * along + 4.5 * along * along - 1.5 * inlet_speed * inlet_speed))
    inlet_feq = jnp.stack([jnp.full(popul.shape[1:], value, popul.dtype) for value in inlet_values])
    return jnp.where(wall_mask[None] > 0, bounce, jnp.where(inlet_mask[None] > 0, inlet_feq, post))

def pick(padded, sign):
    depth, rows, cols = (padded.shape[1] - 2, padded.shape[2] - 2, padded.shape[3] - 2)
    outputs = []
    for i in range(19):
        start_z = 1 - sign * int(velocities[i][0])
        start_y = 1 - sign * int(velocities[i][1])
        start_x = 1 - sign * int(velocities[i][2])
        outputs.append(padded[i, start_z:start_z + depth, start_y:start_y + rows, start_x:start_x + cols])
    return jnp.stack(outputs)

def smooth_padded(padded):
    along_z = 0.25 * padded[:-2] + 0.5 * padded[1:-1] + 0.25 * padded[2:]
    along_y = 0.25 * along_z[:, :-2] + 0.5 * along_z[:, 1:-1] + 0.25 * along_z[:, 2:]
    return 0.25 * along_y[:, :, :-2] + 0.5 * along_y[:, :, 1:-1] + 0.25 * along_y[:, :, 2:]

def project(filtered, thresh, beta):
    denom = jnp.tanh(beta * thresh) + jnp.tanh(beta * (1.0 - thresh))
    return (jnp.tanh(beta * thresh) + jnp.tanh(beta * (filtered - thresh))) / denom

def shift_all(popul, sign):
    return pick(jnp.pad(popul, ((0, 0), (1, 1), (1, 1), (1, 1))), sign)

def reference(design, populations, cotangent, wall_mask, inlet_mask, beta_step):
    beta = jnp.exp2(beta_step.astype(jnp.float32) / 16.0)
    filtered = smooth_padded(jnp.pad(design, 1))
    cells = filtered.size
    low = jnp.zeros((), jnp.float32)
    high = jnp.ones((), jnp.float32)
    for step in range(BISECT):
        middle = 0.5 * (low + high)
        above = jnp.sum(project(filtered, middle, beta)) > fluid_share * cells
        low = jnp.where(above, middle, low)
        high = jnp.where(above, high, middle)
    eta = 0.5 * (low + high)
    density_hat = project(filtered, eta, beta)
    alpha = alpha_most * penalty_shape * (1.0 - density_hat) / (penalty_shape + density_hat)
    states = []
    popul = populations
    for step in range(STEPS):
        states.append(popul)
        popul = shift_all(collide(popul, alpha, wall_mask, inlet_mask), 1)
    final_populations = popul
    adjoint = cotangent
    alpha_grad = jnp.zeros_like(alpha)
    for step in reversed(range(STEPS)):
        back = shift_all(adjoint, -1)
        unused, pullback = jax.vjp(lambda p, a: collide(p, a, wall_mask, inlet_mask), states[step], alpha)
        adjoint, term = pullback(back)
        alpha_grad = alpha_grad + term
    denom = jnp.tanh(beta * eta) + jnp.tanh(beta * (1.0 - eta))
    slope = beta * (1.0 - jnp.tanh(beta * (filtered - eta)) ** 2) / denom
    factor = -alpha_most * penalty_shape * (1.0 + penalty_shape) / (penalty_shape + density_hat) ** 2
    design_grad = smooth_padded(jnp.pad(alpha_grad * factor * slope, 1))
    return (final_populations, design_grad)
```

```python
import functools

import jax
import jax.numpy as jnp
import numpy as np
from jax import lax
from jax.experimental import pallas as pl
from jax.experimental.pallas import tpu as pltpu
from jax.sharding import PartitionSpec as P

STEPS = 4
BISECT = 30


velocities = np.array(
    [
        [0, 0, 0],
        [1, 0, 0],
        [-1, 0, 0],
        [0, 1, 0],
        [0, -1, 0],
        [0, 0, 1],
        [0, 0, -1],
        [1, 1, 0],
        [-1, -1, 0],
        [1, -1, 0],
        [-1, 1, 0],
        [1, 0, 1],
        [-1, 0, -1],
        [1, 0, -1],
        [-1, 0, 1],
        [0, 1, 1],
        [0, -1, -1],
        [0, 1, -1],
        [0, -1, 1],
    ]
)
opposite = [0, 2, 1, 4, 3, 6, 5, 8, 7, 10, 9, 12, 11, 14, 13, 16, 15, 18, 17]
lattice_weights = [1.0 / 3.0] + [1.0 / 18.0] * 6 + [1.0 / 36.0] * 12
relax_rate = 0.8
inlet_speed = 0.05
alpha_most = 8.0
penalty_shape = 0.1
fluid_share = 0.4


def extended(value, sides, width):
    for axis, dim in sides:
        size, length = (lax.axis_size(axis), value.shape[dim])
        up = [(i, (i + 1) % size) for i in range(size - 1)]
        down = [(j, i) for i, j in up]
        last = lax.slice_in_dim(value, length - width, length, axis=dim)
        leading = lax.slice_in_dim(value, 0, width, axis=dim)
        before = lax.ppermute(last, axis, up)
        after = lax.ppermute(leading, axis, down)
        value = jnp.concatenate([before, value, after], axis=dim)
    return value


def equilibrium(density, speed_z, speed_y, speed_x):
    square = speed_z * speed_z + speed_y * speed_y + speed_x * speed_x
    comps = []
    for i in range(19):
        along = (
            float(velocities[i][0]) * speed_z
            + float(velocities[i][1]) * speed_y
            + float(velocities[i][2]) * speed_x
        )
        comps.append(
            lattice_weights[i] * density * (1.0 + 3.0 * along + 4.5 * along * along - 1.5 * square)
        )
    return jnp.stack(comps)


def moment(popul, axis):
    total = jnp.zeros(popul.shape[1:], popul.dtype)
    for i in range(1, 19):
        if velocities[i][axis] != 0:
            total = total + float(velocities[i][axis]) * popul[i]
    return total


def collide(popul, alpha, wall_mask, inlet_mask):
    density = jnp.sum(popul, axis=0)
    scale = density * (1.0 + alpha)
    feq = equilibrium(
        density, moment(popul, 0) / scale, moment(popul, 1) / scale, moment(popul, 2) / scale
    )
    post = popul + relax_rate * (feq - popul)
    bounce = jnp.stack([popul[opposite[i]] for i in range(19)])
    inlet_values = []
    for i in range(19):
        along = float(velocities[i][0]) * inlet_speed
        inlet_values.append(
            lattice_weights[i]
            * (1.0 + 3.0 * along + 4.5 * along * along - 1.5 * inlet_speed * inlet_speed)
        )
    inlet_feq = jnp.stack([jnp.full(popul.shape[1:], value, popul.dtype) for value in inlet_values])
    return jnp.where(wall_mask[None] > 0, bounce, jnp.where(inlet_mask[None] > 0, inlet_feq, post))


def pick(padded, sign):
    depth, rows, cols = (padded.shape[1] - 2, padded.shape[2] - 2, padded.shape[3] - 2)
    outputs = []
    for i in range(19):
        start_z = 1 - sign * int(velocities[i][0])
        start_y = 1 - sign * int(velocities[i][1])
        start_x = 1 - sign * int(velocities[i][2])
        outputs.append(
            padded[i, start_z : start_z + depth, start_y : start_y + rows, start_x : start_x + cols]
        )
    return jnp.stack(outputs)


def shift_all(popul, sign):
    padded = extended(popul, (("grp", 1), ("gy", 2), ("gx", 3)), 1)
    return pick(padded, sign)


def smooth_field(field):
    padded = extended(field, (("grp", 0), ("gy", 1), ("gx", 2)), 1)
    along_z = 0.25 * padded[:-2] + 0.5 * padded[1:-1] + 0.25 * padded[2:]
    along_y = 0.25 * along_z[:, :-2] + 0.5 * along_z[:, 1:-1] + 0.25 * along_z[:, 2:]
    return 0.25 * along_y[:, :, :-2] + 0.5 * along_y[:, :, 1:-1] + 0.25 * along_y[:, :, 2:]


def project(filtered, thresh, beta):
    denom = jnp.tanh(beta * thresh) + jnp.tanh(beta * (1.0 - thresh))
    return (jnp.tanh(beta * thresh) + jnp.tanh(beta * (filtered - thresh))) / denom


def threshold_kernel(cells, beta_ref, filtered_ref, eta_ref, raised_ref):
    beta = jnp.full((8, 128), beta_ref[0], jnp.float32)
    raised_ref[...] = jnp.exp(2.0 * beta_ref[0] * filtered_ref[...])
    top = jnp.exp(2.0 * beta)
    rows = filtered_ref.shape[0]
    span = min(rows, 512)

    def halve(step, ends):
        low, high = ends
        middle = 0.5 * (low + high)
        level = jnp.exp(2.0 * beta * middle)

        def part(index, total):
            for row in range(0, span, 8):
                raised = raised_ref[pl.ds(pl.multiple_of(index * span + row, 8), 8), :]
                total = total + (raised - 1.0) / (raised + level)
            return total

        total = lax.fori_loop(0, rows // span, part, jnp.zeros((8, 128), jnp.float32))
        volume = jnp.sum(jnp.sum(total, axis=0, keepdims=True), axis=1, keepdims=True)
        above = volume * ((top + level) / (top - 1.0)) > fluid_share * cells
        return jnp.where(above, middle, low), jnp.where(above, high, middle)

    low, high = lax.fori_loop(
        0, BISECT, halve, (jnp.zeros((8, 128), jnp.float32), jnp.ones((8, 128), jnp.float32))
    )
    eta_ref[...] = 0.5 * (low + high)


def threshold(filtered, beta, cells):
    eta = pl.pallas_call(
        functools.partial(threshold_kernel, cells),
        out_shape=jax.ShapeDtypeStruct((8, 128), jnp.float32),
        in_specs=[
            pl.BlockSpec(memory_space=pltpu.SMEM),
            pl.BlockSpec(memory_space=pltpu.VMEM),
        ],
        out_specs=pl.BlockSpec(memory_space=pltpu.VMEM),
        scratch_shapes=[pltpu.VMEM(filtered.shape, jnp.float32)],
        compiler_params=pltpu.CompilerParams(vmem_limit_bytes=40 * 2**20),
        name="threshold",
    )(beta.reshape(1), filtered)
    return eta[0, 0]


def body(design, populations, cotangent, wall_mask, inlet_mask, beta_step):
    beta = jnp.exp2(beta_step.astype(jnp.float32) / 16.0)
    filtered = smooth_field(design)
    cells = design.size * lax.axis_size("grp") * lax.axis_size("gy") * lax.axis_size("gx")
    everywhere = lax.all_gather(filtered, ("grp", "gy", "gx"))
    eta = threshold(everywhere.reshape(-1, filtered.shape[-1]), beta, cells)
    density_hat = project(filtered, eta, beta)
    alpha = alpha_most * penalty_shape * (1.0 - density_hat) / (penalty_shape + density_hat)
    states = []
    popul = populations
    for step in range(STEPS):
        states.append(popul)
        popul = shift_all(collide(popul, alpha, wall_mask, inlet_mask), 1)
    adjoint = cotangent
    alpha_grad = jnp.zeros_like(alpha)
    for step in reversed(range(STEPS)):
        back = shift_all(adjoint, -1)
        unused, pullback = jax.vjp(
            lambda p, a: collide(p, a, wall_mask, inlet_mask), states[step], alpha
        )
        adjoint, term = pullback(back)
        alpha_grad = alpha_grad + term
    denom = jnp.tanh(beta * eta) + jnp.tanh(beta * (1.0 - eta))
    slope = beta * (1.0 - jnp.tanh(beta * (filtered - eta)) ** 2) / denom
    factor = (
        -alpha_most * penalty_shape * (1.0 + penalty_shape) / (penalty_shape + density_hat) ** 2
    )
    design_grad = smooth_field(alpha_grad * factor * slope)
    return (popul, design_grad)


def solution(mesh):
    placed = (
        P("grp", "gy", "gx"),
        P(None, "grp", "gy", "gx"),
        P(None, "grp", "gy", "gx"),
        P("grp", "gy", "gx"),
        P("grp", "gy", "gx"),
        P(),
    )
    return jax.shard_map(
        body,
        mesh=mesh,
        in_specs=placed,
        out_specs=(P(None, "grp", "gy", "gx"), P("grp", "gy", "gx")),
        check_vma=False,
    )
```

```python
import functools

import jax
import jax.numpy as jnp
import numpy as np
from jax import lax
from jax.experimental import pallas as pl
from jax.experimental.pallas import tpu as pltpu
from jax.sharding import PartitionSpec as P

STEPS = 4
BISECT = 30


velocities = np.array(
    [
        [0, 0, 0],
        [1, 0, 0],
        [-1, 0, 0],
        [0, 1, 0],
        [0, -1, 0],
        [0, 0, 1],
        [0, 0, -1],
        [1, 1, 0],
        [-1, -1, 0],
        [1, -1, 0],
        [-1, 1, 0],
        [1, 0, 1],
        [-1, 0, -1],
        [1, 0, -1],
        [-1, 0, 1],
        [0, 1, 1],
        [0, -1, -1],
        [0, 1, -1],
        [0, -1, 1],
    ]
)
opposite = [0, 2, 1, 4, 3, 6, 5, 8, 7, 10, 9, 12, 11, 14, 13, 16, 15, 18, 17]
lattice_weights = [1.0 / 3.0] + [1.0 / 18.0] * 6 + [1.0 / 36.0] * 12
relax_rate = 0.8
inlet_speed = 0.05
alpha_most = 8.0
penalty_shape = 0.1
fluid_share = 0.4


def extended(value, sides, width):
    for axis, dim in sides:
        size, length = (lax.axis_size(axis), value.shape[dim])
        up = [(i, (i + 1) % size) for i in range(size - 1)]
        down = [(j, i) for i, j in up]
        last = lax.slice_in_dim(value, length - width, length, axis=dim)
        leading = lax.slice_in_dim(value, 0, width, axis=dim)
        before = lax.ppermute(last, axis, up)
        after = lax.ppermute(leading, axis, down)
        value = jnp.concatenate([before, value, after], axis=dim)
    return value


def equilibrium(density, speed_z, speed_y, speed_x):
    square = speed_z * speed_z + speed_y * speed_y + speed_x * speed_x
    comps = []
    for i in range(19):
        along = (
            float(velocities[i][0]) * speed_z
            + float(velocities[i][1]) * speed_y
            + float(velocities[i][2]) * speed_x
        )
        comps.append(
            lattice_weights[i] * density * (1.0 + 3.0 * along + 4.5 * along * along - 1.5 * square)
        )
    return jnp.stack(comps)


def moment(popul, axis):
    total = jnp.zeros(popul.shape[1:], popul.dtype)
    for i in range(1, 19):
        if velocities[i][axis] != 0:
            total = total + float(velocities[i][axis]) * popul[i]
    return total


def collide(popul, alpha, wall_mask, inlet_mask):
    density = jnp.sum(popul, axis=0)
    scale = density * (1.0 + alpha)
    feq = equilibrium(
        density, moment(popul, 0) / scale, moment(popul, 1) / scale, moment(popul, 2) / scale
    )
    post = popul + relax_rate * (feq - popul)
    bounce = jnp.stack([popul[opposite[i]] for i in range(19)])
    inlet_values = []
    for i in range(19):
        along = float(velocities[i][0]) * inlet_speed
        inlet_values.append(
            lattice_weights[i]
            * (1.0 + 3.0 * along + 4.5 * along * along - 1.5 * inlet_speed * inlet_speed)
        )
    inlet_feq = jnp.stack([jnp.full(popul.shape[1:], value, popul.dtype) for value in inlet_values])
    return jnp.where(wall_mask[None] > 0, bounce, jnp.where(inlet_mask[None] > 0, inlet_feq, post))


def pick(padded, sign):
    depth, rows, cols = (padded.shape[1] - 2, padded.shape[2] - 2, padded.shape[3] - 2)
    outputs = []
    for i in range(19):
        start_z = 1 - sign * int(velocities[i][0])
        start_y = 1 - sign * int(velocities[i][1])
        start_x = 1 - sign * int(velocities[i][2])
        outputs.append(
            padded[i, start_z : start_z + depth, start_y : start_y + rows, start_x : start_x + cols]
        )
    return jnp.stack(outputs)


def shift_all(popul, sign):
    padded = extended(popul, (("grp", 1), ("gy", 2), ("gx", 3)), 1)
    return pick(padded, sign)


def smooth_field(field):
    padded = extended(field, (("grp", 0), ("gy", 1), ("gx", 2)), 1)
    along_z = 0.25 * padded[:-2] + 0.5 * padded[1:-1] + 0.25 * padded[2:]
    along_y = 0.25 * along_z[:, :-2] + 0.5 * along_z[:, 1:-1] + 0.25 * along_z[:, 2:]
    return 0.25 * along_y[:, :, :-2] + 0.5 * along_y[:, :, 1:-1] + 0.25 * along_y[:, :, 2:]


def project(filtered, thresh, beta):
    denom = jnp.tanh(beta * thresh) + jnp.tanh(beta * (1.0 - thresh))
    return (jnp.tanh(beta * thresh) + jnp.tanh(beta * (filtered - thresh))) / denom


def threshold_kernel(cells, beta_ref, filtered_ref, eta_ref, raised_ref):
    beta = jnp.full((8, 128), beta_ref[0], jnp.float32)
    raised_ref[...] = jnp.exp(2.0 * beta_ref[0] * filtered_ref[...])
    top = jnp.exp(2.0 * beta)
    rows = filtered_ref.shape[0]
    span = min(rows, 512)

    def halve(step, ends):
        low, high = ends
        middle = 0.5 * (low + high)
        level = jnp.exp(2.0 * beta * middle)

        def part(index, total):
            for row in range(0, span, 8):
                raised = raised_ref[pl.ds(pl.multiple_of(index * span + row, 8), 8), :]
                total = total + (raised - 1.0) / (raised + level)
            return total

        total = lax.fori_loop(0, rows // span, part, jnp.zeros((8, 128), jnp.float32))
        volume = jnp.sum(jnp.sum(total, axis=0, keepdims=True), axis=1, keepdims=True)
        above = volume * ((top + level) / (top - 1.0)) > fluid_share * cells
        return jnp.where(above, middle, low), jnp.where(above, high, middle)

    low, high = lax.fori_loop(
        0, BISECT, halve, (jnp.zeros((8, 128), jnp.float32), jnp.ones((8, 128), jnp.float32))
    )
    eta_ref[...] = 0.5 * (low + high)


def threshold(filtered, beta, cells):
    eta = pl.pallas_call(
        functools.partial(threshold_kernel, cells),
        out_shape=jax.ShapeDtypeStruct((8, 128), jnp.float32),
        in_specs=[
            pl.BlockSpec(memory_space=pltpu.SMEM),
            pl.BlockSpec(memory_space=pltpu.VMEM),
        ],
        out_specs=pl.BlockSpec(memory_space=pltpu.VMEM),
        scratch_shapes=[pltpu.VMEM(filtered.shape, jnp.float32)],
        compiler_params=pltpu.CompilerParams(vmem_limit_bytes=40 * 2**20),
        name="threshold",
    )(beta.reshape(1), filtered)
    return eta[0, 0]


def body(design, populations, cotangent, wall_mask, inlet_mask, beta_step):
    beta = jnp.exp2(beta_step.astype(jnp.float32) / 16.0)
    filtered = smooth_field(design)
    cells = design.size * lax.axis_size("grp") * lax.axis_size("gy") * lax.axis_size("gx")
    devices = lax.axis_size("grp") * lax.axis_size("gy") * lax.axis_size("gx")
    copies = jnp.broadcast_to(filtered, (devices, *filtered.shape))
    everywhere = lax.all_to_all(copies, ("grp", "gy", "gx"), 0, 0)
    eta = threshold(everywhere.reshape(-1, filtered.shape[-1]), beta, cells)
    density_hat = project(filtered, eta, beta)
    alpha = alpha_most * penalty_shape * (1.0 - density_hat) / (penalty_shape + density_hat)
    states = []
    popul = populations
    for step in range(STEPS):
        states.append(popul)
        popul = shift_all(collide(popul, alpha, wall_mask, inlet_mask), 1)
    adjoint = cotangent
    alpha_grad = jnp.zeros_like(alpha)
    for step in reversed(range(STEPS)):
        back = shift_all(adjoint, -1)
        unused, pullback = jax.vjp(
            lambda p, a: collide(p, a, wall_mask, inlet_mask), states[step], alpha
        )
        adjoint, term = pullback(back)
        alpha_grad = alpha_grad + term
    denom = jnp.tanh(beta * eta) + jnp.tanh(beta * (1.0 - eta))
    slope = beta * (1.0 - jnp.tanh(beta * (filtered - eta)) ** 2) / denom
    factor = (
        -alpha_most * penalty_shape * (1.0 + penalty_shape) / (penalty_shape + density_hat) ** 2
    )
    design_grad = smooth_field(alpha_grad * factor * slope)
    return (popul, design_grad)


def solution(mesh):
    placed = (
        P("grp", "gy", "gx"),
        P(None, "grp", "gy", "gx"),
        P(None, "grp", "gy", "gx"),
        P("grp", "gy", "gx"),
        P("grp", "gy", "gx"),
        P(),
    )
    return jax.shard_map(
        body,
        mesh=mesh,
        in_specs=placed,
        out_specs=(P(None, "grp", "gy", "gx"), P("grp", "gy", "gx")),
        check_vma=False,
    )
```

```python
import functools

import jax
import jax.numpy as jnp
import numpy as np
from jax import lax
from jax.experimental import pallas as pl
from jax.experimental.pallas import tpu as pltpu
from jax.sharding import PartitionSpec as P

STEPS = 4
BISECT = 30


velocities = np.array(
    [
        [0, 0, 0],
        [1, 0, 0],
        [-1, 0, 0],
        [0, 1, 0],
        [0, -1, 0],
        [0, 0, 1],
        [0, 0, -1],
        [1, 1, 0],
        [-1, -1, 0],
        [1, -1, 0],
        [-1, 1, 0],
        [1, 0, 1],
        [-1, 0, -1],
        [1, 0, -1],
        [-1, 0, 1],
        [0, 1, 1],
        [0, -1, -1],
        [0, 1, -1],
        [0, -1, 1],
    ]
)
opposite = [0, 2, 1, 4, 3, 6, 5, 8, 7, 10, 9, 12, 11, 14, 13, 16, 15, 18, 17]
lattice_weights = [1.0 / 3.0] + [1.0 / 18.0] * 6 + [1.0 / 36.0] * 12
relax_rate = 0.8
inlet_speed = 0.05
alpha_most = 8.0
penalty_shape = 0.1
fluid_share = 0.4


def extended(value, sides, width):
    for axis, dim in sides:
        size, length = (lax.axis_size(axis), value.shape[dim])
        up = [(i, (i + 1) % size) for i in range(size - 1)]
        down = [(j, i) for i, j in up]
        last = lax.slice_in_dim(value, length - width, length, axis=dim)
        leading = lax.slice_in_dim(value, 0, width, axis=dim)
        before = lax.ppermute(last, axis, up)
        after = lax.ppermute(leading, axis, down)
        value = jnp.concatenate([before, value, after], axis=dim)
    return value


def equilibrium(density, speed_z, speed_y, speed_x):
    square = speed_z * speed_z + speed_y * speed_y + speed_x * speed_x
    comps = []
    for i in range(19):
        along = (
            float(velocities[i][0]) * speed_z
            + float(velocities[i][1]) * speed_y
            + float(velocities[i][2]) * speed_x
        )
        comps.append(
            lattice_weights[i] * density * (1.0 + 3.0 * along + 4.5 * along * along - 1.5 * square)
        )
    return jnp.stack(comps)


def moment(popul, axis):
    total = jnp.zeros(popul.shape[1:], popul.dtype)
    for i in range(1, 19):
        if velocities[i][axis] != 0:
            total = total + float(velocities[i][axis]) * popul[i]
    return total


def collide(popul, alpha, wall_mask, inlet_mask):
    density = jnp.sum(popul, axis=0)
    scale = density * (1.0 + alpha)
    feq = equilibrium(
        density, moment(popul, 0) / scale, moment(popul, 1) / scale, moment(popul, 2) / scale
    )
    post = popul + relax_rate * (feq - popul)
    bounce = jnp.stack([popul[opposite[i]] for i in range(19)])
    inlet_values = []
    for i in range(19):
        along = float(velocities[i][0]) * inlet_speed
        inlet_values.append(
            lattice_weights[i]
            * (1.0 + 3.0 * along + 4.5 * along * along - 1.5 * inlet_speed * inlet_speed)
        )
    inlet_feq = jnp.stack([jnp.full(popul.shape[1:], value, popul.dtype) for value in inlet_values])
    return jnp.where(wall_mask[None] > 0, bounce, jnp.where(inlet_mask[None] > 0, inlet_feq, post))


def pick(padded, sign):
    depth, rows, cols = (padded.shape[1] - 2, padded.shape[2] - 2, padded.shape[3] - 2)
    outputs = []
    for i in range(19):
        start_z = 1 - sign * int(velocities[i][0])
        start_y = 1 - sign * int(velocities[i][1])
        start_x = 1 - sign * int(velocities[i][2])
        outputs.append(
            padded[i, start_z : start_z + depth, start_y : start_y + rows, start_x : start_x + cols]
        )
    return jnp.stack(outputs)


def shift_all(popul, sign):
    padded = extended(popul, (("grp", 1), ("gy", 2), ("gx", 3)), 1)
    return pick(padded, sign)


def smooth_field(field):
    padded = extended(field, (("grp", 0), ("gy", 1), ("gx", 2)), 1)
    along_z = 0.25 * padded[:-2] + 0.5 * padded[1:-1] + 0.25 * padded[2:]
    along_y = 0.25 * along_z[:, :-2] + 0.5 * along_z[:, 1:-1] + 0.25 * along_z[:, 2:]
    return 0.25 * along_y[:, :, :-2] + 0.5 * along_y[:, :, 1:-1] + 0.25 * along_y[:, :, 2:]


def project(filtered, thresh, beta):
    denom = jnp.tanh(beta * thresh) + jnp.tanh(beta * (1.0 - thresh))
    return (jnp.tanh(beta * thresh) + jnp.tanh(beta * (filtered - thresh))) / denom


def threshold_kernel(cells, beta_ref, filtered_ref, eta_ref, raised_ref):
    beta = jnp.full((8, 128), beta_ref[0], jnp.float32)
    raised_ref[...] = jnp.exp(2.0 * beta_ref[0] * filtered_ref[...])
    top = jnp.exp(2.0 * beta)
    rows = filtered_ref.shape[0]
    span = min(rows, 512)

    def halve(step, ends):
        low, high = ends
        middle = 0.5 * (low + high)
        level = jnp.exp(2.0 * beta * middle)

        def part(index, total):
            for row in range(0, span, 8):
                raised = raised_ref[pl.ds(pl.multiple_of(index * span + row, 8), 8), :]
                total = total + (raised - 1.0) / (raised + level)
            return total

        total = lax.fori_loop(0, rows // span, part, jnp.zeros((8, 128), jnp.float32))
        volume = jnp.sum(jnp.sum(total, axis=0, keepdims=True), axis=1, keepdims=True)
        above = volume * ((top + level) / (top - 1.0)) > fluid_share * cells
        return jnp.where(above, middle, low), jnp.where(above, high, middle)

    low, high = lax.fori_loop(
        0, BISECT, halve, (jnp.zeros((8, 128), jnp.float32), jnp.ones((8, 128), jnp.float32))
    )
    eta_ref[...] = 0.5 * (low + high)


def threshold(filtered, beta, cells):
    eta = pl.pallas_call(
        functools.partial(threshold_kernel, cells),
        out_shape=jax.ShapeDtypeStruct((8, 128), jnp.float32),
        in_specs=[
            pl.BlockSpec(memory_space=pltpu.SMEM),
            pl.BlockSpec(memory_space=pltpu.VMEM),
        ],
        out_specs=pl.BlockSpec(memory_space=pltpu.VMEM),
        scratch_shapes=[pltpu.VMEM(filtered.shape, jnp.float32)],
        compiler_params=pltpu.CompilerParams(vmem_limit_bytes=40 * 2**20),
        name="threshold",
    )(beta.reshape(1), filtered)
    return eta[0, 0]


def body_by_blocks(design, populations, cotangent, wall_mask, inlet_mask, beta_step):
    beta = jnp.exp2(beta_step.astype(jnp.float32) / 16.0)
    filtered = smooth_field(design)
    cells = design.size * lax.axis_size("grp") * lax.axis_size("gy") * lax.axis_size("gx")
    devices = lax.axis_size("grp") * lax.axis_size("gy") * lax.axis_size("gx")
    copies = jnp.broadcast_to(filtered, (devices, *filtered.shape))
    everywhere = lax.all_to_all(copies, ("grp", "gy", "gx"), 0, 0)
    eta = threshold(everywhere.reshape(-1, filtered.shape[-1]), beta, cells)
    density_hat = project(filtered, eta, beta)
    alpha = alpha_most * penalty_shape * (1.0 - density_hat) / (penalty_shape + density_hat)
    states = []
    popul = populations
    for step in range(STEPS):
        states.append(popul)
        popul = shift_all(collide(popul, alpha, wall_mask, inlet_mask), 1)
    adjoint = cotangent
    alpha_grad = jnp.zeros_like(alpha)
    for step in reversed(range(STEPS)):
        back = shift_all(adjoint, -1)
        unused, pullback = jax.vjp(
            lambda p, a: collide(p, a, wall_mask, inlet_mask), states[step], alpha
        )
        adjoint, term = pullback(back)
        alpha_grad = alpha_grad + term
    denom = jnp.tanh(beta * eta) + jnp.tanh(beta * (1.0 - eta))
    slope = beta * (1.0 - jnp.tanh(beta * (filtered - eta)) ** 2) / denom
    factor = (
        -alpha_most * penalty_shape * (1.0 + penalty_shape) / (penalty_shape + density_hat) ** 2
    )
    design_grad = smooth_field(alpha_grad * factor * slope)
    return (popul, design_grad)


HALO = 8
LANES = 128
AROUND = ((1, 0), (-1, 0), (0, 1), (0, -1), (1, 1), (-1, -1), (1, -1), (-1, 1))
FIELDS = 40
PACKED = 20


def rolled(value, amount):
    amount = amount % LANES
    return value if amount == 0 else pltpu.roll(value, amount, 1)


def lane_index():
    return lax.broadcasted_iota(jnp.int32, (8, LANES), 1)


def merge(parts, width):
    lanes = lane_index()
    total = parts[0]
    for index in range(1, len(parts)):
        total = jnp.where(lanes >= index * width, parts[index], total)
    return total


def field(refs, index, layer):
    populations_ref, cotangent_ref, wall_ref, inlet_ref = refs
    if index < 19:
        return populations_ref[index, layer]
    if index < 38:
        return cotangent_ref[index - 19, layer]
    return (wall_ref if index == 38 else inlet_ref)[layer].astype(jnp.float32)


def edge_kernel(design_ref, populations_ref, cotangent_ref, wall_ref, inlet_ref, copies_ref, edges_ref):
    refs = (populations_ref, cotangent_ref, wall_ref, inlet_ref)
    me = lax.axis_index("gx")
    zero = jnp.zeros((8, LANES), jnp.float32)
    for layer in range(design_ref.shape[0]):
        for device in range(copies_ref.shape[0]):
            copies_ref[device, layer] = design_ref[layer]
        for group in range(edges_ref.shape[1]):
            first, last = [], []
            for slot in range(16):
                index = group * 16 + slot
                if index < FIELDS:
                    value = field(refs, index, layer)
                    first.append(rolled(value, 8 * slot))
                    last.append(rolled(value, 8 * slot + HALO))
                else:
                    first.append(zero)
                    last.append(zero)
            first, last = merge(first, 8), merge(last, 8)
            for device in range(edges_ref.shape[0]):
                edges_ref[device, group, layer] = jnp.where(me > device, first, last)


def window_kernel(populations_ref, cotangent_ref, wall_ref, inlet_ref, edges_ref, windows_ref):
    refs = (populations_ref, cotangent_ref, wall_ref, inlet_ref)
    me, size = lax.axis_index("gx"), edges_ref.shape[0]
    before, after = jnp.maximum(me - 1, 0), jnp.minimum(me + 1, size - 1)
    lanes = lane_index()
    column = lanes % 32
    devices = windows_ref.shape[0]
    for layer in range(wall_ref.shape[0]):
        for group in range(FIELDS // 4):
            values = [field(refs, group * 4 + slot, layer) for slot in range(4)]
            for device in range(devices):
                start = 16 * device - HALO
                window = merge([rolled(values[slot], 32 * slot - start) for slot in range(4)], 32)
                if device in (0, devices - 1):
                    source, offset = (before, 0) if device == 0 else (after, 24)
                    known = (me > 0) if device == 0 else (me < size - 1)
                    edge = edges_ref[source, group // 4, layer]
                    place = (group % 4) * 4
                    outer = merge(
                        [rolled(edge, 32 * slot + offset - 8 * (place + slot)) for slot in range(4)], 32
                    )
                    outer = jnp.where(known, outer, 0.0)
                    inside = (column >= HALO) if device == 0 else (column < 24)
                    window = jnp.where(inside, window, outer)
                windows_ref[device, group, layer] = window


def exponent(step_ref):
    steps = jnp.full((8, LANES), step_ref[0], jnp.int32).astype(jnp.float32)
    return jnp.exp2(steps / 16.0)


def plane_masks(rows):
    lanes = lane_index()
    depth, place_z, place_y = LANES // rows, lanes // rows, lanes % rows
    masks = {}
    for cz, cy in AROUND:
        inside = None
        for shift, place, count in ((cz, place_z, depth), (cy, place_y, rows)):
            if shift:
                here = (place >= 1) if shift > 0 else (place < count - 1)
                inside = here if inside is None else inside & here
        masks[cz, cy] = inside
    return masks


def plane_shift(value, cz, cy, rows, masks):
    if cz == 0 and cy == 0:
        return value
    return jnp.where(masks[cz, cy], rolled(value, cz * rows + cy), 0.0)


def plane_smooth(value, rows, masks):
    for cz, cy in ((1, 0), (0, 1)):
        value = 0.5 * value + 0.25 * (
            plane_shift(value, cz, cy, rows, masks) + plane_shift(value, -cz, -cy, rows, masks)
        )
    return value


def gather_plane(read, planes, splits):
    blocks = []
    for z in range(planes):
        for part in range(splits):
            blocks.append(read(z, part))
    return jnp.concatenate(blocks, axis=0)


def level_kernel(rows, splits, size, step_ref, copies_ref, eta_ref, window_ref, design_ref, filtered_ref, raised_ref):
    layers = copies_ref.shape[1]
    planes = LANES // rows
    columns = size * LANES
    masks = plane_masks(rows)
    zero = jnp.zeros((8, LANES), jnp.float32)
    for ref in (design_ref, filtered_ref):
        ref[0:8, :] = zero
        ref[columns + 8 : columns + 16, :] = zero
    for block in range(size):
        plane = gather_plane(
            lambda z, part: copies_ref[((z // layers) * splits + part) * size + block, z % layers],
            planes,
            splits,
        )
        design_ref[8 + block * LANES : 8 + (block + 1) * LANES, :] = plane.T
    for row in range(8, columns + 8, 8):
        design_ref[row : row + 8, :] = plane_smooth(design_ref[row : row + 8, :], rows, masks)
    beta = exponent(step_ref)
    for row in range(8, columns + 8, 8):
        value = 0.5 * design_ref[row : row + 8, :] + 0.25 * (
            design_ref[row - 1 : row + 7, :] + design_ref[row + 1 : row + 9, :]
        )
        filtered_ref[row : row + 8, :] = value
        raised_ref[row - 8 : row, :] = jnp.exp(2.0 * beta * value)
    top = jnp.exp(2.0 * beta)

    def halve(step, ends):
        low, high = ends
        middle = 0.5 * (low + high)
        level = jnp.exp(2.0 * beta * middle)
        totals = [zero] * 4
        for index, row in enumerate(range(0, columns, 8)):
            raised = raised_ref[row : row + 8, :]
            totals[index % 4] = totals[index % 4] + (raised - 1.0) / (raised + level)
        total = (totals[0] + totals[1]) + (totals[2] + totals[3])
        volume = jnp.sum(jnp.sum(total, axis=0, keepdims=True), axis=1, keepdims=True)
        above = volume * ((top + level) / (top - 1.0)) > fluid_share * (columns * LANES)
        return jnp.where(above, middle, low), jnp.where(above, high, middle)

    low, high = lax.fori_loop(0, BISECT, halve, (zero, jnp.ones((8, LANES), jnp.float32)))
    eta_ref[...] = 0.5 * (low + high)
    place = (lax.axis_index("gx") * lax.axis_size("grp") + lax.axis_index("grp")) * splits + lax.axis_index("gy")
    window_ref[...] = filtered_ref[pl.ds(pl.multiple_of(place * 16, 8), 32), :]


def flow(rho, speed):
    square = 1.0 - 1.5 * (speed[0] * speed[0] + speed[1] * speed[1] + speed[2] * speed[2])
    comps = [lattice_weights[0] * rho * square]
    weighted = {1.0 / 18.0: rho * (1.0 / 18.0), 1.0 / 36.0: rho * (1.0 / 36.0)}
    for i in range(1, 19, 2):
        along = along_of(speed, i)
        weight = weighted[lattice_weights[i]]
        even = weight * (square + 4.5 * along * along)
        odd = weight * (3.0 * along)
        comps += [even + odd, even - odd]
    return comps


def along_of(speed, i):
    total = None
    for axis in range(3):
        sign = int(velocities[i][axis])
        if sign:
            if total is None:
                total = speed[axis] if sign > 0 else -speed[axis]
            else:
                total = total + speed[axis] if sign > 0 else total - speed[axis]
    return total


def add_along(totals, value, i):
    for axis in range(3):
        sign = int(velocities[i][axis])
        if sign:
            if totals[axis] is None:
                totals[axis] = value if sign > 0 else -value
            else:
                totals[axis] = totals[axis] + value if sign > 0 else totals[axis] - value


def inlet_value(i):
    along = float(velocities[i][0]) * inlet_speed
    return lattice_weights[i] * (1.0 + 3.0 * along + 4.5 * along * along - 1.5 * inlet_speed * inlet_speed)


def flow_kernel(
    rows, splits, size, step_ref, eta_ref, filtered_ref, windows_ref, packed_ref,
    input_ref, even_ref, odd_ref, kept_ref, share_ref, grad_ref, smooth_ref, output_ref,
):
    layers = windows_ref.shape[2]
    planes = LANES // rows
    masks = plane_masks(rows)
    zero = jnp.zeros((8, LANES), jnp.float32)
    place = (lax.axis_index("gx") * lax.axis_size("grp") + lax.axis_index("grp")) * splits + lax.axis_index("gy")
    last = size * (planes // layers) * splits - 1

    def inside(value, block):
        if block == 0:
            return jnp.where(place > 0, value, 0.0)
        if block == 3:
            return jnp.where(place < last, value, 0.0)
        return value

    input_ref[0:8, :] = zero
    input_ref[FIELDS * 32 + 8 : FIELDS * 32 + 16, :] = zero
    for group in range(FIELDS // 4):
        plane = gather_plane(
            lambda z, part: windows_ref[(z // layers) * splits + part, group, z % layers],
            planes,
            splits,
        )
        input_ref[8 + group * LANES : 8 + (group + 1) * LANES, :] = plane.T

    def initial(i, row):
        return input_ref[8 + 32 * i + row : 16 + 32 * i + row, :]

    beta = exponent(step_ref)
    level = jnp.exp(2.0 * beta * eta_ref[...])
    top = jnp.exp(2.0 * beta)
    whole = (top + level) / (top - 1.0)
    for block in range(4):
        at = slice(8 * block, 8 * block + 8)
        raised = jnp.exp(2.0 * beta * filtered_ref[at, :])
        part = 1.0 / (raised + level)
        density_hat = ((raised - 1.0) * part) * whole
        strength = alpha_most * penalty_shape
        share_ref[0, at, :] = (penalty_shape + density_hat) / (
            penalty_shape + strength + (1.0 - strength) * density_hat
        )
        slope = 2.0 * beta * (raised * part) * ((level + 1.0) * part) * whole
        factor = -strength * (1.0 + penalty_shape) / (
            (penalty_shape + density_hat) * (penalty_shape + density_hat)
        )
        share_ref[1, at, :] = slope * factor

    for ref in (even_ref, odd_ref):
        for i in range(19):
            ref[i, 0:8, :] = zero
            ref[i, 40:48, :] = zero

    def arrived(ref, i, row):
        cz, cy, cx = (int(c) for c in velocities[i])
        return plane_shift(ref[i, row + 8 - cx : row + 16 - cx, :], cz, cy, rows, masks)

    buffers = (even_ref, odd_ref)
    for step in range(STEPS):
        source, target = buffers[(step + 1) % 2], buffers[step % 2]
        for block in range(4):
            row = 8 * block
            at = slice(row, row + 8)
            if step == 0:
                popul = [initial(i, row) for i in range(19)]
            else:
                popul = [arrived(source, i, row) for i in range(19)]
            wall = initial(38, row) > 0.0
            inlet = initial(39, row) > 0.0
            rho = popul[0]
            momentum = [None, None, None]
            for i in range(1, 19, 2):
                rho = rho + (popul[i] + popul[i + 1])
                add_along(momentum, popul[i] - popul[i + 1], i)
            scale = share_ref[0, at, :] / rho
            speed = [value * scale for value in momentum]
            kept_ref[step, 0, at, :] = rho
            for axis in range(3):
                kept_ref[step, 1 + axis, at, :] = speed[axis]
            settled = flow(relax_rate * rho, speed)
            for i in range(19):
                post = (1.0 - relax_rate) * popul[i] + settled[i]
                post = jnp.where(wall, popul[opposite[i]], jnp.where(inlet, inlet_value(i), post))
                target[i, row + 8 : row + 16, :] = inside(post, block)
    output_ref[16 * PACKED :, :] = jnp.zeros((3 * LANES - 16 * PACKED, LANES), jnp.float32)
    source = buffers[(STEPS - 1) % 2]
    for i in range(19):
        for row in (8, 16):
            output_ref[16 * i + row - 8 : 16 * i + row, :] = arrived(source, i, row)

    for step in reversed(range(STEPS)):
        source, target = buffers[step % 2], buffers[(step + 1) % 2]
        for block in range(4):
            row = 8 * block
            at = slice(row, row + 8)
            back = []
            for i in range(19):
                cz, cy, cx = (int(c) for c in velocities[i])
                value = initial(19 + i, row + cx) if step == STEPS - 1 else source[i, row + 8 + cx : row + 16 + cx, :]
                back.append(plane_shift(value, -cz, -cy, rows, masks))
            wall = initial(38, row) > 0.0
            inlet = initial(39, row) > 0.0
            rho = kept_ref[step, 0, at, :]
            speed = [kept_ref[step, 1 + axis, at, :] for axis in range(3)]
            square = speed[0] * speed[0] + speed[1] * speed[1] + speed[2] * speed[2]
            share = share_ref[0, at, :]
            faces, edges = None, None
            first, second = [None, None, None], [None, None, None]
            for i in range(1, 19, 2):
                both, apart = back[i] + back[i + 1], back[i] - back[i + 1]
                if i < 7:
                    faces = both if faces is None else faces + both
                    both, apart = 2.0 * both, 2.0 * apart
                else:
                    edges = both if edges is None else edges + both
                add_along(first, apart, i)
                add_along(second, along_of(speed, i) * both, i)
            mean = lattice_weights[0] * back[0] + (1.0 / 18.0) * faces + (1.0 / 36.0) * edges
            first = [value * (3.0 / 36.0) for value in first]
            second = [value * (9.0 / 36.0) for value in second]
            twice = speed[0] * second[0] + speed[1] * second[1] + speed[2] * second[2]
            once = speed[0] * first[0] + speed[1] * first[1] + speed[2] * first[2]
            drag = once + twice - 3.0 * square * mean
            term = jnp.where(wall | inlet, 0.0, -relax_rate * (rho * share * drag))
            grad_ref[at, :] = term if step == STEPS - 1 else grad_ref[at, :] + term
            if step == 0:
                continue
            rest = relax_rate * (mean * (1.0 + 1.5 * square) - 0.5 * twice)
            push = [
                (relax_rate * share) * (first[axis] + second[axis] - 3.0 * mean * speed[axis]) for axis in range(3)
            ]
            for i in range(19):
                if i == 0:
                    post = (1.0 - relax_rate) * back[0] + rest
                else:
                    way = along_of(push, i if i % 2 else i - 1)
                    post = (1.0 - relax_rate) * back[i] + (rest + way if i % 2 else rest - way)
                post = jnp.where(wall, back[opposite[i]], jnp.where(inlet, 0.0, post))
                target[i, row + 8 : row + 16, :] = inside(post, block)

    smooth_ref[0:8, :] = zero
    smooth_ref[40:48, :] = zero
    for block in range(4):
        at = slice(8 * block, 8 * block + 8)
        value = inside(grad_ref[at, :] * share_ref[1, at, :], block)
        smooth_ref[8 * block + 8 : 8 * block + 16, :] = plane_smooth(value, rows, masks)
    for row in (8, 16):
        output_ref[16 * 19 + row - 8 : 16 * 19 + row, :] = 0.5 * smooth_ref[row + 8 : row + 16, :] + 0.25 * (
            smooth_ref[row + 7 : row + 15, :] + smooth_ref[row + 9 : row + 17, :]
        )
    for group in range(packed_ref.shape[1]):
        plane = output_ref[group * LANES : (group + 1) * LANES, :].T
        for z in range(planes):
            for part in range(splits):
                at = (z * splits + part) * 8
                packed_ref[(z // layers) * splits + part, group, z % layers] = plane[at : at + 8, :]


def result_kernel(packed_ref, populations_ref, grad_ref):
    for layer in range(grad_ref.shape[0]):
        for index in range(PACKED):
            group, slot = divmod(index, 8)
            value = merge(
                [rolled(packed_ref[device, group, layer], 16 * (device - slot)) for device in range(packed_ref.shape[0])],
                16,
            )
            if index < 19:
                populations_ref[index, layer] = value
            else:
                grad_ref[layer] = value


def in_vmem(kernel, outs, name, scalars=0, scratch=()):
    vmem = pl.BlockSpec(memory_space=pltpu.VMEM)
    many = len(outs) > 1
    shapes = tuple(jax.ShapeDtypeStruct(shape, jnp.float32) for shape in outs)

    def call(*operands):
        return pl.pallas_call(
            kernel,
            out_shape=shapes if many else shapes[0],
            in_specs=[pl.BlockSpec(memory_space=pltpu.SMEM)] * scalars + [vmem] * (len(operands) - scalars),
            out_specs=(vmem,) * len(outs) if many else vmem,
            scratch_shapes=[pltpu.VMEM(shape, jnp.float32) for shape in scratch],
            compiler_params=pltpu.CompilerParams(vmem_limit_bytes=40 * 2**20),
            name=name,
        )(*operands)

    return call


def body_by_columns(design, populations, cotangent, wall_mask, inlet_mask, beta_step):
    grp, splits, size = (lax.axis_size(axis) for axis in ("grp", "gy", "gx"))
    layers, height, width = design.shape
    rows, plane = height * splits, (grp * splits)
    step = beta_step.reshape(1)
    tile = (layers, 8, LANES)
    copies, edges = in_vmem(edge_kernel, ((plane * size, *tile), (size, 3, *tile)), "edges")(
        design, populations, cotangent, wall_mask, inlet_mask
    )
    copies = lax.all_to_all(copies, ("grp", "gy", "gx"), 0, 0)
    edges = lax.all_to_all(edges, "gx", 0, 0)
    windows = in_vmem(window_kernel, ((plane, FIELDS // 4, *tile),), "windows")(
        populations, cotangent, wall_mask, inlet_mask, edges
    )
    windows = lax.all_to_all(windows, ("grp", "gy"), 0, 0)
    columns = size * LANES
    padded = (columns + 16, LANES)
    eta, filtered = in_vmem(
        functools.partial(level_kernel, rows, splits, size),
        ((8, LANES), (32, LANES)),
        "level",
        1,
        (padded, padded, (columns, LANES)),
    )(step, copies)
    packed = in_vmem(
        functools.partial(flow_kernel, rows, splits, size),
        ((plane, 3, *tile),),
        "flow",
        1,
        (
            (FIELDS * 32 + 16, LANES),
            (19, 48, LANES),
            (19, 48, LANES),
            (STEPS, 4, 32, LANES),
            (2, 32, LANES),
            (32, LANES),
            (48, LANES),
            (3 * LANES, LANES),
        ),
    )(step, eta, filtered, windows)
    packed = lax.all_to_all(packed, ("grp", "gy"), 0, 0)
    return in_vmem(result_kernel, (populations.shape, design.shape), "result")(packed)


def body(design, populations, cotangent, wall_mask, inlet_mask, beta_step):
    grp, splits = lax.axis_size("grp"), lax.axis_size("gy")
    layers, height, width = design.shape
    fits = height == 8 and width == LANES and layers * grp * height * splits == LANES
    whole = body_by_columns if fits and grp * splits * 16 == LANES else body_by_blocks
    return whole(design, populations, cotangent, wall_mask, inlet_mask, beta_step)


def solution(mesh):
    placed = (
        P("grp", "gy", "gx"),
        P(None, "grp", "gy", "gx"),
        P(None, "grp", "gy", "gx"),
        P("grp", "gy", "gx"),
        P("grp", "gy", "gx"),
        P(),
    )
    return jax.shard_map(
        body,
        mesh=mesh,
        in_specs=placed,
        out_specs=(P(None, "grp", "gy", "gx"), P("grp", "gy", "gx")),
        check_vma=False,
    )
```

```python
import functools

import jax
import jax.numpy as jnp
import numpy as np
from jax import lax
from jax.experimental import pallas as pl
from jax.experimental.pallas import tpu as pltpu
from jax.sharding import PartitionSpec as P

STEPS = 4
BISECT = 30


velocities = np.array(
    [
        [0, 0, 0],
        [1, 0, 0],
        [-1, 0, 0],
        [0, 1, 0],
        [0, -1, 0],
        [0, 0, 1],
        [0, 0, -1],
        [1, 1, 0],
        [-1, -1, 0],
        [1, -1, 0],
        [-1, 1, 0],
        [1, 0, 1],
        [-1, 0, -1],
        [1, 0, -1],
        [-1, 0, 1],
        [0, 1, 1],
        [0, -1, -1],
        [0, 1, -1],
        [0, -1, 1],
    ]
)
opposite = [0, 2, 1, 4, 3, 6, 5, 8, 7, 10, 9, 12, 11, 14, 13, 16, 15, 18, 17]
lattice_weights = [1.0 / 3.0] + [1.0 / 18.0] * 6 + [1.0 / 36.0] * 12
relax_rate = 0.8
inlet_speed = 0.05
alpha_most = 8.0
penalty_shape = 0.1
fluid_share = 0.4


def extended(value, sides, width):
    for axis, dim in sides:
        size, length = (lax.axis_size(axis), value.shape[dim])
        up = [(i, (i + 1) % size) for i in range(size - 1)]
        down = [(j, i) for i, j in up]
        last = lax.slice_in_dim(value, length - width, length, axis=dim)
        leading = lax.slice_in_dim(value, 0, width, axis=dim)
        before = lax.ppermute(last, axis, up)
        after = lax.ppermute(leading, axis, down)
        value = jnp.concatenate([before, value, after], axis=dim)
    return value


def equilibrium(density, speed_z, speed_y, speed_x):
    square = speed_z * speed_z + speed_y * speed_y + speed_x * speed_x
    comps = []
    for i in range(19):
        along = (
            float(velocities[i][0]) * speed_z
            + float(velocities[i][1]) * speed_y
            + float(velocities[i][2]) * speed_x
        )
        comps.append(
            lattice_weights[i] * density * (1.0 + 3.0 * along + 4.5 * along * along - 1.5 * square)
        )
    return jnp.stack(comps)


def moment(popul, axis):
    total = jnp.zeros(popul.shape[1:], popul.dtype)
    for i in range(1, 19):
        if velocities[i][axis] != 0:
            total = total + float(velocities[i][axis]) * popul[i]
    return total


def collide(popul, alpha, wall_mask, inlet_mask):
    density = jnp.sum(popul, axis=0)
    scale = density * (1.0 + alpha)
    feq = equilibrium(
        density, moment(popul, 0) / scale, moment(popul, 1) / scale, moment(popul, 2) / scale
    )
    post = popul + relax_rate * (feq - popul)
    bounce = jnp.stack([popul[opposite[i]] for i in range(19)])
    inlet_values = []
    for i in range(19):
        along = float(velocities[i][0]) * inlet_speed
        inlet_values.append(
            lattice_weights[i]
            * (1.0 + 3.0 * along + 4.5 * along * along - 1.5 * inlet_speed * inlet_speed)
        )
    inlet_feq = jnp.stack([jnp.full(popul.shape[1:], value, popul.dtype) for value in inlet_values])
    return jnp.where(wall_mask[None] > 0, bounce, jnp.where(inlet_mask[None] > 0, inlet_feq, post))


def pick(padded, sign):
    depth, rows, cols = (padded.shape[1] - 2, padded.shape[2] - 2, padded.shape[3] - 2)
    outputs = []
    for i in range(19):
        start_z = 1 - sign * int(velocities[i][0])
        start_y = 1 - sign * int(velocities[i][1])
        start_x = 1 - sign * int(velocities[i][2])
        outputs.append(
            padded[i, start_z : start_z + depth, start_y : start_y + rows, start_x : start_x + cols]
        )
    return jnp.stack(outputs)


def shift_all(popul, sign):
    padded = extended(popul, (("grp", 1), ("gy", 2), ("gx", 3)), 1)
    return pick(padded, sign)


def smooth_field(field):
    padded = extended(field, (("grp", 0), ("gy", 1), ("gx", 2)), 1)
    along_z = 0.25 * padded[:-2] + 0.5 * padded[1:-1] + 0.25 * padded[2:]
    along_y = 0.25 * along_z[:, :-2] + 0.5 * along_z[:, 1:-1] + 0.25 * along_z[:, 2:]
    return 0.25 * along_y[:, :, :-2] + 0.5 * along_y[:, :, 1:-1] + 0.25 * along_y[:, :, 2:]


def project(filtered, thresh, beta):
    denom = jnp.tanh(beta * thresh) + jnp.tanh(beta * (1.0 - thresh))
    return (jnp.tanh(beta * thresh) + jnp.tanh(beta * (filtered - thresh))) / denom


def threshold_kernel(cells, beta_ref, filtered_ref, eta_ref, raised_ref):
    beta = jnp.full((8, 128), beta_ref[0], jnp.float32)
    raised_ref[...] = jnp.exp(2.0 * beta_ref[0] * filtered_ref[...])
    top = jnp.exp(2.0 * beta)
    rows = filtered_ref.shape[0]
    span = min(rows, 512)

    def halve(step, ends):
        low, high = ends
        middle = 0.5 * (low + high)
        level = jnp.exp(2.0 * beta * middle)

        def part(index, total):
            for row in range(0, span, 8):
                raised = raised_ref[pl.ds(pl.multiple_of(index * span + row, 8), 8), :]
                total = total + (raised - 1.0) / (raised + level)
            return total

        total = lax.fori_loop(0, rows // span, part, jnp.zeros((8, 128), jnp.float32))
        volume = jnp.sum(jnp.sum(total, axis=0, keepdims=True), axis=1, keepdims=True)
        above = volume * ((top + level) / (top - 1.0)) > fluid_share * cells
        return jnp.where(above, middle, low), jnp.where(above, high, middle)

    low, high = lax.fori_loop(
        0, BISECT, halve, (jnp.zeros((8, 128), jnp.float32), jnp.ones((8, 128), jnp.float32))
    )
    eta_ref[...] = 0.5 * (low + high)


def threshold(filtered, beta, cells):
    eta = pl.pallas_call(
        functools.partial(threshold_kernel, cells),
        out_shape=jax.ShapeDtypeStruct((8, 128), jnp.float32),
        in_specs=[
            pl.BlockSpec(memory_space=pltpu.SMEM),
            pl.BlockSpec(memory_space=pltpu.VMEM),
        ],
        out_specs=pl.BlockSpec(memory_space=pltpu.VMEM),
        scratch_shapes=[pltpu.VMEM(filtered.shape, jnp.float32)],
        compiler_params=pltpu.CompilerParams(vmem_limit_bytes=40 * 2**20),
        name="threshold",
    )(beta.reshape(1), filtered)
    return eta[0, 0]


def body_by_blocks(design, populations, cotangent, wall_mask, inlet_mask, beta_step):
    beta = jnp.exp2(beta_step.astype(jnp.float32) / 16.0)
    filtered = smooth_field(design)
    cells = design.size * lax.axis_size("grp") * lax.axis_size("gy") * lax.axis_size("gx")
    devices = lax.axis_size("grp") * lax.axis_size("gy") * lax.axis_size("gx")
    copies = jnp.broadcast_to(filtered, (devices, *filtered.shape))
    everywhere = lax.all_to_all(copies, ("grp", "gy", "gx"), 0, 0)
    eta = threshold(everywhere.reshape(-1, filtered.shape[-1]), beta, cells)
    density_hat = project(filtered, eta, beta)
    alpha = alpha_most * penalty_shape * (1.0 - density_hat) / (penalty_shape + density_hat)
    states = []
    popul = populations
    for step in range(STEPS):
        states.append(popul)
        popul = shift_all(collide(popul, alpha, wall_mask, inlet_mask), 1)
    adjoint = cotangent
    alpha_grad = jnp.zeros_like(alpha)
    for step in reversed(range(STEPS)):
        back = shift_all(adjoint, -1)
        unused, pullback = jax.vjp(
            lambda p, a: collide(p, a, wall_mask, inlet_mask), states[step], alpha
        )
        adjoint, term = pullback(back)
        alpha_grad = alpha_grad + term
    denom = jnp.tanh(beta * eta) + jnp.tanh(beta * (1.0 - eta))
    slope = beta * (1.0 - jnp.tanh(beta * (filtered - eta)) ** 2) / denom
    factor = (
        -alpha_most * penalty_shape * (1.0 + penalty_shape) / (penalty_shape + density_hat) ** 2
    )
    design_grad = smooth_field(alpha_grad * factor * slope)
    return (popul, design_grad)


LANES = 128
AROUND = ((1, 0), (-1, 0), (0, 1), (0, -1), (1, 1), (-1, -1), (1, -1), (-1, 1))
FIELDS = 40
PACKED = 20
CLOSE = 2.0**-20


def rolled(value, amount):
    amount = amount % LANES
    return value if amount == 0 else pltpu.roll(value, amount, 1)


def lane_index():
    return lax.broadcasted_iota(jnp.int32, (8, LANES), 1)


def mixed(values):
    place = lane_index() // 16
    for half in (4, 2, 1):
        upper = (place & half) != 0
        values = [jnp.where(upper, values[(index + half) % 8], values[index]) for index in range(8)]
    return values


def pack_kernel(
    design_ref, populations_ref, cotangent_ref, wall_ref, inlet_ref, design_out_ref, packed_ref,
    fields_ref, masks_ref, sems,
):
    moves = [
        pltpu.make_async_copy(populations_ref, fields_ref.at[0:19], sems.at[0]),
        pltpu.make_async_copy(cotangent_ref, fields_ref.at[19:38], sems.at[1]),
        pltpu.make_async_copy(wall_ref, masks_ref.at[0], sems.at[2]),
        pltpu.make_async_copy(inlet_ref, masks_ref.at[1], sems.at[3]),
        pltpu.make_async_copy(design_ref, design_out_ref, sems.at[4]),
    ]
    for move in moves:
        move.start()
    for move in moves:
        move.wait()
    for layer in range(masks_ref.shape[1]):
        for group in range(FIELDS // 8):
            values = []
            for slot in range(8):
                index = group * 8 + slot
                if index < 38:
                    value = fields_ref[index, layer]
                else:
                    value = masks_ref[index - 38, layer].astype(jnp.float32)
                values.append(rolled(value, 16 * slot))
            values = mixed(values)
            for device in range(8):
                packed_ref[device, group, layer] = values[-device % 8]


def arrange_kernel(size, splits, packed_ref, *refs):
    design_refs, (body_ref, first_ref, last_ref, copies_ref) = refs[:size], refs[size:]
    layers = packed_ref.shape[2]
    planes = packed_ref.shape[0] // splits * layers
    me = lax.axis_index("grp") * splits + lax.axis_index("gy")
    for group in range(FIELDS // 8):
        plane = gather_plane(
            lambda z, part: packed_ref[(z // layers) * splits + part, group, z % layers], planes, splits
        ).T
        for slot in range(8):
            index = group * 8 + lax.rem(slot + 8 - me, 8)
            body_ref[index] = plane[16 * slot : 16 * slot + 16, :]
            first_ref[index] = plane[16 * slot : 16 * slot + 8, :]
            last_ref[index] = plane[16 * slot + 8 : 16 * slot + 16, :]
    here = lax.axis_index("gx")
    for turn in range(size):
        index = lax.rem(here + size - turn, size)
        value = design_refs[turn][...]
        for device in range(copies_ref.shape[0]):
            copies_ref[device, index] = value


def exponent(step_ref):
    steps = jnp.full((8, LANES), step_ref[0], jnp.int32).astype(jnp.float32)
    return jnp.exp2(steps / 16.0)


def plane_masks(rows):
    lanes = lane_index()
    depth, place_z, place_y = LANES // rows, lanes // rows, lanes % rows
    masks = {}
    for cz, cy in AROUND:
        inside = None
        for shift, place, count in ((cz, place_z, depth), (cy, place_y, rows)):
            if shift:
                here = (place >= 1) if shift > 0 else (place < count - 1)
                inside = here if inside is None else inside & here
        masks[cz, cy] = inside
    return masks


def plane_shift(value, cz, cy, rows, masks):
    if cz == 0 and cy == 0:
        return value
    return jnp.where(masks[cz, cy], rolled(value, cz * rows + cy), 0.0)


def plane_smooth(value, rows, masks):
    for cz, cy in ((1, 0), (0, 1)):
        value = 0.5 * value + 0.25 * (
            plane_shift(value, cz, cy, rows, masks) + plane_shift(value, -cz, -cy, rows, masks)
        )
    return value


def gather_plane(read, planes, splits):
    blocks = []
    for z in range(planes):
        for part in range(splits):
            blocks.append(read(z, part))
    return jnp.concatenate(blocks, axis=0)


def volume_root(raised_ref, columns, beta):
    zero = jnp.zeros((8, LANES), jnp.float32)
    wanted = fluid_share * (columns * LANES)
    top = jnp.exp(2.0 * beta)
    scale = 1.0 / (top - 1.0)

    def total(parts):
        value = (parts[0] + parts[1]) + (parts[2] + parts[3])
        return jnp.sum(jnp.sum(value, axis=0, keepdims=True), axis=1, keepdims=True)

    def advance(state):
        low, high, middle, _ = state
        level = jnp.exp(2.0 * beta * middle)
        sums, slopes = [zero] * 4, [zero] * 4
        for index, row in enumerate(range(0, columns, 8)):
            raised = raised_ref[row : row + 8, :]
            part = 1.0 / (raised + level)
            share = (raised - 1.0) * part
            sums[index % 4] = sums[index % 4] + share
            slopes[index % 4] = slopes[index % 4] + share * part
        volume, slope = total(sums), total(slopes)
        excess = volume * ((top + level) * scale) - wanted
        slope = (2.0 * beta * level) * (volume - (top + level) * slope) * scale
        low = jnp.where(excess > 0.0, middle, low)
        high = jnp.where(excess > 0.0, high, middle)
        guess = middle - excess / slope
        taken = (guess >= low) & (guess <= high)
        change = jnp.where(taken, jnp.abs(guess - middle), 1024.0 * (high - low))
        return low, high, jnp.where(taken, guess, 0.5 * (low + high)), change

    def going(carry):
        step, state = carry
        return (step < 64) & (jnp.max(state[3]) > CLOSE)

    state = (zero, jnp.ones((8, LANES), jnp.float32), jnp.full((8, LANES), 0.5, jnp.float32), zero)
    state = lax.fori_loop(0, 4, lambda step, state: advance(state), state)
    step, state = lax.while_loop(going, lambda carry: (carry[0] + 1, advance(carry[1])), (4, state))
    return state[2]


def filtered_level(rows, splits, size, beta, copies_ref, design_ref, filtered_ref, raised_ref, masks):
    layers = copies_ref.shape[2]
    planes = LANES // rows
    columns = size * LANES
    zero = jnp.zeros((8, LANES), jnp.float32)
    for ref in (design_ref, filtered_ref):
        ref[0:8, :] = zero
        ref[columns + 8 : columns + 16, :] = zero
    for block in range(size):
        plane = gather_plane(
            lambda z, part: copies_ref[(z // layers) * splits + part, block, z % layers], planes, splits
        )
        design_ref[8 + block * LANES : 8 + (block + 1) * LANES, :] = plane.T
    for row in range(8, columns + 8, 8):
        design_ref[row : row + 8, :] = plane_smooth(design_ref[row : row + 8, :], rows, masks)
    for row in range(8, columns + 8, 8):
        value = 0.5 * design_ref[row : row + 8, :] + 0.25 * (
            design_ref[row - 1 : row + 7, :] + design_ref[row + 1 : row + 9, :]
        )
        filtered_ref[row : row + 8, :] = value
        raised_ref[row - 8 : row, :] = jnp.exp(2.0 * beta * value)
    return volume_root(raised_ref, columns, beta)


def flow(rho, speed):
    square = 1.0 - 1.5 * (speed[0] * speed[0] + speed[1] * speed[1] + speed[2] * speed[2])
    comps = [lattice_weights[0] * rho * square]
    weighted = {1.0 / 18.0: rho * (1.0 / 18.0), 1.0 / 36.0: rho * (1.0 / 36.0)}
    for i in range(1, 19, 2):
        along = along_of(speed, i)
        weight = weighted[lattice_weights[i]]
        even = weight * (square + 4.5 * along * along)
        odd = weight * (3.0 * along)
        comps += [even + odd, even - odd]
    return comps


def along_of(speed, i):
    total = None
    for axis in range(3):
        sign = int(velocities[i][axis])
        if sign:
            if total is None:
                total = speed[axis] if sign > 0 else -speed[axis]
            else:
                total = total + speed[axis] if sign > 0 else total - speed[axis]
    return total


def add_along(totals, value, i):
    for axis in range(3):
        sign = int(velocities[i][axis])
        if sign:
            if totals[axis] is None:
                totals[axis] = value if sign > 0 else -value
            else:
                totals[axis] = totals[axis] + value if sign > 0 else totals[axis] - value


def inlet_value(i):
    along = float(velocities[i][0]) * inlet_speed
    return lattice_weights[i] * (1.0 + 3.0 * along + 4.5 * along * along - 1.5 * inlet_speed * inlet_speed)


def flow_kernel(
    rows, splits, size, step_ref, copies_ref, body_ref, before_ref, after_ref, packed_ref,
    design_ref, filtered_ref, raised_ref,
    cotangent_ref, even_ref, odd_ref, kept_ref, share_ref, grad_ref, smooth_ref, output_ref,
):
    layers = copies_ref.shape[2]
    planes = LANES // rows
    masks = plane_masks(rows)
    zero = jnp.zeros((8, LANES), jnp.float32)
    me = lax.axis_index("grp") * splits + lax.axis_index("gy")
    place = lax.axis_index("gx") * copies_ref.shape[0] + me
    last = size * copies_ref.shape[0] - 1
    beta = exponent(step_ref)
    eta = filtered_level(rows, splits, size, beta, copies_ref, design_ref, filtered_ref, raised_ref, masks)

    def inside(value, block):
        if block == 0:
            return jnp.where(place > 0, value, 0.0)
        if block == 3:
            return jnp.where(place < last, value, 0.0)
        return value

    def initial(i, row):
        if row == 0:
            return before_ref[i]
        if row == 24:
            return after_ref[i]
        return body_ref[i, row - 8 : row, :]

    level = jnp.exp(2.0 * beta * eta)
    top = jnp.exp(2.0 * beta)
    whole = (top + level) / (top - 1.0)
    for block in range(4):
        at = slice(8 * block, 8 * block + 8)
        start = pl.multiple_of(place * 16 + 8 * block, 8)
        raised = jnp.exp(2.0 * beta * filtered_ref[pl.ds(start, 8), :])
        part = 1.0 / (raised + level)
        density_hat = ((raised - 1.0) * part) * whole
        strength = alpha_most * penalty_shape
        share_ref[0, at, :] = (penalty_shape + density_hat) / (
            penalty_shape + strength + (1.0 - strength) * density_hat
        )
        slope = 2.0 * beta * (raised * part) * ((level + 1.0) * part) * whole
        factor = -strength * (1.0 + penalty_shape) / (
            (penalty_shape + density_hat) * (penalty_shape + density_hat)
        )
        share_ref[1, at, :] = slope * factor

    for ref in (even_ref, odd_ref, cotangent_ref):
        for i in range(19):
            ref[i, 0:8, :] = zero
            ref[i, 40:48, :] = zero
    for i in range(19):
        for row in range(0, 32, 8):
            cotangent_ref[i, row + 8 : row + 16, :] = initial(19 + i, row)

    def arrived(ref, i, row):
        cz, cy, cx = (int(c) for c in velocities[i])
        return plane_shift(ref[i, row + 8 - cx : row + 16 - cx, :], cz, cy, rows, masks)

    buffers = (even_ref, odd_ref)
    for step in range(STEPS):
        source, target = buffers[(step + 1) % 2], buffers[step % 2]
        for block in range(4):
            row = 8 * block
            at = slice(row, row + 8)
            if step == 0:
                popul = [initial(i, row) for i in range(19)]
            else:
                popul = [arrived(source, i, row) for i in range(19)]
            wall = initial(38, row) > 0.0
            inlet = initial(39, row) > 0.0
            rho = popul[0]
            momentum = [None, None, None]
            for i in range(1, 19, 2):
                rho = rho + (popul[i] + popul[i + 1])
                add_along(momentum, popul[i] - popul[i + 1], i)
            scale = share_ref[0, at, :] / rho
            speed = [value * scale for value in momentum]
            kept_ref[step, 0, at, :] = rho
            for axis in range(3):
                kept_ref[step, 1 + axis, at, :] = speed[axis]
            settled = flow(relax_rate * rho, speed)
            for i in range(19):
                post = (1.0 - relax_rate) * popul[i] + settled[i]
                post = jnp.where(wall, popul[opposite[i]], jnp.where(inlet, inlet_value(i), post))
                target[i, row + 8 : row + 16, :] = inside(post, block)
    def turned(index):
        return (index // 8) * LANES + 16 * lax.rem(index + me, 8)

    output_ref[16 * PACKED // LANES * LANES :, :] = jnp.zeros((LANES, LANES), jnp.float32)
    source = buffers[(STEPS - 1) % 2]
    for i in range(19):
        for row in (8, 16):
            output_ref[pl.ds(pl.multiple_of(turned(i) + row - 8, 8), 8), :] = arrived(source, i, row)

    for step in reversed(range(STEPS)):
        source = cotangent_ref if step == STEPS - 1 else buffers[step % 2]
        target = buffers[(step + 1) % 2]
        for block in range(4):
            row = 8 * block
            at = slice(row, row + 8)
            back = []
            for i in range(19):
                cz, cy, cx = (int(c) for c in velocities[i])
                value = source[i, row + 8 + cx : row + 16 + cx, :]
                back.append(plane_shift(value, -cz, -cy, rows, masks))
            wall = initial(38, row) > 0.0
            inlet = initial(39, row) > 0.0
            rho = kept_ref[step, 0, at, :]
            speed = [kept_ref[step, 1 + axis, at, :] for axis in range(3)]
            square = speed[0] * speed[0] + speed[1] * speed[1] + speed[2] * speed[2]
            share = share_ref[0, at, :]
            faces, edges = None, None
            first, second = [None, None, None], [None, None, None]
            for i in range(1, 19, 2):
                both, apart = back[i] + back[i + 1], back[i] - back[i + 1]
                if i < 7:
                    faces = both if faces is None else faces + both
                    both, apart = 2.0 * both, 2.0 * apart
                else:
                    edges = both if edges is None else edges + both
                add_along(first, apart, i)
                add_along(second, along_of(speed, i) * both, i)
            mean = lattice_weights[0] * back[0] + (1.0 / 18.0) * faces + (1.0 / 36.0) * edges
            first = [value * (3.0 / 36.0) for value in first]
            second = [value * (9.0 / 36.0) for value in second]
            twice = speed[0] * second[0] + speed[1] * second[1] + speed[2] * second[2]
            once = speed[0] * first[0] + speed[1] * first[1] + speed[2] * first[2]
            drag = once + twice - 3.0 * square * mean
            term = jnp.where(wall | inlet, 0.0, -relax_rate * (rho * share * drag))
            grad_ref[at, :] = term if step == STEPS - 1 else grad_ref[at, :] + term
            if step == 0:
                continue
            rest = relax_rate * (mean * (1.0 + 1.5 * square) - 0.5 * twice)
            push = [
                (relax_rate * share) * (first[axis] + second[axis] - 3.0 * mean * speed[axis]) for axis in range(3)
            ]
            for i in range(19):
                if i == 0:
                    post = (1.0 - relax_rate) * back[0] + rest
                else:
                    way = along_of(push, i if i % 2 else i - 1)
                    post = (1.0 - relax_rate) * back[i] + (rest + way if i % 2 else rest - way)
                post = jnp.where(wall, back[opposite[i]], jnp.where(inlet, 0.0, post))
                target[i, row + 8 : row + 16, :] = inside(post, block)

    smooth_ref[0:8, :] = zero
    smooth_ref[40:48, :] = zero
    for block in range(4):
        at = slice(8 * block, 8 * block + 8)
        value = inside(grad_ref[at, :] * share_ref[1, at, :], block)
        smooth_ref[8 * block + 8 : 8 * block + 16, :] = plane_smooth(value, rows, masks)
    for row in (8, 16):
        output_ref[pl.ds(pl.multiple_of(turned(19) + row - 8, 8), 8), :] = 0.5 * smooth_ref[row + 8 : row + 16, :] + 0.25 * (
            smooth_ref[row + 7 : row + 15, :] + smooth_ref[row + 9 : row + 17, :]
        )
    for group in range(packed_ref.shape[1]):
        plane = output_ref[group * LANES : (group + 1) * LANES, :].T
        for z in range(planes):
            for part in range(splits):
                at = (z * splits + part) * 8
                packed_ref[(z // layers) * splits + part, group, z % layers] = plane[at : at + 8, :]


def result_kernel(packed_ref, populations_ref, grad_ref):
    for layer in range(grad_ref.shape[0]):
        for group in range(packed_ref.shape[1]):
            values = mixed([packed_ref[device, group, layer] for device in range(8)])
            for slot in range(min(8, PACKED - 8 * group)):
                index, value = 8 * group + slot, rolled(values[-slot % 8], -16 * slot)
                if index < 19:
                    populations_ref[index, layer] = value
                else:
                    grad_ref[layer] = value


def call(kernel, outs, name, operands, spaces, scratch=(), room=32):
    vmem = pl.BlockSpec(memory_space=pltpu.VMEM)
    shapes = tuple(jax.ShapeDtypeStruct(shape, jnp.float32) for shape in outs)
    many = len(outs) > 1
    return pl.pallas_call(
        kernel,
        out_shape=shapes if many else shapes[0],
        in_specs=[pl.BlockSpec(memory_space=space) for space in spaces],
        out_specs=(vmem,) * len(outs) if many else vmem,
        scratch_shapes=list(scratch),
        compiler_params=pltpu.CompilerParams(vmem_limit_bytes=room * 2**20),
        name=name,
    )(*operands)


def body_by_columns(design, populations, cotangent, wall_mask, inlet_mask, beta_step):
    grp, splits, size = (lax.axis_size(axis) for axis in ("grp", "gy", "gx"))
    layers, height, width = design.shape
    rows, plane = height * splits, grp * splits
    tile = (layers, 8, LANES)
    vmem, real = pltpu.VMEM, jnp.float32
    design, packed = call(
        pack_kernel,
        (tile, (plane, FIELDS // 8, *tile)),
        "pack",
        (design, populations, cotangent, wall_mask, inlet_mask),
        [pl.ANY] * 5,
        [vmem((38, *tile), real), vmem((2, *tile), jnp.int32), pltpu.SemaphoreType.DMA((5,))],
        60,
    )
    packed = lax.all_to_all(packed, ("grp", "gy"), 0, 0)
    designs = [design]
    for turn in range(1, size):
        designs.append(lax.ppermute(design, "gx", [(i, (i + turn) % size) for i in range(size)]))
    body, first, last, copies = call(
        functools.partial(arrange_kernel, size, splits),
        ((FIELDS, 16, LANES), (FIELDS, 8, LANES), (FIELDS, 8, LANES), (plane, size, *tile)),
        "arrange",
        (packed, *designs),
        [vmem] * (1 + size),
    )
    copies = lax.all_to_all(copies, ("grp", "gy"), 0, 0)
    order = [(i % plane) * size + i // plane for i in range(size * plane)]
    up = list(zip(order[:-1], order[1:]))
    line = ("grp", "gy", "gx")
    before = lax.ppermute(last, line, up)
    after = lax.ppermute(first, line, [(j, i) for i, j in up])
    columns = size * LANES
    shapes = [
        (columns + 16, LANES),
        (columns + 16, LANES),
        (columns, LANES),
        (19, 48, LANES),
        (19, 48, LANES),
        (19, 48, LANES),
        (STEPS, 4, 32, LANES),
        (2, 32, LANES),
        (32, LANES),
        (48, LANES),
        (3 * LANES, LANES),
    ]
    packed = call(
        functools.partial(flow_kernel, rows, splits, size),
        ((plane, 3, *tile),),
        "flow",
        (beta_step.reshape(1), copies, body, before, after),
        [pltpu.SMEM] + [vmem] * 4,
        [vmem(shape, real) for shape in shapes],
    )
    packed = lax.all_to_all(packed, ("grp", "gy"), 0, 0)
    return call(result_kernel, (populations.shape, design.shape), "result", (packed,), [vmem])


def body(design, populations, cotangent, wall_mask, inlet_mask, beta_step):
    grp, splits = lax.axis_size("grp"), lax.axis_size("gy")
    layers, height, width = design.shape
    fits = height == 8 and width == LANES and layers * grp * height * splits == LANES
    whole = body_by_columns if fits and grp * splits * 16 == LANES else body_by_blocks
    return whole(design, populations, cotangent, wall_mask, inlet_mask, beta_step)


def solution(mesh):
    placed = (
        P("grp", "gy", "gx"),
        P(None, "grp", "gy", "gx"),
        P(None, "grp", "gy", "gx"),
        P("grp", "gy", "gx"),
        P("grp", "gy", "gx"),
        P(),
    )
    return jax.shard_map(
        body,
        mesh=mesh,
        in_specs=placed,
        out_specs=(P(None, "grp", "gy", "gx"), P("grp", "gy", "gx")),
        check_vma=False,
    )
```

```python
import functools

import jax
import jax.numpy as jnp
import numpy as np
from jax import lax
from jax.experimental import pallas as pl
from jax.experimental.pallas import tpu as pltpu
from jax.sharding import PartitionSpec as P

STEPS = 4
BISECT = 30


velocities = np.array(
    [
        [0, 0, 0],
        [1, 0, 0],
        [-1, 0, 0],
        [0, 1, 0],
        [0, -1, 0],
        [0, 0, 1],
        [0, 0, -1],
        [1, 1, 0],
        [-1, -1, 0],
        [1, -1, 0],
        [-1, 1, 0],
        [1, 0, 1],
        [-1, 0, -1],
        [1, 0, -1],
        [-1, 0, 1],
        [0, 1, 1],
        [0, -1, -1],
        [0, 1, -1],
        [0, -1, 1],
    ]
)
opposite = [0, 2, 1, 4, 3, 6, 5, 8, 7, 10, 9, 12, 11, 14, 13, 16, 15, 18, 17]
lattice_weights = [1.0 / 3.0] + [1.0 / 18.0] * 6 + [1.0 / 36.0] * 12
relax_rate = 0.8
inlet_speed = 0.05
alpha_most = 8.0
penalty_shape = 0.1
fluid_share = 0.4


def extended(value, sides, width):
    for axis, dim in sides:
        size, length = (lax.axis_size(axis), value.shape[dim])
        up = [(i, (i + 1) % size) for i in range(size - 1)]
        down = [(j, i) for i, j in up]
        last = lax.slice_in_dim(value, length - width, length, axis=dim)
        leading = lax.slice_in_dim(value, 0, width, axis=dim)
        before = lax.ppermute(last, axis, up)
        after = lax.ppermute(leading, axis, down)
        value = jnp.concatenate([before, value, after], axis=dim)
    return value


def equilibrium(density, speed_z, speed_y, speed_x):
    square = speed_z * speed_z + speed_y * speed_y + speed_x * speed_x
    comps = []
    for i in range(19):
        along = (
            float(velocities[i][0]) * speed_z
            + float(velocities[i][1]) * speed_y
            + float(velocities[i][2]) * speed_x
        )
        comps.append(
            lattice_weights[i] * density * (1.0 + 3.0 * along + 4.5 * along * along - 1.5 * square)
        )
    return jnp.stack(comps)


def moment(popul, axis):
    total = jnp.zeros(popul.shape[1:], popul.dtype)
    for i in range(1, 19):
        if velocities[i][axis] != 0:
            total = total + float(velocities[i][axis]) * popul[i]
    return total


def collide(popul, alpha, wall_mask, inlet_mask):
    density = jnp.sum(popul, axis=0)
    scale = density * (1.0 + alpha)
    feq = equilibrium(
        density, moment(popul, 0) / scale, moment(popul, 1) / scale, moment(popul, 2) / scale
    )
    post = popul + relax_rate * (feq - popul)
    bounce = jnp.stack([popul[opposite[i]] for i in range(19)])
    inlet_values = []
    for i in range(19):
        along = float(velocities[i][0]) * inlet_speed
        inlet_values.append(
            lattice_weights[i]
            * (1.0 + 3.0 * along + 4.5 * along * along - 1.5 * inlet_speed * inlet_speed)
        )
    inlet_feq = jnp.stack([jnp.full(popul.shape[1:], value, popul.dtype) for value in inlet_values])
    return jnp.where(wall_mask[None] > 0, bounce, jnp.where(inlet_mask[None] > 0, inlet_feq, post))


def pick(padded, sign):
    depth, rows, cols = (padded.shape[1] - 2, padded.shape[2] - 2, padded.shape[3] - 2)
    outputs = []
    for i in range(19):
        start_z = 1 - sign * int(velocities[i][0])
        start_y = 1 - sign * int(velocities[i][1])
        start_x = 1 - sign * int(velocities[i][2])
        outputs.append(
            padded[i, start_z : start_z + depth, start_y : start_y + rows, start_x : start_x + cols]
        )
    return jnp.stack(outputs)


def shift_all(popul, sign):
    padded = extended(popul, (("grp", 1), ("gy", 2), ("gx", 3)), 1)
    return pick(padded, sign)


def smooth_field(field):
    padded = extended(field, (("grp", 0), ("gy", 1), ("gx", 2)), 1)
    along_z = 0.25 * padded[:-2] + 0.5 * padded[1:-1] + 0.25 * padded[2:]
    along_y = 0.25 * along_z[:, :-2] + 0.5 * along_z[:, 1:-1] + 0.25 * along_z[:, 2:]
    return 0.25 * along_y[:, :, :-2] + 0.5 * along_y[:, :, 1:-1] + 0.25 * along_y[:, :, 2:]


def project(filtered, thresh, beta):
    denom = jnp.tanh(beta * thresh) + jnp.tanh(beta * (1.0 - thresh))
    return (jnp.tanh(beta * thresh) + jnp.tanh(beta * (filtered - thresh))) / denom


def threshold_kernel(cells, beta_ref, filtered_ref, eta_ref, raised_ref):
    beta = jnp.full((8, 128), beta_ref[0], jnp.float32)
    raised_ref[...] = jnp.exp(2.0 * beta_ref[0] * filtered_ref[...])
    top = jnp.exp(2.0 * beta)
    rows = filtered_ref.shape[0]
    span = min(rows, 512)

    def halve(step, ends):
        low, high = ends
        middle = 0.5 * (low + high)
        level = jnp.exp(2.0 * beta * middle)

        def part(index, total):
            for row in range(0, span, 8):
                raised = raised_ref[pl.ds(pl.multiple_of(index * span + row, 8), 8), :]
                total = total + (raised - 1.0) / (raised + level)
            return total

        total = lax.fori_loop(0, rows // span, part, jnp.zeros((8, 128), jnp.float32))
        volume = jnp.sum(jnp.sum(total, axis=0, keepdims=True), axis=1, keepdims=True)
        above = volume * ((top + level) / (top - 1.0)) > fluid_share * cells
        return jnp.where(above, middle, low), jnp.where(above, high, middle)

    low, high = lax.fori_loop(
        0, BISECT, halve, (jnp.zeros((8, 128), jnp.float32), jnp.ones((8, 128), jnp.float32))
    )
    eta_ref[...] = 0.5 * (low + high)


def threshold(filtered, beta, cells):
    eta = pl.pallas_call(
        functools.partial(threshold_kernel, cells),
        out_shape=jax.ShapeDtypeStruct((8, 128), jnp.float32),
        in_specs=[
            pl.BlockSpec(memory_space=pltpu.SMEM),
            pl.BlockSpec(memory_space=pltpu.VMEM),
        ],
        out_specs=pl.BlockSpec(memory_space=pltpu.VMEM),
        scratch_shapes=[pltpu.VMEM(filtered.shape, jnp.float32)],
        compiler_params=pltpu.CompilerParams(vmem_limit_bytes=40 * 2**20),
        name="threshold",
    )(beta.reshape(1), filtered)
    return eta[0, 0]


def body_by_blocks(design, populations, cotangent, wall_mask, inlet_mask, beta_step):
    beta = jnp.exp2(beta_step.astype(jnp.float32) / 16.0)
    filtered = smooth_field(design)
    cells = design.size * lax.axis_size("grp") * lax.axis_size("gy") * lax.axis_size("gx")
    devices = lax.axis_size("grp") * lax.axis_size("gy") * lax.axis_size("gx")
    copies = jnp.broadcast_to(filtered, (devices, *filtered.shape))
    everywhere = lax.all_to_all(copies, ("grp", "gy", "gx"), 0, 0)
    eta = threshold(everywhere.reshape(-1, filtered.shape[-1]), beta, cells)
    density_hat = project(filtered, eta, beta)
    alpha = alpha_most * penalty_shape * (1.0 - density_hat) / (penalty_shape + density_hat)
    states = []
    popul = populations
    for step in range(STEPS):
        states.append(popul)
        popul = shift_all(collide(popul, alpha, wall_mask, inlet_mask), 1)
    adjoint = cotangent
    alpha_grad = jnp.zeros_like(alpha)
    for step in reversed(range(STEPS)):
        back = shift_all(adjoint, -1)
        unused, pullback = jax.vjp(
            lambda p, a: collide(p, a, wall_mask, inlet_mask), states[step], alpha
        )
        adjoint, term = pullback(back)
        alpha_grad = alpha_grad + term
    denom = jnp.tanh(beta * eta) + jnp.tanh(beta * (1.0 - eta))
    slope = beta * (1.0 - jnp.tanh(beta * (filtered - eta)) ** 2) / denom
    factor = (
        -alpha_most * penalty_shape * (1.0 + penalty_shape) / (penalty_shape + density_hat) ** 2
    )
    design_grad = smooth_field(alpha_grad * factor * slope)
    return (popul, design_grad)


LANES = 128
AROUND = ((1, 0), (-1, 0), (0, 1), (0, -1), (1, 1), (-1, -1), (1, -1), (-1, 1))
FIELDS = 40
PACKED = 20
CLOSE = 2.0**-20


def rolled(value, amount):
    amount = amount % LANES
    return value if amount == 0 else pltpu.roll(value, amount, 1)


def lane_index():
    return lax.broadcasted_iota(jnp.int32, (8, LANES), 1)


def on_path(index, grp, splits):
    part, step = index // grp, index % grp
    return (step if part % 2 == 0 else grp - 1 - step) * splits + part


def device_at(index, grp, splits):
    odd = lax.rem(lax.axis_index("gx"), 2)
    return jnp.where(odd == 0, on_path(index, grp, splits), on_path(grp * splits - 1 - index, grp, splits))


def block_here(grp, splits):
    step, part = lax.axis_index("grp"), lax.axis_index("gy")
    index = part * grp + jnp.where(lax.rem(part, 2) == 0, step, grp - 1 - step)
    return jnp.where(lax.rem(lax.axis_index("gx"), 2) == 0, index, grp * splits - 1 - index)


def mixed(values):
    place = lane_index() // 16
    for half in (4, 2, 1):
        upper = (place & half) != 0
        values = [jnp.where(upper, values[(index + half) % 8], values[index]) for index in range(8)]
    return values


def pack_kernel(
    splits, design_ref, populations_ref, cotangent_ref, wall_ref, inlet_ref, design_out_ref, packed_ref,
    fields_ref, masks_ref, sems,
):
    moves = [
        pltpu.make_async_copy(populations_ref, fields_ref.at[0:19], sems.at[0]),
        pltpu.make_async_copy(cotangent_ref, fields_ref.at[19:38], sems.at[1]),
        pltpu.make_async_copy(wall_ref, masks_ref.at[0], sems.at[2]),
        pltpu.make_async_copy(inlet_ref, masks_ref.at[1], sems.at[3]),
        pltpu.make_async_copy(design_ref, design_out_ref, sems.at[4]),
    ]
    for move in moves:
        move.start()
    for move in moves:
        move.wait()
    devices = [device_at(index, 8 // splits, splits) for index in range(8)]
    for layer in range(masks_ref.shape[1]):
        for group in range(FIELDS // 8):
            values = []
            for slot in range(8):
                index = group * 8 + slot
                if index < 38:
                    value = fields_ref[index, layer]
                else:
                    value = masks_ref[index - 38, layer].astype(jnp.float32)
                values.append(rolled(value, 16 * slot))
            values = mixed(values)
            for index in range(8):
                packed_ref[devices[index], group, layer] = values[-index % 8]


def arrange_kernel(size, splits, packed_ref, *refs):
    design_refs, (body_ref, first_ref, last_ref, copies_ref) = refs[:size], refs[size:]
    layers = packed_ref.shape[2]
    planes = packed_ref.shape[0] // splits * layers
    me = block_here(packed_ref.shape[0] // splits, splits)
    for group in range(FIELDS // 8):
        plane = gather_plane(
            lambda z, part: packed_ref[(z // layers) * splits + part, group, z % layers], planes, splits
        ).T
        for slot in range(8):
            index = group * 8 + lax.rem(slot + 8 - me, 8)
            body_ref[index] = plane[16 * slot : 16 * slot + 16, :]
            first_ref[index] = plane[16 * slot : 16 * slot + 8, :]
            last_ref[index] = plane[16 * slot + 8 : 16 * slot + 16, :]
    here = lax.axis_index("gx")
    for turn in range(size):
        index = lax.rem(here + size - turn, size)
        value = design_refs[turn][...]
        for device in range(copies_ref.shape[0]):
            copies_ref[device, index] = value


def exponent(step_ref):
    steps = jnp.full((8, LANES), step_ref[0], jnp.int32).astype(jnp.float32)
    return jnp.exp2(steps / 16.0)


def plane_masks(rows):
    lanes = lane_index()
    depth, place_z, place_y = LANES // rows, lanes // rows, lanes % rows
    masks = {}
    for cz, cy in AROUND:
        inside = None
        for shift, place, count in ((cz, place_z, depth), (cy, place_y, rows)):
            if shift:
                here = (place >= 1) if shift > 0 else (place < count - 1)
                inside = here if inside is None else inside & here
        masks[cz, cy] = inside
    return masks


def plane_shift(value, cz, cy, rows, masks):
    if cz == 0 and cy == 0:
        return value
    return jnp.where(masks[cz, cy], rolled(value, cz * rows + cy), 0.0)


def plane_smooth(value, rows, masks):
    for cz, cy in ((1, 0), (0, 1)):
        value = 0.5 * value + 0.25 * (
            plane_shift(value, cz, cy, rows, masks) + plane_shift(value, -cz, -cy, rows, masks)
        )
    return value


def gather_plane(read, planes, splits):
    blocks = []
    for z in range(planes):
        for part in range(splits):
            blocks.append(read(z, part))
    return jnp.concatenate(blocks, axis=0)


def volume_root(raised_ref, columns, beta):
    zero = jnp.zeros((8, LANES), jnp.float32)
    wanted = fluid_share * (columns * LANES)
    top = jnp.exp(2.0 * beta)
    scale = 1.0 / (top - 1.0)

    def total(parts):
        value = (parts[0] + parts[1]) + (parts[2] + parts[3])
        return jnp.sum(jnp.sum(value, axis=0, keepdims=True), axis=1, keepdims=True)

    def advance(state):
        low, high, middle, _ = state
        level = jnp.exp(2.0 * beta * middle)
        sums, slopes = [zero] * 4, [zero] * 4
        for index, row in enumerate(range(0, columns, 8)):
            raised = raised_ref[row : row + 8, :]
            part = 1.0 / (raised + level)
            share = (raised - 1.0) * part
            sums[index % 4] = sums[index % 4] + share
            slopes[index % 4] = slopes[index % 4] + share * part
        volume, slope = total(sums), total(slopes)
        excess = volume * ((top + level) * scale) - wanted
        slope = (2.0 * beta * level) * (volume - (top + level) * slope) * scale
        low = jnp.where(excess > 0.0, middle, low)
        high = jnp.where(excess > 0.0, high, middle)
        guess = middle - excess / slope
        taken = (guess >= low) & (guess <= high)
        change = jnp.where(taken, jnp.abs(guess - middle), 1024.0 * (high - low))
        return low, high, jnp.where(taken, guess, 0.5 * (low + high)), change

    def going(carry):
        step, state = carry
        return (step < 64) & (jnp.max(state[3]) > CLOSE)

    state = (zero, jnp.ones((8, LANES), jnp.float32), jnp.full((8, LANES), 0.5, jnp.float32), zero)
    state = lax.fori_loop(0, 4, lambda step, state: advance(state), state)
    step, state = lax.while_loop(going, lambda carry: (carry[0] + 1, advance(carry[1])), (4, state))
    return state[2]


def filtered_level(rows, splits, size, beta, copies_ref, design_ref, filtered_ref, raised_ref, masks):
    layers = copies_ref.shape[2]
    planes = LANES // rows
    columns = size * LANES
    zero = jnp.zeros((8, LANES), jnp.float32)
    for ref in (design_ref, filtered_ref):
        ref[0:8, :] = zero
        ref[columns + 8 : columns + 16, :] = zero
    for block in range(size):
        plane = gather_plane(
            lambda z, part: copies_ref[(z // layers) * splits + part, block, z % layers], planes, splits
        )
        design_ref[8 + block * LANES : 8 + (block + 1) * LANES, :] = plane.T
    for row in range(8, columns + 8, 8):
        design_ref[row : row + 8, :] = plane_smooth(design_ref[row : row + 8, :], rows, masks)
    for row in range(8, columns + 8, 8):
        value = 0.5 * design_ref[row : row + 8, :] + 0.25 * (
            design_ref[row - 1 : row + 7, :] + design_ref[row + 1 : row + 9, :]
        )
        filtered_ref[row : row + 8, :] = value
        raised_ref[row - 8 : row, :] = jnp.exp(2.0 * beta * value)
    return volume_root(raised_ref, columns, beta)


def flow(rho, speed):
    square = 1.0 - 1.5 * (speed[0] * speed[0] + speed[1] * speed[1] + speed[2] * speed[2])
    comps = [lattice_weights[0] * rho * square]
    weighted = {1.0 / 18.0: rho * (1.0 / 18.0), 1.0 / 36.0: rho * (1.0 / 36.0)}
    for i in range(1, 19, 2):
        along = along_of(speed, i)
        weight = weighted[lattice_weights[i]]
        even = weight * (square + 4.5 * along * along)
        odd = weight * (3.0 * along)
        comps += [even + odd, even - odd]
    return comps


def along_of(speed, i):
    total = None
    for axis in range(3):
        sign = int(velocities[i][axis])
        if sign:
            if total is None:
                total = speed[axis] if sign > 0 else -speed[axis]
            else:
                total = total + speed[axis] if sign > 0 else total - speed[axis]
    return total


def add_along(totals, value, i):
    for axis in range(3):
        sign = int(velocities[i][axis])
        if sign:
            if totals[axis] is None:
                totals[axis] = value if sign > 0 else -value
            else:
                totals[axis] = totals[axis] + value if sign > 0 else totals[axis] - value


def inlet_value(i):
    along = float(velocities[i][0]) * inlet_speed
    return lattice_weights[i] * (1.0 + 3.0 * along + 4.5 * along * along - 1.5 * inlet_speed * inlet_speed)


def flow_kernel(
    rows, splits, size, step_ref, copies_ref, body_ref, before_ref, after_ref, packed_ref,
    design_ref, filtered_ref, raised_ref,
    cotangent_ref, even_ref, odd_ref, kept_ref, share_ref, grad_ref, smooth_ref, output_ref,
):
    layers = copies_ref.shape[2]
    planes = LANES // rows
    masks = plane_masks(rows)
    zero = jnp.zeros((8, LANES), jnp.float32)
    me = block_here(copies_ref.shape[0] // splits, splits)
    place = lax.axis_index("gx") * copies_ref.shape[0] + me
    last = size * copies_ref.shape[0] - 1
    beta = exponent(step_ref)
    eta = filtered_level(rows, splits, size, beta, copies_ref, design_ref, filtered_ref, raised_ref, masks)

    def inside(value, block):
        if block == 0:
            return jnp.where(place > 0, value, 0.0)
        if block == 3:
            return jnp.where(place < last, value, 0.0)
        return value

    def initial(i, row):
        if row == 0:
            return before_ref[i]
        if row == 24:
            return after_ref[i]
        return body_ref[i, row - 8 : row, :]

    level = jnp.exp(2.0 * beta * eta)
    top = jnp.exp(2.0 * beta)
    whole = (top + level) / (top - 1.0)
    for block in range(4):
        at = slice(8 * block, 8 * block + 8)
        start = pl.multiple_of(place * 16 + 8 * block, 8)
        raised = jnp.exp(2.0 * beta * filtered_ref[pl.ds(start, 8), :])
        part = 1.0 / (raised + level)
        density_hat = ((raised - 1.0) * part) * whole
        strength = alpha_most * penalty_shape
        share_ref[0, at, :] = (penalty_shape + density_hat) / (
            penalty_shape + strength + (1.0 - strength) * density_hat
        )
        slope = 2.0 * beta * (raised * part) * ((level + 1.0) * part) * whole
        factor = -strength * (1.0 + penalty_shape) / (
            (penalty_shape + density_hat) * (penalty_shape + density_hat)
        )
        share_ref[1, at, :] = slope * factor

    for ref in (even_ref, odd_ref, cotangent_ref):
        for i in range(19):
            ref[i, 0:8, :] = zero
            ref[i, 40:48, :] = zero
    for i in range(19):
        for row in range(0, 32, 8):
            cotangent_ref[i, row + 8 : row + 16, :] = initial(19 + i, row)

    def arrived(ref, i, row):
        cz, cy, cx = (int(c) for c in velocities[i])
        return plane_shift(ref[i, row + 8 - cx : row + 16 - cx, :], cz, cy, rows, masks)

    buffers = (even_ref, odd_ref)
    for step in range(STEPS):
        source, target = buffers[(step + 1) % 2], buffers[step % 2]
        for block in range(4):
            row = 8 * block
            at = slice(row, row + 8)
            if step == 0:
                popul = [initial(i, row) for i in range(19)]
            else:
                popul = [arrived(source, i, row) for i in range(19)]
            wall = initial(38, row) > 0.0
            inlet = initial(39, row) > 0.0
            rho = popul[0]
            momentum = [None, None, None]
            for i in range(1, 19, 2):
                rho = rho + (popul[i] + popul[i + 1])
                add_along(momentum, popul[i] - popul[i + 1], i)
            scale = share_ref[0, at, :] / rho
            speed = [value * scale for value in momentum]
            kept_ref[step, 0, at, :] = rho
            for axis in range(3):
                kept_ref[step, 1 + axis, at, :] = speed[axis]
            settled = flow(relax_rate * rho, speed)
            for i in range(19):
                post = (1.0 - relax_rate) * popul[i] + settled[i]
                post = jnp.where(wall, popul[opposite[i]], jnp.where(inlet, inlet_value(i), post))
                target[i, row + 8 : row + 16, :] = inside(post, block)
    def turned(index):
        return (index // 8) * LANES + 16 * lax.rem(index + me, 8)

    output_ref[16 * PACKED // LANES * LANES :, :] = jnp.zeros((LANES, LANES), jnp.float32)
    source = buffers[(STEPS - 1) % 2]
    for i in range(19):
        for row in (8, 16):
            output_ref[pl.ds(pl.multiple_of(turned(i) + row - 8, 8), 8), :] = arrived(source, i, row)

    for step in reversed(range(STEPS)):
        source = cotangent_ref if step == STEPS - 1 else buffers[step % 2]
        target = buffers[(step + 1) % 2]
        for block in range(4):
            row = 8 * block
            at = slice(row, row + 8)
            back = []
            for i in range(19):
                cz, cy, cx = (int(c) for c in velocities[i])
                value = source[i, row + 8 + cx : row + 16 + cx, :]
                back.append(plane_shift(value, -cz, -cy, rows, masks))
            wall = initial(38, row) > 0.0
            inlet = initial(39, row) > 0.0
            rho = kept_ref[step, 0, at, :]
            speed = [kept_ref[step, 1 + axis, at, :] for axis in range(3)]
            square = speed[0] * speed[0] + speed[1] * speed[1] + speed[2] * speed[2]
            share = share_ref[0, at, :]
            faces, edges = None, None
            first, second = [None, None, None], [None, None, None]
            for i in range(1, 19, 2):
                both, apart = back[i] + back[i + 1], back[i] - back[i + 1]
                if i < 7:
                    faces = both if faces is None else faces + both
                    both, apart = 2.0 * both, 2.0 * apart
                else:
                    edges = both if edges is None else edges + both
                add_along(first, apart, i)
                add_along(second, along_of(speed, i) * both, i)
            mean = lattice_weights[0] * back[0] + (1.0 / 18.0) * faces + (1.0 / 36.0) * edges
            first = [value * (3.0 / 36.0) for value in first]
            second = [value * (9.0 / 36.0) for value in second]
            twice = speed[0] * second[0] + speed[1] * second[1] + speed[2] * second[2]
            once = speed[0] * first[0] + speed[1] * first[1] + speed[2] * first[2]
            drag = once + twice - 3.0 * square * mean
            term = jnp.where(wall | inlet, 0.0, -relax_rate * (rho * share * drag))
            grad_ref[at, :] = term if step == STEPS - 1 else grad_ref[at, :] + term
            if step == 0:
                continue
            rest = relax_rate * (mean * (1.0 + 1.5 * square) - 0.5 * twice)
            push = [
                (relax_rate * share) * (first[axis] + second[axis] - 3.0 * mean * speed[axis]) for axis in range(3)
            ]
            for i in range(19):
                if i == 0:
                    post = (1.0 - relax_rate) * back[0] + rest
                else:
                    way = along_of(push, i if i % 2 else i - 1)
                    post = (1.0 - relax_rate) * back[i] + (rest + way if i % 2 else rest - way)
                post = jnp.where(wall, back[opposite[i]], jnp.where(inlet, 0.0, post))
                target[i, row + 8 : row + 16, :] = inside(post, block)

    smooth_ref[0:8, :] = zero
    smooth_ref[40:48, :] = zero
    for block in range(4):
        at = slice(8 * block, 8 * block + 8)
        value = inside(grad_ref[at, :] * share_ref[1, at, :], block)
        smooth_ref[8 * block + 8 : 8 * block + 16, :] = plane_smooth(value, rows, masks)
    for row in (8, 16):
        output_ref[pl.ds(pl.multiple_of(turned(19) + row - 8, 8), 8), :] = 0.5 * smooth_ref[row + 8 : row + 16, :] + 0.25 * (
            smooth_ref[row + 7 : row + 15, :] + smooth_ref[row + 9 : row + 17, :]
        )
    for group in range(packed_ref.shape[1]):
        plane = output_ref[group * LANES : (group + 1) * LANES, :].T
        for z in range(planes):
            for part in range(splits):
                at = (z * splits + part) * 8
                packed_ref[(z // layers) * splits + part, group, z % layers] = plane[at : at + 8, :]


def result_kernel(splits, packed_ref, populations_ref, grad_ref):
    devices = [device_at(index, 8 // splits, splits) for index in range(8)]
    for layer in range(grad_ref.shape[0]):
        for group in range(packed_ref.shape[1]):
            values = mixed([packed_ref[device, group, layer] for device in devices])
            for slot in range(min(8, PACKED - 8 * group)):
                index, value = 8 * group + slot, rolled(values[-slot % 8], -16 * slot)
                if index < 19:
                    populations_ref[index, layer] = value
                else:
                    grad_ref[layer] = value


def call(kernel, outs, name, operands, spaces, scratch=(), room=32):
    vmem = pl.BlockSpec(memory_space=pltpu.VMEM)
    shapes = tuple(jax.ShapeDtypeStruct(shape, jnp.float32) for shape in outs)
    many = len(outs) > 1
    return pl.pallas_call(
        kernel,
        out_shape=shapes if many else shapes[0],
        in_specs=[pl.BlockSpec(memory_space=space) for space in spaces],
        out_specs=(vmem,) * len(outs) if many else vmem,
        scratch_shapes=list(scratch),
        compiler_params=pltpu.CompilerParams(vmem_limit_bytes=room * 2**20),
        name=name,
    )(*operands)


def body_by_columns(design, populations, cotangent, wall_mask, inlet_mask, beta_step):
    grp, splits, size = (lax.axis_size(axis) for axis in ("grp", "gy", "gx"))
    layers, height, width = design.shape
    rows, plane = height * splits, grp * splits
    tile = (layers, 8, LANES)
    vmem, real = pltpu.VMEM, jnp.float32
    design, packed = call(
        functools.partial(pack_kernel, splits),
        (tile, (plane, FIELDS // 8, *tile)),
        "pack",
        (design, populations, cotangent, wall_mask, inlet_mask),
        [pl.ANY] * 5,
        [vmem((38, *tile), real), vmem((2, *tile), jnp.int32), pltpu.SemaphoreType.DMA((5,))],
        60,
    )
    packed = lax.all_to_all(packed, ("grp", "gy"), 0, 0)
    designs = [design]
    for turn in range(1, size):
        designs.append(lax.ppermute(design, "gx", [(i, (i + turn) % size) for i in range(size)]))
    body, first, last, copies = call(
        functools.partial(arrange_kernel, size, splits),
        ((FIELDS, 16, LANES), (FIELDS, 8, LANES), (FIELDS, 8, LANES), (plane, size, *tile)),
        "arrange",
        (packed, *designs),
        [vmem] * (1 + size),
    )
    copies = lax.all_to_all(copies, ("grp", "gy"), 0, 0)
    path = [on_path(index, grp, splits) for index in range(plane)]
    order = [(path if gx % 2 == 0 else path[::-1])[index] * size + gx for gx in range(size) for index in range(plane)]
    up = list(zip(order[:-1], order[1:]))
    line = ("grp", "gy", "gx")
    before = lax.ppermute(last, line, up)
    after = lax.ppermute(first, line, [(j, i) for i, j in up])
    columns = size * LANES
    shapes = [
        (columns + 16, LANES),
        (columns + 16, LANES),
        (columns, LANES),
        (19, 48, LANES),
        (19, 48, LANES),
        (19, 48, LANES),
        (STEPS, 4, 32, LANES),
        (2, 32, LANES),
        (32, LANES),
        (48, LANES),
        (3 * LANES, LANES),
    ]
    packed = call(
        functools.partial(flow_kernel, rows, splits, size),
        ((plane, 3, *tile),),
        "flow",
        (beta_step.reshape(1), copies, body, before, after),
        [pltpu.SMEM] + [vmem] * 4,
        [vmem(shape, real) for shape in shapes],
    )
    packed = lax.all_to_all(packed, ("grp", "gy"), 0, 0)
    return call(functools.partial(result_kernel, splits), (populations.shape, design.shape), "result", (packed,), [vmem])


def body(design, populations, cotangent, wall_mask, inlet_mask, beta_step):
    grp, splits = lax.axis_size("grp"), lax.axis_size("gy")
    layers, height, width = design.shape
    fits = height == 8 and width == LANES and layers * grp * height * splits == LANES
    whole = body_by_columns if fits and grp * splits * 16 == LANES else body_by_blocks
    return whole(design, populations, cotangent, wall_mask, inlet_mask, beta_step)


def solution(mesh):
    placed = (
        P("grp", "gy", "gx"),
        P(None, "grp", "gy", "gx"),
        P(None, "grp", "gy", "gx"),
        P("grp", "gy", "gx"),
        P("grp", "gy", "gx"),
        P(),
    )
    return jax.shard_map(
        body,
        mesh=mesh,
        in_specs=placed,
        out_specs=(P(None, "grp", "gy", "gx"), P("grp", "gy", "gx")),
        check_vma=False,
    )
```

```python
import functools

import jax
import jax.numpy as jnp
import numpy as np
from jax import lax
from jax.experimental import pallas as pl
from jax.experimental.pallas import tpu as pltpu
from jax.sharding import PartitionSpec as P

STEPS = 4
BISECT = 30


velocities = np.array(
    [
        [0, 0, 0],
        [1, 0, 0],
        [-1, 0, 0],
        [0, 1, 0],
        [0, -1, 0],
        [0, 0, 1],
        [0, 0, -1],
        [1, 1, 0],
        [-1, -1, 0],
        [1, -1, 0],
        [-1, 1, 0],
        [1, 0, 1],
        [-1, 0, -1],
        [1, 0, -1],
        [-1, 0, 1],
        [0, 1, 1],
        [0, -1, -1],
        [0, 1, -1],
        [0, -1, 1],
    ]
)
opposite = [0, 2, 1, 4, 3, 6, 5, 8, 7, 10, 9, 12, 11, 14, 13, 16, 15, 18, 17]
lattice_weights = [1.0 / 3.0] + [1.0 / 18.0] * 6 + [1.0 / 36.0] * 12
relax_rate = 0.8
inlet_speed = 0.05
alpha_most = 8.0
penalty_shape = 0.1
fluid_share = 0.4


def extended(value, sides, width):
    for axis, dim in sides:
        size, length = (lax.axis_size(axis), value.shape[dim])
        up = [(i, (i + 1) % size) for i in range(size - 1)]
        down = [(j, i) for i, j in up]
        last = lax.slice_in_dim(value, length - width, length, axis=dim)
        leading = lax.slice_in_dim(value, 0, width, axis=dim)
        before = lax.ppermute(last, axis, up)
        after = lax.ppermute(leading, axis, down)
        value = jnp.concatenate([before, value, after], axis=dim)
    return value


def equilibrium(density, speed_z, speed_y, speed_x):
    square = speed_z * speed_z + speed_y * speed_y + speed_x * speed_x
    comps = []
    for i in range(19):
        along = (
            float(velocities[i][0]) * speed_z
            + float(velocities[i][1]) * speed_y
            + float(velocities[i][2]) * speed_x
        )
        comps.append(
            lattice_weights[i] * density * (1.0 + 3.0 * along + 4.5 * along * along - 1.5 * square)
        )
    return jnp.stack(comps)


def moment(popul, axis):
    total = jnp.zeros(popul.shape[1:], popul.dtype)
    for i in range(1, 19):
        if velocities[i][axis] != 0:
            total = total + float(velocities[i][axis]) * popul[i]
    return total


def collide(popul, alpha, wall_mask, inlet_mask):
    density = jnp.sum(popul, axis=0)
    scale = density * (1.0 + alpha)
    feq = equilibrium(
        density, moment(popul, 0) / scale, moment(popul, 1) / scale, moment(popul, 2) / scale
    )
    post = popul + relax_rate * (feq - popul)
    bounce = jnp.stack([popul[opposite[i]] for i in range(19)])
    inlet_values = []
    for i in range(19):
        along = float(velocities[i][0]) * inlet_speed
        inlet_values.append(
            lattice_weights[i]
            * (1.0 + 3.0 * along + 4.5 * along * along - 1.5 * inlet_speed * inlet_speed)
        )
    inlet_feq = jnp.stack([jnp.full(popul.shape[1:], value, popul.dtype) for value in inlet_values])
    return jnp.where(wall_mask[None] > 0, bounce, jnp.where(inlet_mask[None] > 0, inlet_feq, post))


def pick(padded, sign):
    depth, rows, cols = (padded.shape[1] - 2, padded.shape[2] - 2, padded.shape[3] - 2)
    outputs = []
    for i in range(19):
        start_z = 1 - sign * int(velocities[i][0])
        start_y = 1 - sign * int(velocities[i][1])
        start_x = 1 - sign * int(velocities[i][2])
        outputs.append(
            padded[i, start_z : start_z + depth, start_y : start_y + rows, start_x : start_x + cols]
        )
    return jnp.stack(outputs)


def shift_all(popul, sign):
    padded = extended(popul, (("grp", 1), ("gy", 2), ("gx", 3)), 1)
    return pick(padded, sign)


def smooth_field(field):
    padded = extended(field, (("grp", 0), ("gy", 1), ("gx", 2)), 1)
    along_z = 0.25 * padded[:-2] + 0.5 * padded[1:-1] + 0.25 * padded[2:]
    along_y = 0.25 * along_z[:, :-2] + 0.5 * along_z[:, 1:-1] + 0.25 * along_z[:, 2:]
    return 0.25 * along_y[:, :, :-2] + 0.5 * along_y[:, :, 1:-1] + 0.25 * along_y[:, :, 2:]


def project(filtered, thresh, beta):
    denom = jnp.tanh(beta * thresh) + jnp.tanh(beta * (1.0 - thresh))
    return (jnp.tanh(beta * thresh) + jnp.tanh(beta * (filtered - thresh))) / denom


def threshold_kernel(cells, beta_ref, filtered_ref, eta_ref, raised_ref):
    beta = jnp.full((8, 128), beta_ref[0], jnp.float32)
    raised_ref[...] = jnp.exp(2.0 * beta_ref[0] * filtered_ref[...])
    top = jnp.exp(2.0 * beta)
    rows = filtered_ref.shape[0]
    span = min(rows, 512)

    def halve(step, ends):
        low, high = ends
        middle = 0.5 * (low + high)
        level = jnp.exp(2.0 * beta * middle)

        def part(index, total):
            for row in range(0, span, 8):
                raised = raised_ref[pl.ds(pl.multiple_of(index * span + row, 8), 8), :]
                total = total + (raised - 1.0) / (raised + level)
            return total

        total = lax.fori_loop(0, rows // span, part, jnp.zeros((8, 128), jnp.float32))
        volume = jnp.sum(jnp.sum(total, axis=0, keepdims=True), axis=1, keepdims=True)
        above = volume * ((top + level) / (top - 1.0)) > fluid_share * cells
        return jnp.where(above, middle, low), jnp.where(above, high, middle)

    low, high = lax.fori_loop(
        0, BISECT, halve, (jnp.zeros((8, 128), jnp.float32), jnp.ones((8, 128), jnp.float32))
    )
    eta_ref[...] = 0.5 * (low + high)


def threshold(filtered, beta, cells):
    eta = pl.pallas_call(
        functools.partial(threshold_kernel, cells),
        out_shape=jax.ShapeDtypeStruct((8, 128), jnp.float32),
        in_specs=[
            pl.BlockSpec(memory_space=pltpu.SMEM),
            pl.BlockSpec(memory_space=pltpu.VMEM),
        ],
        out_specs=pl.BlockSpec(memory_space=pltpu.VMEM),
        scratch_shapes=[pltpu.VMEM(filtered.shape, jnp.float32)],
        compiler_params=pltpu.CompilerParams(vmem_limit_bytes=40 * 2**20),
        name="threshold",
    )(beta.reshape(1), filtered)
    return eta[0, 0]


def body_by_blocks(design, populations, cotangent, wall_mask, inlet_mask, beta_step):
    beta = jnp.exp2(beta_step.astype(jnp.float32) / 16.0)
    filtered = smooth_field(design)
    cells = design.size * lax.axis_size("grp") * lax.axis_size("gy") * lax.axis_size("gx")
    devices = lax.axis_size("grp") * lax.axis_size("gy") * lax.axis_size("gx")
    copies = jnp.broadcast_to(filtered, (devices, *filtered.shape))
    everywhere = lax.all_to_all(copies, ("grp", "gy", "gx"), 0, 0)
    eta = threshold(everywhere.reshape(-1, filtered.shape[-1]), beta, cells)
    density_hat = project(filtered, eta, beta)
    alpha = alpha_most * penalty_shape * (1.0 - density_hat) / (penalty_shape + density_hat)
    states = []
    popul = populations
    for step in range(STEPS):
        states.append(popul)
        popul = shift_all(collide(popul, alpha, wall_mask, inlet_mask), 1)
    adjoint = cotangent
    alpha_grad = jnp.zeros_like(alpha)
    for step in reversed(range(STEPS)):
        back = shift_all(adjoint, -1)
        unused, pullback = jax.vjp(
            lambda p, a: collide(p, a, wall_mask, inlet_mask), states[step], alpha
        )
        adjoint, term = pullback(back)
        alpha_grad = alpha_grad + term
    denom = jnp.tanh(beta * eta) + jnp.tanh(beta * (1.0 - eta))
    slope = beta * (1.0 - jnp.tanh(beta * (filtered - eta)) ** 2) / denom
    factor = (
        -alpha_most * penalty_shape * (1.0 + penalty_shape) / (penalty_shape + density_hat) ** 2
    )
    design_grad = smooth_field(alpha_grad * factor * slope)
    return (popul, design_grad)


LANES = 128
AROUND = ((1, 0), (-1, 0), (0, 1), (0, -1), (1, 1), (-1, -1), (1, -1), (-1, 1))
FIELDS = 40
CLOSE = 2.0**-14


def rolled(value, amount):
    amount = amount % LANES
    return value if amount == 0 else pltpu.roll(value, amount, 1)


def lane_index():
    return lax.broadcasted_iota(jnp.int32, (8, LANES), 1)


def on_path(index, grp, splits):
    part, step = index // grp, index % grp
    return (step if part % 2 == 0 else grp - 1 - step) * splits + part


def device_at(index, grp, splits):
    odd = lax.rem(lax.axis_index("gx"), 2)
    return jnp.where(odd == 0, on_path(index, grp, splits), on_path(grp * splits - 1 - index, grp, splits))


def block_here(grp, splits):
    step, part = lax.axis_index("grp"), lax.axis_index("gy")
    index = part * grp + jnp.where(lax.rem(part, 2) == 0, step, grp - 1 - step)
    return jnp.where(lax.rem(lax.axis_index("gx"), 2) == 0, index, grp * splits - 1 - index)


def mixed(values):
    place = lane_index() // 16
    for half in (4, 2, 1):
        upper = (place & half) != 0
        values = [jnp.where(upper, values[(index + half) % 8], values[index]) for index in range(8)]
    return values


def pack_kernel(
    splits, design_ref, populations_ref, cotangent_ref, wall_ref, inlet_ref, design_out_ref, packed_ref,
    fields_ref, masks_ref, sems,
):
    moves = [
        pltpu.make_async_copy(populations_ref, fields_ref.at[0:19], sems.at[0]),
        pltpu.make_async_copy(cotangent_ref, fields_ref.at[19:38], sems.at[1]),
        pltpu.make_async_copy(wall_ref, masks_ref.at[0], sems.at[2]),
        pltpu.make_async_copy(inlet_ref, masks_ref.at[1], sems.at[3]),
        pltpu.make_async_copy(design_ref, design_out_ref, sems.at[4]),
    ]
    for move in moves:
        move.start()
    for move in moves:
        move.wait()
    devices = [device_at(index, 8 // splits, splits) for index in range(8)]
    for layer in range(masks_ref.shape[1]):
        for group in range(FIELDS // 8):
            values = []
            for slot in range(8):
                index = group * 8 + slot
                if index < 38:
                    value = fields_ref[index, layer]
                else:
                    value = masks_ref[index - 38, layer].astype(jnp.float32)
                values.append(rolled(value, 16 * slot))
            values = mixed(values)
            for index in range(8):
                packed_ref[devices[index], group, layer] = values[-index % 8]


def arrange_kernel(size, splits, packed_ref, *refs):
    design_refs, (body_ref, first_ref, last_ref, copies_ref, design_ref) = refs[:size], refs[size:]
    layers = packed_ref.shape[2]
    planes = packed_ref.shape[0] // splits * layers
    me = block_here(packed_ref.shape[0] // splits, splits)
    for group in range(FIELDS // 8):
        plane = gather_plane(
            lambda z, part: packed_ref[(z // layers) * splits + part, group, z % layers], planes, splits
        ).T
        for slot in range(8):
            index = group * 8 + lax.rem(slot + 8 - me, 8)
            body_ref[index] = plane[16 * slot : 16 * slot + 16, :]
            first_ref[index] = plane[16 * slot : 16 * slot + 8, :]
            last_ref[index] = plane[16 * slot + 8 : 16 * slot + 16, :]
    here = lax.axis_index("gx")
    for turn in range(size):
        design_ref[lax.rem(here + size - turn, size)] = design_refs[turn][...]
    lanes = lane_index()
    zero = jnp.zeros((8, LANES), jnp.float32)
    for layer in range(layers):
        tiles = [zero] + [design_ref[index, layer] for index in range(size)] + [zero]
        ahead = [rolled(tile, 1) for tile in tiles]
        behind = [rolled(tile, -1) for tile in tiles]
        for index in range(1, size + 1):
            value = 0.5 * tiles[index] + 0.25 * (
                jnp.where(lanes == 0, ahead[index - 1], ahead[index])
                + jnp.where(lanes == LANES - 1, behind[index + 1], behind[index])
            )
            for device in range(copies_ref.shape[0]):
                copies_ref[device, index - 1, layer] = value


def exponent(step_ref):
    steps = jnp.full((8, LANES), step_ref[0], jnp.int32).astype(jnp.float32)
    return jnp.exp2(steps / 16.0)


def plane_masks(rows):
    lanes = lane_index()
    depth, place_z, place_y = LANES // rows, lanes // rows, lanes % rows
    masks = {}
    for cz, cy in AROUND:
        inside = None
        for shift, place, count in ((cz, place_z, depth), (cy, place_y, rows)):
            if shift:
                here = (place >= 1) if shift > 0 else (place < count - 1)
                inside = here if inside is None else inside & here
        masks[cz, cy] = inside
    return masks


def plane_shift(value, cz, cy, rows, masks):
    if cz == 0 and cy == 0:
        return value
    return jnp.where(masks[cz, cy], rolled(value, cz * rows + cy), 0.0)


def plane_smooth(value, rows, masks):
    for cz, cy in ((1, 0), (0, 1)):
        value = 0.5 * value + 0.25 * (
            plane_shift(value, cz, cy, rows, masks) + plane_shift(value, -cz, -cy, rows, masks)
        )
    return value


def gather_plane(read, planes, splits):
    blocks = []
    for z in range(planes):
        for part in range(splits):
            blocks.append(read(z, part))
    return jnp.concatenate(blocks, axis=0)


def volume_root(raised_ref, columns, beta):
    zero = jnp.zeros((8, LANES), jnp.float32)
    one = jnp.ones((8, LANES), jnp.float32)
    cells = columns * LANES
    top = jnp.exp(2.0 * beta)
    scale = 1.0 / (top - 1.0)

    def total(parts):
        value = (parts[0] + parts[1]) + (parts[2] + parts[3])
        return jnp.sum(jnp.sum(value, axis=0, keepdims=True), axis=1, keepdims=True)

    def advance(state):
        low, high, low_known, high_known, middle, _ = state
        level = jnp.exp(2.0 * beta * middle)
        sums, squares = [zero] * 4, [zero] * 4
        for index, row in enumerate(range(0, columns, 8)):
            raised = raised_ref[row : row + 8, :] + level
            part = pl.reciprocal(raised, approx=True)
            part = part * (2.0 - raised * part)
            sums[index % 4] = sums[index % 4] + part
            squares[index % 4] = squares[index % 4] + part * part
        first, second = total(sums), total(squares)
        volume = cells - (1.0 + level) * first
        slope = first - (1.0 + level) * second
        whole = (top + level) * scale
        excess = volume * whole - fluid_share * cells
        slope = (2.0 * beta * level) * (volume * scale - whole * slope)
        above = excess > 0.0
        low, low_known = jnp.where(above, middle, low), jnp.where(above, 1.0, low_known)
        high, high_known = jnp.where(above, high, middle), jnp.where(above, high_known, 1.0)
        guess = middle - excess / slope
        taken = (guess >= low) & (guess <= high)
        other = jnp.where(
            (guess > high) & (high_known == 0.0),
            high,
            jnp.where((guess < low) & (low_known == 0.0), low, 0.5 * (low + high)),
        )
        change = jnp.where(taken, jnp.abs(guess - middle), 2.0**16 * (high - low))
        return low, high, low_known, high_known, jnp.where(taken, guess, other), change

    def going(carry):
        step, state = carry
        return (step < 64) & (jnp.max(state[5]) > CLOSE)

    state = advance(advance((zero, one, zero, zero, 0.5 * one, zero)))
    _, state = lax.while_loop(going, lambda carry: (carry[0] + 1, advance(carry[1])), (2, state))
    return jnp.clip(state[4], 0.5**31, 1.0)


def level_kernel(rows, splits, size, step_ref, copies_ref, share_ref, filtered_ref, raised_ref):
    layers = copies_ref.shape[2]
    planes = LANES // rows
    columns = size * LANES
    masks = plane_masks(rows)
    zero = jnp.zeros((8, LANES), jnp.float32)
    beta = exponent(step_ref)
    filtered_ref[0:8, :] = zero
    filtered_ref[columns + 8 : columns + 16, :] = zero
    for block in range(size):
        plane = gather_plane(
            lambda z, part: copies_ref[(z // layers) * splits + part, block, z % layers], planes, splits
        )
        filtered_ref[8 + block * LANES : 8 + (block + 1) * LANES, :] = plane.T
    for row in range(8, columns + 8, 8):
        value = plane_smooth(filtered_ref[row : row + 8, :], rows, masks)
        filtered_ref[row : row + 8, :] = value
        raised_ref[row - 8 : row, :] = jnp.exp(2.0 * beta * value)
    eta = volume_root(raised_ref, columns, beta)
    place = lax.axis_index("gx") * copies_ref.shape[0] + block_here(copies_ref.shape[0] // splits, splits)
    level = jnp.exp(2.0 * beta * eta)
    top = jnp.exp(2.0 * beta)
    whole = (top + level) / (top - 1.0)
    strength = alpha_most * penalty_shape
    for block in range(4):
        at = slice(8 * block, 8 * block + 8)
        start = pl.multiple_of(place * 16 + 8 * block, 8)
        raised = jnp.exp(2.0 * beta * filtered_ref[pl.ds(start, 8), :])
        part = 1.0 / (raised + level)
        density_hat = ((raised - 1.0) * part) * whole
        share_ref[0, at, :] = (penalty_shape + density_hat) / (
            penalty_shape + strength + (1.0 - strength) * density_hat
        )
        slope = 2.0 * beta * (raised * part) * ((level + 1.0) * part) * whole
        factor = -strength * (1.0 + penalty_shape) / (
            (penalty_shape + density_hat) * (penalty_shape + density_hat)
        )
        share_ref[1, at, :] = slope * factor


def flow(rho, speed):
    square = 1.0 - 1.5 * (speed[0] * speed[0] + speed[1] * speed[1] + speed[2] * speed[2])
    comps = [lattice_weights[0] * rho * square]
    weighted = {1.0 / 18.0: rho * (1.0 / 18.0), 1.0 / 36.0: rho * (1.0 / 36.0)}
    for i in range(1, 19, 2):
        along = along_of(speed, i)
        weight = weighted[lattice_weights[i]]
        even = weight * (square + 4.5 * along * along)
        odd = weight * (3.0 * along)
        comps += [even + odd, even - odd]
    return comps


def along_of(speed, i):
    total = None
    for axis in range(3):
        sign = int(velocities[i][axis])
        if sign:
            if total is None:
                total = speed[axis] if sign > 0 else -speed[axis]
            else:
                total = total + speed[axis] if sign > 0 else total - speed[axis]
    return total


def add_along(totals, value, i):
    for axis in range(3):
        sign = int(velocities[i][axis])
        if sign:
            if totals[axis] is None:
                totals[axis] = value if sign > 0 else -value
            else:
                totals[axis] = totals[axis] + value if sign > 0 else totals[axis] - value


def inlet_value(i):
    along = float(velocities[i][0]) * inlet_speed
    return lattice_weights[i] * (1.0 + 3.0 * along + 4.5 * along * along - 1.5 * inlet_speed * inlet_speed)


def flow_kernel(
    rows, splits, size, share_ref, body_ref, before_ref, after_ref, packed_ref,
    cotangent_ref, even_ref, odd_ref, kept_ref, grad_ref, smooth_ref, output_ref,
):
    devices = packed_ref.shape[0]
    planes = LANES // rows
    layers = planes * splits // devices
    masks = plane_masks(rows)
    zero = jnp.zeros((8, LANES), jnp.float32)
    me = block_here(devices // splits, splits)
    place = lax.axis_index("gx") * devices + me
    last = size * devices - 1

    def inside(value, block):
        if block == 0:
            return jnp.where(place > 0, value, 0.0)
        if block == 3:
            return jnp.where(place < last, value, 0.0)
        return value

    def initial(i, row):
        if row == 0:
            return before_ref[i]
        if row == 24:
            return after_ref[i]
        return body_ref[i, row - 8 : row, :]

    for ref in (even_ref, odd_ref, cotangent_ref):
        for i in range(19):
            ref[i, 0:8, :] = zero
            ref[i, 40:48, :] = zero
    for i in range(19):
        for row in range(0, 32, 8):
            cotangent_ref[i, row + 8 : row + 16, :] = initial(19 + i, row)

    def arrived(ref, i, row):
        cz, cy, cx = (int(c) for c in velocities[i])
        return plane_shift(ref[i, row + 8 - cx : row + 16 - cx, :], cz, cy, rows, masks)

    buffers = (even_ref, odd_ref)
    for step in range(STEPS):
        source, target = buffers[(step + 1) % 2], buffers[step % 2]
        for block in range(4):
            row = 8 * block
            at = slice(row, row + 8)
            if step == 0:
                popul = [initial(i, row) for i in range(19)]
            else:
                popul = [arrived(source, i, row) for i in range(19)]
            wall = initial(38, row) > 0.0
            inlet = initial(39, row) > 0.0
            rho = popul[0]
            momentum = [None, None, None]
            for i in range(1, 19, 2):
                rho = rho + (popul[i] + popul[i + 1])
                add_along(momentum, popul[i] - popul[i + 1], i)
            scale = share_ref[0, at, :] / rho
            speed = [value * scale for value in momentum]
            kept_ref[step, 0, at, :] = rho
            for axis in range(3):
                kept_ref[step, 1 + axis, at, :] = speed[axis]
            settled = flow(relax_rate * rho, speed)
            for i in range(19):
                post = (1.0 - relax_rate) * popul[i] + settled[i]
                post = jnp.where(wall, popul[opposite[i]], jnp.where(inlet, inlet_value(i), post))
                target[i, row + 8 : row + 16, :] = inside(post, block)
    def put(index, row, value):
        group, slot = divmod(index, 8)
        for slot in (slot,) if group < 2 else (slot, slot + 4):
            start = group * LANES + 16 * lax.rem(slot + me, 8) + row
            output_ref[pl.ds(pl.multiple_of(start, 8), 8), :] = value

    source = buffers[(STEPS - 1) % 2]
    for i in range(19):
        for row in (8, 16):
            put(i, row - 8, arrived(source, i, row))

    for step in reversed(range(STEPS)):
        source = cotangent_ref if step == STEPS - 1 else buffers[step % 2]
        target = buffers[(step + 1) % 2]
        for block in range(4):
            row = 8 * block
            at = slice(row, row + 8)
            back = []
            for i in range(19):
                cz, cy, cx = (int(c) for c in velocities[i])
                value = source[i, row + 8 + cx : row + 16 + cx, :]
                back.append(plane_shift(value, -cz, -cy, rows, masks))
            wall = initial(38, row) > 0.0
            inlet = initial(39, row) > 0.0
            rho = kept_ref[step, 0, at, :]
            speed = [kept_ref[step, 1 + axis, at, :] for axis in range(3)]
            square = speed[0] * speed[0] + speed[1] * speed[1] + speed[2] * speed[2]
            share = share_ref[0, at, :]
            faces, edges = None, None
            first, second = [None, None, None], [None, None, None]
            for i in range(1, 19, 2):
                both, apart = back[i] + back[i + 1], back[i] - back[i + 1]
                if i < 7:
                    faces = both if faces is None else faces + both
                    both, apart = 2.0 * both, 2.0 * apart
                else:
                    edges = both if edges is None else edges + both
                add_along(first, apart, i)
                add_along(second, along_of(speed, i) * both, i)
            mean = lattice_weights[0] * back[0] + (1.0 / 18.0) * faces + (1.0 / 36.0) * edges
            first = [value * (3.0 / 36.0) for value in first]
            second = [value * (9.0 / 36.0) for value in second]
            twice = speed[0] * second[0] + speed[1] * second[1] + speed[2] * second[2]
            once = speed[0] * first[0] + speed[1] * first[1] + speed[2] * first[2]
            drag = once + twice - 3.0 * square * mean
            term = jnp.where(wall | inlet, 0.0, -relax_rate * (rho * share * drag))
            grad_ref[at, :] = term if step == STEPS - 1 else grad_ref[at, :] + term
            if step == 0:
                continue
            rest = relax_rate * (mean * (1.0 + 1.5 * square) - 0.5 * twice)
            push = [
                (relax_rate * share) * (first[axis] + second[axis] - 3.0 * mean * speed[axis]) for axis in range(3)
            ]
            for i in range(19):
                if i == 0:
                    post = (1.0 - relax_rate) * back[0] + rest
                else:
                    way = along_of(push, i if i % 2 else i - 1)
                    post = (1.0 - relax_rate) * back[i] + (rest + way if i % 2 else rest - way)
                post = jnp.where(wall, back[opposite[i]], jnp.where(inlet, 0.0, post))
                target[i, row + 8 : row + 16, :] = inside(post, block)

    smooth_ref[0:8, :] = zero
    smooth_ref[40:48, :] = zero
    for block in range(4):
        at = slice(8 * block, 8 * block + 8)
        value = inside(grad_ref[at, :] * share_ref[1, at, :], block)
        smooth_ref[8 * block + 8 : 8 * block + 16, :] = plane_smooth(value, rows, masks)
    for row in (8, 16):
        value = 0.5 * smooth_ref[row + 8 : row + 16, :] + 0.25 * (
            smooth_ref[row + 7 : row + 15, :] + smooth_ref[row + 9 : row + 17, :]
        )
        put(19, row - 8, value)
    second = lax.rem(lane_index() // 16 + 8 - me, 8) >= 4
    for group in range(3):
        plane = output_ref[group * LANES : (group + 1) * LANES, :].T
        for device in range(devices):
            tiles = []
            for layer in range(layers):
                at = (((device // splits) * layers + layer) * splits + device % splits) * 8
                tiles.append(plane[at : at + 8, :])
            if group < 2:
                for layer in range(layers):
                    packed_ref[device, group * layers + layer] = tiles[layer]
            else:
                packed_ref[device, group * layers] = jnp.where(second, tiles[1], tiles[0])


def result_kernel(splits, packed_ref, populations_ref, grad_ref):
    devices = [device_at(index, 8 // splits, splits) for index in range(8)]
    for tile in range(packed_ref.shape[1]):
        values = mixed([packed_ref[device, tile] for device in devices])
        for slot in range(8):
            value = rolled(values[-slot % 8], -16 * slot)
            if tile < 4:
                populations_ref[tile // 2 * 8 + slot, tile % 2] = value
            elif slot % 4 < 3:
                populations_ref[16 + slot % 4, slot // 4] = value
            else:
                grad_ref[slot // 4] = value


def call(kernel, outs, name, operands, spaces, scratch=(), room=32):
    vmem = pl.BlockSpec(memory_space=pltpu.VMEM)
    shapes = tuple(jax.ShapeDtypeStruct(shape, jnp.float32) for shape in outs)
    many = len(outs) > 1
    return pl.pallas_call(
        kernel,
        out_shape=shapes if many else shapes[0],
        in_specs=[pl.BlockSpec(memory_space=space) for space in spaces],
        out_specs=(vmem,) * len(outs) if many else vmem,
        scratch_shapes=list(scratch),
        compiler_params=pltpu.CompilerParams(vmem_limit_bytes=room * 2**20),
        name=name,
    )(*operands)


def body_by_columns(design, populations, cotangent, wall_mask, inlet_mask, beta_step):
    grp, splits, size = (lax.axis_size(axis) for axis in ("grp", "gy", "gx"))
    layers, height, width = design.shape
    rows, plane = height * splits, grp * splits
    tile = (layers, 8, LANES)
    vmem, real = pltpu.VMEM, jnp.float32
    design, packed = call(
        functools.partial(pack_kernel, splits),
        (tile, (plane, FIELDS // 8, *tile)),
        "pack",
        (design, populations, cotangent, wall_mask, inlet_mask),
        [pl.ANY] * 5,
        [vmem((38, *tile), real), vmem((2, *tile), jnp.int32), pltpu.SemaphoreType.DMA((5,))],
        60,
    )
    packed = lax.all_to_all(packed, ("grp", "gy"), 0, 0)
    designs = [design]
    for turn in range(1, size):
        designs.append(lax.ppermute(design, "gx", [(i, (i + turn) % size) for i in range(size)]))
    body, first, last, copies = call(
        functools.partial(arrange_kernel, size, splits),
        ((FIELDS, 16, LANES), (FIELDS, 8, LANES), (FIELDS, 8, LANES), (plane, size, *tile)),
        "arrange",
        (packed, *designs),
        [vmem] * (1 + size),
        [vmem((size, *tile), real)],
    )
    copies = lax.all_to_all(copies, ("grp", "gy"), 0, 0)
    path = [on_path(index, grp, splits) for index in range(plane)]
    order = [(path if gx % 2 == 0 else path[::-1])[index] * size + gx for gx in range(size) for index in range(plane)]
    up = list(zip(order[:-1], order[1:]))
    line = ("grp", "gy", "gx")
    before = lax.ppermute(last, line, up)
    after = lax.ppermute(first, line, [(j, i) for i, j in up])
    columns = size * LANES
    share = call(
        functools.partial(level_kernel, rows, splits, size),
        ((2, 32, LANES),),
        "level",
        (beta_step.reshape(1), copies),
        [pltpu.SMEM, vmem],
        [vmem((columns + 16, LANES), real), vmem((columns, LANES), real)],
    )
    shapes = [
        (19, 48, LANES),
        (19, 48, LANES),
        (19, 48, LANES),
        (STEPS, 4, 32, LANES),
        (32, LANES),
        (48, LANES),
        (3 * LANES, LANES),
    ]
    packed = call(
        functools.partial(flow_kernel, rows, splits, size),
        ((plane, 5, 8, LANES),),
        "flow",
        (share, body, before, after),
        [vmem] * 4,
        [vmem(shape, real) for shape in shapes],
    )
    packed = lax.all_to_all(packed, ("grp", "gy"), 0, 0)
    return call(functools.partial(result_kernel, splits), (populations.shape, design.shape), "result", (packed,), [vmem])


def body(design, populations, cotangent, wall_mask, inlet_mask, beta_step):
    grp, splits = lax.axis_size("grp"), lax.axis_size("gy")
    layers, height, width = design.shape
    fits = height == 8 and width == LANES and layers * grp * height * splits == LANES
    whole = body_by_columns if fits and grp * splits * 16 == LANES else body_by_blocks
    return whole(design, populations, cotangent, wall_mask, inlet_mask, beta_step)


def solution(mesh):
    placed = (
        P("grp", "gy", "gx"),
        P(None, "grp", "gy", "gx"),
        P(None, "grp", "gy", "gx"),
        P("grp", "gy", "gx"),
        P("grp", "gy", "gx"),
        P(),
    )
    return jax.shard_map(
        body,
        mesh=mesh,
        in_specs=placed,
        out_specs=(P(None, "grp", "gy", "gx"), P("grp", "gy", "gx")),
        check_vma=False,
    )
```

```python
import functools

import jax
import jax.numpy as jnp
import numpy as np
from jax import lax
from jax.experimental import pallas as pl
from jax.experimental.pallas import tpu as pltpu
from jax.sharding import PartitionSpec as P

STEPS = 4
BISECT = 30


velocities = np.array(
    [
        [0, 0, 0],
        [1, 0, 0],
        [-1, 0, 0],
        [0, 1, 0],
        [0, -1, 0],
        [0, 0, 1],
        [0, 0, -1],
        [1, 1, 0],
        [-1, -1, 0],
        [1, -1, 0],
        [-1, 1, 0],
        [1, 0, 1],
        [-1, 0, -1],
        [1, 0, -1],
        [-1, 0, 1],
        [0, 1, 1],
        [0, -1, -1],
        [0, 1, -1],
        [0, -1, 1],
    ]
)
opposite = [0, 2, 1, 4, 3, 6, 5, 8, 7, 10, 9, 12, 11, 14, 13, 16, 15, 18, 17]
lattice_weights = [1.0 / 3.0] + [1.0 / 18.0] * 6 + [1.0 / 36.0] * 12
relax_rate = 0.8
inlet_speed = 0.05
alpha_most = 8.0
penalty_shape = 0.1
fluid_share = 0.4


def extended(value, sides, width):
    for axis, dim in sides:
        size, length = (lax.axis_size(axis), value.shape[dim])
        up = [(i, (i + 1) % size) for i in range(size - 1)]
        down = [(j, i) for i, j in up]
        last = lax.slice_in_dim(value, length - width, length, axis=dim)
        leading = lax.slice_in_dim(value, 0, width, axis=dim)
        before = lax.ppermute(last, axis, up)
        after = lax.ppermute(leading, axis, down)
        value = jnp.concatenate([before, value, after], axis=dim)
    return value


def equilibrium(density, speed_z, speed_y, speed_x):
    square = speed_z * speed_z + speed_y * speed_y + speed_x * speed_x
    comps = []
    for i in range(19):
        along = (
            float(velocities[i][0]) * speed_z
            + float(velocities[i][1]) * speed_y
            + float(velocities[i][2]) * speed_x
        )
        comps.append(
            lattice_weights[i] * density * (1.0 + 3.0 * along + 4.5 * along * along - 1.5 * square)
        )
    return jnp.stack(comps)


def moment(popul, axis):
    total = jnp.zeros(popul.shape[1:], popul.dtype)
    for i in range(1, 19):
        if velocities[i][axis] != 0:
            total = total + float(velocities[i][axis]) * popul[i]
    return total


def collide(popul, alpha, wall_mask, inlet_mask):
    density = jnp.sum(popul, axis=0)
    scale = density * (1.0 + alpha)
    feq = equilibrium(
        density, moment(popul, 0) / scale, moment(popul, 1) / scale, moment(popul, 2) / scale
    )
    post = popul + relax_rate * (feq - popul)
    bounce = jnp.stack([popul[opposite[i]] for i in range(19)])
    inlet_values = []
    for i in range(19):
        along = float(velocities[i][0]) * inlet_speed
        inlet_values.append(
            lattice_weights[i]
            * (1.0 + 3.0 * along + 4.5 * along * along - 1.5 * inlet_speed * inlet_speed)
        )
    inlet_feq = jnp.stack([jnp.full(popul.shape[1:], value, popul.dtype) for value in inlet_values])
    return jnp.where(wall_mask[None] > 0, bounce, jnp.where(inlet_mask[None] > 0, inlet_feq, post))


def pick(padded, sign):
    depth, rows, cols = (padded.shape[1] - 2, padded.shape[2] - 2, padded.shape[3] - 2)
    outputs = []
    for i in range(19):
        start_z = 1 - sign * int(velocities[i][0])
        start_y = 1 - sign * int(velocities[i][1])
        start_x = 1 - sign * int(velocities[i][2])
        outputs.append(
            padded[i, start_z : start_z + depth, start_y : start_y + rows, start_x : start_x + cols]
        )
    return jnp.stack(outputs)


def shift_all(popul, sign):
    padded = extended(popul, (("grp", 1), ("gy", 2), ("gx", 3)), 1)
    return pick(padded, sign)


def smooth_field(field):
    padded = extended(field, (("grp", 0), ("gy", 1), ("gx", 2)), 1)
    along_z = 0.25 * padded[:-2] + 0.5 * padded[1:-1] + 0.25 * padded[2:]
    along_y = 0.25 * along_z[:, :-2] + 0.5 * along_z[:, 1:-1] + 0.25 * along_z[:, 2:]
    return 0.25 * along_y[:, :, :-2] + 0.5 * along_y[:, :, 1:-1] + 0.25 * along_y[:, :, 2:]


def project(filtered, thresh, beta):
    denom = jnp.tanh(beta * thresh) + jnp.tanh(beta * (1.0 - thresh))
    return (jnp.tanh(beta * thresh) + jnp.tanh(beta * (filtered - thresh))) / denom


def threshold_kernel(cells, beta_ref, filtered_ref, eta_ref, raised_ref):
    beta = jnp.full((8, 128), beta_ref[0], jnp.float32)
    raised_ref[...] = jnp.exp(2.0 * beta_ref[0] * filtered_ref[...])
    top = jnp.exp(2.0 * beta)
    rows = filtered_ref.shape[0]
    span = min(rows, 512)

    def halve(step, ends):
        low, high = ends
        middle = 0.5 * (low + high)
        level = jnp.exp(2.0 * beta * middle)

        def part(index, total):
            for row in range(0, span, 8):
                raised = raised_ref[pl.ds(pl.multiple_of(index * span + row, 8), 8), :]
                total = total + (raised - 1.0) / (raised + level)
            return total

        total = lax.fori_loop(0, rows // span, part, jnp.zeros((8, 128), jnp.float32))
        volume = jnp.sum(jnp.sum(total, axis=0, keepdims=True), axis=1, keepdims=True)
        above = volume * ((top + level) / (top - 1.0)) > fluid_share * cells
        return jnp.where(above, middle, low), jnp.where(above, high, middle)

    low, high = lax.fori_loop(
        0, BISECT, halve, (jnp.zeros((8, 128), jnp.float32), jnp.ones((8, 128), jnp.float32))
    )
    eta_ref[...] = 0.5 * (low + high)


def threshold(filtered, beta, cells):
    eta = pl.pallas_call(
        functools.partial(threshold_kernel, cells),
        out_shape=jax.ShapeDtypeStruct((8, 128), jnp.float32),
        in_specs=[
            pl.BlockSpec(memory_space=pltpu.SMEM),
            pl.BlockSpec(memory_space=pltpu.VMEM),
        ],
        out_specs=pl.BlockSpec(memory_space=pltpu.VMEM),
        scratch_shapes=[pltpu.VMEM(filtered.shape, jnp.float32)],
        compiler_params=pltpu.CompilerParams(vmem_limit_bytes=40 * 2**20),
        name="threshold",
    )(beta.reshape(1), filtered)
    return eta[0, 0]


def body_by_blocks(design, populations, cotangent, wall_mask, inlet_mask, beta_step):
    beta = jnp.exp2(beta_step.astype(jnp.float32) / 16.0)
    filtered = smooth_field(design)
    cells = design.size * lax.axis_size("grp") * lax.axis_size("gy") * lax.axis_size("gx")
    devices = lax.axis_size("grp") * lax.axis_size("gy") * lax.axis_size("gx")
    copies = jnp.broadcast_to(filtered, (devices, *filtered.shape))
    everywhere = lax.all_to_all(copies, ("grp", "gy", "gx"), 0, 0)
    eta = threshold(everywhere.reshape(-1, filtered.shape[-1]), beta, cells)
    density_hat = project(filtered, eta, beta)
    alpha = alpha_most * penalty_shape * (1.0 - density_hat) / (penalty_shape + density_hat)
    states = []
    popul = populations
    for step in range(STEPS):
        states.append(popul)
        popul = shift_all(collide(popul, alpha, wall_mask, inlet_mask), 1)
    adjoint = cotangent
    alpha_grad = jnp.zeros_like(alpha)
    for step in reversed(range(STEPS)):
        back = shift_all(adjoint, -1)
        unused, pullback = jax.vjp(
            lambda p, a: collide(p, a, wall_mask, inlet_mask), states[step], alpha
        )
        adjoint, term = pullback(back)
        alpha_grad = alpha_grad + term
    denom = jnp.tanh(beta * eta) + jnp.tanh(beta * (1.0 - eta))
    slope = beta * (1.0 - jnp.tanh(beta * (filtered - eta)) ** 2) / denom
    factor = (
        -alpha_most * penalty_shape * (1.0 + penalty_shape) / (penalty_shape + density_hat) ** 2
    )
    design_grad = smooth_field(alpha_grad * factor * slope)
    return (popul, design_grad)


LANES = 128
AROUND = ((1, 0), (-1, 0), (0, 1), (0, -1), (1, 1), (-1, -1), (1, -1), (-1, 1))
FIELDS = 40
NEAR = STEPS + 1
OUTER = 8 * 21 + NEAR * 19
CLOSE = 2.0**-14


def rolled(value, amount):
    amount = amount % LANES
    return value if amount == 0 else pltpu.roll(value, amount, 1)


def lane_index():
    return lax.broadcasted_iota(jnp.int32, (8, LANES), 1)


def on_path(index, grp, splits):
    part, step = index // grp, index % grp
    return (step if part % 2 == 0 else grp - 1 - step) * splits + part


def device_at(index, grp, splits):
    odd = lax.rem(lax.axis_index("gx"), 2)
    return jnp.where(odd == 0, on_path(index, grp, splits), on_path(grp * splits - 1 - index, grp, splits))


def block_here(grp, splits):
    step, part = lax.axis_index("grp"), lax.axis_index("gy")
    index = part * grp + jnp.where(lax.rem(part, 2) == 0, step, grp - 1 - step)
    return jnp.where(lax.rem(lax.axis_index("gx"), 2) == 0, index, grp * splits - 1 - index)


def mixed(values):
    place = lane_index() // 16
    for half in (4, 2, 1):
        upper = (place & half) != 0
        values = [jnp.where(upper, values[(index + half) % 8], values[index]) for index in range(8)]
    return values


def pack_kernel(
    splits, design_ref, populations_ref, cotangent_ref, wall_ref, inlet_ref, design_out_ref, packed_ref,
    fields_ref, masks_ref, sems,
):
    moves = [
        pltpu.make_async_copy(populations_ref, fields_ref.at[0:19], sems.at[0]),
        pltpu.make_async_copy(cotangent_ref, fields_ref.at[19:38], sems.at[1]),
        pltpu.make_async_copy(wall_ref, masks_ref.at[0], sems.at[2]),
        pltpu.make_async_copy(inlet_ref, masks_ref.at[1], sems.at[3]),
        pltpu.make_async_copy(design_ref, design_out_ref, sems.at[4]),
    ]
    for move in moves:
        move.start()
    for move in moves:
        move.wait()
    devices = [device_at(index, 8 // splits, splits) for index in range(8)]
    for layer in range(masks_ref.shape[1]):
        for group in range(FIELDS // 8):
            values = []
            for slot in range(8):
                index = group * 8 + slot
                if index in (19, 20):
                    value = masks_ref[index - 19, layer].astype(jnp.float32)
                else:
                    value = fields_ref[index if index < 19 else index - 2, layer]
                values.append(rolled(value, 16 * slot))
            values = mixed(values)
            for index in range(8):
                packed_ref[devices[index], group, layer] = values[-index % 8]


def arrange_kernel(splits, packed_ref, body_ref, first_ref, last_ref):
    layers = packed_ref.shape[2]
    planes = packed_ref.shape[0] // splits * layers
    me = block_here(packed_ref.shape[0] // splits, splits)
    for group in range(FIELDS // 8):
        plane = gather_plane(
            lambda z, part: packed_ref[(z // layers) * splits + part, group, z % layers], planes, splits
        ).T
        for slot in range(8):
            index = group * 8 + lax.rem(slot + 8 - me, 8)
            body_ref[index] = plane[16 * slot : 16 * slot + 16, :]
    for index in range(FIELDS):
        if index < 21:
            first_ref[8 * index : 8 * index + 8, :] = body_ref[index, 0:8, :]
            last_ref[8 * index : 8 * index + 8, :] = body_ref[index, 8:16, :]
        else:
            start = 8 * 21 + NEAR * (index - 21)
            first_ref[start : start + NEAR, :] = body_ref[index, 0:NEAR, :]
            last_ref[start : start + NEAR, :] = body_ref[index, 16 - NEAR : 16, :]
    for ref in (first_ref, last_ref):
        rest = ref.shape[0] - OUTER
        ref[OUTER:, :] = jnp.zeros((rest, LANES), jnp.float32)


def spread_kernel(size, *refs):
    design_refs, (copies_ref, design_ref) = refs[:size], refs[size:]
    here = lax.axis_index("gx")
    for turn in range(size):
        design_ref[lax.rem(here + size - turn, size)] = design_refs[turn][...]
    lanes = lane_index()
    zero = jnp.zeros((8, LANES), jnp.float32)
    for layer in range(copies_ref.shape[2]):
        tiles = [zero] + [design_ref[index, layer] for index in range(size)] + [zero]
        ahead = [rolled(tile, 1) for tile in tiles]
        behind = [rolled(tile, -1) for tile in tiles]
        for index in range(1, size + 1):
            value = 0.5 * tiles[index] + 0.25 * (
                jnp.where(lanes == 0, ahead[index - 1], ahead[index])
                + jnp.where(lanes == LANES - 1, behind[index + 1], behind[index])
            )
            for device in range(copies_ref.shape[0]):
                copies_ref[device, index - 1, layer] = value


def exponent(step_ref):
    steps = jnp.full((8, LANES), step_ref[0], jnp.int32).astype(jnp.float32)
    return jnp.exp2(steps / 16.0)


def plane_masks(rows):
    lanes = lane_index()
    depth, place_z, place_y = LANES // rows, lanes // rows, lanes % rows
    masks = {}
    for cz, cy in AROUND:
        inside = None
        for shift, place, count in ((cz, place_z, depth), (cy, place_y, rows)):
            if shift:
                here = (place >= 1) if shift > 0 else (place < count - 1)
                inside = here if inside is None else inside & here
        masks[cz, cy] = inside
    return masks


def plane_shift(value, cz, cy, rows, masks):
    if cz == 0 and cy == 0:
        return value
    return jnp.where(masks[cz, cy], rolled(value, cz * rows + cy), 0.0)


def plane_smooth(value, rows, masks):
    for cz, cy in ((1, 0), (0, 1)):
        value = 0.5 * value + 0.25 * (
            plane_shift(value, cz, cy, rows, masks) + plane_shift(value, -cz, -cy, rows, masks)
        )
    return value


def gather_plane(read, planes, splits):
    blocks = []
    for z in range(planes):
        for part in range(splits):
            blocks.append(read(z, part))
    return jnp.concatenate(blocks, axis=0)


def volume_root(raised_ref, columns, beta):
    zero = jnp.zeros((8, LANES), jnp.float32)
    one = jnp.ones((8, LANES), jnp.float32)
    cells = columns * LANES
    top = jnp.exp(2.0 * beta)
    scale = 1.0 / (top - 1.0)

    def total(parts):
        value = (parts[0] + parts[1]) + (parts[2] + parts[3])
        return jnp.sum(jnp.sum(value, axis=0, keepdims=True), axis=1, keepdims=True)

    def advance(state):
        low, high, low_known, high_known, middle, _ = state
        level = jnp.exp(2.0 * beta * middle)
        sums, squares = [zero] * 4, [zero] * 4
        for index, row in enumerate(range(0, columns, 8)):
            raised = raised_ref[row : row + 8, :] + level
            part = pl.reciprocal(raised, approx=True)
            part = part * (2.0 - raised * part)
            sums[index % 4] = sums[index % 4] + part
            squares[index % 4] = squares[index % 4] + part * part
        first, second = total(sums), total(squares)
        volume = cells - (1.0 + level) * first
        slope = first - (1.0 + level) * second
        whole = (top + level) * scale
        excess = volume * whole - fluid_share * cells
        slope = (2.0 * beta * level) * (volume * scale - whole * slope)
        above = excess > 0.0
        low, low_known = jnp.where(above, middle, low), jnp.where(above, 1.0, low_known)
        high, high_known = jnp.where(above, high, middle), jnp.where(above, high_known, 1.0)
        guess = middle - excess / slope
        taken = (guess >= low) & (guess <= high)
        other = jnp.where(
            (guess > high) & (high_known == 0.0),
            high,
            jnp.where((guess < low) & (low_known == 0.0), low, 0.5 * (low + high)),
        )
        change = jnp.where(taken, jnp.abs(guess - middle), 2.0**16 * (high - low))
        return low, high, low_known, high_known, jnp.where(taken, guess, other), change

    def going(carry):
        step, state = carry
        return (step < 64) & (jnp.max(state[5]) > CLOSE)

    state = advance(advance((zero, one, zero, zero, 0.5 * one, zero)))
    _, state = lax.while_loop(going, lambda carry: (carry[0] + 1, advance(carry[1])), (2, state))
    return jnp.clip(state[4], 0.5**31, 1.0)


def level_kernel(rows, splits, size, step_ref, copies_ref, share_ref, filtered_ref, raised_ref):
    layers = copies_ref.shape[2]
    planes = LANES // rows
    columns = size * LANES
    masks = plane_masks(rows)
    zero = jnp.zeros((8, LANES), jnp.float32)
    beta = exponent(step_ref)
    filtered_ref[0:8, :] = zero
    filtered_ref[columns + 8 : columns + 16, :] = zero
    for block in range(size):
        plane = gather_plane(
            lambda z, part: copies_ref[(z // layers) * splits + part, block, z % layers], planes, splits
        )
        filtered_ref[8 + block * LANES : 8 + (block + 1) * LANES, :] = plane.T
    for row in range(8, columns + 8, 8):
        value = plane_smooth(filtered_ref[row : row + 8, :], rows, masks)
        filtered_ref[row : row + 8, :] = value
        raised_ref[row - 8 : row, :] = jnp.exp(2.0 * beta * value)
    eta = volume_root(raised_ref, columns, beta)
    place = lax.axis_index("gx") * copies_ref.shape[0] + block_here(copies_ref.shape[0] // splits, splits)
    level = jnp.exp(2.0 * beta * eta)
    top = jnp.exp(2.0 * beta)
    whole = (top + level) / (top - 1.0)
    strength = alpha_most * penalty_shape
    for block in range(4):
        at = slice(8 * block, 8 * block + 8)
        start = pl.multiple_of(place * 16 + 8 * block, 8)
        raised = jnp.exp(2.0 * beta * filtered_ref[pl.ds(start, 8), :])
        part = 1.0 / (raised + level)
        density_hat = ((raised - 1.0) * part) * whole
        share_ref[0, at, :] = (penalty_shape + density_hat) / (
            penalty_shape + strength + (1.0 - strength) * density_hat
        )
        slope = 2.0 * beta * (raised * part) * ((level + 1.0) * part) * whole
        factor = -strength * (1.0 + penalty_shape) / (
            (penalty_shape + density_hat) * (penalty_shape + density_hat)
        )
        share_ref[1, at, :] = slope * factor


def flow(rho, speed):
    square = 1.0 - 1.5 * (speed[0] * speed[0] + speed[1] * speed[1] + speed[2] * speed[2])
    comps = [lattice_weights[0] * rho * square]
    weighted = {1.0 / 18.0: rho * (1.0 / 18.0), 1.0 / 36.0: rho * (1.0 / 36.0)}
    for i in range(1, 19, 2):
        along = along_of(speed, i)
        weight = weighted[lattice_weights[i]]
        even = weight * (square + 4.5 * along * along)
        odd = weight * (3.0 * along)
        comps += [even + odd, even - odd]
    return comps


def along_of(speed, i):
    total = None
    for axis in range(3):
        sign = int(velocities[i][axis])
        if sign:
            if total is None:
                total = speed[axis] if sign > 0 else -speed[axis]
            else:
                total = total + speed[axis] if sign > 0 else total - speed[axis]
    return total


def add_along(totals, value, i):
    for axis in range(3):
        sign = int(velocities[i][axis])
        if sign:
            if totals[axis] is None:
                totals[axis] = value if sign > 0 else -value
            else:
                totals[axis] = totals[axis] + value if sign > 0 else totals[axis] - value


def inlet_value(i):
    along = float(velocities[i][0]) * inlet_speed
    return lattice_weights[i] * (1.0 + 3.0 * along + 4.5 * along * along - 1.5 * inlet_speed * inlet_speed)


def flow_kernel(
    rows, splits, size, share_ref, body_ref, before_ref, after_ref, packed_ref,
    cotangent_ref, even_ref, odd_ref, kept_ref, grad_ref, smooth_ref, output_ref,
):
    devices = packed_ref.shape[0]
    planes = LANES // rows
    layers = planes * splits // devices
    masks = plane_masks(rows)
    zero = jnp.zeros((8, LANES), jnp.float32)
    me = block_here(devices // splits, splits)
    place = lax.axis_index("gx") * devices + me
    last = size * devices - 1

    def inside(value, block):
        if block == 0:
            return jnp.where(place > 0, value, 0.0)
        if block == 3:
            return jnp.where(place < last, value, 0.0)
        return value

    def initial(i, row):
        if row == 0:
            return before_ref[8 * i : 8 * i + 8, :]
        if row == 24:
            return after_ref[8 * i : 8 * i + 8, :]
        return body_ref[i, row - 8 : row, :]

    for ref in (even_ref, odd_ref, cotangent_ref):
        for i in range(19):
            ref[i, 0:8, :] = zero
            ref[i, 40:48, :] = zero
    for i in range(19):
        start = 8 * 21 + NEAR * i
        cotangent_ref[i, 8:16, :] = zero
        cotangent_ref[i, 16 - NEAR : 16, :] = before_ref[start : start + NEAR, :]
        cotangent_ref[i, 16:32, :] = body_ref[21 + i]
        cotangent_ref[i, 32:40, :] = zero
        cotangent_ref[i, 32 : 32 + NEAR, :] = after_ref[start : start + NEAR, :]

    def arrived(ref, i, row):
        cz, cy, cx = (int(c) for c in velocities[i])
        return plane_shift(ref[i, row + 8 - cx : row + 16 - cx, :], cz, cy, rows, masks)

    buffers = (even_ref, odd_ref)
    for step in range(STEPS):
        source, target = buffers[(step + 1) % 2], buffers[step % 2]
        for block in range(4):
            row = 8 * block
            at = slice(row, row + 8)
            if step == 0:
                popul = [initial(i, row) for i in range(19)]
            else:
                popul = [arrived(source, i, row) for i in range(19)]
            wall = initial(19, row) > 0.0
            inlet = initial(20, row) > 0.0
            rho = popul[0]
            momentum = [None, None, None]
            for i in range(1, 19, 2):
                rho = rho + (popul[i] + popul[i + 1])
                add_along(momentum, popul[i] - popul[i + 1], i)
            scale = share_ref[0, at, :] / rho
            speed = [value * scale for value in momentum]
            kept_ref[step, 0, at, :] = rho
            for axis in range(3):
                kept_ref[step, 1 + axis, at, :] = speed[axis]
            settled = flow(relax_rate * rho, speed)
            for i in range(19):
                post = (1.0 - relax_rate) * popul[i] + settled[i]
                post = jnp.where(wall, popul[opposite[i]], jnp.where(inlet, inlet_value(i), post))
                target[i, row + 8 : row + 16, :] = inside(post, block)
    def put(index, row, value):
        group, slot = divmod(index, 8)
        for slot in (slot,) if group < 2 else (slot, slot + 4):
            start = group * LANES + 16 * lax.rem(slot + me, 8) + row
            output_ref[pl.ds(pl.multiple_of(start, 8), 8), :] = value

    source = buffers[(STEPS - 1) % 2]
    for i in range(19):
        for row in (8, 16):
            put(i, row - 8, arrived(source, i, row))

    for step in reversed(range(STEPS)):
        source = cotangent_ref if step == STEPS - 1 else buffers[step % 2]
        target = buffers[(step + 1) % 2]
        for block in range(4):
            row = 8 * block
            at = slice(row, row + 8)
            back = []
            for i in range(19):
                cz, cy, cx = (int(c) for c in velocities[i])
                value = source[i, row + 8 + cx : row + 16 + cx, :]
                back.append(plane_shift(value, -cz, -cy, rows, masks))
            wall = initial(19, row) > 0.0
            inlet = initial(20, row) > 0.0
            rho = kept_ref[step, 0, at, :]
            speed = [kept_ref[step, 1 + axis, at, :] for axis in range(3)]
            square = speed[0] * speed[0] + speed[1] * speed[1] + speed[2] * speed[2]
            share = share_ref[0, at, :]
            faces, edges = None, None
            first, second = [None, None, None], [None, None, None]
            for i in range(1, 19, 2):
                both, apart = back[i] + back[i + 1], back[i] - back[i + 1]
                if i < 7:
                    faces = both if faces is None else faces + both
                    both, apart = 2.0 * both, 2.0 * apart
                else:
                    edges = both if edges is None else edges + both
                add_along(first, apart, i)
                add_along(second, along_of(speed, i) * both, i)
            mean = lattice_weights[0] * back[0] + (1.0 / 18.0) * faces + (1.0 / 36.0) * edges
            first = [value * (3.0 / 36.0) for value in first]
            second = [value * (9.0 / 36.0) for value in second]
            twice = speed[0] * second[0] + speed[1] * second[1] + speed[2] * second[2]
            once = speed[0] * first[0] + speed[1] * first[1] + speed[2] * first[2]
            drag = once + twice - 3.0 * square * mean
            term = jnp.where(wall | inlet, 0.0, -relax_rate * (rho * share * drag))
            grad_ref[at, :] = term if step == STEPS - 1 else grad_ref[at, :] + term
            if step == 0:
                continue
            rest = relax_rate * (mean * (1.0 + 1.5 * square) - 0.5 * twice)
            push = [
                (relax_rate * share) * (first[axis] + second[axis] - 3.0 * mean * speed[axis]) for axis in range(3)
            ]
            for i in range(19):
                if i == 0:
                    post = (1.0 - relax_rate) * back[0] + rest
                else:
                    way = along_of(push, i if i % 2 else i - 1)
                    post = (1.0 - relax_rate) * back[i] + (rest + way if i % 2 else rest - way)
                post = jnp.where(wall, back[opposite[i]], jnp.where(inlet, 0.0, post))
                target[i, row + 8 : row + 16, :] = inside(post, block)

    smooth_ref[0:8, :] = zero
    smooth_ref[40:48, :] = zero
    for block in range(4):
        at = slice(8 * block, 8 * block + 8)
        value = inside(grad_ref[at, :] * share_ref[1, at, :], block)
        smooth_ref[8 * block + 8 : 8 * block + 16, :] = plane_smooth(value, rows, masks)
    for row in (8, 16):
        value = 0.5 * smooth_ref[row + 8 : row + 16, :] + 0.25 * (
            smooth_ref[row + 7 : row + 15, :] + smooth_ref[row + 9 : row + 17, :]
        )
        put(19, row - 8, value)
    second = lax.rem(lane_index() // 16 + 8 - me, 8) >= 4
    for group in range(3):
        plane = output_ref[group * LANES : (group + 1) * LANES, :].T
        for device in range(devices):
            tiles = []
            for layer in range(layers):
                at = (((device // splits) * layers + layer) * splits + device % splits) * 8
                tiles.append(plane[at : at + 8, :])
            if group < 2:
                for layer in range(layers):
                    packed_ref[device, group * layers + layer] = tiles[layer]
            else:
                packed_ref[device, group * layers] = jnp.where(second, tiles[1], tiles[0])


def result_kernel(splits, packed_ref, populations_ref, grad_ref):
    devices = [device_at(index, 8 // splits, splits) for index in range(8)]
    for tile in range(packed_ref.shape[1]):
        values = mixed([packed_ref[device, tile] for device in devices])
        for slot in range(8):
            value = rolled(values[-slot % 8], -16 * slot)
            if tile < 4:
                populations_ref[tile // 2 * 8 + slot, tile % 2] = value
            elif slot % 4 < 3:
                populations_ref[16 + slot % 4, slot // 4] = value
            else:
                grad_ref[slot // 4] = value


def call(kernel, outs, name, operands, spaces, scratch=(), room=32):
    vmem = pl.BlockSpec(memory_space=pltpu.VMEM)
    shapes = tuple(jax.ShapeDtypeStruct(shape, jnp.float32) for shape in outs)
    many = len(outs) > 1
    return pl.pallas_call(
        kernel,
        out_shape=shapes if many else shapes[0],
        in_specs=[pl.BlockSpec(memory_space=space) for space in spaces],
        out_specs=(vmem,) * len(outs) if many else vmem,
        scratch_shapes=list(scratch),
        compiler_params=pltpu.CompilerParams(vmem_limit_bytes=room * 2**20),
        name=name,
    )(*operands)


def body_by_columns(design, populations, cotangent, wall_mask, inlet_mask, beta_step):
    grp, splits, size = (lax.axis_size(axis) for axis in ("grp", "gy", "gx"))
    layers, height, width = design.shape
    rows, plane = height * splits, grp * splits
    tile = (layers, 8, LANES)
    vmem, real = pltpu.VMEM, jnp.float32
    design, packed = call(
        functools.partial(pack_kernel, splits),
        (tile, (plane, FIELDS // 8, *tile)),
        "pack",
        (design, populations, cotangent, wall_mask, inlet_mask),
        [pl.ANY] * 5,
        [vmem((38, *tile), real), vmem((2, *tile), jnp.int32), pltpu.SemaphoreType.DMA((5,))],
        60,
    )
    packed = lax.all_to_all(packed, ("grp", "gy"), 0, 0)
    designs = [design]
    for turn in range(1, size):
        designs.append(lax.ppermute(design, "gx", [(i, (i + turn) % size) for i in range(size)]))
    copies = call(
        functools.partial(spread_kernel, size),
        ((plane, size, *tile),),
        "spread",
        designs,
        [vmem] * size,
        [vmem((size, *tile), real)],
    )
    outer = (-(-OUTER // 8) * 8, LANES)
    body, first, last = call(
        functools.partial(arrange_kernel, splits),
        ((FIELDS, 16, LANES), outer, outer),
        "arrange",
        (packed,),
        [vmem],
    )
    copies = lax.all_to_all(copies, ("grp", "gy"), 0, 0)
    path = [on_path(index, grp, splits) for index in range(plane)]
    order = [(path if gx % 2 == 0 else path[::-1])[index] * size + gx for gx in range(size) for index in range(plane)]
    up = list(zip(order[:-1], order[1:]))
    line = ("grp", "gy", "gx")
    before = lax.ppermute(last, line, up)
    after = lax.ppermute(first, line, [(j, i) for i, j in up])
    columns = size * LANES
    share = call(
        functools.partial(level_kernel, rows, splits, size),
        ((2, 32, LANES),),
        "level",
        (beta_step.reshape(1), copies),
        [pltpu.SMEM, vmem],
        [vmem((columns + 16, LANES), real), vmem((columns, LANES), real)],
    )
    shapes = [
        (19, 48, LANES),
        (19, 48, LANES),
        (19, 48, LANES),
        (STEPS, 4, 32, LANES),
        (32, LANES),
        (48, LANES),
        (3 * LANES, LANES),
    ]
    packed = call(
        functools.partial(flow_kernel, rows, splits, size),
        ((plane, 5, 8, LANES),),
        "flow",
        (share, body, before, after),
        [vmem] * 4,
        [vmem(shape, real) for shape in shapes],
    )
    packed = lax.all_to_all(packed, ("grp", "gy"), 0, 0)
    return call(functools.partial(result_kernel, splits), (populations.shape, design.shape), "result", (packed,), [vmem])


def body(design, populations, cotangent, wall_mask, inlet_mask, beta_step):
    grp, splits = lax.axis_size("grp"), lax.axis_size("gy")
    layers, height, width = design.shape
    fits = height == 8 and width == LANES and layers * grp * height * splits == LANES
    whole = body_by_columns if fits and grp * splits * 16 == LANES else body_by_blocks
    return whole(design, populations, cotangent, wall_mask, inlet_mask, beta_step)


def solution(mesh):
    placed = (
        P("grp", "gy", "gx"),
        P(None, "grp", "gy", "gx"),
        P(None, "grp", "gy", "gx"),
        P("grp", "gy", "gx"),
        P("grp", "gy", "gx"),
        P(),
    )
    return jax.shard_map(
        body,
        mesh=mesh,
        in_specs=placed,
        out_specs=(P(None, "grp", "gy", "gx"), P("grp", "gy", "gx")),
        check_vma=False,
    )
```

```python
import functools

import jax
import jax.numpy as jnp
import numpy as np
from jax import lax
from jax.experimental import pallas as pl
from jax.experimental.pallas import tpu as pltpu
from jax.sharding import PartitionSpec as P

STEPS = 4
BISECT = 30


velocities = np.array(
    [
        [0, 0, 0],
        [1, 0, 0],
        [-1, 0, 0],
        [0, 1, 0],
        [0, -1, 0],
        [0, 0, 1],
        [0, 0, -1],
        [1, 1, 0],
        [-1, -1, 0],
        [1, -1, 0],
        [-1, 1, 0],
        [1, 0, 1],
        [-1, 0, -1],
        [1, 0, -1],
        [-1, 0, 1],
        [0, 1, 1],
        [0, -1, -1],
        [0, 1, -1],
        [0, -1, 1],
    ]
)
opposite = [0, 2, 1, 4, 3, 6, 5, 8, 7, 10, 9, 12, 11, 14, 13, 16, 15, 18, 17]
lattice_weights = [1.0 / 3.0] + [1.0 / 18.0] * 6 + [1.0 / 36.0] * 12
relax_rate = 0.8
inlet_speed = 0.05
alpha_most = 8.0
penalty_shape = 0.1
fluid_share = 0.4


def extended(value, sides, width):
    for axis, dim in sides:
        size, length = (lax.axis_size(axis), value.shape[dim])
        up = [(i, (i + 1) % size) for i in range(size - 1)]
        down = [(j, i) for i, j in up]
        last = lax.slice_in_dim(value, length - width, length, axis=dim)
        leading = lax.slice_in_dim(value, 0, width, axis=dim)
        before = lax.ppermute(last, axis, up)
        after = lax.ppermute(leading, axis, down)
        value = jnp.concatenate([before, value, after], axis=dim)
    return value


def equilibrium(density, speed_z, speed_y, speed_x):
    square = speed_z * speed_z + speed_y * speed_y + speed_x * speed_x
    comps = []
    for i in range(19):
        along = (
            float(velocities[i][0]) * speed_z
            + float(velocities[i][1]) * speed_y
            + float(velocities[i][2]) * speed_x
        )
        comps.append(
            lattice_weights[i] * density * (1.0 + 3.0 * along + 4.5 * along * along - 1.5 * square)
        )
    return jnp.stack(comps)


def moment(popul, axis):
    total = jnp.zeros(popul.shape[1:], popul.dtype)
    for i in range(1, 19):
        if velocities[i][axis] != 0:
            total = total + float(velocities[i][axis]) * popul[i]
    return total


def collide(popul, alpha, wall_mask, inlet_mask):
    density = jnp.sum(popul, axis=0)
    scale = density * (1.0 + alpha)
    feq = equilibrium(
        density, moment(popul, 0) / scale, moment(popul, 1) / scale, moment(popul, 2) / scale
    )
    post = popul + relax_rate * (feq - popul)
    bounce = jnp.stack([popul[opposite[i]] for i in range(19)])
    inlet_values = []
    for i in range(19):
        along = float(velocities[i][0]) * inlet_speed
        inlet_values.append(
            lattice_weights[i]
            * (1.0 + 3.0 * along + 4.5 * along * along - 1.5 * inlet_speed * inlet_speed)
        )
    inlet_feq = jnp.stack([jnp.full(popul.shape[1:], value, popul.dtype) for value in inlet_values])
    return jnp.where(wall_mask[None] > 0, bounce, jnp.where(inlet_mask[None] > 0, inlet_feq, post))


def pick(padded, sign):
    depth, rows, cols = (padded.shape[1] - 2, padded.shape[2] - 2, padded.shape[3] - 2)
    outputs = []
    for i in range(19):
        start_z = 1 - sign * int(velocities[i][0])
        start_y = 1 - sign * int(velocities[i][1])
        start_x = 1 - sign * int(velocities[i][2])
        outputs.append(
            padded[i, start_z : start_z + depth, start_y : start_y + rows, start_x : start_x + cols]
        )
    return jnp.stack(outputs)


def shift_all(popul, sign):
    padded = extended(popul, (("grp", 1), ("gy", 2), ("gx", 3)), 1)
    return pick(padded, sign)


def smooth_field(field):
    padded = extended(field, (("grp", 0), ("gy", 1), ("gx", 2)), 1)
    along_z = 0.25 * padded[:-2] + 0.5 * padded[1:-1] + 0.25 * padded[2:]
    along_y = 0.25 * along_z[:, :-2] + 0.5 * along_z[:, 1:-1] + 0.25 * along_z[:, 2:]
    return 0.25 * along_y[:, :, :-2] + 0.5 * along_y[:, :, 1:-1] + 0.25 * along_y[:, :, 2:]


def project(filtered, thresh, beta):
    denom = jnp.tanh(beta * thresh) + jnp.tanh(beta * (1.0 - thresh))
    return (jnp.tanh(beta * thresh) + jnp.tanh(beta * (filtered - thresh))) / denom


def threshold_kernel(cells, beta_ref, filtered_ref, eta_ref, raised_ref):
    beta = jnp.full((8, 128), beta_ref[0], jnp.float32)
    raised_ref[...] = jnp.exp(2.0 * beta_ref[0] * filtered_ref[...])
    top = jnp.exp(2.0 * beta)
    rows = filtered_ref.shape[0]
    span = min(rows, 512)

    def halve(step, ends):
        low, high = ends
        middle = 0.5 * (low + high)
        level = jnp.exp(2.0 * beta * middle)

        def part(index, total):
            for row in range(0, span, 8):
                raised = raised_ref[pl.ds(pl.multiple_of(index * span + row, 8), 8), :]
                total = total + (raised - 1.0) / (raised + level)
            return total

        total = lax.fori_loop(0, rows // span, part, jnp.zeros((8, 128), jnp.float32))
        volume = jnp.sum(jnp.sum(total, axis=0, keepdims=True), axis=1, keepdims=True)
        above = volume * ((top + level) / (top - 1.0)) > fluid_share * cells
        return jnp.where(above, middle, low), jnp.where(above, high, middle)

    low, high = lax.fori_loop(
        0, BISECT, halve, (jnp.zeros((8, 128), jnp.float32), jnp.ones((8, 128), jnp.float32))
    )
    eta_ref[...] = 0.5 * (low + high)


def threshold(filtered, beta, cells):
    eta = pl.pallas_call(
        functools.partial(threshold_kernel, cells),
        out_shape=jax.ShapeDtypeStruct((8, 128), jnp.float32),
        in_specs=[
            pl.BlockSpec(memory_space=pltpu.SMEM),
            pl.BlockSpec(memory_space=pltpu.VMEM),
        ],
        out_specs=pl.BlockSpec(memory_space=pltpu.VMEM),
        scratch_shapes=[pltpu.VMEM(filtered.shape, jnp.float32)],
        compiler_params=pltpu.CompilerParams(vmem_limit_bytes=40 * 2**20),
        name="threshold",
    )(beta.reshape(1), filtered)
    return eta[0, 0]


def body_by_blocks(design, populations, cotangent, wall_mask, inlet_mask, beta_step):
    beta = jnp.exp2(beta_step.astype(jnp.float32) / 16.0)
    filtered = smooth_field(design)
    cells = design.size * lax.axis_size("grp") * lax.axis_size("gy") * lax.axis_size("gx")
    devices = lax.axis_size("grp") * lax.axis_size("gy") * lax.axis_size("gx")
    copies = jnp.broadcast_to(filtered, (devices, *filtered.shape))
    everywhere = lax.all_to_all(copies, ("grp", "gy", "gx"), 0, 0)
    eta = threshold(everywhere.reshape(-1, filtered.shape[-1]), beta, cells)
    density_hat = project(filtered, eta, beta)
    alpha = alpha_most * penalty_shape * (1.0 - density_hat) / (penalty_shape + density_hat)
    states = []
    popul = populations
    for step in range(STEPS):
        states.append(popul)
        popul = shift_all(collide(popul, alpha, wall_mask, inlet_mask), 1)
    adjoint = cotangent
    alpha_grad = jnp.zeros_like(alpha)
    for step in reversed(range(STEPS)):
        back = shift_all(adjoint, -1)
        unused, pullback = jax.vjp(
            lambda p, a: collide(p, a, wall_mask, inlet_mask), states[step], alpha
        )
        adjoint, term = pullback(back)
        alpha_grad = alpha_grad + term
    denom = jnp.tanh(beta * eta) + jnp.tanh(beta * (1.0 - eta))
    slope = beta * (1.0 - jnp.tanh(beta * (filtered - eta)) ** 2) / denom
    factor = (
        -alpha_most * penalty_shape * (1.0 + penalty_shape) / (penalty_shape + density_hat) ** 2
    )
    design_grad = smooth_field(alpha_grad * factor * slope)
    return (popul, design_grad)


LANES = 128
AROUND = ((1, 0), (-1, 0), (0, 1), (0, -1), (1, 1), (-1, -1), (1, -1), (-1, 1))
FIELDS = 40
NEAR = STEPS + 1
OUTER = 8 * 21 + NEAR * 19
CLOSE = 2.0**-14


def rolled(value, amount):
    amount = amount % LANES
    return value if amount == 0 else pltpu.roll(value, amount, 1)


def lane_index():
    return lax.broadcasted_iota(jnp.int32, (8, LANES), 1)


def on_path(index, grp, splits):
    part, step = index // grp, index % grp
    return (step if part % 2 == 0 else grp - 1 - step) * splits + part


def device_at(index, grp, splits):
    odd = lax.rem(lax.axis_index("gx"), 2)
    return jnp.where(odd == 0, on_path(index, grp, splits), on_path(grp * splits - 1 - index, grp, splits))


def block_here(grp, splits):
    step, part = lax.axis_index("grp"), lax.axis_index("gy")
    index = part * grp + jnp.where(lax.rem(part, 2) == 0, step, grp - 1 - step)
    return jnp.where(lax.rem(lax.axis_index("gx"), 2) == 0, index, grp * splits - 1 - index)


def mixed(values):
    place = lane_index() // 16
    for half in (4, 2, 1):
        upper = (place & half) != 0
        values = [jnp.where(upper, values[(index + half) % 8], values[index]) for index in range(8)]
    return values


def pack_kernel(
    splits, design_ref, populations_ref, cotangent_ref, wall_ref, inlet_ref, design_out_ref, packed_ref,
    fields_ref, masks_ref, sems,
):
    moves = [
        pltpu.make_async_copy(populations_ref, fields_ref.at[0:19], sems.at[0]),
        pltpu.make_async_copy(cotangent_ref, fields_ref.at[19:38], sems.at[1]),
        pltpu.make_async_copy(wall_ref, masks_ref.at[0], sems.at[2]),
        pltpu.make_async_copy(inlet_ref, masks_ref.at[1], sems.at[3]),
        pltpu.make_async_copy(design_ref, design_out_ref, sems.at[4]),
    ]
    for move in moves:
        move.start()
    for move in moves:
        move.wait()
    devices = [device_at(index, 8 // splits, splits) for index in range(8)]
    for layer in range(masks_ref.shape[1]):
        for group in range(FIELDS // 8):
            values = []
            for slot in range(8):
                index = group * 8 + slot
                if index in (19, 20):
                    value = masks_ref[index - 19, layer].astype(jnp.float32)
                else:
                    value = fields_ref[index if index < 19 else index - 2, layer]
                values.append(rolled(value, 16 * slot))
            values = mixed(values)
            for index in range(8):
                packed_ref[devices[index], group, layer] = values[-index % 8]


def arrange_kernel(splits, packed_ref, body_ref, first_ref, last_ref):
    layers = packed_ref.shape[2]
    planes = packed_ref.shape[0] // splits * layers
    me = block_here(packed_ref.shape[0] // splits, splits)
    for group in range(FIELDS // 8):
        plane = gather_plane(
            lambda z, part: packed_ref[(z // layers) * splits + part, group, z % layers], planes, splits
        ).T
        for slot in range(8):
            index = group * 8 + lax.rem(slot + 8 - me, 8)
            body_ref[index] = plane[16 * slot : 16 * slot + 16, :]
    for index in range(FIELDS):
        if index < 21:
            first_ref[8 * index : 8 * index + 8, :] = body_ref[index, 0:8, :]
            last_ref[8 * index : 8 * index + 8, :] = body_ref[index, 8:16, :]
        else:
            start = 8 * 21 + NEAR * (index - 21)
            first_ref[start : start + NEAR, :] = body_ref[index, 0:NEAR, :]
            last_ref[start : start + NEAR, :] = body_ref[index, 16 - NEAR : 16, :]
    for ref in (first_ref, last_ref):
        rest = ref.shape[0] - OUTER
        ref[OUTER:, :] = jnp.zeros((rest, LANES), jnp.float32)


def spread_kernel(size, *refs):
    design_refs, (copies_ref, design_ref) = refs[:size], refs[size:]
    here = lax.axis_index("gx")
    for turn in range(size):
        design_ref[lax.rem(here + size - turn, size)] = design_refs[turn][...]
    lanes = lane_index()
    zero = jnp.zeros((8, LANES), jnp.float32)
    for layer in range(copies_ref.shape[2]):
        tiles = [zero] + [design_ref[index, layer] for index in range(size)] + [zero]
        ahead = [rolled(tile, 1) for tile in tiles]
        behind = [rolled(tile, -1) for tile in tiles]
        for index in range(1, size + 1):
            value = 0.5 * tiles[index] + 0.25 * (
                jnp.where(lanes == 0, ahead[index - 1], ahead[index])
                + jnp.where(lanes == LANES - 1, behind[index + 1], behind[index])
            )
            for device in range(copies_ref.shape[0]):
                copies_ref[device, index - 1, layer] = value


def exponent(step_ref):
    steps = jnp.full((8, LANES), step_ref[0], jnp.int32).astype(jnp.float32)
    return jnp.exp2(steps / 16.0)


def plane_masks(rows):
    lanes = lane_index()
    depth, place_z, place_y = LANES // rows, lanes // rows, lanes % rows
    masks = {}
    for cz, cy in AROUND:
        inside = None
        for shift, place, count in ((cz, place_z, depth), (cy, place_y, rows)):
            if shift:
                here = (place >= 1) if shift > 0 else (place < count - 1)
                inside = here if inside is None else inside & here
        masks[cz, cy] = inside
    return masks


def plane_shift(value, cz, cy, rows, masks):
    if cz == 0 and cy == 0:
        return value
    return jnp.where(masks[cz, cy], rolled(value, cz * rows + cy), 0.0)


def plane_smooth(value, rows, masks):
    for cz, cy in ((1, 0), (0, 1)):
        value = 0.5 * value + 0.25 * (
            plane_shift(value, cz, cy, rows, masks) + plane_shift(value, -cz, -cy, rows, masks)
        )
    return value


def gather_plane(read, planes, splits):
    blocks = []
    for z in range(planes):
        for part in range(splits):
            blocks.append(read(z, part))
    return jnp.concatenate(blocks, axis=0)


def volume_root(raised_ref, columns, beta):
    zero = jnp.zeros((8, LANES), jnp.float32)
    one = jnp.ones((8, LANES), jnp.float32)
    cells = columns * LANES
    top = jnp.exp(2.0 * beta)
    scale = 1.0 / (top - 1.0)

    def total(parts):
        value = (parts[0] + parts[1]) + (parts[2] + parts[3])
        return jnp.sum(jnp.sum(value, axis=0, keepdims=True), axis=1, keepdims=True)

    def advance(state):
        low, high, low_known, high_known, middle, _ = state
        level = jnp.exp(2.0 * beta * middle)
        sums, squares = [zero] * 4, [zero] * 4
        for index, row in enumerate(range(0, columns, 8)):
            raised = raised_ref[row : row + 8, :] + level
            part = pl.reciprocal(raised, approx=True)
            part = part * (2.0 - raised * part)
            sums[index % 4] = sums[index % 4] + part
            squares[index % 4] = squares[index % 4] + part * part
        first, second = total(sums), total(squares)
        volume = cells - (1.0 + level) * first
        slope = first - (1.0 + level) * second
        whole = (top + level) * scale
        excess = volume * whole - fluid_share * cells
        slope = (2.0 * beta * level) * (volume * scale - whole * slope)
        above = excess > 0.0
        low, low_known = jnp.where(above, middle, low), jnp.where(above, 1.0, low_known)
        high, high_known = jnp.where(above, high, middle), jnp.where(above, high_known, 1.0)
        guess = middle - excess / slope
        taken = (guess >= low) & (guess <= high)
        other = jnp.where(
            (guess > high) & (high_known == 0.0),
            high,
            jnp.where((guess < low) & (low_known == 0.0), low, 0.5 * (low + high)),
        )
        change = jnp.where(taken, jnp.abs(guess - middle), 2.0**16 * (high - low))
        return low, high, low_known, high_known, jnp.where(taken, guess, other), change

    def going(carry):
        step, state = carry
        return (step < 64) & (jnp.max(state[5]) > CLOSE)

    state = advance(advance((zero, one, zero, zero, 0.5 * one, zero)))
    _, state = lax.while_loop(going, lambda carry: (carry[0] + 1, advance(carry[1])), (2, state))
    return jnp.clip(state[4], 0.5**31, 1.0)


def level_kernel(rows, splits, size, step_ref, copies_ref, share_ref, filtered_ref, raised_ref):
    layers = copies_ref.shape[2]
    planes = LANES // rows
    columns = size * LANES
    masks = plane_masks(rows)
    zero = jnp.zeros((8, LANES), jnp.float32)
    beta = exponent(step_ref)
    filtered_ref[0:8, :] = zero
    filtered_ref[columns + 8 : columns + 16, :] = zero
    for block in range(size):
        plane = gather_plane(
            lambda z, part: copies_ref[(z // layers) * splits + part, block, z % layers], planes, splits
        )
        filtered_ref[8 + block * LANES : 8 + (block + 1) * LANES, :] = plane.T
    for row in range(8, columns + 8, 8):
        value = plane_smooth(filtered_ref[row : row + 8, :], rows, masks)
        filtered_ref[row : row + 8, :] = value
        raised_ref[row - 8 : row, :] = jnp.exp(2.0 * beta * value)
    eta = volume_root(raised_ref, columns, beta)
    place = lax.axis_index("gx") * copies_ref.shape[0] + block_here(copies_ref.shape[0] // splits, splits)
    level = jnp.exp(2.0 * beta * eta)
    top = jnp.exp(2.0 * beta)
    whole = (top + level) / (top - 1.0)
    strength = alpha_most * penalty_shape
    for block in range(4):
        at = slice(8 * block, 8 * block + 8)
        start = pl.multiple_of(place * 16 + 8 * block, 8)
        raised = jnp.exp(2.0 * beta * filtered_ref[pl.ds(start, 8), :])
        part = 1.0 / (raised + level)
        density_hat = ((raised - 1.0) * part) * whole
        share_ref[0, at, :] = (penalty_shape + density_hat) / (
            penalty_shape + strength + (1.0 - strength) * density_hat
        )
        slope = 2.0 * beta * (raised * part) * ((level + 1.0) * part) * whole
        factor = -strength * (1.0 + penalty_shape) / (
            (penalty_shape + density_hat) * (penalty_shape + density_hat)
        )
        share_ref[1, at, :] = slope * factor


def flow(rho, speed):
    square = 1.0 - 1.5 * (speed[0] * speed[0] + speed[1] * speed[1] + speed[2] * speed[2])
    comps = [lattice_weights[0] * rho * square]
    weighted = {1.0 / 18.0: rho * (1.0 / 18.0), 1.0 / 36.0: rho * (1.0 / 36.0)}
    for i in range(1, 19, 2):
        along = along_of(speed, i)
        weight = weighted[lattice_weights[i]]
        even = weight * (square + 4.5 * along * along)
        odd = weight * (3.0 * along)
        comps += [even + odd, even - odd]
    return comps


def along_of(speed, i):
    total = None
    for axis in range(3):
        sign = int(velocities[i][axis])
        if sign:
            if total is None:
                total = speed[axis] if sign > 0 else -speed[axis]
            else:
                total = total + speed[axis] if sign > 0 else total - speed[axis]
    return total


def add_along(totals, value, i):
    for axis in range(3):
        sign = int(velocities[i][axis])
        if sign:
            if totals[axis] is None:
                totals[axis] = value if sign > 0 else -value
            else:
                totals[axis] = totals[axis] + value if sign > 0 else totals[axis] - value


def inlet_value(i):
    along = float(velocities[i][0]) * inlet_speed
    return lattice_weights[i] * (1.0 + 3.0 * along + 4.5 * along * along - 1.5 * inlet_speed * inlet_speed)


def flow_kernel(
    rows, splits, size, share_ref, body_ref, before_ref, after_ref, packed_ref,
    cotangent_ref, even_ref, odd_ref, kept_ref, grad_ref, smooth_ref, output_ref,
):
    devices = packed_ref.shape[0]
    planes = LANES // rows
    layers = planes * splits // devices
    masks = plane_masks(rows)
    zero = jnp.zeros((8, LANES), jnp.float32)
    me = block_here(devices // splits, splits)
    place = lax.axis_index("gx") * devices + me
    last = size * devices - 1

    def inside(value, block):
        if block == 0:
            return jnp.where(place > 0, value, 0.0)
        if block == 3:
            return jnp.where(place < last, value, 0.0)
        return value

    def initial(i, row):
        if row == 0:
            return before_ref[8 * i : 8 * i + 8, :]
        if row == 24:
            return after_ref[8 * i : 8 * i + 8, :]
        return body_ref[i, row - 8 : row, :]

    for ref in (even_ref, odd_ref, cotangent_ref):
        for i in range(19):
            ref[i, 0:8, :] = zero
            ref[i, 40:48, :] = zero
    for i in range(19):
        start = 8 * 21 + NEAR * i
        cotangent_ref[i, 8:16, :] = zero
        cotangent_ref[i, 16 - NEAR : 16, :] = before_ref[start : start + NEAR, :]
        cotangent_ref[i, 16:32, :] = body_ref[21 + i]
        cotangent_ref[i, 32:40, :] = zero
        cotangent_ref[i, 32 : 32 + NEAR, :] = after_ref[start : start + NEAR, :]

    def arrived(ref, i, row):
        cz, cy, cx = (int(c) for c in velocities[i])
        return plane_shift(ref[i, row + 8 - cx : row + 16 - cx, :], cz, cy, rows, masks)

    buffers = (even_ref, odd_ref)
    for step in range(STEPS):
        source, target = buffers[(step + 1) % 2], buffers[step % 2]
        for block in range(4):
            row = 8 * block
            at = slice(row, row + 8)
            if step == 0:
                popul = [initial(i, row) for i in range(19)]
            else:
                popul = [arrived(source, i, row) for i in range(19)]
            wall = initial(19, row) > 0.0
            inlet = initial(20, row) > 0.0
            rho = popul[0]
            momentum = [None, None, None]
            for i in range(1, 19, 2):
                rho = rho + (popul[i] + popul[i + 1])
                add_along(momentum, popul[i] - popul[i + 1], i)
            scale = share_ref[0, at, :] / rho
            speed = [value * scale for value in momentum]
            kept_ref[step, 0, at, :] = rho
            for axis in range(3):
                kept_ref[step, 1 + axis, at, :] = speed[axis]
            settled = flow(relax_rate * rho, speed)
            for i in range(19):
                post = (1.0 - relax_rate) * popul[i] + settled[i]
                post = jnp.where(wall, popul[opposite[i]], jnp.where(inlet, inlet_value(i), post))
                target[i, row + 8 : row + 16, :] = inside(post, block)
    def put(index, row, value):
        group, slot = divmod(index, 8)
        for slot in (slot,) if group < 2 else (slot, slot + 4):
            start = group * LANES + 16 * lax.rem(slot + me, 8) + row
            output_ref[pl.ds(pl.multiple_of(start, 8), 8), :] = value

    source = buffers[(STEPS - 1) % 2]
    for i in range(19):
        for row in (8, 16):
            put(i, row - 8, arrived(source, i, row))

    for step in reversed(range(STEPS)):
        source = cotangent_ref if step == STEPS - 1 else buffers[step % 2]
        target = buffers[(step + 1) % 2]
        for block in range(4):
            row = 8 * block
            at = slice(row, row + 8)
            back = []
            for i in range(19):
                cz, cy, cx = (int(c) for c in velocities[i])
                value = source[i, row + 8 + cx : row + 16 + cx, :]
                back.append(plane_shift(value, -cz, -cy, rows, masks))
            wall = initial(19, row) > 0.0
            inlet = initial(20, row) > 0.0
            rho = kept_ref[step, 0, at, :]
            speed = [kept_ref[step, 1 + axis, at, :] for axis in range(3)]
            square = speed[0] * speed[0] + speed[1] * speed[1] + speed[2] * speed[2]
            share = share_ref[0, at, :]
            faces, edges = None, None
            first, second = [None, None, None], [None, None, None]
            for i in range(1, 19, 2):
                both, apart = back[i] + back[i + 1], back[i] - back[i + 1]
                if i < 7:
                    faces = both if faces is None else faces + both
                    both, apart = 2.0 * both, 2.0 * apart
                else:
                    edges = both if edges is None else edges + both
                add_along(first, apart, i)
                add_along(second, along_of(speed, i) * both, i)
            mean = lattice_weights[0] * back[0] + (1.0 / 18.0) * faces + (1.0 / 36.0) * edges
            first = [value * (3.0 / 36.0) for value in first]
            second = [value * (9.0 / 36.0) for value in second]
            twice = speed[0] * second[0] + speed[1] * second[1] + speed[2] * second[2]
            once = speed[0] * first[0] + speed[1] * first[1] + speed[2] * first[2]
            drag = once + twice - 3.0 * square * mean
            term = jnp.where(wall | inlet, 0.0, -relax_rate * (rho * share * drag))
            grad_ref[at, :] = term if step == STEPS - 1 else grad_ref[at, :] + term
            if step == 0:
                continue
            rest = relax_rate * (mean * (1.0 + 1.5 * square) - 0.5 * twice)
            push = [
                (relax_rate * share) * (first[axis] + second[axis] - 3.0 * mean * speed[axis]) for axis in range(3)
            ]
            for i in range(19):
                if i == 0:
                    post = (1.0 - relax_rate) * back[0] + rest
                else:
                    way = along_of(push, i if i % 2 else i - 1)
                    post = (1.0 - relax_rate) * back[i] + (rest + way if i % 2 else rest - way)
                post = jnp.where(wall, back[opposite[i]], jnp.where(inlet, 0.0, post))
                target[i, row + 8 : row + 16, :] = inside(post, block)

    smooth_ref[0:8, :] = zero
    smooth_ref[40:48, :] = zero
    for block in range(4):
        at = slice(8 * block, 8 * block + 8)
        value = inside(grad_ref[at, :] * share_ref[1, at, :], block)
        smooth_ref[8 * block + 8 : 8 * block + 16, :] = plane_smooth(value, rows, masks)
    for row in (8, 16):
        value = 0.5 * smooth_ref[row + 8 : row + 16, :] + 0.25 * (
            smooth_ref[row + 7 : row + 15, :] + smooth_ref[row + 9 : row + 17, :]
        )
        put(19, row - 8, value)
    second = lax.rem(lane_index() // 16 + 8 - me, 8) >= 4
    for group in range(3):
        plane = output_ref[group * LANES : (group + 1) * LANES, :].T
        for device in range(devices):
            tiles = []
            for layer in range(layers):
                at = (((device // splits) * layers + layer) * splits + device % splits) * 8
                tiles.append(plane[at : at + 8, :])
            if group < 2:
                for layer in range(layers):
                    packed_ref[device, group * layers + layer] = tiles[layer]
            else:
                packed_ref[device, group * layers] = jnp.where(second, tiles[1], tiles[0])


def result_kernel(splits, packed_ref, populations_ref, grad_ref):
    devices = [device_at(index, 8 // splits, splits) for index in range(8)]
    for tile in range(packed_ref.shape[1]):
        values = mixed([packed_ref[device, tile] for device in devices])
        for slot in range(8):
            value = rolled(values[-slot % 8], -16 * slot)
            if tile < 4:
                populations_ref[tile // 2 * 8 + slot, tile % 2] = value
            elif slot % 4 < 3:
                populations_ref[16 + slot % 4, slot // 4] = value
            else:
                grad_ref[slot // 4] = value


def call(kernel, outs, name, operands, spaces, scratch=(), room=32):
    vmem = pl.BlockSpec(memory_space=pltpu.VMEM)
    shapes = tuple(jax.ShapeDtypeStruct(shape, jnp.float32) for shape in outs)
    many = len(outs) > 1
    return pl.pallas_call(
        kernel,
        out_shape=shapes if many else shapes[0],
        in_specs=[pl.BlockSpec(memory_space=space) for space in spaces],
        out_specs=(vmem,) * len(outs) if many else vmem,
        scratch_shapes=list(scratch),
        compiler_params=pltpu.CompilerParams(vmem_limit_bytes=room * 2**20),
        name=name,
    )(*operands)


def body_by_columns(design, populations, cotangent, wall_mask, inlet_mask, beta_step):
    grp, splits, size = (lax.axis_size(axis) for axis in ("grp", "gy", "gx"))
    layers, height, width = design.shape
    rows, plane = height * splits, grp * splits
    tile = (layers, 8, LANES)
    vmem, real = pltpu.VMEM, jnp.float32
    design, packed = call(
        functools.partial(pack_kernel, splits),
        (tile, (plane, FIELDS // 8, *tile)),
        "pack",
        (design, populations, cotangent, wall_mask, inlet_mask),
        [pl.ANY] * 5,
        [vmem((38, *tile), real), vmem((2, *tile), jnp.int32), pltpu.SemaphoreType.DMA((5,))],
        60,
    )
    packed = lax.all_to_all(packed, ("grp", "gy"), 0, 0)
    designs = [design] * size
    for turn in reversed(range(1, size)):
        designs[turn] = lax.ppermute(design, "gx", [(i, (i + turn) % size) for i in range(size)])
    copies = call(
        functools.partial(spread_kernel, size),
        ((plane, size, *tile),),
        "spread",
        designs,
        [vmem] * size,
        [vmem((size, *tile), real)],
    )
    outer = (-(-OUTER // 8) * 8, LANES)
    body, first, last = call(
        functools.partial(arrange_kernel, splits),
        ((FIELDS, 16, LANES), outer, outer),
        "arrange",
        (packed,),
        [vmem],
    )
    copies = lax.all_to_all(copies, ("grp", "gy"), 0, 0)
    path = [on_path(index, grp, splits) for index in range(plane)]
    order = [(path if gx % 2 == 0 else path[::-1])[index] * size + gx for gx in range(size) for index in range(plane)]
    up = list(zip(order[:-1], order[1:]))
    line = ("grp", "gy", "gx")
    before = lax.ppermute(last, line, up)
    after = lax.ppermute(first, line, [(j, i) for i, j in up])
    columns = size * LANES
    share = call(
        functools.partial(level_kernel, rows, splits, size),
        ((2, 32, LANES),),
        "level",
        (beta_step.reshape(1), copies),
        [pltpu.SMEM, vmem],
        [vmem((columns + 16, LANES), real), vmem((columns, LANES), real)],
    )
    shapes = [
        (19, 48, LANES),
        (19, 48, LANES),
        (19, 48, LANES),
        (STEPS, 4, 32, LANES),
        (32, LANES),
        (48, LANES),
        (3 * LANES, LANES),
    ]
    packed = call(
        functools.partial(flow_kernel, rows, splits, size),
        ((plane, 5, 8, LANES),),
        "flow",
        (share, body, before, after),
        [vmem] * 4,
        [vmem(shape, real) for shape in shapes],
    )
    packed = lax.all_to_all(packed, ("grp", "gy"), 0, 0)
    return call(functools.partial(result_kernel, splits), (populations.shape, design.shape), "result", (packed,), [vmem])


def body(design, populations, cotangent, wall_mask, inlet_mask, beta_step):
    grp, splits = lax.axis_size("grp"), lax.axis_size("gy")
    layers, height, width = design.shape
    fits = height == 8 and width == LANES and layers * grp * height * splits == LANES
    whole = body_by_columns if fits and grp * splits * 16 == LANES else body_by_blocks
    return whole(design, populations, cotangent, wall_mask, inlet_mask, beta_step)


def solution(mesh):
    placed = (
        P("grp", "gy", "gx"),
        P(None, "grp", "gy", "gx"),
        P(None, "grp", "gy", "gx"),
        P("grp", "gy", "gx"),
        P("grp", "gy", "gx"),
        P(),
    )
    return jax.shard_map(
        body,
        mesh=mesh,
        in_specs=placed,
        out_specs=(P(None, "grp", "gy", "gx"), P("grp", "gy", "gx")),
        check_vma=False,
    )
```

```python
import functools

import jax
import jax.numpy as jnp
import numpy as np
from jax import lax
from jax.experimental import pallas as pl
from jax.experimental.pallas import tpu as pltpu
from jax.sharding import PartitionSpec as P

STEPS = 4
BISECT = 30


velocities = np.array(
    [
        [0, 0, 0],
        [1, 0, 0],
        [-1, 0, 0],
        [0, 1, 0],
        [0, -1, 0],
        [0, 0, 1],
        [0, 0, -1],
        [1, 1, 0],
        [-1, -1, 0],
        [1, -1, 0],
        [-1, 1, 0],
        [1, 0, 1],
        [-1, 0, -1],
        [1, 0, -1],
        [-1, 0, 1],
        [0, 1, 1],
        [0, -1, -1],
        [0, 1, -1],
        [0, -1, 1],
    ]
)
opposite = [0, 2, 1, 4, 3, 6, 5, 8, 7, 10, 9, 12, 11, 14, 13, 16, 15, 18, 17]
lattice_weights = [1.0 / 3.0] + [1.0 / 18.0] * 6 + [1.0 / 36.0] * 12
relax_rate = 0.8
inlet_speed = 0.05
alpha_most = 8.0
penalty_shape = 0.1
fluid_share = 0.4


def extended(value, sides, width):
    for axis, dim in sides:
        size, length = (lax.axis_size(axis), value.shape[dim])
        up = [(i, (i + 1) % size) for i in range(size - 1)]
        down = [(j, i) for i, j in up]
        last = lax.slice_in_dim(value, length - width, length, axis=dim)
        leading = lax.slice_in_dim(value, 0, width, axis=dim)
        before = lax.ppermute(last, axis, up)
        after = lax.ppermute(leading, axis, down)
        value = jnp.concatenate([before, value, after], axis=dim)
    return value


def equilibrium(density, speed_z, speed_y, speed_x):
    square = speed_z * speed_z + speed_y * speed_y + speed_x * speed_x
    comps = []
    for i in range(19):
        along = (
            float(velocities[i][0]) * speed_z
            + float(velocities[i][1]) * speed_y
            + float(velocities[i][2]) * speed_x
        )
        comps.append(
            lattice_weights[i] * density * (1.0 + 3.0 * along + 4.5 * along * along - 1.5 * square)
        )
    return jnp.stack(comps)


def moment(popul, axis):
    total = jnp.zeros(popul.shape[1:], popul.dtype)
    for i in range(1, 19):
        if velocities[i][axis] != 0:
            total = total + float(velocities[i][axis]) * popul[i]
    return total


def collide(popul, alpha, wall_mask, inlet_mask):
    density = jnp.sum(popul, axis=0)
    scale = density * (1.0 + alpha)
    feq = equilibrium(
        density, moment(popul, 0) / scale, moment(popul, 1) / scale, moment(popul, 2) / scale
    )
    post = popul + relax_rate * (feq - popul)
    bounce = jnp.stack([popul[opposite[i]] for i in range(19)])
    inlet_values = []
    for i in range(19):
        along = float(velocities[i][0]) * inlet_speed
        inlet_values.append(
            lattice_weights[i]
            * (1.0 + 3.0 * along + 4.5 * along * along - 1.5 * inlet_speed * inlet_speed)
        )
    inlet_feq = jnp.stack([jnp.full(popul.shape[1:], value, popul.dtype) for value in inlet_values])
    return jnp.where(wall_mask[None] > 0, bounce, jnp.where(inlet_mask[None] > 0, inlet_feq, post))


def pick(padded, sign):
    depth, rows, cols = (padded.shape[1] - 2, padded.shape[2] - 2, padded.shape[3] - 2)
    outputs = []
    for i in range(19):
        start_z = 1 - sign * int(velocities[i][0])
        start_y = 1 - sign * int(velocities[i][1])
        start_x = 1 - sign * int(velocities[i][2])
        outputs.append(
            padded[i, start_z : start_z + depth, start_y : start_y + rows, start_x : start_x + cols]
        )
    return jnp.stack(outputs)


def shift_all(popul, sign):
    padded = extended(popul, (("grp", 1), ("gy", 2), ("gx", 3)), 1)
    return pick(padded, sign)


def smooth_field(field):
    padded = extended(field, (("grp", 0), ("gy", 1), ("gx", 2)), 1)
    along_z = 0.25 * padded[:-2] + 0.5 * padded[1:-1] + 0.25 * padded[2:]
    along_y = 0.25 * along_z[:, :-2] + 0.5 * along_z[:, 1:-1] + 0.25 * along_z[:, 2:]
    return 0.25 * along_y[:, :, :-2] + 0.5 * along_y[:, :, 1:-1] + 0.25 * along_y[:, :, 2:]


def project(filtered, thresh, beta):
    denom = jnp.tanh(beta * thresh) + jnp.tanh(beta * (1.0 - thresh))
    return (jnp.tanh(beta * thresh) + jnp.tanh(beta * (filtered - thresh))) / denom


def threshold_kernel(cells, beta_ref, filtered_ref, eta_ref, raised_ref):
    beta = jnp.full((8, 128), beta_ref[0], jnp.float32)
    raised_ref[...] = jnp.exp(2.0 * beta_ref[0] * filtered_ref[...])
    top = jnp.exp(2.0 * beta)
    rows = filtered_ref.shape[0]
    span = min(rows, 512)

    def halve(step, ends):
        low, high = ends
        middle = 0.5 * (low + high)
        level = jnp.exp(2.0 * beta * middle)

        def part(index, total):
            for row in range(0, span, 8):
                raised = raised_ref[pl.ds(pl.multiple_of(index * span + row, 8), 8), :]
                total = total + (raised - 1.0) / (raised + level)
            return total

        total = lax.fori_loop(0, rows // span, part, jnp.zeros((8, 128), jnp.float32))
        volume = jnp.sum(jnp.sum(total, axis=0, keepdims=True), axis=1, keepdims=True)
        above = volume * ((top + level) / (top - 1.0)) > fluid_share * cells
        return jnp.where(above, middle, low), jnp.where(above, high, middle)

    low, high = lax.fori_loop(
        0, BISECT, halve, (jnp.zeros((8, 128), jnp.float32), jnp.ones((8, 128), jnp.float32))
    )
    eta_ref[...] = 0.5 * (low + high)


def threshold(filtered, beta, cells):
    eta = pl.pallas_call(
        functools.partial(threshold_kernel, cells),
        out_shape=jax.ShapeDtypeStruct((8, 128), jnp.float32),
        in_specs=[
            pl.BlockSpec(memory_space=pltpu.SMEM),
            pl.BlockSpec(memory_space=pltpu.VMEM),
        ],
        out_specs=pl.BlockSpec(memory_space=pltpu.VMEM),
        scratch_shapes=[pltpu.VMEM(filtered.shape, jnp.float32)],
        compiler_params=pltpu.CompilerParams(vmem_limit_bytes=40 * 2**20),
        name="threshold",
    )(beta.reshape(1), filtered)
    return eta[0, 0]


def body_by_blocks(design, populations, cotangent, wall_mask, inlet_mask, beta_step):
    beta = jnp.exp2(beta_step.astype(jnp.float32) / 16.0)
    filtered = smooth_field(design)
    cells = design.size * lax.axis_size("grp") * lax.axis_size("gy") * lax.axis_size("gx")
    devices = lax.axis_size("grp") * lax.axis_size("gy") * lax.axis_size("gx")
    copies = jnp.broadcast_to(filtered, (devices, *filtered.shape))
    everywhere = lax.all_to_all(copies, ("grp", "gy", "gx"), 0, 0)
    eta = threshold(everywhere.reshape(-1, filtered.shape[-1]), beta, cells)
    density_hat = project(filtered, eta, beta)
    alpha = alpha_most * penalty_shape * (1.0 - density_hat) / (penalty_shape + density_hat)
    states = []
    popul = populations
    for step in range(STEPS):
        states.append(popul)
        popul = shift_all(collide(popul, alpha, wall_mask, inlet_mask), 1)
    adjoint = cotangent
    alpha_grad = jnp.zeros_like(alpha)
    for step in reversed(range(STEPS)):
        back = shift_all(adjoint, -1)
        unused, pullback = jax.vjp(
            lambda p, a: collide(p, a, wall_mask, inlet_mask), states[step], alpha
        )
        adjoint, term = pullback(back)
        alpha_grad = alpha_grad + term
    denom = jnp.tanh(beta * eta) + jnp.tanh(beta * (1.0 - eta))
    slope = beta * (1.0 - jnp.tanh(beta * (filtered - eta)) ** 2) / denom
    factor = (
        -alpha_most * penalty_shape * (1.0 + penalty_shape) / (penalty_shape + density_hat) ** 2
    )
    design_grad = smooth_field(alpha_grad * factor * slope)
    return (popul, design_grad)


LANES = 128
AROUND = ((1, 0), (-1, 0), (0, 1), (0, -1), (1, 1), (-1, -1), (1, -1), (-1, 1))
FIELDS = 40
NEAR = STEPS + 1
OUTER = 8 * 21 + NEAR * 19
CLOSE = 2.0**-14


def rolled(value, amount):
    amount = amount % LANES
    return value if amount == 0 else pltpu.roll(value, amount, 1)


def lane_index():
    return lax.broadcasted_iota(jnp.int32, (8, LANES), 1)


def on_path(index, grp, splits):
    part, step = index // grp, index % grp
    return (step if part % 2 == 0 else grp - 1 - step) * splits + part


def device_at(index, grp, splits):
    odd = lax.rem(lax.axis_index("gx"), 2)
    return jnp.where(odd == 0, on_path(index, grp, splits), on_path(grp * splits - 1 - index, grp, splits))


def block_here(grp, splits):
    step, part = lax.axis_index("grp"), lax.axis_index("gy")
    index = part * grp + jnp.where(lax.rem(part, 2) == 0, step, grp - 1 - step)
    return jnp.where(lax.rem(lax.axis_index("gx"), 2) == 0, index, grp * splits - 1 - index)


def mixed(values):
    place = lane_index() // 16
    for half in (4, 2, 1):
        upper = (place & half) != 0
        values = [jnp.where(upper, values[(index + half) % 8], values[index]) for index in range(8)]
    return values


def pack_kernel(
    splits, design_ref, populations_ref, cotangent_ref, wall_ref, inlet_ref, design_out_ref, packed_ref,
    fields_ref, masks_ref, sems,
):
    moves = [
        pltpu.make_async_copy(populations_ref, fields_ref.at[0:19], sems.at[0]),
        pltpu.make_async_copy(cotangent_ref, fields_ref.at[19:38], sems.at[1]),
        pltpu.make_async_copy(wall_ref, masks_ref.at[0], sems.at[2]),
        pltpu.make_async_copy(inlet_ref, masks_ref.at[1], sems.at[3]),
        pltpu.make_async_copy(design_ref, design_out_ref, sems.at[4]),
    ]
    for move in moves:
        move.start()
    for move in moves:
        move.wait()
    devices = [device_at(index, 8 // splits, splits) for index in range(8)]
    for layer in range(masks_ref.shape[1]):
        for group in range(FIELDS // 8):
            values = []
            for slot in range(8):
                index = group * 8 + slot
                if index in (19, 20):
                    value = masks_ref[index - 19, layer].astype(jnp.float32)
                else:
                    value = fields_ref[index if index < 19 else index - 2, layer]
                values.append(rolled(value, 16 * slot))
            values = mixed(values)
            for index in range(8):
                packed_ref[devices[index], group, layer] = values[-index % 8]


def arrange_kernel(splits, packed_ref, body_ref, first_ref, last_ref):
    layers = packed_ref.shape[2]
    planes = packed_ref.shape[0] // splits * layers
    me = block_here(packed_ref.shape[0] // splits, splits)
    for group in range(FIELDS // 8):
        plane = gather_plane(
            lambda z, part: packed_ref[(z // layers) * splits + part, group, z % layers], planes, splits
        ).T
        for slot in range(8):
            index = group * 8 + lax.rem(slot + 8 - me, 8)
            body_ref[index] = plane[16 * slot : 16 * slot + 16, :]
    for index in range(FIELDS):
        if index < 21:
            first_ref[8 * index : 8 * index + 8, :] = body_ref[index, 0:8, :]
            last_ref[8 * index : 8 * index + 8, :] = body_ref[index, 8:16, :]
        else:
            start = 8 * 21 + NEAR * (index - 21)
            first_ref[start : start + NEAR, :] = body_ref[index, 0:NEAR, :]
            last_ref[start : start + NEAR, :] = body_ref[index, 16 - NEAR : 16, :]
    for ref in (first_ref, last_ref):
        rest = ref.shape[0] - OUTER
        ref[OUTER:, :] = jnp.zeros((rest, LANES), jnp.float32)


def spread_kernel(size, *refs):
    design_refs, (copies_ref, design_ref) = refs[:size], refs[size:]
    here = lax.axis_index("gx")
    for turn in range(size):
        design_ref[lax.rem(here + turn, size)] = design_refs[turn][...]
    lanes = lane_index()
    zero = jnp.zeros((8, LANES), jnp.float32)
    for layer in range(copies_ref.shape[2]):
        tiles = [zero] + [design_ref[index, layer] for index in range(size)] + [zero]
        ahead = [rolled(tile, 1) for tile in tiles]
        behind = [rolled(tile, -1) for tile in tiles]
        for index in range(1, size + 1):
            value = 0.5 * tiles[index] + 0.25 * (
                jnp.where(lanes == 0, ahead[index - 1], ahead[index])
                + jnp.where(lanes == LANES - 1, behind[index + 1], behind[index])
            )
            for device in range(copies_ref.shape[0]):
                copies_ref[device, index - 1, layer] = value


def exponent(step_ref):
    steps = jnp.full((8, LANES), step_ref[0], jnp.int32).astype(jnp.float32)
    return jnp.exp2(steps / 16.0)


def plane_masks(rows):
    lanes = lane_index()
    depth, place_z, place_y = LANES // rows, lanes // rows, lanes % rows
    masks = {}
    for cz, cy in AROUND:
        inside = None
        for shift, place, count in ((cz, place_z, depth), (cy, place_y, rows)):
            if shift:
                here = (place >= 1) if shift > 0 else (place < count - 1)
                inside = here if inside is None else inside & here
        masks[cz, cy] = inside
    return masks


def plane_shift(value, cz, cy, rows, masks):
    if cz == 0 and cy == 0:
        return value
    return jnp.where(masks[cz, cy], rolled(value, cz * rows + cy), 0.0)


def plane_smooth(value, rows, masks):
    for cz, cy in ((1, 0), (0, 1)):
        value = 0.5 * value + 0.25 * (
            plane_shift(value, cz, cy, rows, masks) + plane_shift(value, -cz, -cy, rows, masks)
        )
    return value


def gather_plane(read, planes, splits):
    blocks = []
    for z in range(planes):
        for part in range(splits):
            blocks.append(read(z, part))
    return jnp.concatenate(blocks, axis=0)


def volume_root(raised_ref, columns, beta):
    zero = jnp.zeros((8, LANES), jnp.float32)
    one = jnp.ones((8, LANES), jnp.float32)
    cells = columns * LANES
    top = jnp.exp(2.0 * beta)
    scale = 1.0 / (top - 1.0)

    def total(parts):
        value = (parts[0] + parts[1]) + (parts[2] + parts[3])
        return jnp.sum(jnp.sum(value, axis=0, keepdims=True), axis=1, keepdims=True)

    def advance(state):
        low, high, low_known, high_known, middle, _ = state
        level = jnp.exp(2.0 * beta * middle)
        sums, squares = [zero] * 4, [zero] * 4
        for index, row in enumerate(range(0, columns, 8)):
            raised = raised_ref[row : row + 8, :] + level
            part = pl.reciprocal(raised, approx=True)
            part = part * (2.0 - raised * part)
            sums[index % 4] = sums[index % 4] + part
            squares[index % 4] = squares[index % 4] + part * part
        first, second = total(sums), total(squares)
        volume = cells - (1.0 + level) * first
        slope = first - (1.0 + level) * second
        whole = (top + level) * scale
        excess = volume * whole - fluid_share * cells
        slope = (2.0 * beta * level) * (volume * scale - whole * slope)
        above = excess > 0.0
        low, low_known = jnp.where(above, middle, low), jnp.where(above, 1.0, low_known)
        high, high_known = jnp.where(above, high, middle), jnp.where(above, high_known, 1.0)
        guess = middle - excess / slope
        taken = (guess >= low) & (guess <= high)
        other = jnp.where(
            (guess > high) & (high_known == 0.0),
            high,
            jnp.where((guess < low) & (low_known == 0.0), low, 0.5 * (low + high)),
        )
        change = jnp.where(taken, jnp.abs(guess - middle), 2.0**16 * (high - low))
        return low, high, low_known, high_known, jnp.where(taken, guess, other), change

    def going(carry):
        step, state = carry
        return (step < 64) & (jnp.max(state[5]) > CLOSE)

    state = advance(advance((zero, one, zero, zero, 0.5 * one, zero)))
    _, state = lax.while_loop(going, lambda carry: (carry[0] + 1, advance(carry[1])), (2, state))
    return jnp.clip(state[4], 0.5**31, 1.0)


def level_kernel(rows, splits, size, step_ref, copies_ref, share_ref, filtered_ref, raised_ref):
    layers = copies_ref.shape[2]
    planes = LANES // rows
    columns = size * LANES
    masks = plane_masks(rows)
    zero = jnp.zeros((8, LANES), jnp.float32)
    beta = exponent(step_ref)
    filtered_ref[0:8, :] = zero
    filtered_ref[columns + 8 : columns + 16, :] = zero
    for block in range(size):
        plane = gather_plane(
            lambda z, part: copies_ref[(z // layers) * splits + part, block, z % layers], planes, splits
        )
        filtered_ref[8 + block * LANES : 8 + (block + 1) * LANES, :] = plane.T
    for row in range(8, columns + 8, 8):
        value = plane_smooth(filtered_ref[row : row + 8, :], rows, masks)
        filtered_ref[row : row + 8, :] = value
        raised_ref[row - 8 : row, :] = jnp.exp(2.0 * beta * value)
    eta = volume_root(raised_ref, columns, beta)
    place = lax.axis_index("gx") * copies_ref.shape[0] + block_here(copies_ref.shape[0] // splits, splits)
    level = jnp.exp(2.0 * beta * eta)
    top = jnp.exp(2.0 * beta)
    whole = (top + level) / (top - 1.0)
    strength = alpha_most * penalty_shape
    for block in range(4):
        at = slice(8 * block, 8 * block + 8)
        start = pl.multiple_of(place * 16 + 8 * block, 8)
        raised = jnp.exp(2.0 * beta * filtered_ref[pl.ds(start, 8), :])
        part = 1.0 / (raised + level)
        density_hat = ((raised - 1.0) * part) * whole
        share_ref[0, at, :] = (penalty_shape + density_hat) / (
            penalty_shape + strength + (1.0 - strength) * density_hat
        )
        slope = 2.0 * beta * (raised * part) * ((level + 1.0) * part) * whole
        factor = -strength * (1.0 + penalty_shape) / (
            (penalty_shape + density_hat) * (penalty_shape + density_hat)
        )
        share_ref[1, at, :] = slope * factor


def flow(rho, speed):
    square = 1.0 - 1.5 * (speed[0] * speed[0] + speed[1] * speed[1] + speed[2] * speed[2])
    comps = [lattice_weights[0] * rho * square]
    weighted = {1.0 / 18.0: rho * (1.0 / 18.0), 1.0 / 36.0: rho * (1.0 / 36.0)}
    for i in range(1, 19, 2):
        along = along_of(speed, i)
        weight = weighted[lattice_weights[i]]
        even = weight * (square + 4.5 * along * along)
        odd = weight * (3.0 * along)
        comps += [even + odd, even - odd]
    return comps


def along_of(speed, i):
    total = None
    for axis in range(3):
        sign = int(velocities[i][axis])
        if sign:
            if total is None:
                total = speed[axis] if sign > 0 else -speed[axis]
            else:
                total = total + speed[axis] if sign > 0 else total - speed[axis]
    return total


def add_along(totals, value, i):
    for axis in range(3):
        sign = int(velocities[i][axis])
        if sign:
            if totals[axis] is None:
                totals[axis] = value if sign > 0 else -value
            else:
                totals[axis] = totals[axis] + value if sign > 0 else totals[axis] - value


def inlet_value(i):
    along = float(velocities[i][0]) * inlet_speed
    return lattice_weights[i] * (1.0 + 3.0 * along + 4.5 * along * along - 1.5 * inlet_speed * inlet_speed)


def flow_kernel(
    rows, splits, size, share_ref, body_ref, before_ref, after_ref, packed_ref,
    cotangent_ref, even_ref, odd_ref, kept_ref, grad_ref, smooth_ref, output_ref,
):
    devices = packed_ref.shape[0]
    planes = LANES // rows
    layers = planes * splits // devices
    masks = plane_masks(rows)
    zero = jnp.zeros((8, LANES), jnp.float32)
    me = block_here(devices // splits, splits)
    place = lax.axis_index("gx") * devices + me
    last = size * devices - 1

    def inside(value, block):
        if block == 0:
            return jnp.where(place > 0, value, 0.0)
        if block == 3:
            return jnp.where(place < last, value, 0.0)
        return value

    def initial(i, row):
        if row == 0:
            return before_ref[8 * i : 8 * i + 8, :]
        if row == 24:
            return after_ref[8 * i : 8 * i + 8, :]
        return body_ref[i, row - 8 : row, :]

    for ref in (even_ref, odd_ref, cotangent_ref):
        for i in range(19):
            ref[i, 0:8, :] = zero
            ref[i, 40:48, :] = zero
    for i in range(19):
        start = 8 * 21 + NEAR * i
        cotangent_ref[i, 8:16, :] = zero
        cotangent_ref[i, 16 - NEAR : 16, :] = before_ref[start : start + NEAR, :]
        cotangent_ref[i, 16:32, :] = body_ref[21 + i]
        cotangent_ref[i, 32:40, :] = zero
        cotangent_ref[i, 32 : 32 + NEAR, :] = after_ref[start : start + NEAR, :]

    def arrived(ref, i, row):
        cz, cy, cx = (int(c) for c in velocities[i])
        return plane_shift(ref[i, row + 8 - cx : row + 16 - cx, :], cz, cy, rows, masks)

    buffers = (even_ref, odd_ref)
    for step in range(STEPS):
        source, target = buffers[(step + 1) % 2], buffers[step % 2]
        for block in range(4):
            row = 8 * block
            at = slice(row, row + 8)
            if step == 0:
                popul = [initial(i, row) for i in range(19)]
            else:
                popul = [arrived(source, i, row) for i in range(19)]
            wall = initial(19, row) > 0.0
            inlet = initial(20, row) > 0.0
            rho = popul[0]
            momentum = [None, None, None]
            for i in range(1, 19, 2):
                rho = rho + (popul[i] + popul[i + 1])
                add_along(momentum, popul[i] - popul[i + 1], i)
            scale = share_ref[0, at, :] / rho
            speed = [value * scale for value in momentum]
            kept_ref[step, 0, at, :] = rho
            for axis in range(3):
                kept_ref[step, 1 + axis, at, :] = speed[axis]
            settled = flow(relax_rate * rho, speed)
            for i in range(19):
                post = (1.0 - relax_rate) * popul[i] + settled[i]
                post = jnp.where(wall, popul[opposite[i]], jnp.where(inlet, inlet_value(i), post))
                target[i, row + 8 : row + 16, :] = inside(post, block)
    def put(index, row, value):
        group, slot = divmod(index, 8)
        for slot in (slot,) if group < 2 else (slot, slot + 4):
            start = group * LANES + 16 * lax.rem(slot + me, 8) + row
            output_ref[pl.ds(pl.multiple_of(start, 8), 8), :] = value

    source = buffers[(STEPS - 1) % 2]
    for i in range(19):
        for row in (8, 16):
            put(i, row - 8, arrived(source, i, row))

    for step in reversed(range(STEPS)):
        source = cotangent_ref if step == STEPS - 1 else buffers[step % 2]
        target = buffers[(step + 1) % 2]
        for block in range(4):
            row = 8 * block
            at = slice(row, row + 8)
            back = []
            for i in range(19):
                cz, cy, cx = (int(c) for c in velocities[i])
                value = source[i, row + 8 + cx : row + 16 + cx, :]
                back.append(plane_shift(value, -cz, -cy, rows, masks))
            wall = initial(19, row) > 0.0
            inlet = initial(20, row) > 0.0
            rho = kept_ref[step, 0, at, :]
            speed = [kept_ref[step, 1 + axis, at, :] for axis in range(3)]
            square = speed[0] * speed[0] + speed[1] * speed[1] + speed[2] * speed[2]
            share = share_ref[0, at, :]
            faces, edges = None, None
            first, second = [None, None, None], [None, None, None]
            for i in range(1, 19, 2):
                both, apart = back[i] + back[i + 1], back[i] - back[i + 1]
                if i < 7:
                    faces = both if faces is None else faces + both
                    both, apart = 2.0 * both, 2.0 * apart
                else:
                    edges = both if edges is None else edges + both
                add_along(first, apart, i)
                add_along(second, along_of(speed, i) * both, i)
            mean = lattice_weights[0] * back[0] + (1.0 / 18.0) * faces + (1.0 / 36.0) * edges
            first = [value * (3.0 / 36.0) for value in first]
            second = [value * (9.0 / 36.0) for value in second]
            twice = speed[0] * second[0] + speed[1] * second[1] + speed[2] * second[2]
            once = speed[0] * first[0] + speed[1] * first[1] + speed[2] * first[2]
            drag = once + twice - 3.0 * square * mean
            term = jnp.where(wall | inlet, 0.0, -relax_rate * (rho * share * drag))
            grad_ref[at, :] = term if step == STEPS - 1 else grad_ref[at, :] + term
            if step == 0:
                continue
            rest = relax_rate * (mean * (1.0 + 1.5 * square) - 0.5 * twice)
            push = [
                (relax_rate * share) * (first[axis] + second[axis] - 3.0 * mean * speed[axis]) for axis in range(3)
            ]
            for i in range(19):
                if i == 0:
                    post = (1.0 - relax_rate) * back[0] + rest
                else:
                    way = along_of(push, i if i % 2 else i - 1)
                    post = (1.0 - relax_rate) * back[i] + (rest + way if i % 2 else rest - way)
                post = jnp.where(wall, back[opposite[i]], jnp.where(inlet, 0.0, post))
                target[i, row + 8 : row + 16, :] = inside(post, block)

    smooth_ref[0:8, :] = zero
    smooth_ref[40:48, :] = zero
    for block in range(4):
        at = slice(8 * block, 8 * block + 8)
        value = inside(grad_ref[at, :] * share_ref[1, at, :], block)
        smooth_ref[8 * block + 8 : 8 * block + 16, :] = plane_smooth(value, rows, masks)
    for row in (8, 16):
        value = 0.5 * smooth_ref[row + 8 : row + 16, :] + 0.25 * (
            smooth_ref[row + 7 : row + 15, :] + smooth_ref[row + 9 : row + 17, :]
        )
        put(19, row - 8, value)
    second = lax.rem(lane_index() // 16 + 8 - me, 8) >= 4
    for group in range(3):
        plane = output_ref[group * LANES : (group + 1) * LANES, :].T
        for device in range(devices):
            tiles = []
            for layer in range(layers):
                at = (((device // splits) * layers + layer) * splits + device % splits) * 8
                tiles.append(plane[at : at + 8, :])
            if group < 2:
                for layer in range(layers):
                    packed_ref[device, group * layers + layer] = tiles[layer]
            else:
                packed_ref[device, group * layers] = jnp.where(second, tiles[1], tiles[0])


def result_kernel(splits, packed_ref, populations_ref, grad_ref):
    devices = [device_at(index, 8 // splits, splits) for index in range(8)]
    for tile in range(packed_ref.shape[1]):
        values = mixed([packed_ref[device, tile] for device in devices])
        for slot in range(8):
            value = rolled(values[-slot % 8], -16 * slot)
            if tile < 4:
                populations_ref[tile // 2 * 8 + slot, tile % 2] = value
            elif slot % 4 < 3:
                populations_ref[16 + slot % 4, slot // 4] = value
            else:
                grad_ref[slot // 4] = value


def call(kernel, outs, name, operands, spaces, scratch=(), room=32):
    vmem = pl.BlockSpec(memory_space=pltpu.VMEM)
    shapes = tuple(jax.ShapeDtypeStruct(shape, jnp.float32) for shape in outs)
    many = len(outs) > 1
    return pl.pallas_call(
        kernel,
        out_shape=shapes if many else shapes[0],
        in_specs=[pl.BlockSpec(memory_space=space) for space in spaces],
        out_specs=(vmem,) * len(outs) if many else vmem,
        scratch_shapes=list(scratch),
        compiler_params=pltpu.CompilerParams(vmem_limit_bytes=room * 2**20),
        name=name,
    )(*operands)


def body_by_columns(design, populations, cotangent, wall_mask, inlet_mask, beta_step):
    grp, splits, size = (lax.axis_size(axis) for axis in ("grp", "gy", "gx"))
    layers, height, width = design.shape
    rows, plane = height * splits, grp * splits
    tile = (layers, 8, LANES)
    vmem, real = pltpu.VMEM, jnp.float32
    design, packed = call(
        functools.partial(pack_kernel, splits),
        (tile, (plane, FIELDS // 8, *tile)),
        "pack",
        (design, populations, cotangent, wall_mask, inlet_mask),
        [pl.ANY] * 5,
        [vmem((38, *tile), real), vmem((2, *tile), jnp.int32), pltpu.SemaphoreType.DMA((5,))],
        60,
    )
    packed = lax.all_to_all(packed, ("grp", "gy"), 0, 0)
    designs = [design] * size
    for turn in reversed(range(1, size)):
        designs[turn] = lax.ppermute(design, "gx", [((i + turn) % size, i) for i in range(size)])
    copies = call(
        functools.partial(spread_kernel, size),
        ((plane, size, *tile),),
        "spread",
        designs,
        [vmem] * size,
        [vmem((size, *tile), real)],
    )
    outer = (-(-OUTER // 8) * 8, LANES)
    body, first, last = call(
        functools.partial(arrange_kernel, splits),
        ((FIELDS, 16, LANES), outer, outer),
        "arrange",
        (packed,),
        [vmem],
    )
    copies = lax.all_to_all(copies, ("grp", "gy"), 0, 0)
    path = [on_path(index, grp, splits) for index in range(plane)]
    order = [(path if gx % 2 == 0 else path[::-1])[index] * size + gx for gx in range(size) for index in range(plane)]
    up = list(zip(order[:-1], order[1:]))
    line = ("grp", "gy", "gx")
    before = lax.ppermute(last, line, up)
    after = lax.ppermute(first, line, [(j, i) for i, j in up])
    columns = size * LANES
    share = call(
        functools.partial(level_kernel, rows, splits, size),
        ((2, 32, LANES),),
        "level",
        (beta_step.reshape(1), copies),
        [pltpu.SMEM, vmem],
        [vmem((columns + 16, LANES), real), vmem((columns, LANES), real)],
    )
    shapes = [
        (19, 48, LANES),
        (19, 48, LANES),
        (19, 48, LANES),
        (STEPS, 4, 32, LANES),
        (32, LANES),
        (48, LANES),
        (3 * LANES, LANES),
    ]
    packed = call(
        functools.partial(flow_kernel, rows, splits, size),
        ((plane, 5, 8, LANES),),
        "flow",
        (share, body, before, after),
        [vmem] * 4,
        [vmem(shape, real) for shape in shapes],
    )
    packed = lax.all_to_all(packed, ("grp", "gy"), 0, 0)
    return call(functools.partial(result_kernel, splits), (populations.shape, design.shape), "result", (packed,), [vmem])


def body(design, populations, cotangent, wall_mask, inlet_mask, beta_step):
    grp, splits = lax.axis_size("grp"), lax.axis_size("gy")
    layers, height, width = design.shape
    fits = height == 8 and width == LANES and layers * grp * height * splits == LANES
    whole = body_by_columns if fits and grp * splits * 16 == LANES else body_by_blocks
    return whole(design, populations, cotangent, wall_mask, inlet_mask, beta_step)


def solution(mesh):
    placed = (
        P("grp", "gy", "gx"),
        P(None, "grp", "gy", "gx"),
        P(None, "grp", "gy", "gx"),
        P("grp", "gy", "gx"),
        P("grp", "gy", "gx"),
        P(),
    )
    return jax.shard_map(
        body,
        mesh=mesh,
        in_specs=placed,
        out_specs=(P(None, "grp", "gy", "gx"), P("grp", "gy", "gx")),
        check_vma=False,
    )
```

```python
import functools

import jax
import jax.numpy as jnp
import numpy as np
from jax import lax
from jax.experimental import pallas as pl
from jax.experimental.pallas import tpu as pltpu
from jax.sharding import PartitionSpec as P

STEPS = 4
BISECT = 30


velocities = np.array(
    [
        [0, 0, 0],
        [1, 0, 0],
        [-1, 0, 0],
        [0, 1, 0],
        [0, -1, 0],
        [0, 0, 1],
        [0, 0, -1],
        [1, 1, 0],
        [-1, -1, 0],
        [1, -1, 0],
        [-1, 1, 0],
        [1, 0, 1],
        [-1, 0, -1],
        [1, 0, -1],
        [-1, 0, 1],
        [0, 1, 1],
        [0, -1, -1],
        [0, 1, -1],
        [0, -1, 1],
    ]
)
opposite = [0, 2, 1, 4, 3, 6, 5, 8, 7, 10, 9, 12, 11, 14, 13, 16, 15, 18, 17]
lattice_weights = [1.0 / 3.0] + [1.0 / 18.0] * 6 + [1.0 / 36.0] * 12
relax_rate = 0.8
inlet_speed = 0.05
alpha_most = 8.0
penalty_shape = 0.1
fluid_share = 0.4


def extended(value, sides, width):
    for axis, dim in sides:
        size, length = (lax.axis_size(axis), value.shape[dim])
        up = [(i, (i + 1) % size) for i in range(size - 1)]
        down = [(j, i) for i, j in up]
        last = lax.slice_in_dim(value, length - width, length, axis=dim)
        leading = lax.slice_in_dim(value, 0, width, axis=dim)
        before = lax.ppermute(last, axis, up)
        after = lax.ppermute(leading, axis, down)
        value = jnp.concatenate([before, value, after], axis=dim)
    return value


def equilibrium(density, speed_z, speed_y, speed_x):
    square = speed_z * speed_z + speed_y * speed_y + speed_x * speed_x
    comps = []
    for i in range(19):
        along = (
            float(velocities[i][0]) * speed_z
            + float(velocities[i][1]) * speed_y
            + float(velocities[i][2]) * speed_x
        )
        comps.append(
            lattice_weights[i] * density * (1.0 + 3.0 * along + 4.5 * along * along - 1.5 * square)
        )
    return jnp.stack(comps)


def moment(popul, axis):
    total = jnp.zeros(popul.shape[1:], popul.dtype)
    for i in range(1, 19):
        if velocities[i][axis] != 0:
            total = total + float(velocities[i][axis]) * popul[i]
    return total


def collide(popul, alpha, wall_mask, inlet_mask):
    density = jnp.sum(popul, axis=0)
    scale = density * (1.0 + alpha)
    feq = equilibrium(
        density, moment(popul, 0) / scale, moment(popul, 1) / scale, moment(popul, 2) / scale
    )
    post = popul + relax_rate * (feq - popul)
    bounce = jnp.stack([popul[opposite[i]] for i in range(19)])
    inlet_values = []
    for i in range(19):
        along = float(velocities[i][0]) * inlet_speed
        inlet_values.append(
            lattice_weights[i]
            * (1.0 + 3.0 * along + 4.5 * along * along - 1.5 * inlet_speed * inlet_speed)
        )
    inlet_feq = jnp.stack([jnp.full(popul.shape[1:], value, popul.dtype) for value in inlet_values])
    return jnp.where(wall_mask[None] > 0, bounce, jnp.where(inlet_mask[None] > 0, inlet_feq, post))


def pick(padded, sign):
    depth, rows, cols = (padded.shape[1] - 2, padded.shape[2] - 2, padded.shape[3] - 2)
    outputs = []
    for i in range(19):
        start_z = 1 - sign * int(velocities[i][0])
        start_y = 1 - sign * int(velocities[i][1])
        start_x = 1 - sign * int(velocities[i][2])
        outputs.append(
            padded[i, start_z : start_z + depth, start_y : start_y + rows, start_x : start_x + cols]
        )
    return jnp.stack(outputs)


def shift_all(popul, sign):
    padded = extended(popul, (("grp", 1), ("gy", 2), ("gx", 3)), 1)
    return pick(padded, sign)


def smooth_field(field):
    padded = extended(field, (("grp", 0), ("gy", 1), ("gx", 2)), 1)
    along_z = 0.25 * padded[:-2] + 0.5 * padded[1:-1] + 0.25 * padded[2:]
    along_y = 0.25 * along_z[:, :-2] + 0.5 * along_z[:, 1:-1] + 0.25 * along_z[:, 2:]
    return 0.25 * along_y[:, :, :-2] + 0.5 * along_y[:, :, 1:-1] + 0.25 * along_y[:, :, 2:]


def project(filtered, thresh, beta):
    denom = jnp.tanh(beta * thresh) + jnp.tanh(beta * (1.0 - thresh))
    return (jnp.tanh(beta * thresh) + jnp.tanh(beta * (filtered - thresh))) / denom


def threshold_kernel(cells, beta_ref, filtered_ref, eta_ref, raised_ref):
    beta = jnp.full((8, 128), beta_ref[0], jnp.float32)
    raised_ref[...] = jnp.exp(2.0 * beta_ref[0] * filtered_ref[...])
    top = jnp.exp(2.0 * beta)
    rows = filtered_ref.shape[0]
    span = min(rows, 512)

    def halve(step, ends):
        low, high = ends
        middle = 0.5 * (low + high)
        level = jnp.exp(2.0 * beta * middle)

        def part(index, total):
            for row in range(0, span, 8):
                raised = raised_ref[pl.ds(pl.multiple_of(index * span + row, 8), 8), :]
                total = total + (raised - 1.0) / (raised + level)
            return total

        total = lax.fori_loop(0, rows // span, part, jnp.zeros((8, 128), jnp.float32))
        volume = jnp.sum(jnp.sum(total, axis=0, keepdims=True), axis=1, keepdims=True)
        above = volume * ((top + level) / (top - 1.0)) > fluid_share * cells
        return jnp.where(above, middle, low), jnp.where(above, high, middle)

    low, high = lax.fori_loop(
        0, BISECT, halve, (jnp.zeros((8, 128), jnp.float32), jnp.ones((8, 128), jnp.float32))
    )
    eta_ref[...] = 0.5 * (low + high)


def threshold(filtered, beta, cells):
    eta = pl.pallas_call(
        functools.partial(threshold_kernel, cells),
        out_shape=jax.ShapeDtypeStruct((8, 128), jnp.float32),
        in_specs=[
            pl.BlockSpec(memory_space=pltpu.SMEM),
            pl.BlockSpec(memory_space=pltpu.VMEM),
        ],
        out_specs=pl.BlockSpec(memory_space=pltpu.VMEM),
        scratch_shapes=[pltpu.VMEM(filtered.shape, jnp.float32)],
        compiler_params=pltpu.CompilerParams(vmem_limit_bytes=40 * 2**20),
        name="threshold",
    )(beta.reshape(1), filtered)
    return eta[0, 0]


def body_by_blocks(design, populations, cotangent, wall_mask, inlet_mask, beta_step):
    beta = jnp.exp2(beta_step.astype(jnp.float32) / 16.0)
    filtered = smooth_field(design)
    cells = design.size * lax.axis_size("grp") * lax.axis_size("gy") * lax.axis_size("gx")
    devices = lax.axis_size("grp") * lax.axis_size("gy") * lax.axis_size("gx")
    copies = jnp.broadcast_to(filtered, (devices, *filtered.shape))
    everywhere = lax.all_to_all(copies, ("grp", "gy", "gx"), 0, 0)
    eta = threshold(everywhere.reshape(-1, filtered.shape[-1]), beta, cells)
    density_hat = project(filtered, eta, beta)
    alpha = alpha_most * penalty_shape * (1.0 - density_hat) / (penalty_shape + density_hat)
    states = []
    popul = populations
    for step in range(STEPS):
        states.append(popul)
        popul = shift_all(collide(popul, alpha, wall_mask, inlet_mask), 1)
    adjoint = cotangent
    alpha_grad = jnp.zeros_like(alpha)
    for step in reversed(range(STEPS)):
        back = shift_all(adjoint, -1)
        unused, pullback = jax.vjp(
            lambda p, a: collide(p, a, wall_mask, inlet_mask), states[step], alpha
        )
        adjoint, term = pullback(back)
        alpha_grad = alpha_grad + term
    denom = jnp.tanh(beta * eta) + jnp.tanh(beta * (1.0 - eta))
    slope = beta * (1.0 - jnp.tanh(beta * (filtered - eta)) ** 2) / denom
    factor = (
        -alpha_most * penalty_shape * (1.0 + penalty_shape) / (penalty_shape + density_hat) ** 2
    )
    design_grad = smooth_field(alpha_grad * factor * slope)
    return (popul, design_grad)


LANES = 128
AROUND = ((1, 0), (-1, 0), (0, 1), (0, -1), (1, 1), (-1, -1), (1, -1), (-1, 1))
FIELDS = 40
NEAR = STEPS + 1
OUTER = 8 * 21 + NEAR * 19
CLOSE = 2.0**-14


def rolled(value, amount):
    amount = amount % LANES
    return value if amount == 0 else pltpu.roll(value, amount, 1)


def lane_index():
    return lax.broadcasted_iota(jnp.int32, (8, LANES), 1)


def on_path(index, grp, splits):
    part, step = index // grp, index % grp
    return (step if part % 2 == 0 else grp - 1 - step) * splits + part


def device_at(index, grp, splits):
    odd = lax.rem(lax.axis_index("gx"), 2)
    return jnp.where(odd == 0, on_path(index, grp, splits), on_path(grp * splits - 1 - index, grp, splits))


def block_here(grp, splits):
    step, part = lax.axis_index("grp"), lax.axis_index("gy")
    index = part * grp + jnp.where(lax.rem(part, 2) == 0, step, grp - 1 - step)
    return jnp.where(lax.rem(lax.axis_index("gx"), 2) == 0, index, grp * splits - 1 - index)


def mixed(values):
    place = lane_index() // 16
    for half in (4, 2, 1):
        upper = (place & half) != 0
        values = [jnp.where(upper, values[(index + half) % 8], values[index]) for index in range(8)]
    return values


def pack_kernel(
    splits, design_ref, populations_ref, cotangent_ref, wall_ref, inlet_ref, design_out_ref, packed_ref,
    fields_ref, masks_ref, stage_ref, sems, out_sems,
):
    moves = [
        pltpu.make_async_copy(populations_ref, fields_ref.at[0:19], sems.at[0]),
        pltpu.make_async_copy(wall_ref, masks_ref.at[0], sems.at[1]),
        pltpu.make_async_copy(inlet_ref, masks_ref.at[1], sems.at[2]),
        pltpu.make_async_copy(cotangent_ref, fields_ref.at[19:38], sems.at[3]),
        pltpu.make_async_copy(design_ref, design_out_ref, sems.at[4]),
    ]
    for move in moves:
        move.start()
    devices = [device_at(index, 8 // splits, splits) for index in range(8)]
    needs = {0: moves[:1], 2: moves[1:4]}
    results = []
    for group in range(FIELDS // 8):
        for move in needs.get(group, ()):
            move.wait()
        for layer in range(masks_ref.shape[1]):
            values = []
            for slot in range(8):
                index = group * 8 + slot
                if index in (19, 20):
                    value = masks_ref[index - 19, layer].astype(jnp.float32)
                else:
                    value = fields_ref[index if index < 19 else index - 2, layer]
                values.append(rolled(value, 16 * slot))
            values = mixed(values)
            for index in range(8):
                stage_ref[group, devices[index], layer] = values[-index % 8]
        results.append(pltpu.make_async_copy(stage_ref.at[group], packed_ref.at[:, group], out_sems.at[group]))
        results[-1].start()
    for move in results + moves[4:]:
        move.wait()


def arrange_kernel(splits, packed_ref, body_ref, first_ref, last_ref):
    layers = packed_ref.shape[2]
    planes = packed_ref.shape[0] // splits * layers
    me = block_here(packed_ref.shape[0] // splits, splits)
    for group in range(FIELDS // 8):
        plane = gather_plane(
            lambda z, part: packed_ref[(z // layers) * splits + part, group, z % layers], planes, splits
        ).T
        for slot in range(8):
            index = group * 8 + lax.rem(slot + 8 - me, 8)
            body_ref[index] = plane[16 * slot : 16 * slot + 16, :]
    for index in range(FIELDS):
        if index < 21:
            first_ref[8 * index : 8 * index + 8, :] = body_ref[index, 0:8, :]
            last_ref[8 * index : 8 * index + 8, :] = body_ref[index, 8:16, :]
        else:
            start = 8 * 21 + NEAR * (index - 21)
            first_ref[start : start + NEAR, :] = body_ref[index, 0:NEAR, :]
            last_ref[start : start + NEAR, :] = body_ref[index, 16 - NEAR : 16, :]
    for ref in (first_ref, last_ref):
        rest = ref.shape[0] - OUTER
        ref[OUTER:, :] = jnp.zeros((rest, LANES), jnp.float32)


def spread_kernel(size, *refs):
    design_refs, (copies_ref, design_ref, smooth_ref, sems) = refs[:size], refs[size:]
    here = lax.axis_index("gx")
    for turn in range(size):
        design_ref[here ^ turn] = design_refs[turn][...]
    lanes = lane_index()
    zero = jnp.zeros((8, LANES), jnp.float32)
    for layer in range(copies_ref.shape[2]):
        tiles = [zero] + [design_ref[index, layer] for index in range(size)] + [zero]
        ahead = [rolled(tile, 1) for tile in tiles]
        behind = [rolled(tile, -1) for tile in tiles]
        for index in range(1, size + 1):
            smooth_ref[index - 1, layer] = 0.5 * tiles[index] + 0.25 * (
                jnp.where(lanes == 0, ahead[index - 1], ahead[index])
                + jnp.where(lanes == LANES - 1, behind[index + 1], behind[index])
            )
    moves = [
        pltpu.make_async_copy(smooth_ref, copies_ref.at[device], sems.at[device])
        for device in range(copies_ref.shape[0])
    ]
    for move in moves:
        move.start()
    for move in moves:
        move.wait()


def exponent(step_ref):
    steps = jnp.full((8, LANES), step_ref[0], jnp.int32).astype(jnp.float32)
    return jnp.exp2(steps / 16.0)


def plane_masks(rows):
    lanes = lane_index()
    depth, place_z, place_y = LANES // rows, lanes // rows, lanes % rows
    masks = {}
    for cz, cy in AROUND:
        inside = None
        for shift, place, count in ((cz, place_z, depth), (cy, place_y, rows)):
            if shift:
                here = (place >= 1) if shift > 0 else (place < count - 1)
                inside = here if inside is None else inside & here
        masks[cz, cy] = inside
    return masks


def plane_shift(value, cz, cy, rows, masks):
    if cz == 0 and cy == 0:
        return value
    return jnp.where(masks[cz, cy], rolled(value, cz * rows + cy), 0.0)


def plane_smooth(value, rows, masks):
    for cz, cy in ((1, 0), (0, 1)):
        value = 0.5 * value + 0.25 * (
            plane_shift(value, cz, cy, rows, masks) + plane_shift(value, -cz, -cy, rows, masks)
        )
    return value


def gather_plane(read, planes, splits):
    blocks = []
    for z in range(planes):
        for part in range(splits):
            blocks.append(read(z, part))
    return jnp.concatenate(blocks, axis=0)


def volume_root(raised_ref, columns, beta):
    zero = jnp.zeros((8, LANES), jnp.float32)
    one = jnp.ones((8, LANES), jnp.float32)
    cells = columns * LANES
    top = jnp.exp(2.0 * beta)
    scale = 1.0 / (top - 1.0)

    def total(parts):
        value = (parts[0] + parts[1]) + (parts[2] + parts[3])
        return jnp.sum(jnp.sum(value, axis=0, keepdims=True), axis=1, keepdims=True)

    def advance(state):
        low, high, low_known, high_known, middle, _ = state
        level = jnp.exp(2.0 * beta * middle)
        sums, squares = [zero] * 4, [zero] * 4
        for index, row in enumerate(range(0, columns, 8)):
            raised = raised_ref[row : row + 8, :] + level
            part = pl.reciprocal(raised, approx=True)
            part = part * (2.0 - raised * part)
            sums[index % 4] = sums[index % 4] + part
            squares[index % 4] = squares[index % 4] + part * part
        first, second = total(sums), total(squares)
        volume = cells - (1.0 + level) * first
        slope = first - (1.0 + level) * second
        whole = (top + level) * scale
        excess = volume * whole - fluid_share * cells
        slope = (2.0 * beta * level) * (volume * scale - whole * slope)
        above = excess > 0.0
        low, low_known = jnp.where(above, middle, low), jnp.where(above, 1.0, low_known)
        high, high_known = jnp.where(above, high, middle), jnp.where(above, high_known, 1.0)
        guess = middle - excess / slope
        taken = (guess >= low) & (guess <= high)
        other = jnp.where(
            (guess > high) & (high_known == 0.0),
            high,
            jnp.where((guess < low) & (low_known == 0.0), low, 0.5 * (low + high)),
        )
        change = jnp.where(taken, jnp.abs(guess - middle), 2.0**16 * (high - low))
        return low, high, low_known, high_known, jnp.where(taken, guess, other), change

    def going(carry):
        step, state = carry
        return (step < 64) & (jnp.max(state[5]) > CLOSE)

    state = advance(advance((zero, one, zero, zero, 0.5 * one, zero)))
    _, state = lax.while_loop(going, lambda carry: (carry[0] + 1, advance(carry[1])), (2, state))
    return jnp.clip(state[4], 0.5**31, 1.0)


def level_kernel(rows, splits, size, step_ref, copies_ref, share_ref, filtered_ref, raised_ref):
    layers = copies_ref.shape[2]
    planes = LANES // rows
    columns = size * LANES
    masks = plane_masks(rows)
    zero = jnp.zeros((8, LANES), jnp.float32)
    beta = exponent(step_ref)
    filtered_ref[0:8, :] = zero
    filtered_ref[columns + 8 : columns + 16, :] = zero
    for block in range(size):
        plane = gather_plane(
            lambda z, part: copies_ref[(z // layers) * splits + part, block, z % layers], planes, splits
        )
        filtered_ref[8 + block * LANES : 8 + (block + 1) * LANES, :] = plane.T
    for row in range(8, columns + 8, 8):
        value = plane_smooth(filtered_ref[row : row + 8, :], rows, masks)
        filtered_ref[row : row + 8, :] = value
        raised_ref[row - 8 : row, :] = jnp.exp(2.0 * beta * value)
    eta = volume_root(raised_ref, columns, beta)
    place = lax.axis_index("gx") * copies_ref.shape[0] + block_here(copies_ref.shape[0] // splits, splits)
    level = jnp.exp(2.0 * beta * eta)
    top = jnp.exp(2.0 * beta)
    whole = (top + level) / (top - 1.0)
    strength = alpha_most * penalty_shape
    for block in range(4):
        at = slice(8 * block, 8 * block + 8)
        start = pl.multiple_of(place * 16 + 8 * block, 8)
        raised = jnp.exp(2.0 * beta * filtered_ref[pl.ds(start, 8), :])
        part = 1.0 / (raised + level)
        density_hat = ((raised - 1.0) * part) * whole
        share_ref[0, at, :] = (penalty_shape + density_hat) / (
            penalty_shape + strength + (1.0 - strength) * density_hat
        )
        slope = 2.0 * beta * (raised * part) * ((level + 1.0) * part) * whole
        factor = -strength * (1.0 + penalty_shape) / (
            (penalty_shape + density_hat) * (penalty_shape + density_hat)
        )
        share_ref[1, at, :] = slope * factor


def flow(rho, speed):
    square = 1.0 - 1.5 * (speed[0] * speed[0] + speed[1] * speed[1] + speed[2] * speed[2])
    comps = [lattice_weights[0] * rho * square]
    weighted = {1.0 / 18.0: rho * (1.0 / 18.0), 1.0 / 36.0: rho * (1.0 / 36.0)}
    for i in range(1, 19, 2):
        along = along_of(speed, i)
        weight = weighted[lattice_weights[i]]
        even = weight * (square + 4.5 * along * along)
        odd = weight * (3.0 * along)
        comps += [even + odd, even - odd]
    return comps


def along_of(speed, i):
    total = None
    for axis in range(3):
        sign = int(velocities[i][axis])
        if sign:
            if total is None:
                total = speed[axis] if sign > 0 else -speed[axis]
            else:
                total = total + speed[axis] if sign > 0 else total - speed[axis]
    return total


def add_along(totals, value, i):
    for axis in range(3):
        sign = int(velocities[i][axis])
        if sign:
            if totals[axis] is None:
                totals[axis] = value if sign > 0 else -value
            else:
                totals[axis] = totals[axis] + value if sign > 0 else totals[axis] - value


def inlet_value(i):
    along = float(velocities[i][0]) * inlet_speed
    return lattice_weights[i] * (1.0 + 3.0 * along + 4.5 * along * along - 1.5 * inlet_speed * inlet_speed)


def flow_kernel(
    rows, splits, size, share_ref, body_ref, before_ref, after_ref, packed_ref,
    cotangent_ref, even_ref, odd_ref, kept_ref, grad_ref, smooth_ref, output_ref,
):
    devices = packed_ref.shape[0]
    planes = LANES // rows
    layers = planes * splits // devices
    masks = plane_masks(rows)
    zero = jnp.zeros((8, LANES), jnp.float32)
    me = block_here(devices // splits, splits)
    place = lax.axis_index("gx") * devices + me
    last = size * devices - 1

    def inside(value, block):
        if block == 0:
            return jnp.where(place > 0, value, 0.0)
        if block == 3:
            return jnp.where(place < last, value, 0.0)
        return value

    def initial(i, row):
        if row == 0:
            return before_ref[8 * i : 8 * i + 8, :]
        if row == 24:
            return after_ref[8 * i : 8 * i + 8, :]
        return body_ref[i, row - 8 : row, :]

    for ref in (even_ref, odd_ref, cotangent_ref):
        for i in range(19):
            ref[i, 0:8, :] = zero
            ref[i, 40:48, :] = zero
    for i in range(19):
        start = 8 * 21 + NEAR * i
        cotangent_ref[i, 8:16, :] = zero
        cotangent_ref[i, 16 - NEAR : 16, :] = before_ref[start : start + NEAR, :]
        cotangent_ref[i, 16:32, :] = body_ref[21 + i]
        cotangent_ref[i, 32:40, :] = zero
        cotangent_ref[i, 32 : 32 + NEAR, :] = after_ref[start : start + NEAR, :]

    def arrived(ref, i, row):
        cz, cy, cx = (int(c) for c in velocities[i])
        return plane_shift(ref[i, row + 8 - cx : row + 16 - cx, :], cz, cy, rows, masks)

    buffers = (even_ref, odd_ref)
    for step in range(STEPS):
        source, target = buffers[(step + 1) % 2], buffers[step % 2]
        for block in range(4):
            row = 8 * block
            at = slice(row, row + 8)
            if step == 0:
                popul = [initial(i, row) for i in range(19)]
            else:
                popul = [arrived(source, i, row) for i in range(19)]
            wall = initial(19, row) > 0.0
            inlet = initial(20, row) > 0.0
            rho = popul[0]
            momentum = [None, None, None]
            for i in range(1, 19, 2):
                rho = rho + (popul[i] + popul[i + 1])
                add_along(momentum, popul[i] - popul[i + 1], i)
            scale = share_ref[0, at, :] / rho
            speed = [value * scale for value in momentum]
            kept_ref[step, 0, at, :] = rho
            for axis in range(3):
                kept_ref[step, 1 + axis, at, :] = speed[axis]
            settled = flow(relax_rate * rho, speed)
            for i in range(19):
                post = (1.0 - relax_rate) * popul[i] + settled[i]
                post = jnp.where(wall, popul[opposite[i]], jnp.where(inlet, inlet_value(i), post))
                target[i, row + 8 : row + 16, :] = inside(post, block)
    def put(index, row, value):
        group, slot = divmod(index, 8)
        for slot in (slot,) if group < 2 else (slot, slot + 4):
            start = group * LANES + 16 * lax.rem(slot + me, 8) + row
            output_ref[pl.ds(pl.multiple_of(start, 8), 8), :] = value

    source = buffers[(STEPS - 1) % 2]
    for i in range(19):
        for row in (8, 16):
            put(i, row - 8, arrived(source, i, row))

    for step in reversed(range(STEPS)):
        source = cotangent_ref if step == STEPS - 1 else buffers[step % 2]
        target = buffers[(step + 1) % 2]
        for block in range(4):
            row = 8 * block
            at = slice(row, row + 8)
            back = []
            for i in range(19):
                cz, cy, cx = (int(c) for c in velocities[i])
                value = source[i, row + 8 + cx : row + 16 + cx, :]
                back.append(plane_shift(value, -cz, -cy, rows, masks))
            wall = initial(19, row) > 0.0
            inlet = initial(20, row) > 0.0
            rho = kept_ref[step, 0, at, :]
            speed = [kept_ref[step, 1 + axis, at, :] for axis in range(3)]
            square = speed[0] * speed[0] + speed[1] * speed[1] + speed[2] * speed[2]
            share = share_ref[0, at, :]
            faces, edges = None, None
            first, second = [None, None, None], [None, None, None]
            for i in range(1, 19, 2):
                both, apart = back[i] + back[i + 1], back[i] - back[i + 1]
                if i < 7:
                    faces = both if faces is None else faces + both
                    both, apart = 2.0 * both, 2.0 * apart
                else:
                    edges = both if edges is None else edges + both
                add_along(first, apart, i)
                add_along(second, along_of(speed, i) * both, i)
            mean = lattice_weights[0] * back[0] + (1.0 / 18.0) * faces + (1.0 / 36.0) * edges
            first = [value * (3.0 / 36.0) for value in first]
            second = [value * (9.0 / 36.0) for value in second]
            twice = speed[0] * second[0] + speed[1] * second[1] + speed[2] * second[2]
            once = speed[0] * first[0] + speed[1] * first[1] + speed[2] * first[2]
            drag = once + twice - 3.0 * square * mean
            term = jnp.where(wall | inlet, 0.0, -relax_rate * (rho * share * drag))
            grad_ref[at, :] = term if step == STEPS - 1 else grad_ref[at, :] + term
            if step == 0:
                continue
            rest = relax_rate * (mean * (1.0 + 1.5 * square) - 0.5 * twice)
            push = [
                (relax_rate * share) * (first[axis] + second[axis] - 3.0 * mean * speed[axis]) for axis in range(3)
            ]
            for i in range(19):
                if i == 0:
                    post = (1.0 - relax_rate) * back[0] + rest
                else:
                    way = along_of(push, i if i % 2 else i - 1)
                    post = (1.0 - relax_rate) * back[i] + (rest + way if i % 2 else rest - way)
                post = jnp.where(wall, back[opposite[i]], jnp.where(inlet, 0.0, post))
                target[i, row + 8 : row + 16, :] = inside(post, block)

    smooth_ref[0:8, :] = zero
    smooth_ref[40:48, :] = zero
    for block in range(4):
        at = slice(8 * block, 8 * block + 8)
        value = inside(grad_ref[at, :] * share_ref[1, at, :], block)
        smooth_ref[8 * block + 8 : 8 * block + 16, :] = plane_smooth(value, rows, masks)
    for row in (8, 16):
        value = 0.5 * smooth_ref[row + 8 : row + 16, :] + 0.25 * (
            smooth_ref[row + 7 : row + 15, :] + smooth_ref[row + 9 : row + 17, :]
        )
        put(19, row - 8, value)
    second = lax.rem(lane_index() // 16 + 8 - me, 8) >= 4
    for group in range(3):
        plane = output_ref[group * LANES : (group + 1) * LANES, :].T
        for device in range(devices):
            tiles = []
            for layer in range(layers):
                at = (((device // splits) * layers + layer) * splits + device % splits) * 8
                tiles.append(plane[at : at + 8, :])
            if group < 2:
                for layer in range(layers):
                    packed_ref[device, group * layers + layer] = tiles[layer]
            else:
                packed_ref[device, group * layers] = jnp.where(second, tiles[1], tiles[0])


def result_kernel(splits, packed_ref, populations_ref, grad_ref):
    devices = [device_at(index, 8 // splits, splits) for index in range(8)]
    for tile in range(packed_ref.shape[1]):
        values = mixed([packed_ref[device, tile] for device in devices])
        for slot in range(8):
            value = rolled(values[-slot % 8], -16 * slot)
            if tile < 4:
                populations_ref[tile // 2 * 8 + slot, tile % 2] = value
            elif slot % 4 < 3:
                populations_ref[16 + slot % 4, slot // 4] = value
            else:
                grad_ref[slot // 4] = value


def call(kernel, outs, name, operands, spaces, scratch=(), room=32, results=None):
    shapes = tuple(jax.ShapeDtypeStruct(shape, jnp.float32) for shape in outs)
    places = tuple(pl.BlockSpec(memory_space=space) for space in results or [pltpu.VMEM] * len(outs))
    many = len(outs) > 1
    return pl.pallas_call(
        kernel,
        out_shape=shapes if many else shapes[0],
        in_specs=[pl.BlockSpec(memory_space=space) for space in spaces],
        out_specs=places if many else places[0],
        scratch_shapes=list(scratch),
        compiler_params=pltpu.CompilerParams(vmem_limit_bytes=room * 2**20),
        name=name,
    )(*operands)


def body_by_columns(design, populations, cotangent, wall_mask, inlet_mask, beta_step):
    grp, splits, size = (lax.axis_size(axis) for axis in ("grp", "gy", "gx"))
    layers, height, width = design.shape
    rows, plane = height * splits, grp * splits
    tile = (layers, 8, LANES)
    vmem, real = pltpu.VMEM, jnp.float32
    design, packed = call(
        functools.partial(pack_kernel, splits),
        (tile, (plane, FIELDS // 8, *tile)),
        "pack",
        (design, populations, cotangent, wall_mask, inlet_mask),
        [pl.ANY] * 5,
        [
            vmem((38, *tile), real),
            vmem((2, *tile), jnp.int32),
            vmem((FIELDS // 8, plane, *tile), real),
            pltpu.SemaphoreType.DMA((5,)),
            pltpu.SemaphoreType.DMA((FIELDS // 8,)),
        ],
        60,
        [pl.ANY, pl.ANY],
    )
    packed = lax.all_to_all(packed, ("grp", "gy"), 0, 0)
    designs = [design]
    while len(designs) < size:
        pairs = [(i, i ^ len(designs)) for i in range(size)]
        designs += [lax.ppermute(value, "gx", pairs) for value in designs]
    copies = call(
        functools.partial(spread_kernel, size),
        ((plane, size, *tile),),
        "spread",
        designs,
        [vmem] * size,
        [vmem((size, *tile), real), vmem((size, *tile), real), pltpu.SemaphoreType.DMA((plane,))],
        results=[pl.ANY],
    )
    outer = (-(-OUTER // 8) * 8, LANES)
    body, first, last = call(
        functools.partial(arrange_kernel, splits),
        ((FIELDS, 16, LANES), outer, outer),
        "arrange",
        (packed,),
        [vmem],
    )
    copies = lax.all_to_all(copies, ("grp", "gy"), 0, 0)
    path = [on_path(index, grp, splits) for index in range(plane)]
    order = [(path if gx % 2 == 0 else path[::-1])[index] * size + gx for gx in range(size) for index in range(plane)]
    up = list(zip(order[:-1], order[1:]))
    line = ("grp", "gy", "gx")
    before = lax.ppermute(last, line, up)
    after = lax.ppermute(first, line, [(j, i) for i, j in up])
    columns = size * LANES
    share = call(
        functools.partial(level_kernel, rows, splits, size),
        ((2, 32, LANES),),
        "level",
        (beta_step.reshape(1), copies),
        [pltpu.SMEM, vmem],
        [vmem((columns + 16, LANES), real), vmem((columns, LANES), real)],
    )
    shapes = [
        (19, 48, LANES),
        (19, 48, LANES),
        (19, 48, LANES),
        (STEPS, 4, 32, LANES),
        (32, LANES),
        (48, LANES),
        (3 * LANES, LANES),
    ]
    packed = call(
        functools.partial(flow_kernel, rows, splits, size),
        ((plane, 5, 8, LANES),),
        "flow",
        (share, body, before, after),
        [vmem] * 4,
        [vmem(shape, real) for shape in shapes],
    )
    packed = lax.all_to_all(packed, ("grp", "gy"), 0, 0)
    return call(functools.partial(result_kernel, splits), (populations.shape, design.shape), "result", (packed,), [vmem])


def body(design, populations, cotangent, wall_mask, inlet_mask, beta_step):
    grp, splits = lax.axis_size("grp"), lax.axis_size("gy")
    layers, height, width = design.shape
    fits = height == 8 and width == LANES and layers * grp * height * splits == LANES
    size = lax.axis_size("gx")
    fits = fits and grp * splits * 16 == LANES and size & (size - 1) == 0
    whole = body_by_columns if fits else body_by_blocks
    return whole(design, populations, cotangent, wall_mask, inlet_mask, beta_step)


def solution(mesh):
    placed = (
        P("grp", "gy", "gx"),
        P(None, "grp", "gy", "gx"),
        P(None, "grp", "gy", "gx"),
        P("grp", "gy", "gx"),
        P("grp", "gy", "gx"),
        P(),
    )
    return jax.shard_map(
        body,
        mesh=mesh,
        in_specs=placed,
        out_specs=(P(None, "grp", "gy", "gx"), P("grp", "gy", "gx")),
        check_vma=False,
    )
```

```python
import functools

import jax
import jax.numpy as jnp
import numpy as np
from jax import lax
from jax.experimental import pallas as pl
from jax.experimental.pallas import tpu as pltpu
from jax.sharding import PartitionSpec as P

STEPS = 4
BISECT = 30


velocities = np.array(
    [
        [0, 0, 0],
        [1, 0, 0],
        [-1, 0, 0],
        [0, 1, 0],
        [0, -1, 0],
        [0, 0, 1],
        [0, 0, -1],
        [1, 1, 0],
        [-1, -1, 0],
        [1, -1, 0],
        [-1, 1, 0],
        [1, 0, 1],
        [-1, 0, -1],
        [1, 0, -1],
        [-1, 0, 1],
        [0, 1, 1],
        [0, -1, -1],
        [0, 1, -1],
        [0, -1, 1],
    ]
)
opposite = [0, 2, 1, 4, 3, 6, 5, 8, 7, 10, 9, 12, 11, 14, 13, 16, 15, 18, 17]
lattice_weights = [1.0 / 3.0] + [1.0 / 18.0] * 6 + [1.0 / 36.0] * 12
relax_rate = 0.8
inlet_speed = 0.05
alpha_most = 8.0
penalty_shape = 0.1
fluid_share = 0.4


def extended(value, sides, width):
    for axis, dim in sides:
        size, length = (lax.axis_size(axis), value.shape[dim])
        up = [(i, (i + 1) % size) for i in range(size - 1)]
        down = [(j, i) for i, j in up]
        last = lax.slice_in_dim(value, length - width, length, axis=dim)
        leading = lax.slice_in_dim(value, 0, width, axis=dim)
        before = lax.ppermute(last, axis, up)
        after = lax.ppermute(leading, axis, down)
        value = jnp.concatenate([before, value, after], axis=dim)
    return value


def equilibrium(density, speed_z, speed_y, speed_x):
    square = speed_z * speed_z + speed_y * speed_y + speed_x * speed_x
    comps = []
    for i in range(19):
        along = (
            float(velocities[i][0]) * speed_z
            + float(velocities[i][1]) * speed_y
            + float(velocities[i][2]) * speed_x
        )
        comps.append(
            lattice_weights[i] * density * (1.0 + 3.0 * along + 4.5 * along * along - 1.5 * square)
        )
    return jnp.stack(comps)


def moment(popul, axis):
    total = jnp.zeros(popul.shape[1:], popul.dtype)
    for i in range(1, 19):
        if velocities[i][axis] != 0:
            total = total + float(velocities[i][axis]) * popul[i]
    return total


def collide(popul, alpha, wall_mask, inlet_mask):
    density = jnp.sum(popul, axis=0)
    scale = density * (1.0 + alpha)
    feq = equilibrium(
        density, moment(popul, 0) / scale, moment(popul, 1) / scale, moment(popul, 2) / scale
    )
    post = popul + relax_rate * (feq - popul)
    bounce = jnp.stack([popul[opposite[i]] for i in range(19)])
    inlet_values = []
    for i in range(19):
        along = float(velocities[i][0]) * inlet_speed
        inlet_values.append(
            lattice_weights[i]
            * (1.0 + 3.0 * along + 4.5 * along * along - 1.5 * inlet_speed * inlet_speed)
        )
    inlet_feq = jnp.stack([jnp.full(popul.shape[1:], value, popul.dtype) for value in inlet_values])
    return jnp.where(wall_mask[None] > 0, bounce, jnp.where(inlet_mask[None] > 0, inlet_feq, post))


def pick(padded, sign):
    depth, rows, cols = (padded.shape[1] - 2, padded.shape[2] - 2, padded.shape[3] - 2)
    outputs = []
    for i in range(19):
        start_z = 1 - sign * int(velocities[i][0])
        start_y = 1 - sign * int(velocities[i][1])
        start_x = 1 - sign * int(velocities[i][2])
        outputs.append(
            padded[i, start_z : start_z + depth, start_y : start_y + rows, start_x : start_x + cols]
        )
    return jnp.stack(outputs)


def shift_all(popul, sign):
    padded = extended(popul, (("grp", 1), ("gy", 2), ("gx", 3)), 1)
    return pick(padded, sign)


def smooth_field(field):
    padded = extended(field, (("grp", 0), ("gy", 1), ("gx", 2)), 1)
    along_z = 0.25 * padded[:-2] + 0.5 * padded[1:-1] + 0.25 * padded[2:]
    along_y = 0.25 * along_z[:, :-2] + 0.5 * along_z[:, 1:-1] + 0.25 * along_z[:, 2:]
    return 0.25 * along_y[:, :, :-2] + 0.5 * along_y[:, :, 1:-1] + 0.25 * along_y[:, :, 2:]


def project(filtered, thresh, beta):
    denom = jnp.tanh(beta * thresh) + jnp.tanh(beta * (1.0 - thresh))
    return (jnp.tanh(beta * thresh) + jnp.tanh(beta * (filtered - thresh))) / denom


def threshold_kernel(cells, beta_ref, filtered_ref, eta_ref, raised_ref):
    beta = jnp.full((8, 128), beta_ref[0], jnp.float32)
    raised_ref[...] = jnp.exp(2.0 * beta_ref[0] * filtered_ref[...])
    top = jnp.exp(2.0 * beta)
    rows = filtered_ref.shape[0]
    span = min(rows, 512)

    def halve(step, ends):
        low, high = ends
        middle = 0.5 * (low + high)
        level = jnp.exp(2.0 * beta * middle)

        def part(index, total):
            for row in range(0, span, 8):
                raised = raised_ref[pl.ds(pl.multiple_of(index * span + row, 8), 8), :]
                total = total + (raised - 1.0) / (raised + level)
            return total

        total = lax.fori_loop(0, rows // span, part, jnp.zeros((8, 128), jnp.float32))
        volume = jnp.sum(jnp.sum(total, axis=0, keepdims=True), axis=1, keepdims=True)
        above = volume * ((top + level) / (top - 1.0)) > fluid_share * cells
        return jnp.where(above, middle, low), jnp.where(above, high, middle)

    low, high = lax.fori_loop(
        0, BISECT, halve, (jnp.zeros((8, 128), jnp.float32), jnp.ones((8, 128), jnp.float32))
    )
    eta_ref[...] = 0.5 * (low + high)


def threshold(filtered, beta, cells):
    eta = pl.pallas_call(
        functools.partial(threshold_kernel, cells),
        out_shape=jax.ShapeDtypeStruct((8, 128), jnp.float32),
        in_specs=[
            pl.BlockSpec(memory_space=pltpu.SMEM),
            pl.BlockSpec(memory_space=pltpu.VMEM),
        ],
        out_specs=pl.BlockSpec(memory_space=pltpu.VMEM),
        scratch_shapes=[pltpu.VMEM(filtered.shape, jnp.float32)],
        compiler_params=pltpu.CompilerParams(vmem_limit_bytes=40 * 2**20),
        name="threshold",
    )(beta.reshape(1), filtered)
    return eta[0, 0]


def body_by_blocks(design, populations, cotangent, wall_mask, inlet_mask, beta_step):
    beta = jnp.exp2(beta_step.astype(jnp.float32) / 16.0)
    filtered = smooth_field(design)
    cells = design.size * lax.axis_size("grp") * lax.axis_size("gy") * lax.axis_size("gx")
    devices = lax.axis_size("grp") * lax.axis_size("gy") * lax.axis_size("gx")
    copies = jnp.broadcast_to(filtered, (devices, *filtered.shape))
    everywhere = lax.all_to_all(copies, ("grp", "gy", "gx"), 0, 0)
    eta = threshold(everywhere.reshape(-1, filtered.shape[-1]), beta, cells)
    density_hat = project(filtered, eta, beta)
    alpha = alpha_most * penalty_shape * (1.0 - density_hat) / (penalty_shape + density_hat)
    states = []
    popul = populations
    for step in range(STEPS):
        states.append(popul)
        popul = shift_all(collide(popul, alpha, wall_mask, inlet_mask), 1)
    adjoint = cotangent
    alpha_grad = jnp.zeros_like(alpha)
    for step in reversed(range(STEPS)):
        back = shift_all(adjoint, -1)
        unused, pullback = jax.vjp(
            lambda p, a: collide(p, a, wall_mask, inlet_mask), states[step], alpha
        )
        adjoint, term = pullback(back)
        alpha_grad = alpha_grad + term
    denom = jnp.tanh(beta * eta) + jnp.tanh(beta * (1.0 - eta))
    slope = beta * (1.0 - jnp.tanh(beta * (filtered - eta)) ** 2) / denom
    factor = (
        -alpha_most * penalty_shape * (1.0 + penalty_shape) / (penalty_shape + density_hat) ** 2
    )
    design_grad = smooth_field(alpha_grad * factor * slope)
    return (popul, design_grad)


LANES = 128
AROUND = ((1, 0), (-1, 0), (0, 1), (0, -1), (1, 1), (-1, -1), (1, -1), (-1, 1))
FIELDS = 40
NEAR = STEPS + 1
OUTER = 8 * 21 + NEAR * 19
CLOSE = 2.0**-14


def rolled(value, amount):
    amount = amount % LANES
    return value if amount == 0 else pltpu.roll(value, amount, 1)


def lane_index():
    return lax.broadcasted_iota(jnp.int32, (8, LANES), 1)


def on_path(index, grp, splits):
    part, step = index // grp, index % grp
    return (step if part % 2 == 0 else grp - 1 - step) * splits + part


def device_at(index, grp, splits):
    odd = lax.rem(lax.axis_index("gx"), 2)
    return jnp.where(odd == 0, on_path(index, grp, splits), on_path(grp * splits - 1 - index, grp, splits))


def block_here(grp, splits):
    step, part = lax.axis_index("grp"), lax.axis_index("gy")
    index = part * grp + jnp.where(lax.rem(part, 2) == 0, step, grp - 1 - step)
    return jnp.where(lax.rem(lax.axis_index("gx"), 2) == 0, index, grp * splits - 1 - index)


def mixed(values):
    place = lane_index() // 16
    for half in (4, 2, 1):
        upper = (place & half) != 0
        values = [jnp.where(upper, values[(index + half) % 8], values[index]) for index in range(8)]
    return values


def pack_kernel(
    splits, design_ref, populations_ref, cotangent_ref, wall_ref, inlet_ref, design_out_ref, packed_ref,
    fields_ref, masks_ref, sems,
):
    moves = [
        pltpu.make_async_copy(populations_ref, fields_ref.at[0:19], sems.at[0]),
        pltpu.make_async_copy(cotangent_ref, fields_ref.at[19:38], sems.at[1]),
        pltpu.make_async_copy(wall_ref, masks_ref.at[0], sems.at[2]),
        pltpu.make_async_copy(inlet_ref, masks_ref.at[1], sems.at[3]),
        pltpu.make_async_copy(design_ref, design_out_ref, sems.at[4]),
    ]
    for move in moves:
        move.start()
    for move in moves:
        move.wait()
    devices = [device_at(index, 8 // splits, splits) for index in range(8)]
    for layer in range(masks_ref.shape[1]):
        for group in range(FIELDS // 8):
            values = []
            for slot in range(8):
                index = group * 8 + slot
                if index in (19, 20):
                    value = masks_ref[index - 19, layer].astype(jnp.float32)
                else:
                    value = fields_ref[index if index < 19 else index - 2, layer]
                values.append(rolled(value, 16 * slot))
            values = mixed(values)
            for index in range(8):
                packed_ref[devices[index], group, layer] = values[-index % 8]


def arrange_kernel(splits, packed_ref, body_ref, first_ref, last_ref):
    layers = packed_ref.shape[2]
    planes = packed_ref.shape[0] // splits * layers
    me = block_here(packed_ref.shape[0] // splits, splits)
    for group in range(FIELDS // 8):
        plane = gather_plane(
            lambda z, part: packed_ref[(z // layers) * splits + part, group, z % layers], planes, splits
        ).T
        for slot in range(8):
            index = group * 8 + lax.rem(slot + 8 - me, 8)
            body_ref[index] = plane[16 * slot : 16 * slot + 16, :]
    for index in range(FIELDS):
        if index < 21:
            first_ref[8 * index : 8 * index + 8, :] = body_ref[index, 0:8, :]
            last_ref[8 * index : 8 * index + 8, :] = body_ref[index, 8:16, :]
        else:
            start = 8 * 21 + NEAR * (index - 21)
            first_ref[start : start + NEAR, :] = body_ref[index, 0:NEAR, :]
            last_ref[start : start + NEAR, :] = body_ref[index, 16 - NEAR : 16, :]
    for ref in (first_ref, last_ref):
        rest = ref.shape[0] - OUTER
        ref[OUTER:, :] = jnp.zeros((rest, LANES), jnp.float32)


def spread_kernel(size, *refs):
    design_refs, (copies_ref, design_ref) = refs[:size], refs[size:]
    here = lax.axis_index("gx")
    for turn in range(size):
        design_ref[lax.rem(here + turn, size)] = design_refs[turn][...]
    lanes = lane_index()
    zero = jnp.zeros((8, LANES), jnp.float32)
    for layer in range(copies_ref.shape[2]):
        tiles = [zero] + [design_ref[index, layer] for index in range(size)] + [zero]
        ahead = [rolled(tile, 1) for tile in tiles]
        behind = [rolled(tile, -1) for tile in tiles]
        for index in range(1, size + 1):
            value = 0.5 * tiles[index] + 0.25 * (
                jnp.where(lanes == 0, ahead[index - 1], ahead[index])
                + jnp.where(lanes == LANES - 1, behind[index + 1], behind[index])
            )
            for device in range(copies_ref.shape[0]):
                copies_ref[device, index - 1, layer] = value


def exponent(step_ref):
    steps = jnp.full((8, LANES), step_ref[0], jnp.int32).astype(jnp.float32)
    return jnp.exp2(steps / 16.0)


def plane_masks(rows):
    lanes = lane_index()
    depth, place_z, place_y = LANES // rows, lanes // rows, lanes % rows
    masks = {}
    for cz, cy in AROUND:
        inside = None
        for shift, place, count in ((cz, place_z, depth), (cy, place_y, rows)):
            if shift:
                here = (place >= 1) if shift > 0 else (place < count - 1)
                inside = here if inside is None else inside & here
        masks[cz, cy] = inside
    return masks


def plane_shift(value, cz, cy, rows, masks):
    if cz == 0 and cy == 0:
        return value
    return jnp.where(masks[cz, cy], rolled(value, cz * rows + cy), 0.0)


def plane_smooth(value, rows, masks):
    for cz, cy in ((1, 0), (0, 1)):
        value = 0.5 * value + 0.25 * (
            plane_shift(value, cz, cy, rows, masks) + plane_shift(value, -cz, -cy, rows, masks)
        )
    return value


def gather_plane(read, planes, splits):
    blocks = []
    for z in range(planes):
        for part in range(splits):
            blocks.append(read(z, part))
    return jnp.concatenate(blocks, axis=0)


def volume_root(raised_ref, columns, beta):
    zero = jnp.zeros((8, LANES), jnp.float32)
    one = jnp.ones((8, LANES), jnp.float32)
    cells = columns * LANES
    top = jnp.exp(2.0 * beta)
    scale = 1.0 / (top - 1.0)

    def total(parts):
        value = (parts[0] + parts[1]) + (parts[2] + parts[3])
        return jnp.sum(jnp.sum(value, axis=0, keepdims=True), axis=1, keepdims=True)

    def advance(state):
        low, high, low_known, high_known, middle, _ = state
        level = jnp.exp(2.0 * beta * middle)
        sums, slopes = [zero] * 4, [zero] * 4
        for index, row in enumerate(range(0, columns, 8)):
            raised = raised_ref[row : row + 8, :]
            below = raised + level
            part = pl.reciprocal(below, approx=True)
            part = part * (2.0 - below * part)
            share = (raised - 1.0) * part
            sums[index % 4] = sums[index % 4] + share
            slopes[index % 4] = slopes[index % 4] + share * part
        volume, slope = total(sums), total(slopes)
        whole = (top + level) * scale
        excess = volume * whole - fluid_share * cells
        slope = (2.0 * beta * level) * (volume * scale - whole * slope)
        above = excess > 0.0
        low, low_known = jnp.where(above, middle, low), jnp.where(above, 1.0, low_known)
        high, high_known = jnp.where(above, high, middle), jnp.where(above, high_known, 1.0)
        guess = middle - excess / slope
        taken = (guess >= low) & (guess <= high)
        other = jnp.where(
            (guess > high) & (high_known == 0.0),
            high,
            jnp.where((guess < low) & (low_known == 0.0), low, 0.5 * (low + high)),
        )
        change = jnp.where(taken, jnp.abs(guess - middle), 2.0**16 * (high - low))
        return low, high, low_known, high_known, jnp.where(taken, guess, other), change

    def going(carry):
        step, state = carry
        return (step < 64) & (jnp.max(state[5]) > CLOSE)

    state = advance(advance((zero, one, zero, zero, 0.5 * one, zero)))
    _, state = lax.while_loop(going, lambda carry: (carry[0] + 1, advance(carry[1])), (2, state))
    return jnp.clip(state[4], 0.5**31, 1.0)


def level_kernel(rows, splits, size, step_ref, copies_ref, share_ref, filtered_ref, raised_ref):
    layers = copies_ref.shape[2]
    planes = LANES // rows
    columns = size * LANES
    masks = plane_masks(rows)
    zero = jnp.zeros((8, LANES), jnp.float32)
    beta = exponent(step_ref)
    filtered_ref[0:8, :] = zero
    filtered_ref[columns + 8 : columns + 16, :] = zero
    for block in range(size):
        plane = gather_plane(
            lambda z, part: copies_ref[(z // layers) * splits + part, block, z % layers], planes, splits
        )
        filtered_ref[8 + block * LANES : 8 + (block + 1) * LANES, :] = plane.T
    for row in range(8, columns + 8, 8):
        value = plane_smooth(filtered_ref[row : row + 8, :], rows, masks)
        filtered_ref[row : row + 8, :] = value
        raised_ref[row - 8 : row, :] = jnp.exp(2.0 * beta * value)
    eta = volume_root(raised_ref, columns, beta)
    place = lax.axis_index("gx") * copies_ref.shape[0] + block_here(copies_ref.shape[0] // splits, splits)
    level = jnp.exp(2.0 * beta * eta)
    top = jnp.exp(2.0 * beta)
    whole = (top + level) / (top - 1.0)
    strength = alpha_most * penalty_shape
    for block in range(4):
        at = slice(8 * block, 8 * block + 8)
        start = pl.multiple_of(place * 16 + 8 * block, 8)
        raised = jnp.exp(2.0 * beta * filtered_ref[pl.ds(start, 8), :])
        part = 1.0 / (raised + level)
        density_hat = ((raised - 1.0) * part) * whole
        share_ref[0, at, :] = (penalty_shape + density_hat) / (
            penalty_shape + strength + (1.0 - strength) * density_hat
        )
        slope = 2.0 * beta * (raised * part) * ((level + 1.0) * part) * whole
        factor = -strength * (1.0 + penalty_shape) / (
            (penalty_shape + density_hat) * (penalty_shape + density_hat)
        )
        share_ref[1, at, :] = slope * factor


def flow(rho, speed):
    square = 1.0 - 1.5 * (speed[0] * speed[0] + speed[1] * speed[1] + speed[2] * speed[2])
    comps = [lattice_weights[0] * rho * square]
    weighted = {1.0 / 18.0: rho * (1.0 / 18.0), 1.0 / 36.0: rho * (1.0 / 36.0)}
    for i in range(1, 19, 2):
        along = along_of(speed, i)
        weight = weighted[lattice_weights[i]]
        even = weight * (square + 4.5 * along * along)
        odd = weight * (3.0 * along)
        comps += [even + odd, even - odd]
    return comps


def along_of(speed, i):
    total = None
    for axis in range(3):
        sign = int(velocities[i][axis])
        if sign:
            if total is None:
                total = speed[axis] if sign > 0 else -speed[axis]
            else:
                total = total + speed[axis] if sign > 0 else total - speed[axis]
    return total


def add_along(totals, value, i):
    for axis in range(3):
        sign = int(velocities[i][axis])
        if sign:
            if totals[axis] is None:
                totals[axis] = value if sign > 0 else -value
            else:
                totals[axis] = totals[axis] + value if sign > 0 else totals[axis] - value


def inlet_value(i):
    along = float(velocities[i][0]) * inlet_speed
    return lattice_weights[i] * (1.0 + 3.0 * along + 4.5 * along * along - 1.5 * inlet_speed * inlet_speed)


def flow_kernel(
    rows, splits, size, share_ref, body_ref, before_ref, after_ref, packed_ref,
    cotangent_ref, even_ref, odd_ref, kept_ref, grad_ref, smooth_ref, output_ref,
):
    devices = packed_ref.shape[0]
    planes = LANES // rows
    layers = planes * splits // devices
    masks = plane_masks(rows)
    zero = jnp.zeros((8, LANES), jnp.float32)
    me = block_here(devices // splits, splits)
    place = lax.axis_index("gx") * devices + me
    last = size * devices - 1

    def inside(value, block):
        if block == 0:
            return jnp.where(place > 0, value, 0.0)
        if block == 3:
            return jnp.where(place < last, value, 0.0)
        return value

    def initial(i, row):
        if row == 0:
            return before_ref[8 * i : 8 * i + 8, :]
        if row == 24:
            return after_ref[8 * i : 8 * i + 8, :]
        return body_ref[i, row - 8 : row, :]

    for ref in (even_ref, odd_ref, cotangent_ref):
        for i in range(19):
            ref[i, 0:8, :] = zero
            ref[i, 40:48, :] = zero
    for i in range(19):
        start = 8 * 21 + NEAR * i
        cotangent_ref[i, 8:16, :] = zero
        cotangent_ref[i, 16 - NEAR : 16, :] = before_ref[start : start + NEAR, :]
        cotangent_ref[i, 16:32, :] = body_ref[21 + i]
        cotangent_ref[i, 32:40, :] = zero
        cotangent_ref[i, 32 : 32 + NEAR, :] = after_ref[start : start + NEAR, :]

    def arrived(ref, i, row):
        cz, cy, cx = (int(c) for c in velocities[i])
        return plane_shift(ref[i, row + 8 - cx : row + 16 - cx, :], cz, cy, rows, masks)

    buffers = (even_ref, odd_ref)
    for step in range(STEPS):
        source, target = buffers[(step + 1) % 2], buffers[step % 2]
        for block in range(4):
            row = 8 * block
            at = slice(row, row + 8)
            if step == 0:
                popul = [initial(i, row) for i in range(19)]
            else:
                popul = [arrived(source, i, row) for i in range(19)]
            wall = initial(19, row) > 0.0
            inlet = initial(20, row) > 0.0
            rho = popul[0]
            momentum = [None, None, None]
            for i in range(1, 19, 2):
                rho = rho + (popul[i] + popul[i + 1])
                add_along(momentum, popul[i] - popul[i + 1], i)
            scale = share_ref[0, at, :] / rho
            speed = [value * scale for value in momentum]
            kept_ref[step, 0, at, :] = rho
            for axis in range(3):
                kept_ref[step, 1 + axis, at, :] = speed[axis]
            settled = flow(relax_rate * rho, speed)
            for i in range(19):
                post = (1.0 - relax_rate) * popul[i] + settled[i]
                post = jnp.where(wall, popul[opposite[i]], jnp.where(inlet, inlet_value(i), post))
                target[i, row + 8 : row + 16, :] = inside(post, block)
    def put(index, row, value):
        group, slot = divmod(index, 8)
        for slot in (slot,) if group < 2 else (slot, slot + 4):
            start = group * LANES + 16 * lax.rem(slot + me, 8) + row
            output_ref[pl.ds(pl.multiple_of(start, 8), 8), :] = value

    source = buffers[(STEPS - 1) % 2]
    for i in range(19):
        for row in (8, 16):
            put(i, row - 8, arrived(source, i, row))

    for step in reversed(range(STEPS)):
        source = cotangent_ref if step == STEPS - 1 else buffers[step % 2]
        target = buffers[(step + 1) % 2]
        for block in range(4):
            row = 8 * block
            at = slice(row, row + 8)
            back = []
            for i in range(19):
                cz, cy, cx = (int(c) for c in velocities[i])
                value = source[i, row + 8 + cx : row + 16 + cx, :]
                back.append(plane_shift(value, -cz, -cy, rows, masks))
            wall = initial(19, row) > 0.0
            inlet = initial(20, row) > 0.0
            rho = kept_ref[step, 0, at, :]
            speed = [kept_ref[step, 1 + axis, at, :] for axis in range(3)]
            square = speed[0] * speed[0] + speed[1] * speed[1] + speed[2] * speed[2]
            share = share_ref[0, at, :]
            faces, edges = None, None
            first, second = [None, None, None], [None, None, None]
            for i in range(1, 19, 2):
                both, apart = back[i] + back[i + 1], back[i] - back[i + 1]
                if i < 7:
                    faces = both if faces is None else faces + both
                    both, apart = 2.0 * both, 2.0 * apart
                else:
                    edges = both if edges is None else edges + both
                add_along(first, apart, i)
                add_along(second, along_of(speed, i) * both, i)
            mean = lattice_weights[0] * back[0] + (1.0 / 18.0) * faces + (1.0 / 36.0) * edges
            first = [value * (3.0 / 36.0) for value in first]
            second = [value * (9.0 / 36.0) for value in second]
            twice = speed[0] * second[0] + speed[1] * second[1] + speed[2] * second[2]
            once = speed[0] * first[0] + speed[1] * first[1] + speed[2] * first[2]
            drag = once + twice - 3.0 * square * mean
            term = jnp.where(wall | inlet, 0.0, -relax_rate * (rho * share * drag))
            grad_ref[at, :] = term if step == STEPS - 1 else grad_ref[at, :] + term
            if step == 0:
                continue
            rest = relax_rate * (mean * (1.0 + 1.5 * square) - 0.5 * twice)
            push = [
                (relax_rate * share) * (first[axis] + second[axis] - 3.0 * mean * speed[axis]) for axis in range(3)
            ]
            for i in range(19):
                if i == 0:
                    post = (1.0 - relax_rate) * back[0] + rest
                else:
                    way = along_of(push, i if i % 2 else i - 1)
                    post = (1.0 - relax_rate) * back[i] + (rest + way if i % 2 else rest - way)
                post = jnp.where(wall, back[opposite[i]], jnp.where(inlet, 0.0, post))
                target[i, row + 8 : row + 16, :] = inside(post, block)

    smooth_ref[0:8, :] = zero
    smooth_ref[40:48, :] = zero
    for block in range(4):
        at = slice(8 * block, 8 * block + 8)
        value = inside(grad_ref[at, :] * share_ref[1, at, :], block)
        smooth_ref[8 * block + 8 : 8 * block + 16, :] = plane_smooth(value, rows, masks)
    for row in (8, 16):
        value = 0.5 * smooth_ref[row + 8 : row + 16, :] + 0.25 * (
            smooth_ref[row + 7 : row + 15, :] + smooth_ref[row + 9 : row + 17, :]
        )
        put(19, row - 8, value)
    second = lax.rem(lane_index() // 16 + 8 - me, 8) >= 4
    for group in range(3):
        plane = output_ref[group * LANES : (group + 1) * LANES, :].T
        for device in range(devices):
            tiles = []
            for layer in range(layers):
                at = (((device // splits) * layers + layer) * splits + device % splits) * 8
                tiles.append(plane[at : at + 8, :])
            if group < 2:
                for layer in range(layers):
                    packed_ref[device, group * layers + layer] = tiles[layer]
            else:
                packed_ref[device, group * layers] = jnp.where(second, tiles[1], tiles[0])


def result_kernel(splits, packed_ref, populations_ref, grad_ref):
    devices = [device_at(index, 8 // splits, splits) for index in range(8)]
    for tile in range(packed_ref.shape[1]):
        values = mixed([packed_ref[device, tile] for device in devices])
        for slot in range(8):
            value = rolled(values[-slot % 8], -16 * slot)
            if tile < 4:
                populations_ref[tile // 2 * 8 + slot, tile % 2] = value
            elif slot % 4 < 3:
                populations_ref[16 + slot % 4, slot // 4] = value
            else:
                grad_ref[slot // 4] = value


def call(kernel, outs, name, operands, spaces, scratch=(), room=32):
    vmem = pl.BlockSpec(memory_space=pltpu.VMEM)
    shapes = tuple(jax.ShapeDtypeStruct(shape, jnp.float32) for shape in outs)
    many = len(outs) > 1
    return pl.pallas_call(
        kernel,
        out_shape=shapes if many else shapes[0],
        in_specs=[pl.BlockSpec(memory_space=space) for space in spaces],
        out_specs=(vmem,) * len(outs) if many else vmem,
        scratch_shapes=list(scratch),
        compiler_params=pltpu.CompilerParams(vmem_limit_bytes=room * 2**20),
        name=name,
    )(*operands)


def body_by_columns(design, populations, cotangent, wall_mask, inlet_mask, beta_step):
    grp, splits, size = (lax.axis_size(axis) for axis in ("grp", "gy", "gx"))
    layers, height, width = design.shape
    rows, plane = height * splits, grp * splits
    tile = (layers, 8, LANES)
    vmem, real = pltpu.VMEM, jnp.float32
    design, packed = call(
        functools.partial(pack_kernel, splits),
        (tile, (plane, FIELDS // 8, *tile)),
        "pack",
        (design, populations, cotangent, wall_mask, inlet_mask),
        [pl.ANY] * 5,
        [vmem((38, *tile), real), vmem((2, *tile), jnp.int32), pltpu.SemaphoreType.DMA((5,))],
        60,
    )
    packed = lax.all_to_all(packed, ("grp", "gy"), 0, 0)
    designs = [design] * size
    for turn in reversed(range(1, size)):
        designs[turn] = lax.ppermute(design, "gx", [((i + turn) % size, i) for i in range(size)])
    copies = call(
        functools.partial(spread_kernel, size),
        ((plane, size, *tile),),
        "spread",
        designs,
        [vmem] * size,
        [vmem((size, *tile), real)],
    )
    outer = (-(-OUTER // 8) * 8, LANES)
    body, first, last = call(
        functools.partial(arrange_kernel, splits),
        ((FIELDS, 16, LANES), outer, outer),
        "arrange",
        (packed,),
        [vmem],
    )
    copies = lax.all_to_all(copies, ("grp", "gy"), 0, 0)
    path = [on_path(index, grp, splits) for index in range(plane)]
    order = [(path if gx % 2 == 0 else path[::-1])[index] * size + gx for gx in range(size) for index in range(plane)]
    up = list(zip(order[:-1], order[1:]))
    line = ("grp", "gy", "gx")
    before = lax.ppermute(last, line, up)
    after = lax.ppermute(first, line, [(j, i) for i, j in up])
    columns = size * LANES
    share = call(
        functools.partial(level_kernel, rows, splits, size),
        ((2, 32, LANES),),
        "level",
        (beta_step.reshape(1), copies),
        [pltpu.SMEM, vmem],
        [vmem((columns + 16, LANES), real), vmem((columns, LANES), real)],
    )
    shapes = [
        (19, 48, LANES),
        (19, 48, LANES),
        (19, 48, LANES),
        (STEPS, 4, 32, LANES),
        (32, LANES),
        (48, LANES),
        (3 * LANES, LANES),
    ]
    packed = call(
        functools.partial(flow_kernel, rows, splits, size),
        ((plane, 5, 8, LANES),),
        "flow",
        (share, body, before, after),
        [vmem] * 4,
        [vmem(shape, real) for shape in shapes],
    )
    packed = lax.all_to_all(packed, ("grp", "gy"), 0, 0)
    return call(functools.partial(result_kernel, splits), (populations.shape, design.shape), "result", (packed,), [vmem])


def body(design, populations, cotangent, wall_mask, inlet_mask, beta_step):
    grp, splits = lax.axis_size("grp"), lax.axis_size("gy")
    layers, height, width = design.shape
    fits = height == 8 and width == LANES and layers * grp * height * splits == LANES
    whole = body_by_columns if fits and grp * splits * 16 == LANES else body_by_blocks
    return whole(design, populations, cotangent, wall_mask, inlet_mask, beta_step)


def solution(mesh):
    placed = (
        P("grp", "gy", "gx"),
        P(None, "grp", "gy", "gx"),
        P(None, "grp", "gy", "gx"),
        P("grp", "gy", "gx"),
        P("grp", "gy", "gx"),
        P(),
    )
    return jax.shard_map(
        body,
        mesh=mesh,
        in_specs=placed,
        out_specs=(P(None, "grp", "gy", "gx"), P("grp", "gy", "gx")),
        check_vma=False,
    )
```

```python
import functools

import jax
import jax.numpy as jnp
import numpy as np
from jax import lax
from jax.experimental import pallas as pl
from jax.experimental.pallas import tpu as pltpu
from jax.sharding import PartitionSpec as P

STEPS = 4
BISECT = 30


velocities = np.array(
    [
        [0, 0, 0],
        [1, 0, 0],
        [-1, 0, 0],
        [0, 1, 0],
        [0, -1, 0],
        [0, 0, 1],
        [0, 0, -1],
        [1, 1, 0],
        [-1, -1, 0],
        [1, -1, 0],
        [-1, 1, 0],
        [1, 0, 1],
        [-1, 0, -1],
        [1, 0, -1],
        [-1, 0, 1],
        [0, 1, 1],
        [0, -1, -1],
        [0, 1, -1],
        [0, -1, 1],
    ]
)
opposite = [0, 2, 1, 4, 3, 6, 5, 8, 7, 10, 9, 12, 11, 14, 13, 16, 15, 18, 17]
lattice_weights = [1.0 / 3.0] + [1.0 / 18.0] * 6 + [1.0 / 36.0] * 12
relax_rate = 0.8
inlet_speed = 0.05
alpha_most = 8.0
penalty_shape = 0.1
fluid_share = 0.4


def extended(value, sides, width):
    for axis, dim in sides:
        size, length = (lax.axis_size(axis), value.shape[dim])
        up = [(i, (i + 1) % size) for i in range(size - 1)]
        down = [(j, i) for i, j in up]
        last = lax.slice_in_dim(value, length - width, length, axis=dim)
        leading = lax.slice_in_dim(value, 0, width, axis=dim)
        before = lax.ppermute(last, axis, up)
        after = lax.ppermute(leading, axis, down)
        value = jnp.concatenate([before, value, after], axis=dim)
    return value


def equilibrium(density, speed_z, speed_y, speed_x):
    square = speed_z * speed_z + speed_y * speed_y + speed_x * speed_x
    comps = []
    for i in range(19):
        along = (
            float(velocities[i][0]) * speed_z
            + float(velocities[i][1]) * speed_y
            + float(velocities[i][2]) * speed_x
        )
        comps.append(
            lattice_weights[i] * density * (1.0 + 3.0 * along + 4.5 * along * along - 1.5 * square)
        )
    return jnp.stack(comps)


def moment(popul, axis):
    total = jnp.zeros(popul.shape[1:], popul.dtype)
    for i in range(1, 19):
        if velocities[i][axis] != 0:
            total = total + float(velocities[i][axis]) * popul[i]
    return total


def collide(popul, alpha, wall_mask, inlet_mask):
    density = jnp.sum(popul, axis=0)
    scale = density * (1.0 + alpha)
    feq = equilibrium(
        density, moment(popul, 0) / scale, moment(popul, 1) / scale, moment(popul, 2) / scale
    )
    post = popul + relax_rate * (feq - popul)
    bounce = jnp.stack([popul[opposite[i]] for i in range(19)])
    inlet_values = []
    for i in range(19):
        along = float(velocities[i][0]) * inlet_speed
        inlet_values.append(
            lattice_weights[i]
            * (1.0 + 3.0 * along + 4.5 * along * along - 1.5 * inlet_speed * inlet_speed)
        )
    inlet_feq = jnp.stack([jnp.full(popul.shape[1:], value, popul.dtype) for value in inlet_values])
    return jnp.where(wall_mask[None] > 0, bounce, jnp.where(inlet_mask[None] > 0, inlet_feq, post))


def pick(padded, sign):
    depth, rows, cols = (padded.shape[1] - 2, padded.shape[2] - 2, padded.shape[3] - 2)
    outputs = []
    for i in range(19):
        start_z = 1 - sign * int(velocities[i][0])
        start_y = 1 - sign * int(velocities[i][1])
        start_x = 1 - sign * int(velocities[i][2])
        outputs.append(
            padded[i, start_z : start_z + depth, start_y : start_y + rows, start_x : start_x + cols]
        )
    return jnp.stack(outputs)


def shift_all(popul, sign):
    padded = extended(popul, (("grp", 1), ("gy", 2), ("gx", 3)), 1)
    return pick(padded, sign)


def smooth_field(field):
    padded = extended(field, (("grp", 0), ("gy", 1), ("gx", 2)), 1)
    along_z = 0.25 * padded[:-2] + 0.5 * padded[1:-1] + 0.25 * padded[2:]
    along_y = 0.25 * along_z[:, :-2] + 0.5 * along_z[:, 1:-1] + 0.25 * along_z[:, 2:]
    return 0.25 * along_y[:, :, :-2] + 0.5 * along_y[:, :, 1:-1] + 0.25 * along_y[:, :, 2:]


def project(filtered, thresh, beta):
    denom = jnp.tanh(beta * thresh) + jnp.tanh(beta * (1.0 - thresh))
    return (jnp.tanh(beta * thresh) + jnp.tanh(beta * (filtered - thresh))) / denom


def threshold_kernel(cells, beta_ref, filtered_ref, eta_ref, raised_ref):
    beta = jnp.full((8, 128), beta_ref[0], jnp.float32)
    raised_ref[...] = jnp.exp(2.0 * beta_ref[0] * filtered_ref[...])
    top = jnp.exp(2.0 * beta)
    rows = filtered_ref.shape[0]
    span = min(rows, 512)

    def halve(step, ends):
        low, high = ends
        middle = 0.5 * (low + high)
        level = jnp.exp(2.0 * beta * middle)

        def part(index, total):
            for row in range(0, span, 8):
                raised = raised_ref[pl.ds(pl.multiple_of(index * span + row, 8), 8), :]
                total = total + (raised - 1.0) / (raised + level)
            return total

        total = lax.fori_loop(0, rows // span, part, jnp.zeros((8, 128), jnp.float32))
        volume = jnp.sum(jnp.sum(total, axis=0, keepdims=True), axis=1, keepdims=True)
        above = volume * ((top + level) / (top - 1.0)) > fluid_share * cells
        return jnp.where(above, middle, low), jnp.where(above, high, middle)

    low, high = lax.fori_loop(
        0, BISECT, halve, (jnp.zeros((8, 128), jnp.float32), jnp.ones((8, 128), jnp.float32))
    )
    eta_ref[...] = 0.5 * (low + high)


def threshold(filtered, beta, cells):
    eta = pl.pallas_call(
        functools.partial(threshold_kernel, cells),
        out_shape=jax.ShapeDtypeStruct((8, 128), jnp.float32),
        in_specs=[
            pl.BlockSpec(memory_space=pltpu.SMEM),
            pl.BlockSpec(memory_space=pltpu.VMEM),
        ],
        out_specs=pl.BlockSpec(memory_space=pltpu.VMEM),
        scratch_shapes=[pltpu.VMEM(filtered.shape, jnp.float32)],
        compiler_params=pltpu.CompilerParams(vmem_limit_bytes=40 * 2**20),
        name="threshold",
    )(beta.reshape(1), filtered)
    return eta[0, 0]


def body_by_blocks(design, populations, cotangent, wall_mask, inlet_mask, beta_step):
    beta = jnp.exp2(beta_step.astype(jnp.float32) / 16.0)
    filtered = smooth_field(design)
    cells = design.size * lax.axis_size("grp") * lax.axis_size("gy") * lax.axis_size("gx")
    devices = lax.axis_size("grp") * lax.axis_size("gy") * lax.axis_size("gx")
    copies = jnp.broadcast_to(filtered, (devices, *filtered.shape))
    everywhere = lax.all_to_all(copies, ("grp", "gy", "gx"), 0, 0)
    eta = threshold(everywhere.reshape(-1, filtered.shape[-1]), beta, cells)
    density_hat = project(filtered, eta, beta)
    alpha = alpha_most * penalty_shape * (1.0 - density_hat) / (penalty_shape + density_hat)
    states = []
    popul = populations
    for step in range(STEPS):
        states.append(popul)
        popul = shift_all(collide(popul, alpha, wall_mask, inlet_mask), 1)
    adjoint = cotangent
    alpha_grad = jnp.zeros_like(alpha)
    for step in reversed(range(STEPS)):
        back = shift_all(adjoint, -1)
        unused, pullback = jax.vjp(
            lambda p, a: collide(p, a, wall_mask, inlet_mask), states[step], alpha
        )
        adjoint, term = pullback(back)
        alpha_grad = alpha_grad + term
    denom = jnp.tanh(beta * eta) + jnp.tanh(beta * (1.0 - eta))
    slope = beta * (1.0 - jnp.tanh(beta * (filtered - eta)) ** 2) / denom
    factor = (
        -alpha_most * penalty_shape * (1.0 + penalty_shape) / (penalty_shape + density_hat) ** 2
    )
    design_grad = smooth_field(alpha_grad * factor * slope)
    return (popul, design_grad)


LANES = 128
AROUND = ((1, 0), (-1, 0), (0, 1), (0, -1), (1, 1), (-1, -1), (1, -1), (-1, 1))
FIELDS = 40
NEAR = STEPS + 1
OUTER = 8 * 21 + NEAR * 19
CLOSE = 2.0**-14


def rolled(value, amount):
    amount = amount % LANES
    return value if amount == 0 else pltpu.roll(value, amount, 1)


def lane_index():
    return lax.broadcasted_iota(jnp.int32, (8, LANES), 1)


def on_path(index, grp, splits):
    part, step = index // grp, index % grp
    return (step if part % 2 == 0 else grp - 1 - step) * splits + part


def device_at(index, grp, splits):
    odd = lax.rem(lax.axis_index("gx"), 2)
    return jnp.where(odd == 0, on_path(index, grp, splits), on_path(grp * splits - 1 - index, grp, splits))


def block_here(grp, splits):
    step, part = lax.axis_index("grp"), lax.axis_index("gy")
    index = part * grp + jnp.where(lax.rem(part, 2) == 0, step, grp - 1 - step)
    return jnp.where(lax.rem(lax.axis_index("gx"), 2) == 0, index, grp * splits - 1 - index)


def mixed(values):
    place = lane_index() // 16
    for half in (4, 2, 1):
        upper = (place & half) != 0
        values = [jnp.where(upper, values[(index + half) % 8], values[index]) for index in range(8)]
    return values


def pack_kernel(
    splits, design_ref, populations_ref, cotangent_ref, wall_ref, inlet_ref, design_out_ref, packed_ref,
    fields_ref, masks_ref, sems,
):
    moves = [
        pltpu.make_async_copy(populations_ref, fields_ref.at[0:19], sems.at[0]),
        pltpu.make_async_copy(cotangent_ref, fields_ref.at[19:38], sems.at[1]),
        pltpu.make_async_copy(wall_ref, masks_ref.at[0], sems.at[2]),
        pltpu.make_async_copy(inlet_ref, masks_ref.at[1], sems.at[3]),
        pltpu.make_async_copy(design_ref, design_out_ref, sems.at[4]),
    ]
    for move in moves:
        move.start()
    for move in moves:
        move.wait()
    devices = [device_at(index, 8 // splits, splits) for index in range(8)]
    for layer in range(masks_ref.shape[1]):
        for group in range(FIELDS // 8):
            values = []
            for slot in range(8):
                index = group * 8 + slot
                if index in (19, 20):
                    value = masks_ref[index - 19, layer].astype(jnp.float32)
                else:
                    value = fields_ref[index if index < 19 else index - 2, layer]
                values.append(rolled(value, 16 * slot))
            values = mixed(values)
            for index in range(8):
                packed_ref[devices[index], group, layer] = values[-index % 8]


def arrange_kernel(splits, packed_ref, body_ref, first_ref, last_ref):
    layers = packed_ref.shape[2]
    planes = packed_ref.shape[0] // splits * layers
    me = block_here(packed_ref.shape[0] // splits, splits)
    for group in range(FIELDS // 8):
        plane = gather_plane(
            lambda z, part: packed_ref[(z // layers) * splits + part, group, z % layers], planes, splits
        ).T
        for slot in range(8):
            index = group * 8 + lax.rem(slot + 8 - me, 8)
            body_ref[index] = plane[16 * slot : 16 * slot + 16, :]
    for index in range(FIELDS):
        if index < 21:
            first_ref[8 * index : 8 * index + 8, :] = body_ref[index, 0:8, :]
            last_ref[8 * index : 8 * index + 8, :] = body_ref[index, 8:16, :]
        else:
            start = 8 * 21 + NEAR * (index - 21)
            first_ref[start : start + NEAR, :] = body_ref[index, 0:NEAR, :]
            last_ref[start : start + NEAR, :] = body_ref[index, 16 - NEAR : 16, :]
    for ref in (first_ref, last_ref):
        rest = ref.shape[0] - OUTER
        ref[OUTER:, :] = jnp.zeros((rest, LANES), jnp.float32)


def turns_of(size):
    return sorted(range(size), key=lambda turn: (turn != 0, turn != size // 2, turn))


def spread_kernel(size, *refs):
    design_refs, (copies_ref, design_ref) = refs[:size], refs[size:]
    here = lax.axis_index("gx")
    for turn, ref in zip(turns_of(size), design_refs):
        design_ref[lax.rem(here + turn, size)] = ref[...]
    lanes = lane_index()
    zero = jnp.zeros((8, LANES), jnp.float32)
    for layer in range(copies_ref.shape[2]):
        tiles = [zero] + [design_ref[index, layer] for index in range(size)] + [zero]
        ahead = [rolled(tile, 1) for tile in tiles]
        behind = [rolled(tile, -1) for tile in tiles]
        for index in range(1, size + 1):
            value = 0.5 * tiles[index] + 0.25 * (
                jnp.where(lanes == 0, ahead[index - 1], ahead[index])
                + jnp.where(lanes == LANES - 1, behind[index + 1], behind[index])
            )
            for device in range(copies_ref.shape[0]):
                copies_ref[device, index - 1, layer] = value


def exponent(step_ref):
    steps = jnp.full((8, LANES), step_ref[0], jnp.int32).astype(jnp.float32)
    return jnp.exp2(steps / 16.0)


def plane_masks(rows):
    lanes = lane_index()
    depth, place_z, place_y = LANES // rows, lanes // rows, lanes % rows
    masks = {}
    for cz, cy in AROUND:
        inside = None
        for shift, place, count in ((cz, place_z, depth), (cy, place_y, rows)):
            if shift:
                here = (place >= 1) if shift > 0 else (place < count - 1)
                inside = here if inside is None else inside & here
        masks[cz, cy] = inside
    return masks


def plane_shift(value, cz, cy, rows, masks):
    if cz == 0 and cy == 0:
        return value
    return jnp.where(masks[cz, cy], rolled(value, cz * rows + cy), 0.0)


def plane_smooth(value, rows, masks):
    for cz, cy in ((1, 0), (0, 1)):
        value = 0.5 * value + 0.25 * (
            plane_shift(value, cz, cy, rows, masks) + plane_shift(value, -cz, -cy, rows, masks)
        )
    return value


def gather_plane(read, planes, splits):
    blocks = []
    for z in range(planes):
        for part in range(splits):
            blocks.append(read(z, part))
    return jnp.concatenate(blocks, axis=0)


def volume_root(raised_ref, columns, beta):
    zero = jnp.zeros((8, LANES), jnp.float32)
    one = jnp.ones((8, LANES), jnp.float32)
    cells = columns * LANES
    top = jnp.exp(2.0 * beta)
    scale = 1.0 / (top - 1.0)

    def total(parts):
        value = (parts[0] + parts[1]) + (parts[2] + parts[3])
        return jnp.sum(jnp.sum(value, axis=0, keepdims=True), axis=1, keepdims=True)

    def advance(state):
        low, high, low_known, high_known, middle, _ = state
        level = jnp.exp(2.0 * beta * middle)
        sums, slopes = [zero] * 4, [zero] * 4
        for index, row in enumerate(range(0, columns, 8)):
            raised = raised_ref[row : row + 8, :]
            below = raised + level
            part = pl.reciprocal(below, approx=True)
            part = part * (2.0 - below * part)
            share = (raised - 1.0) * part
            sums[index % 4] = sums[index % 4] + share
            slopes[index % 4] = slopes[index % 4] + share * part
        volume, slope = total(sums), total(slopes)
        whole = (top + level) * scale
        excess = volume * whole - fluid_share * cells
        slope = (2.0 * beta * level) * (volume * scale - whole * slope)
        above = excess > 0.0
        low, low_known = jnp.where(above, middle, low), jnp.where(above, 1.0, low_known)
        high, high_known = jnp.where(above, high, middle), jnp.where(above, high_known, 1.0)
        guess = middle - excess / slope
        taken = (guess >= low) & (guess <= high)
        other = jnp.where(
            (guess > high) & (high_known == 0.0),
            high,
            jnp.where((guess < low) & (low_known == 0.0), low, 0.5 * (low + high)),
        )
        change = jnp.where(taken, jnp.abs(guess - middle), 2.0**16 * (high - low))
        return low, high, low_known, high_known, jnp.where(taken, guess, other), change

    def going(carry):
        step, state = carry
        return (step < 64) & (jnp.max(state[5]) > CLOSE)

    state = advance(advance((zero, one, zero, zero, 0.5 * one, zero)))
    _, state = lax.while_loop(going, lambda carry: (carry[0] + 1, advance(carry[1])), (2, state))
    return jnp.clip(state[4], 0.5**31, 1.0)


def level_kernel(rows, splits, size, step_ref, copies_ref, share_ref, filtered_ref, raised_ref):
    layers = copies_ref.shape[2]
    planes = LANES // rows
    columns = size * LANES
    masks = plane_masks(rows)
    zero = jnp.zeros((8, LANES), jnp.float32)
    beta = exponent(step_ref)
    filtered_ref[0:8, :] = zero
    filtered_ref[columns + 8 : columns + 16, :] = zero
    for block in range(size):
        plane = gather_plane(
            lambda z, part: copies_ref[(z // layers) * splits + part, block, z % layers], planes, splits
        )
        filtered_ref[8 + block * LANES : 8 + (block + 1) * LANES, :] = plane.T
    for row in range(8, columns + 8, 8):
        value = plane_smooth(filtered_ref[row : row + 8, :], rows, masks)
        filtered_ref[row : row + 8, :] = value
        raised_ref[row - 8 : row, :] = jnp.exp(2.0 * beta * value)
    eta = volume_root(raised_ref, columns, beta)
    place = lax.axis_index("gx") * copies_ref.shape[0] + block_here(copies_ref.shape[0] // splits, splits)
    level = jnp.exp(2.0 * beta * eta)
    top = jnp.exp(2.0 * beta)
    whole = (top + level) / (top - 1.0)
    strength = alpha_most * penalty_shape
    for block in range(4):
        at = slice(8 * block, 8 * block + 8)
        start = pl.multiple_of(place * 16 + 8 * block, 8)
        raised = jnp.exp(2.0 * beta * filtered_ref[pl.ds(start, 8), :])
        part = 1.0 / (raised + level)
        density_hat = ((raised - 1.0) * part) * whole
        share_ref[0, at, :] = (penalty_shape + density_hat) / (
            penalty_shape + strength + (1.0 - strength) * density_hat
        )
        slope = 2.0 * beta * (raised * part) * ((level + 1.0) * part) * whole
        factor = -strength * (1.0 + penalty_shape) / (
            (penalty_shape + density_hat) * (penalty_shape + density_hat)
        )
        share_ref[1, at, :] = slope * factor


def flow(rho, speed):
    square = 1.0 - 1.5 * (speed[0] * speed[0] + speed[1] * speed[1] + speed[2] * speed[2])
    comps = [lattice_weights[0] * rho * square]
    weighted = {1.0 / 18.0: rho * (1.0 / 18.0), 1.0 / 36.0: rho * (1.0 / 36.0)}
    for i in range(1, 19, 2):
        along = along_of(speed, i)
        weight = weighted[lattice_weights[i]]
        even = weight * (square + 4.5 * along * along)
        odd = weight * (3.0 * along)
        comps += [even + odd, even - odd]
    return comps


def along_of(speed, i):
    total = None
    for axis in range(3):
        sign = int(velocities[i][axis])
        if sign:
            if total is None:
                total = speed[axis] if sign > 0 else -speed[axis]
            else:
                total = total + speed[axis] if sign > 0 else total - speed[axis]
    return total


def add_along(totals, value, i):
    for axis in range(3):
        sign = int(velocities[i][axis])
        if sign:
            if totals[axis] is None:
                totals[axis] = value if sign > 0 else -value
            else:
                totals[axis] = totals[axis] + value if sign > 0 else totals[axis] - value


def inlet_value(i):
    along = float(velocities[i][0]) * inlet_speed
    return lattice_weights[i] * (1.0 + 3.0 * along + 4.5 * along * along - 1.5 * inlet_speed * inlet_speed)


def flow_kernel(
    rows, splits, size, share_ref, body_ref, before_ref, after_ref, packed_ref,
    cotangent_ref, even_ref, odd_ref, kept_ref, grad_ref, smooth_ref, output_ref,
):
    devices = packed_ref.shape[0]
    planes = LANES // rows
    layers = planes * splits // devices
    masks = plane_masks(rows)
    zero = jnp.zeros((8, LANES), jnp.float32)
    me = block_here(devices // splits, splits)
    place = lax.axis_index("gx") * devices + me
    last = size * devices - 1

    def inside(value, block):
        if block == 0:
            return jnp.where(place > 0, value, 0.0)
        if block == 3:
            return jnp.where(place < last, value, 0.0)
        return value

    def initial(i, row):
        if row == 0:
            return before_ref[8 * i : 8 * i + 8, :]
        if row == 24:
            return after_ref[8 * i : 8 * i + 8, :]
        return body_ref[i, row - 8 : row, :]

    for ref in (even_ref, odd_ref, cotangent_ref):
        for i in range(19):
            ref[i, 0:8, :] = zero
            ref[i, 40:48, :] = zero
    for i in range(19):
        start = 8 * 21 + NEAR * i
        cotangent_ref[i, 8:16, :] = zero
        cotangent_ref[i, 16 - NEAR : 16, :] = before_ref[start : start + NEAR, :]
        cotangent_ref[i, 16:32, :] = body_ref[21 + i]
        cotangent_ref[i, 32:40, :] = zero
        cotangent_ref[i, 32 : 32 + NEAR, :] = after_ref[start : start + NEAR, :]

    def arrived(ref, i, row):
        cz, cy, cx = (int(c) for c in velocities[i])
        return plane_shift(ref[i, row + 8 - cx : row + 16 - cx, :], cz, cy, rows, masks)

    buffers = (even_ref, odd_ref)
    for step in range(STEPS):
        source, target = buffers[(step + 1) % 2], buffers[step % 2]
        for block in range(4):
            row = 8 * block
            at = slice(row, row + 8)
            if step == 0:
                popul = [initial(i, row) for i in range(19)]
            else:
                popul = [arrived(source, i, row) for i in range(19)]
            wall = initial(19, row) > 0.0
            inlet = initial(20, row) > 0.0
            rho = popul[0]
            momentum = [None, None, None]
            for i in range(1, 19, 2):
                rho = rho + (popul[i] + popul[i + 1])
                add_along(momentum, popul[i] - popul[i + 1], i)
            scale = share_ref[0, at, :] / rho
            speed = [value * scale for value in momentum]
            kept_ref[step, 0, at, :] = rho
            for axis in range(3):
                kept_ref[step, 1 + axis, at, :] = speed[axis]
            settled = flow(relax_rate * rho, speed)
            for i in range(19):
                post = (1.0 - relax_rate) * popul[i] + settled[i]
                post = jnp.where(wall, popul[opposite[i]], jnp.where(inlet, inlet_value(i), post))
                target[i, row + 8 : row + 16, :] = inside(post, block)
    def put(index, row, value):
        group, slot = divmod(index, 8)
        for slot in (slot,) if group < 2 else (slot, slot + 4):
            start = group * LANES + 16 * lax.rem(slot + me, 8) + row
            output_ref[pl.ds(pl.multiple_of(start, 8), 8), :] = value

    source = buffers[(STEPS - 1) % 2]
    for i in range(19):
        for row in (8, 16):
            put(i, row - 8, arrived(source, i, row))

    for step in reversed(range(STEPS)):
        source = cotangent_ref if step == STEPS - 1 else buffers[step % 2]
        target = buffers[(step + 1) % 2]
        for block in range(4):
            row = 8 * block
            at = slice(row, row + 8)
            back = []
            for i in range(19):
                cz, cy, cx = (int(c) for c in velocities[i])
                value = source[i, row + 8 + cx : row + 16 + cx, :]
                back.append(plane_shift(value, -cz, -cy, rows, masks))
            wall = initial(19, row) > 0.0
            inlet = initial(20, row) > 0.0
            rho = kept_ref[step, 0, at, :]
            speed = [kept_ref[step, 1 + axis, at, :] for axis in range(3)]
            square = speed[0] * speed[0] + speed[1] * speed[1] + speed[2] * speed[2]
            share = share_ref[0, at, :]
            faces, edges = None, None
            first, second = [None, None, None], [None, None, None]
            for i in range(1, 19, 2):
                both, apart = back[i] + back[i + 1], back[i] - back[i + 1]
                if i < 7:
                    faces = both if faces is None else faces + both
                    both, apart = 2.0 * both, 2.0 * apart
                else:
                    edges = both if edges is None else edges + both
                add_along(first, apart, i)
                add_along(second, along_of(speed, i) * both, i)
            mean = lattice_weights[0] * back[0] + (1.0 / 18.0) * faces + (1.0 / 36.0) * edges
            first = [value * (3.0 / 36.0) for value in first]
            second = [value * (9.0 / 36.0) for value in second]
            twice = speed[0] * second[0] + speed[1] * second[1] + speed[2] * second[2]
            once = speed[0] * first[0] + speed[1] * first[1] + speed[2] * first[2]
            drag = once + twice - 3.0 * square * mean
            term = jnp.where(wall | inlet, 0.0, -relax_rate * (rho * share * drag))
            grad_ref[at, :] = term if step == STEPS - 1 else grad_ref[at, :] + term
            if step == 0:
                continue
            rest = relax_rate * (mean * (1.0 + 1.5 * square) - 0.5 * twice)
            push = [
                (relax_rate * share) * (first[axis] + second[axis] - 3.0 * mean * speed[axis]) for axis in range(3)
            ]
            for i in range(19):
                if i == 0:
                    post = (1.0 - relax_rate) * back[0] + rest
                else:
                    way = along_of(push, i if i % 2 else i - 1)
                    post = (1.0 - relax_rate) * back[i] + (rest + way if i % 2 else rest - way)
                post = jnp.where(wall, back[opposite[i]], jnp.where(inlet, 0.0, post))
                target[i, row + 8 : row + 16, :] = inside(post, block)

    smooth_ref[0:8, :] = zero
    smooth_ref[40:48, :] = zero
    for block in range(4):
        at = slice(8 * block, 8 * block + 8)
        value = inside(grad_ref[at, :] * share_ref[1, at, :], block)
        smooth_ref[8 * block + 8 : 8 * block + 16, :] = plane_smooth(value, rows, masks)
    for row in (8, 16):
        value = 0.5 * smooth_ref[row + 8 : row + 16, :] + 0.25 * (
            smooth_ref[row + 7 : row + 15, :] + smooth_ref[row + 9 : row + 17, :]
        )
        put(19, row - 8, value)
    second = lax.rem(lane_index() // 16 + 8 - me, 8) >= 4
    for group in range(3):
        plane = output_ref[group * LANES : (group + 1) * LANES, :].T
        for device in range(devices):
            tiles = []
            for layer in range(layers):
                at = (((device // splits) * layers + layer) * splits + device % splits) * 8
                tiles.append(plane[at : at + 8, :])
            if group < 2:
                for layer in range(layers):
                    packed_ref[device, group * layers + layer] = tiles[layer]
            else:
                packed_ref[device, group * layers] = jnp.where(second, tiles[1], tiles[0])


def result_kernel(splits, packed_ref, populations_ref, grad_ref):
    devices = [device_at(index, 8 // splits, splits) for index in range(8)]
    for tile in range(packed_ref.shape[1]):
        values = mixed([packed_ref[device, tile] for device in devices])
        for slot in range(8):
            value = rolled(values[-slot % 8], -16 * slot)
            if tile < 4:
                populations_ref[tile // 2 * 8 + slot, tile % 2] = value
            elif slot % 4 < 3:
                populations_ref[16 + slot % 4, slot // 4] = value
            else:
                grad_ref[slot // 4] = value


def call(kernel, outs, name, operands, spaces, scratch=(), room=32):
    vmem = pl.BlockSpec(memory_space=pltpu.VMEM)
    shapes = tuple(jax.ShapeDtypeStruct(shape, jnp.float32) for shape in outs)
    many = len(outs) > 1
    return pl.pallas_call(
        kernel,
        out_shape=shapes if many else shapes[0],
        in_specs=[pl.BlockSpec(memory_space=space) for space in spaces],
        out_specs=(vmem,) * len(outs) if many else vmem,
        scratch_shapes=list(scratch),
        compiler_params=pltpu.CompilerParams(vmem_limit_bytes=room * 2**20),
        name=name,
    )(*operands)


def body_by_columns(design, populations, cotangent, wall_mask, inlet_mask, beta_step):
    grp, splits, size = (lax.axis_size(axis) for axis in ("grp", "gy", "gx"))
    layers, height, width = design.shape
    rows, plane = height * splits, grp * splits
    tile = (layers, 8, LANES)
    vmem, real = pltpu.VMEM, jnp.float32
    design, packed = call(
        functools.partial(pack_kernel, splits),
        (tile, (plane, FIELDS // 8, *tile)),
        "pack",
        (design, populations, cotangent, wall_mask, inlet_mask),
        [pl.ANY] * 5,
        [vmem((38, *tile), real), vmem((2, *tile), jnp.int32), pltpu.SemaphoreType.DMA((5,))],
        60,
    )
    packed = lax.all_to_all(packed, ("grp", "gy"), 0, 0)
    designs = [design] * size
    for turn in reversed(range(1, size)):
        designs[turn] = lax.ppermute(design, "gx", [((i + turn) % size, i) for i in range(size)])
    copies = call(
        functools.partial(spread_kernel, size),
        ((plane, size, *tile),),
        "spread",
        [designs[turn] for turn in turns_of(size)],
        [vmem] * size,
        [vmem((size, *tile), real)],
    )
    outer = (-(-OUTER // 8) * 8, LANES)
    body, first, last = call(
        functools.partial(arrange_kernel, splits),
        ((FIELDS, 16, LANES), outer, outer),
        "arrange",
        (packed,),
        [vmem],
    )
    copies = lax.all_to_all(copies, ("grp", "gy"), 0, 0)
    path = [on_path(index, grp, splits) for index in range(plane)]
    order = [(path if gx % 2 == 0 else path[::-1])[index] * size + gx for gx in range(size) for index in range(plane)]
    up = list(zip(order[:-1], order[1:]))
    line = ("grp", "gy", "gx")
    before = lax.ppermute(last, line, up)
    after = lax.ppermute(first, line, [(j, i) for i, j in up])
    columns = size * LANES
    share = call(
        functools.partial(level_kernel, rows, splits, size),
        ((2, 32, LANES),),
        "level",
        (beta_step.reshape(1), copies),
        [pltpu.SMEM, vmem],
        [vmem((columns + 16, LANES), real), vmem((columns, LANES), real)],
    )
    shapes = [
        (19, 48, LANES),
        (19, 48, LANES),
        (19, 48, LANES),
        (STEPS, 4, 32, LANES),
        (32, LANES),
        (48, LANES),
        (3 * LANES, LANES),
    ]
    packed = call(
        functools.partial(flow_kernel, rows, splits, size),
        ((plane, 5, 8, LANES),),
        "flow",
        (share, body, before, after),
        [vmem] * 4,
        [vmem(shape, real) for shape in shapes],
    )
    packed = lax.all_to_all(packed, ("grp", "gy"), 0, 0)
    return call(functools.partial(result_kernel, splits), (populations.shape, design.shape), "result", (packed,), [vmem])


def body(design, populations, cotangent, wall_mask, inlet_mask, beta_step):
    grp, splits = lax.axis_size("grp"), lax.axis_size("gy")
    layers, height, width = design.shape
    fits = height == 8 and width == LANES and layers * grp * height * splits == LANES
    whole = body_by_columns if fits and grp * splits * 16 == LANES else body_by_blocks
    return whole(design, populations, cotangent, wall_mask, inlet_mask, beta_step)


def solution(mesh):
    placed = (
        P("grp", "gy", "gx"),
        P(None, "grp", "gy", "gx"),
        P(None, "grp", "gy", "gx"),
        P("grp", "gy", "gx"),
        P("grp", "gy", "gx"),
        P(),
    )
    return jax.shard_map(
        body,
        mesh=mesh,
        in_specs=placed,
        out_specs=(P(None, "grp", "gy", "gx"), P("grp", "gy", "gx")),
        check_vma=False,
    )
```

```python
import functools

import jax
import jax.numpy as jnp
import numpy as np
from jax import lax
from jax.experimental import pallas as pl
from jax.experimental.pallas import tpu as pltpu
from jax.sharding import PartitionSpec as P

STEPS = 4
BISECT = 30


velocities = np.array(
    [
        [0, 0, 0],
        [1, 0, 0],
        [-1, 0, 0],
        [0, 1, 0],
        [0, -1, 0],
        [0, 0, 1],
        [0, 0, -1],
        [1, 1, 0],
        [-1, -1, 0],
        [1, -1, 0],
        [-1, 1, 0],
        [1, 0, 1],
        [-1, 0, -1],
        [1, 0, -1],
        [-1, 0, 1],
        [0, 1, 1],
        [0, -1, -1],
        [0, 1, -1],
        [0, -1, 1],
    ]
)
opposite = [0, 2, 1, 4, 3, 6, 5, 8, 7, 10, 9, 12, 11, 14, 13, 16, 15, 18, 17]
lattice_weights = [1.0 / 3.0] + [1.0 / 18.0] * 6 + [1.0 / 36.0] * 12
relax_rate = 0.8
inlet_speed = 0.05
alpha_most = 8.0
penalty_shape = 0.1
fluid_share = 0.4


def extended(value, sides, width):
    for axis, dim in sides:
        size, length = (lax.axis_size(axis), value.shape[dim])
        up = [(i, (i + 1) % size) for i in range(size - 1)]
        down = [(j, i) for i, j in up]
        last = lax.slice_in_dim(value, length - width, length, axis=dim)
        leading = lax.slice_in_dim(value, 0, width, axis=dim)
        before = lax.ppermute(last, axis, up)
        after = lax.ppermute(leading, axis, down)
        value = jnp.concatenate([before, value, after], axis=dim)
    return value


def equilibrium(density, speed_z, speed_y, speed_x):
    square = speed_z * speed_z + speed_y * speed_y + speed_x * speed_x
    comps = []
    for i in range(19):
        along = (
            float(velocities[i][0]) * speed_z
            + float(velocities[i][1]) * speed_y
            + float(velocities[i][2]) * speed_x
        )
        comps.append(
            lattice_weights[i] * density * (1.0 + 3.0 * along + 4.5 * along * along - 1.5 * square)
        )
    return jnp.stack(comps)


def moment(popul, axis):
    total = jnp.zeros(popul.shape[1:], popul.dtype)
    for i in range(1, 19):
        if velocities[i][axis] != 0:
            total = total + float(velocities[i][axis]) * popul[i]
    return total


def collide(popul, alpha, wall_mask, inlet_mask):
    density = jnp.sum(popul, axis=0)
    scale = density * (1.0 + alpha)
    feq = equilibrium(
        density, moment(popul, 0) / scale, moment(popul, 1) / scale, moment(popul, 2) / scale
    )
    post = popul + relax_rate * (feq - popul)
    bounce = jnp.stack([popul[opposite[i]] for i in range(19)])
    inlet_values = []
    for i in range(19):
        along = float(velocities[i][0]) * inlet_speed
        inlet_values.append(
            lattice_weights[i]
            * (1.0 + 3.0 * along + 4.5 * along * along - 1.5 * inlet_speed * inlet_speed)
        )
    inlet_feq = jnp.stack([jnp.full(popul.shape[1:], value, popul.dtype) for value in inlet_values])
    return jnp.where(wall_mask[None] > 0, bounce, jnp.where(inlet_mask[None] > 0, inlet_feq, post))


def pick(padded, sign):
    depth, rows, cols = (padded.shape[1] - 2, padded.shape[2] - 2, padded.shape[3] - 2)
    outputs = []
    for i in range(19):
        start_z = 1 - sign * int(velocities[i][0])
        start_y = 1 - sign * int(velocities[i][1])
        start_x = 1 - sign * int(velocities[i][2])
        outputs.append(
            padded[i, start_z : start_z + depth, start_y : start_y + rows, start_x : start_x + cols]
        )
    return jnp.stack(outputs)


def shift_all(popul, sign):
    padded = extended(popul, (("grp", 1), ("gy", 2), ("gx", 3)), 1)
    return pick(padded, sign)


def smooth_field(field):
    padded = extended(field, (("grp", 0), ("gy", 1), ("gx", 2)), 1)
    along_z = 0.25 * padded[:-2] + 0.5 * padded[1:-1] + 0.25 * padded[2:]
    along_y = 0.25 * along_z[:, :-2] + 0.5 * along_z[:, 1:-1] + 0.25 * along_z[:, 2:]
    return 0.25 * along_y[:, :, :-2] + 0.5 * along_y[:, :, 1:-1] + 0.25 * along_y[:, :, 2:]


def project(filtered, thresh, beta):
    denom = jnp.tanh(beta * thresh) + jnp.tanh(beta * (1.0 - thresh))
    return (jnp.tanh(beta * thresh) + jnp.tanh(beta * (filtered - thresh))) / denom


def threshold_kernel(cells, beta_ref, filtered_ref, eta_ref, raised_ref):
    beta = jnp.full((8, 128), beta_ref[0], jnp.float32)
    raised_ref[...] = jnp.exp(2.0 * beta_ref[0] * filtered_ref[...])
    top = jnp.exp(2.0 * beta)
    rows = filtered_ref.shape[0]
    span = min(rows, 512)

    def halve(step, ends):
        low, high = ends
        middle = 0.5 * (low + high)
        level = jnp.exp(2.0 * beta * middle)

        def part(index, total):
            for row in range(0, span, 8):
                raised = raised_ref[pl.ds(pl.multiple_of(index * span + row, 8), 8), :]
                total = total + (raised - 1.0) / (raised + level)
            return total

        total = lax.fori_loop(0, rows // span, part, jnp.zeros((8, 128), jnp.float32))
        volume = jnp.sum(jnp.sum(total, axis=0, keepdims=True), axis=1, keepdims=True)
        above = volume * ((top + level) / (top - 1.0)) > fluid_share * cells
        return jnp.where(above, middle, low), jnp.where(above, high, middle)

    low, high = lax.fori_loop(
        0, BISECT, halve, (jnp.zeros((8, 128), jnp.float32), jnp.ones((8, 128), jnp.float32))
    )
    eta_ref[...] = 0.5 * (low + high)


def threshold(filtered, beta, cells):
    eta = pl.pallas_call(
        functools.partial(threshold_kernel, cells),
        out_shape=jax.ShapeDtypeStruct((8, 128), jnp.float32),
        in_specs=[
            pl.BlockSpec(memory_space=pltpu.SMEM),
            pl.BlockSpec(memory_space=pltpu.VMEM),
        ],
        out_specs=pl.BlockSpec(memory_space=pltpu.VMEM),
        scratch_shapes=[pltpu.VMEM(filtered.shape, jnp.float32)],
        compiler_params=pltpu.CompilerParams(vmem_limit_bytes=40 * 2**20),
        name="threshold",
    )(beta.reshape(1), filtered)
    return eta[0, 0]


def body_by_blocks(design, populations, cotangent, wall_mask, inlet_mask, beta_step):
    beta = jnp.exp2(beta_step.astype(jnp.float32) / 16.0)
    filtered = smooth_field(design)
    cells = design.size * lax.axis_size("grp") * lax.axis_size("gy") * lax.axis_size("gx")
    devices = lax.axis_size("grp") * lax.axis_size("gy") * lax.axis_size("gx")
    copies = jnp.broadcast_to(filtered, (devices, *filtered.shape))
    everywhere = lax.all_to_all(copies, ("grp", "gy", "gx"), 0, 0)
    eta = threshold(everywhere.reshape(-1, filtered.shape[-1]), beta, cells)
    density_hat = project(filtered, eta, beta)
    alpha = alpha_most * penalty_shape * (1.0 - density_hat) / (penalty_shape + density_hat)
    states = []
    popul = populations
    for step in range(STEPS):
        states.append(popul)
        popul = shift_all(collide(popul, alpha, wall_mask, inlet_mask), 1)
    adjoint = cotangent
    alpha_grad = jnp.zeros_like(alpha)
    for step in reversed(range(STEPS)):
        back = shift_all(adjoint, -1)
        unused, pullback = jax.vjp(
            lambda p, a: collide(p, a, wall_mask, inlet_mask), states[step], alpha
        )
        adjoint, term = pullback(back)
        alpha_grad = alpha_grad + term
    denom = jnp.tanh(beta * eta) + jnp.tanh(beta * (1.0 - eta))
    slope = beta * (1.0 - jnp.tanh(beta * (filtered - eta)) ** 2) / denom
    factor = (
        -alpha_most * penalty_shape * (1.0 + penalty_shape) / (penalty_shape + density_hat) ** 2
    )
    design_grad = smooth_field(alpha_grad * factor * slope)
    return (popul, design_grad)


LANES = 128
AROUND = ((1, 0), (-1, 0), (0, 1), (0, -1), (1, 1), (-1, -1), (1, -1), (-1, 1))
FIELDS = 40
NEAR = STEPS + 1
OUTER = 8 * 21 + NEAR * 19
CLOSE = 2.0**-14


def rolled(value, amount):
    amount = amount % LANES
    return value if amount == 0 else pltpu.roll(value, amount, 1)


def lane_index():
    return lax.broadcasted_iota(jnp.int32, (8, LANES), 1)


def on_path(index, grp, splits):
    part, step = index // grp, index % grp
    return (step if part % 2 == 0 else grp - 1 - step) * splits + part


def device_at(index, grp, splits):
    odd = lax.rem(lax.axis_index("gx"), 2)
    return jnp.where(odd == 0, on_path(index, grp, splits), on_path(grp * splits - 1 - index, grp, splits))


def block_here(grp, splits):
    step, part = lax.axis_index("grp"), lax.axis_index("gy")
    index = part * grp + jnp.where(lax.rem(part, 2) == 0, step, grp - 1 - step)
    return jnp.where(lax.rem(lax.axis_index("gx"), 2) == 0, index, grp * splits - 1 - index)


def mixed(values):
    place = lane_index() // 16
    for half in (4, 2, 1):
        upper = (place & half) != 0
        values = [jnp.where(upper, values[(index + half) % 8], values[index]) for index in range(8)]
    return values


def pack_kernel(
    splits, design_ref, populations_ref, cotangent_ref, wall_ref, inlet_ref, design_out_ref, packed_ref,
    fields_ref, masks_ref, sems,
):
    moves = [
        pltpu.make_async_copy(populations_ref, fields_ref.at[0:19], sems.at[0]),
        pltpu.make_async_copy(cotangent_ref, fields_ref.at[19:38], sems.at[1]),
        pltpu.make_async_copy(wall_ref, masks_ref.at[0], sems.at[2]),
        pltpu.make_async_copy(inlet_ref, masks_ref.at[1], sems.at[3]),
        pltpu.make_async_copy(design_ref, design_out_ref, sems.at[4]),
    ]
    for move in moves:
        move.start()
    for move in moves:
        move.wait()
    devices = [device_at(index, 8 // splits, splits) for index in range(8)]
    for layer in range(masks_ref.shape[1]):
        for group in range(FIELDS // 8):
            values = []
            for slot in range(8):
                index = group * 8 + slot
                if index in (19, 20):
                    value = masks_ref[index - 19, layer].astype(jnp.float32)
                else:
                    value = fields_ref[index if index < 19 else index - 2, layer]
                values.append(rolled(value, 16 * slot))
            values = mixed(values)
            for index in range(8):
                packed_ref[devices[index], group, layer] = values[-index % 8]


def arrange_kernel(splits, packed_ref, body_ref, first_ref, last_ref):
    layers = packed_ref.shape[2]
    planes = packed_ref.shape[0] // splits * layers
    me = block_here(packed_ref.shape[0] // splits, splits)
    for group in range(FIELDS // 8):
        plane = gather_plane(
            lambda z, part: packed_ref[(z // layers) * splits + part, group, z % layers], planes, splits
        ).T
        for slot in range(8):
            index = group * 8 + lax.rem(slot + 8 - me, 8)
            body_ref[index] = plane[16 * slot : 16 * slot + 16, :]
    for index in range(FIELDS):
        if index < 21:
            first_ref[8 * index : 8 * index + 8, :] = body_ref[index, 0:8, :]
            last_ref[8 * index : 8 * index + 8, :] = body_ref[index, 8:16, :]
        else:
            start = 8 * 21 + NEAR * (index - 21)
            first_ref[start : start + NEAR, :] = body_ref[index, 0:NEAR, :]
            last_ref[start : start + NEAR, :] = body_ref[index, 16 - NEAR : 16, :]
    for ref in (first_ref, last_ref):
        rest = ref.shape[0] - OUTER
        ref[OUTER:, :] = jnp.zeros((rest, LANES), jnp.float32)


def turns_of(size):
    return sorted(range(size), key=lambda turn: (turn != 0, turn != size // 2, turn))


def spread_kernel(size, *refs):
    design_refs, (copies_ref, design_ref) = refs[:size], refs[size:]
    here = lax.axis_index("gx")
    for turn, ref in zip(turns_of(size), design_refs):
        design_ref[lax.rem(here + turn, size)] = ref[...]
    lanes = lane_index()
    zero = jnp.zeros((8, LANES), jnp.float32)
    for layer in range(copies_ref.shape[2]):
        tiles = [zero] + [design_ref[index, layer] for index in range(size)] + [zero]
        ahead = [rolled(tile, 1) for tile in tiles]
        behind = [rolled(tile, -1) for tile in tiles]
        for index in range(1, size + 1):
            value = 0.5 * tiles[index] + 0.25 * (
                jnp.where(lanes == 0, ahead[index - 1], ahead[index])
                + jnp.where(lanes == LANES - 1, behind[index + 1], behind[index])
            )
            for device in range(copies_ref.shape[0]):
                copies_ref[device, index - 1, layer] = value


def exponent(step_ref):
    steps = jnp.full((8, LANES), step_ref[0], jnp.int32).astype(jnp.float32)
    return jnp.exp2(steps / 16.0)


def plane_masks(rows):
    lanes = lane_index()
    depth, place_z, place_y = LANES // rows, lanes // rows, lanes % rows
    masks = {}
    for cz, cy in AROUND:
        inside = None
        for shift, place, count in ((cz, place_z, depth), (cy, place_y, rows)):
            if shift:
                here = (place >= 1) if shift > 0 else (place < count - 1)
                inside = here if inside is None else inside & here
        masks[cz, cy] = inside
    return masks


def plane_shift(value, cz, cy, rows, masks):
    if cz == 0 and cy == 0:
        return value
    return jnp.where(masks[cz, cy], rolled(value, cz * rows + cy), 0.0)


def plane_smooth(value, rows, masks):
    for cz, cy in ((1, 0), (0, 1)):
        value = 0.5 * value + 0.25 * (
            plane_shift(value, cz, cy, rows, masks) + plane_shift(value, -cz, -cy, rows, masks)
        )
    return value


def gather_plane(read, planes, splits):
    blocks = []
    for z in range(planes):
        for part in range(splits):
            blocks.append(read(z, part))
    return jnp.concatenate(blocks, axis=0)


def volume_root(raised_ref, columns, beta):
    zero = jnp.zeros((8, LANES), jnp.float32)
    one = jnp.ones((8, LANES), jnp.float32)
    cells = columns * LANES
    top = jnp.exp(2.0 * beta)
    scale = 1.0 / (top - 1.0)

    def total(parts):
        value = (parts[0] + parts[1]) + (parts[2] + parts[3])
        return jnp.sum(jnp.sum(value, axis=0, keepdims=True), axis=1, keepdims=True)

    def advance(state):
        low, high, low_known, high_known, middle, _ = state
        level = jnp.exp(2.0 * beta * middle)
        sums, slopes = [zero] * 4, [zero] * 4
        for index, row in enumerate(range(0, columns, 8)):
            raised = raised_ref[row : row + 8, :]
            below = raised + level
            part = pl.reciprocal(below, approx=True)
            part = part * (2.0 - below * part)
            share = (raised - 1.0) * part
            sums[index % 4] = sums[index % 4] + share
            slopes[index % 4] = slopes[index % 4] + share * part
        volume, slope = total(sums), total(slopes)
        whole = (top + level) * scale
        excess = volume * whole - fluid_share * cells
        slope = (2.0 * beta * level) * (volume * scale - whole * slope)
        above = excess > 0.0
        low, low_known = jnp.where(above, middle, low), jnp.where(above, 1.0, low_known)
        high, high_known = jnp.where(above, high, middle), jnp.where(above, high_known, 1.0)
        guess = middle - excess / slope
        taken = (guess >= low) & (guess <= high)
        other = jnp.where(
            (guess > high) & (high_known == 0.0),
            high,
            jnp.where((guess < low) & (low_known == 0.0), low, 0.5 * (low + high)),
        )
        change = jnp.where(taken, jnp.abs(guess - middle), 2.0**16 * (high - low))
        return low, high, low_known, high_known, jnp.where(taken, guess, other), change

    def going(carry):
        step, state = carry
        return (step < 64) & (jnp.max(state[5]) > CLOSE)

    state = advance(advance((zero, one, zero, zero, 0.5 * one, zero)))
    _, state = lax.while_loop(going, lambda carry: (carry[0] + 1, advance(carry[1])), (2, state))
    return jnp.clip(state[4], 0.5**31, 1.0)


def level_kernel(rows, splits, size, step_ref, copies_ref, share_ref, filtered_ref, raised_ref):
    layers = copies_ref.shape[2]
    planes = LANES // rows
    columns = size * LANES
    masks = plane_masks(rows)
    zero = jnp.zeros((8, LANES), jnp.float32)
    beta = exponent(step_ref)
    filtered_ref[0:8, :] = zero
    filtered_ref[columns + 8 : columns + 16, :] = zero
    for block in range(size):
        plane = gather_plane(
            lambda z, part: copies_ref[(z // layers) * splits + part, block, z % layers], planes, splits
        )
        filtered_ref[8 + block * LANES : 8 + (block + 1) * LANES, :] = plane.T
    for row in range(8, columns + 8, 8):
        value = plane_smooth(filtered_ref[row : row + 8, :], rows, masks)
        filtered_ref[row : row + 8, :] = value
        raised_ref[row - 8 : row, :] = jnp.exp(2.0 * beta * value)
    eta = volume_root(raised_ref, columns, beta)
    place = lax.axis_index("gx") * copies_ref.shape[0] + block_here(copies_ref.shape[0] // splits, splits)
    level = jnp.exp(2.0 * beta * eta)
    top = jnp.exp(2.0 * beta)
    whole = (top + level) / (top - 1.0)
    strength = alpha_most * penalty_shape
    for block in range(4):
        at = slice(8 * block, 8 * block + 8)
        start = pl.multiple_of(place * 16 + 8 * block, 8)
        raised = jnp.exp(2.0 * beta * filtered_ref[pl.ds(start, 8), :])
        part = 1.0 / (raised + level)
        density_hat = ((raised - 1.0) * part) * whole
        share_ref[0, at, :] = (penalty_shape + density_hat) / (
            penalty_shape + strength + (1.0 - strength) * density_hat
        )
        slope = 2.0 * beta * (raised * part) * ((level + 1.0) * part) * whole
        factor = -strength * (1.0 + penalty_shape) / (
            (penalty_shape + density_hat) * (penalty_shape + density_hat)
        )
        share_ref[1, at, :] = slope * factor


def flow(rho, speed):
    square = 1.0 - 1.5 * (speed[0] * speed[0] + speed[1] * speed[1] + speed[2] * speed[2])
    comps = [lattice_weights[0] * rho * square]
    weighted = {1.0 / 18.0: rho * (1.0 / 18.0), 1.0 / 36.0: rho * (1.0 / 36.0)}
    for i in range(1, 19, 2):
        along = along_of(speed, i)
        weight = weighted[lattice_weights[i]]
        even = weight * (square + 4.5 * along * along)
        odd = weight * (3.0 * along)
        comps += [even + odd, even - odd]
    return comps


def along_of(speed, i):
    total = None
    for axis in range(3):
        sign = int(velocities[i][axis])
        if sign:
            if total is None:
                total = speed[axis] if sign > 0 else -speed[axis]
            else:
                total = total + speed[axis] if sign > 0 else total - speed[axis]
    return total


def add_along(totals, value, i):
    for axis in range(3):
        sign = int(velocities[i][axis])
        if sign:
            if totals[axis] is None:
                totals[axis] = value if sign > 0 else -value
            else:
                totals[axis] = totals[axis] + value if sign > 0 else totals[axis] - value


def inlet_value(i):
    along = float(velocities[i][0]) * inlet_speed
    return lattice_weights[i] * (1.0 + 3.0 * along + 4.5 * along * along - 1.5 * inlet_speed * inlet_speed)


def flow_kernel(
    rows, splits, size, share_ref, body_ref, before_ref, after_ref, packed_ref,
    cotangent_ref, even_ref, odd_ref, kept_ref, grad_ref, smooth_ref, output_ref,
):
    devices = packed_ref.shape[0]
    planes = LANES // rows
    layers = planes * splits // devices
    masks = plane_masks(rows)
    zero = jnp.zeros((8, LANES), jnp.float32)
    me = block_here(devices // splits, splits)
    place = lax.axis_index("gx") * devices + me
    last = size * devices - 1

    def inside(value, block):
        if block == 0:
            return jnp.where(place > 0, value, 0.0)
        if block == 3:
            return jnp.where(place < last, value, 0.0)
        return value

    def initial(i, row):
        if row == 0:
            return before_ref[8 * i : 8 * i + 8, :]
        if row == 24:
            return after_ref[8 * i : 8 * i + 8, :]
        return body_ref[i, row - 8 : row, :]

    for ref in (even_ref, odd_ref, cotangent_ref):
        for i in range(19):
            ref[i, 0:8, :] = zero
            ref[i, 40:48, :] = zero
    for i in range(19):
        start = 8 * 21 + NEAR * i
        cotangent_ref[i, 8:16, :] = zero
        cotangent_ref[i, 16 - NEAR : 16, :] = before_ref[start : start + NEAR, :]
        cotangent_ref[i, 16:32, :] = body_ref[21 + i]
        cotangent_ref[i, 32:40, :] = zero
        cotangent_ref[i, 32 : 32 + NEAR, :] = after_ref[start : start + NEAR, :]

    def arrived(ref, i, row):
        cz, cy, cx = (int(c) for c in velocities[i])
        return plane_shift(ref[i, row + 8 - cx : row + 16 - cx, :], cz, cy, rows, masks)

    buffers = (even_ref, odd_ref)
    for step in range(STEPS):
        source, target = buffers[(step + 1) % 2], buffers[step % 2]
        for block in range(4):
            row = 8 * block
            at = slice(row, row + 8)
            if step == 0:
                popul = [initial(i, row) for i in range(19)]
            else:
                popul = [arrived(source, i, row) for i in range(19)]
            wall = initial(19, row) > 0.0
            inlet = initial(20, row) > 0.0
            rho = popul[0]
            momentum = [None, None, None]
            for i in range(1, 19, 2):
                rho = rho + (popul[i] + popul[i + 1])
                add_along(momentum, popul[i] - popul[i + 1], i)
            scale = share_ref[0, at, :] / rho
            speed = [value * scale for value in momentum]
            kept_ref[step, 0, at, :] = rho
            for axis in range(3):
                kept_ref[step, 1 + axis, at, :] = speed[axis]
            settled = flow(relax_rate * rho, speed)
            for i in range(19):
                post = (1.0 - relax_rate) * popul[i] + settled[i]
                post = jnp.where(wall, popul[opposite[i]], jnp.where(inlet, inlet_value(i), post))
                target[i, row + 8 : row + 16, :] = inside(post, block)
    def put(index, row, value):
        group, slot = divmod(index, 8)
        for slot in (slot,) if group < 2 else (slot, slot + 4):
            start = group * LANES + 16 * lax.rem(slot + me, 8) + row
            output_ref[pl.ds(pl.multiple_of(start, 8), 8), :] = value

    source = buffers[(STEPS - 1) % 2]
    for i in range(19):
        for row in (8, 16):
            put(i, row - 8, arrived(source, i, row))

    for step in reversed(range(STEPS)):
        source = cotangent_ref if step == STEPS - 1 else buffers[step % 2]
        target = buffers[(step + 1) % 2]
        for block in range(4):
            row = 8 * block
            at = slice(row, row + 8)
            back = []
            for i in range(19):
                cz, cy, cx = (int(c) for c in velocities[i])
                value = source[i, row + 8 + cx : row + 16 + cx, :]
                back.append(plane_shift(value, -cz, -cy, rows, masks))
            wall = initial(19, row) > 0.0
            inlet = initial(20, row) > 0.0
            rho = kept_ref[step, 0, at, :]
            speed = [kept_ref[step, 1 + axis, at, :] for axis in range(3)]
            square = speed[0] * speed[0] + speed[1] * speed[1] + speed[2] * speed[2]
            share = share_ref[0, at, :]
            faces, edges = None, None
            first, second = [None, None, None], [None, None, None]
            for i in range(1, 19, 2):
                both, apart = back[i] + back[i + 1], back[i] - back[i + 1]
                if i < 7:
                    faces = both if faces is None else faces + both
                    both, apart = 2.0 * both, 2.0 * apart
                else:
                    edges = both if edges is None else edges + both
                add_along(first, apart, i)
                add_along(second, along_of(speed, i) * both, i)
            mean = lattice_weights[0] * back[0] + (1.0 / 18.0) * faces + (1.0 / 36.0) * edges
            first = [value * (3.0 / 36.0) for value in first]
            second = [value * (9.0 / 36.0) for value in second]
            twice = speed[0] * second[0] + speed[1] * second[1] + speed[2] * second[2]
            once = speed[0] * first[0] + speed[1] * first[1] + speed[2] * first[2]
            drag = once + twice - 3.0 * square * mean
            term = jnp.where(wall | inlet, 0.0, -relax_rate * (rho * share * drag))
            grad_ref[at, :] = term if step == STEPS - 1 else grad_ref[at, :] + term
            if step == 0:
                continue
            rest = relax_rate * (mean * (1.0 + 1.5 * square) - 0.5 * twice)
            push = [
                (relax_rate * share) * (first[axis] + second[axis] - 3.0 * mean * speed[axis]) for axis in range(3)
            ]
            for i in range(19):
                if i == 0:
                    post = (1.0 - relax_rate) * back[0] + rest
                else:
                    way = along_of(push, i if i % 2 else i - 1)
                    post = (1.0 - relax_rate) * back[i] + (rest + way if i % 2 else rest - way)
                post = jnp.where(wall, back[opposite[i]], jnp.where(inlet, 0.0, post))
                target[i, row + 8 : row + 16, :] = inside(post, block)

    smooth_ref[0:8, :] = zero
    smooth_ref[40:48, :] = zero
    for block in range(4):
        at = slice(8 * block, 8 * block + 8)
        value = inside(grad_ref[at, :] * share_ref[1, at, :], block)
        smooth_ref[8 * block + 8 : 8 * block + 16, :] = plane_smooth(value, rows, masks)
    for row in (8, 16):
        value = 0.5 * smooth_ref[row + 8 : row + 16, :] + 0.25 * (
            smooth_ref[row + 7 : row + 15, :] + smooth_ref[row + 9 : row + 17, :]
        )
        put(19, row - 8, value)
    second = lax.rem(lane_index() // 16 + 8 - me, 8) >= 4
    for group in range(3):
        plane = output_ref[group * LANES : (group + 1) * LANES, :].T
        for device in range(devices):
            tiles = []
            for layer in range(layers):
                at = (((device // splits) * layers + layer) * splits + device % splits) * 8
                tiles.append(plane[at : at + 8, :])
            if group < 2:
                for layer in range(layers):
                    packed_ref[device, group * layers + layer] = tiles[layer]
            else:
                packed_ref[device, group * layers] = jnp.where(second, tiles[1], tiles[0])


def result_kernel(splits, packed_ref, populations_ref, grad_ref):
    devices = [device_at(index, 8 // splits, splits) for index in range(8)]
    for tile in range(packed_ref.shape[1]):
        values = mixed([packed_ref[device, tile] for device in devices])
        for slot in range(8):
            value = rolled(values[-slot % 8], -16 * slot)
            if tile < 4:
                populations_ref[tile // 2 * 8 + slot, tile % 2] = value
            elif slot % 4 < 3:
                populations_ref[16 + slot % 4, slot // 4] = value
            else:
                grad_ref[slot // 4] = value


def call(kernel, outs, name, operands, spaces, scratch=(), room=32):
    vmem = pl.BlockSpec(memory_space=pltpu.VMEM)
    shapes = tuple(jax.ShapeDtypeStruct(shape, jnp.float32) for shape in outs)
    many = len(outs) > 1
    return pl.pallas_call(
        kernel,
        out_shape=shapes if many else shapes[0],
        in_specs=[pl.BlockSpec(memory_space=space) for space in spaces],
        out_specs=(vmem,) * len(outs) if many else vmem,
        scratch_shapes=list(scratch),
        compiler_params=pltpu.CompilerParams(vmem_limit_bytes=room * 2**20),
        name=name,
    )(*operands)


def body_by_columns(design, populations, cotangent, wall_mask, inlet_mask, beta_step):
    grp, splits, size = (lax.axis_size(axis) for axis in ("grp", "gy", "gx"))
    layers, height, width = design.shape
    rows, plane = height * splits, grp * splits
    tile = (layers, 8, LANES)
    vmem, real = pltpu.VMEM, jnp.float32
    design, packed = call(
        functools.partial(pack_kernel, splits),
        (tile, (plane, FIELDS // 8, *tile)),
        "pack",
        (design, populations, cotangent, wall_mask, inlet_mask),
        [pl.ANY] * 5,
        [vmem((38, *tile), real), vmem((2, *tile), jnp.int32), pltpu.SemaphoreType.DMA((5,))],
        60,
    )
    packed = lax.all_to_all(packed, ("grp", "gy"), 0, 0)
    designs = [design] * size
    for turn in reversed(range(1, size)):
        designs[turn] = lax.ppermute(design, "gx", [((i + turn) % size, i) for i in range(size)])
    copies = call(
        functools.partial(spread_kernel, size),
        ((plane, size, *tile),),
        "spread",
        [designs[turn] for turn in turns_of(size)],
        [vmem] * size,
        [vmem((size, *tile), real)],
    )
    outer = (-(-OUTER // 8) * 8, LANES)
    body, first, last = call(
        functools.partial(arrange_kernel, splits),
        ((FIELDS, 16, LANES), outer, outer),
        "arrange",
        (packed,),
        [vmem],
    )
    path = [on_path(index, grp, splits) for index in range(plane)]
    order = [(path if gx % 2 == 0 else path[::-1])[index] * size + gx for gx in range(size) for index in range(plane)]
    up = list(zip(order[:-1], order[1:]))
    line = ("grp", "gy", "gx")
    before = lax.ppermute(last, line, up)
    after = lax.ppermute(first, line, [(j, i) for i, j in up])
    columns = size * LANES
    def level(turn, carry):
        here = lax.all_to_all(carry[0], ("grp", "gy"), 0, 0)
        share = call(
            functools.partial(level_kernel, rows, splits, size),
            ((2, 32, LANES),),
            "level",
            (beta_step.reshape(1), here),
            [pltpu.SMEM, vmem],
            [vmem((columns + 16, LANES), real), vmem((columns, LANES), real)],
        )
        return here, share

    once = jnp.minimum(beta_step + 1, 1)
    _, share = lax.fori_loop(0, once, level, (copies, jnp.zeros((2, 32, LANES), real)))
    shapes = [
        (19, 48, LANES),
        (19, 48, LANES),
        (19, 48, LANES),
        (STEPS, 4, 32, LANES),
        (32, LANES),
        (48, LANES),
        (3 * LANES, LANES),
    ]
    packed = call(
        functools.partial(flow_kernel, rows, splits, size),
        ((plane, 5, 8, LANES),),
        "flow",
        (share, body, before, after),
        [vmem] * 4,
        [vmem(shape, real) for shape in shapes],
    )
    packed = lax.all_to_all(packed, ("grp", "gy"), 0, 0)
    return call(functools.partial(result_kernel, splits), (populations.shape, design.shape), "result", (packed,), [vmem])


def body(design, populations, cotangent, wall_mask, inlet_mask, beta_step):
    grp, splits = lax.axis_size("grp"), lax.axis_size("gy")
    layers, height, width = design.shape
    fits = height == 8 and width == LANES and layers * grp * height * splits == LANES
    whole = body_by_columns if fits and grp * splits * 16 == LANES else body_by_blocks
    return whole(design, populations, cotangent, wall_mask, inlet_mask, beta_step)


def solution(mesh):
    placed = (
        P("grp", "gy", "gx"),
        P(None, "grp", "gy", "gx"),
        P(None, "grp", "gy", "gx"),
        P("grp", "gy", "gx"),
        P("grp", "gy", "gx"),
        P(),
    )
    return jax.shard_map(
        body,
        mesh=mesh,
        in_specs=placed,
        out_specs=(P(None, "grp", "gy", "gx"), P("grp", "gy", "gx")),
        check_vma=False,
    )
```

```python
import functools

import jax
import jax.numpy as jnp
import numpy as np
from jax import lax
from jax.experimental import pallas as pl
from jax.experimental.pallas import tpu as pltpu
from jax.sharding import PartitionSpec as P

STEPS = 4
BISECT = 30


velocities = np.array(
    [
        [0, 0, 0],
        [1, 0, 0],
        [-1, 0, 0],
        [0, 1, 0],
        [0, -1, 0],
        [0, 0, 1],
        [0, 0, -1],
        [1, 1, 0],
        [-1, -1, 0],
        [1, -1, 0],
        [-1, 1, 0],
        [1, 0, 1],
        [-1, 0, -1],
        [1, 0, -1],
        [-1, 0, 1],
        [0, 1, 1],
        [0, -1, -1],
        [0, 1, -1],
        [0, -1, 1],
    ]
)
opposite = [0, 2, 1, 4, 3, 6, 5, 8, 7, 10, 9, 12, 11, 14, 13, 16, 15, 18, 17]
lattice_weights = [1.0 / 3.0] + [1.0 / 18.0] * 6 + [1.0 / 36.0] * 12
relax_rate = 0.8
inlet_speed = 0.05
alpha_most = 8.0
penalty_shape = 0.1
fluid_share = 0.4


def extended(value, sides, width):
    for axis, dim in sides:
        size, length = (lax.axis_size(axis), value.shape[dim])
        up = [(i, (i + 1) % size) for i in range(size - 1)]
        down = [(j, i) for i, j in up]
        last = lax.slice_in_dim(value, length - width, length, axis=dim)
        leading = lax.slice_in_dim(value, 0, width, axis=dim)
        before = lax.ppermute(last, axis, up)
        after = lax.ppermute(leading, axis, down)
        value = jnp.concatenate([before, value, after], axis=dim)
    return value


def equilibrium(density, speed_z, speed_y, speed_x):
    square = speed_z * speed_z + speed_y * speed_y + speed_x * speed_x
    comps = []
    for i in range(19):
        along = (
            float(velocities[i][0]) * speed_z
            + float(velocities[i][1]) * speed_y
            + float(velocities[i][2]) * speed_x
        )
        comps.append(
            lattice_weights[i] * density * (1.0 + 3.0 * along + 4.5 * along * along - 1.5 * square)
        )
    return jnp.stack(comps)


def moment(popul, axis):
    total = jnp.zeros(popul.shape[1:], popul.dtype)
    for i in range(1, 19):
        if velocities[i][axis] != 0:
            total = total + float(velocities[i][axis]) * popul[i]
    return total


def collide(popul, alpha, wall_mask, inlet_mask):
    density = jnp.sum(popul, axis=0)
    scale = density * (1.0 + alpha)
    feq = equilibrium(
        density, moment(popul, 0) / scale, moment(popul, 1) / scale, moment(popul, 2) / scale
    )
    post = popul + relax_rate * (feq - popul)
    bounce = jnp.stack([popul[opposite[i]] for i in range(19)])
    inlet_values = []
    for i in range(19):
        along = float(velocities[i][0]) * inlet_speed
        inlet_values.append(
            lattice_weights[i]
            * (1.0 + 3.0 * along + 4.5 * along * along - 1.5 * inlet_speed * inlet_speed)
        )
    inlet_feq = jnp.stack([jnp.full(popul.shape[1:], value, popul.dtype) for value in inlet_values])
    return jnp.where(wall_mask[None] > 0, bounce, jnp.where(inlet_mask[None] > 0, inlet_feq, post))


def pick(padded, sign):
    depth, rows, cols = (padded.shape[1] - 2, padded.shape[2] - 2, padded.shape[3] - 2)
    outputs = []
    for i in range(19):
        start_z = 1 - sign * int(velocities[i][0])
        start_y = 1 - sign * int(velocities[i][1])
        start_x = 1 - sign * int(velocities[i][2])
        outputs.append(
            padded[i, start_z : start_z + depth, start_y : start_y + rows, start_x : start_x + cols]
        )
    return jnp.stack(outputs)


def shift_all(popul, sign):
    padded = extended(popul, (("grp", 1), ("gy", 2), ("gx", 3)), 1)
    return pick(padded, sign)


def smooth_field(field):
    padded = extended(field, (("grp", 0), ("gy", 1), ("gx", 2)), 1)
    along_z = 0.25 * padded[:-2] + 0.5 * padded[1:-1] + 0.25 * padded[2:]
    along_y = 0.25 * along_z[:, :-2] + 0.5 * along_z[:, 1:-1] + 0.25 * along_z[:, 2:]
    return 0.25 * along_y[:, :, :-2] + 0.5 * along_y[:, :, 1:-1] + 0.25 * along_y[:, :, 2:]


def project(filtered, thresh, beta):
    denom = jnp.tanh(beta * thresh) + jnp.tanh(beta * (1.0 - thresh))
    return (jnp.tanh(beta * thresh) + jnp.tanh(beta * (filtered - thresh))) / denom


def threshold_kernel(cells, beta_ref, filtered_ref, eta_ref, raised_ref):
    beta = jnp.full((8, 128), beta_ref[0], jnp.float32)
    raised_ref[...] = jnp.exp(2.0 * beta_ref[0] * filtered_ref[...])
    top = jnp.exp(2.0 * beta)
    rows = filtered_ref.shape[0]
    span = min(rows, 512)

    def halve(step, ends):
        low, high = ends
        middle = 0.5 * (low + high)
        level = jnp.exp(2.0 * beta * middle)

        def part(index, total):
            for row in range(0, span, 8):
                raised = raised_ref[pl.ds(pl.multiple_of(index * span + row, 8), 8), :]
                total = total + (raised - 1.0) / (raised + level)
            return total

        total = lax.fori_loop(0, rows // span, part, jnp.zeros((8, 128), jnp.float32))
        volume = jnp.sum(jnp.sum(total, axis=0, keepdims=True), axis=1, keepdims=True)
        above = volume * ((top + level) / (top - 1.0)) > fluid_share * cells
        return jnp.where(above, middle, low), jnp.where(above, high, middle)

    low, high = lax.fori_loop(
        0, BISECT, halve, (jnp.zeros((8, 128), jnp.float32), jnp.ones((8, 128), jnp.float32))
    )
    eta_ref[...] = 0.5 * (low + high)


def threshold(filtered, beta, cells):
    eta = pl.pallas_call(
        functools.partial(threshold_kernel, cells),
        out_shape=jax.ShapeDtypeStruct((8, 128), jnp.float32),
        in_specs=[
            pl.BlockSpec(memory_space=pltpu.SMEM),
            pl.BlockSpec(memory_space=pltpu.VMEM),
        ],
        out_specs=pl.BlockSpec(memory_space=pltpu.VMEM),
        scratch_shapes=[pltpu.VMEM(filtered.shape, jnp.float32)],
        compiler_params=pltpu.CompilerParams(vmem_limit_bytes=40 * 2**20),
        name="threshold",
    )(beta.reshape(1), filtered)
    return eta[0, 0]


def body_by_blocks(design, populations, cotangent, wall_mask, inlet_mask, beta_step):
    beta = jnp.exp2(beta_step.astype(jnp.float32) / 16.0)
    filtered = smooth_field(design)
    cells = design.size * lax.axis_size("grp") * lax.axis_size("gy") * lax.axis_size("gx")
    devices = lax.axis_size("grp") * lax.axis_size("gy") * lax.axis_size("gx")
    copies = jnp.broadcast_to(filtered, (devices, *filtered.shape))
    everywhere = lax.all_to_all(copies, ("grp", "gy", "gx"), 0, 0)
    eta = threshold(everywhere.reshape(-1, filtered.shape[-1]), beta, cells)
    density_hat = project(filtered, eta, beta)
    alpha = alpha_most * penalty_shape * (1.0 - density_hat) / (penalty_shape + density_hat)
    states = []
    popul = populations
    for step in range(STEPS):
        states.append(popul)
        popul = shift_all(collide(popul, alpha, wall_mask, inlet_mask), 1)
    adjoint = cotangent
    alpha_grad = jnp.zeros_like(alpha)
    for step in reversed(range(STEPS)):
        back = shift_all(adjoint, -1)
        unused, pullback = jax.vjp(
            lambda p, a: collide(p, a, wall_mask, inlet_mask), states[step], alpha
        )
        adjoint, term = pullback(back)
        alpha_grad = alpha_grad + term
    denom = jnp.tanh(beta * eta) + jnp.tanh(beta * (1.0 - eta))
    slope = beta * (1.0 - jnp.tanh(beta * (filtered - eta)) ** 2) / denom
    factor = (
        -alpha_most * penalty_shape * (1.0 + penalty_shape) / (penalty_shape + density_hat) ** 2
    )
    design_grad = smooth_field(alpha_grad * factor * slope)
    return (popul, design_grad)


LANES = 128
AROUND = ((1, 0), (-1, 0), (0, 1), (0, -1), (1, 1), (-1, -1), (1, -1), (-1, 1))
FIELDS = 40
NEAR = STEPS + 1
OUTER = 8 * 21 + NEAR * 19
CLOSE = 2.0**-14


def rolled(value, amount):
    amount = amount % LANES
    return value if amount == 0 else pltpu.roll(value, amount, 1)


def lane_index():
    return lax.broadcasted_iota(jnp.int32, (8, LANES), 1)


def on_path(index, grp, splits):
    part, step = index // grp, index % grp
    return (step if part % 2 == 0 else grp - 1 - step) * splits + part


def device_at(index, grp, splits):
    odd = lax.rem(lax.axis_index("gx"), 2)
    return jnp.where(odd == 0, on_path(index, grp, splits), on_path(grp * splits - 1 - index, grp, splits))


def block_here(grp, splits):
    step, part = lax.axis_index("grp"), lax.axis_index("gy")
    index = part * grp + jnp.where(lax.rem(part, 2) == 0, step, grp - 1 - step)
    return jnp.where(lax.rem(lax.axis_index("gx"), 2) == 0, index, grp * splits - 1 - index)


def mixed(values):
    place = lane_index() // 16
    for half in (4, 2, 1):
        upper = (place & half) != 0
        values = [jnp.where(upper, values[(index + half) % 8], values[index]) for index in range(8)]
    return values


def pack_kernel(
    splits, design_ref, populations_ref, cotangent_ref, wall_ref, inlet_ref, design_out_ref, packed_ref,
    fields_ref, masks_ref, sems,
):
    moves = [
        pltpu.make_async_copy(populations_ref, fields_ref.at[0:19], sems.at[0]),
        pltpu.make_async_copy(cotangent_ref, fields_ref.at[19:38], sems.at[1]),
        pltpu.make_async_copy(wall_ref, masks_ref.at[0], sems.at[2]),
        pltpu.make_async_copy(inlet_ref, masks_ref.at[1], sems.at[3]),
        pltpu.make_async_copy(design_ref, design_out_ref, sems.at[4]),
    ]
    for move in moves:
        move.start()
    for move in moves:
        move.wait()
    devices = [device_at(index, 8 // splits, splits) for index in range(8)]
    for layer in range(masks_ref.shape[1]):
        for group in range(FIELDS // 8):
            values = []
            for slot in range(8):
                index = group * 8 + slot
                if index in (19, 20):
                    value = masks_ref[index - 19, layer].astype(jnp.float32)
                else:
                    value = fields_ref[index if index < 19 else index - 2, layer]
                values.append(rolled(value, 16 * slot))
            values = mixed(values)
            for index in range(8):
                packed_ref[devices[index], group, layer] = values[-index % 8]


def arrange_kernel(splits, packed_ref, body_ref, near_ref, far_ref):
    layers = packed_ref.shape[2]
    planes = packed_ref.shape[0] // splits * layers
    me = block_here(packed_ref.shape[0] // splits, splits)
    for group in range(FIELDS // 8):
        plane = gather_plane(
            lambda z, part: packed_ref[(z // layers) * splits + part, group, z % layers], planes, splits
        ).T
        for slot in range(8):
            index = group * 8 + lax.rem(slot + 8 - me, 8)
            body_ref[index] = plane[16 * slot : 16 * slot + 16, :]
    even = lax.rem(me, 2) == 0

    def send(start, first, last):
        near_ref[start : start + first.shape[0], :] = jnp.where(even, last, first)
        far_ref[start : start + first.shape[0], :] = jnp.where(even, first, last)

    for index in range(FIELDS):
        if index < 21:
            send(8 * index, body_ref[index, 0:8, :], body_ref[index, 8:16, :])
        else:
            start = 8 * 21 + NEAR * (index - 21)
            send(start, body_ref[index, 0:NEAR, :], body_ref[index, 16 - NEAR : 16, :])
    for ref in (near_ref, far_ref):
        ref[OUTER:, :] = jnp.zeros((ref.shape[0] - OUTER, LANES), jnp.float32)


def turns_of(size):
    return sorted(range(size), key=lambda turn: (turn != 0, turn != size // 2, turn))


def spread_kernel(size, *refs):
    design_refs, (copies_ref, design_ref) = refs[:size], refs[size:]
    here = lax.axis_index("gx")
    for turn, ref in zip(turns_of(size), design_refs):
        design_ref[lax.rem(here + turn, size)] = ref[...]
    lanes = lane_index()
    zero = jnp.zeros((8, LANES), jnp.float32)
    for layer in range(copies_ref.shape[2]):
        tiles = [zero] + [design_ref[index, layer] for index in range(size)] + [zero]
        ahead = [rolled(tile, 1) for tile in tiles]
        behind = [rolled(tile, -1) for tile in tiles]
        for index in range(1, size + 1):
            value = 0.5 * tiles[index] + 0.25 * (
                jnp.where(lanes == 0, ahead[index - 1], ahead[index])
                + jnp.where(lanes == LANES - 1, behind[index + 1], behind[index])
            )
            for device in range(copies_ref.shape[0]):
                copies_ref[device, index - 1, layer] = value


def exponent(step_ref):
    steps = jnp.full((8, LANES), step_ref[0], jnp.int32).astype(jnp.float32)
    return jnp.exp2(steps / 16.0)


def plane_masks(rows):
    lanes = lane_index()
    depth, place_z, place_y = LANES // rows, lanes // rows, lanes % rows
    masks = {}
    for cz, cy in AROUND:
        inside = None
        for shift, place, count in ((cz, place_z, depth), (cy, place_y, rows)):
            if shift:
                here = (place >= 1) if shift > 0 else (place < count - 1)
                inside = here if inside is None else inside & here
        masks[cz, cy] = inside
    return masks


def plane_shift(value, cz, cy, rows, masks):
    if cz == 0 and cy == 0:
        return value
    return jnp.where(masks[cz, cy], rolled(value, cz * rows + cy), 0.0)


def plane_smooth(value, rows, masks):
    for cz, cy in ((1, 0), (0, 1)):
        value = 0.5 * value + 0.25 * (
            plane_shift(value, cz, cy, rows, masks) + plane_shift(value, -cz, -cy, rows, masks)
        )
    return value


def gather_plane(read, planes, splits):
    blocks = []
    for z in range(planes):
        for part in range(splits):
            blocks.append(read(z, part))
    return jnp.concatenate(blocks, axis=0)


def volume_root(raised_ref, columns, beta):
    zero = jnp.zeros((8, LANES), jnp.float32)
    one = jnp.ones((8, LANES), jnp.float32)
    cells = columns * LANES
    top = jnp.exp(2.0 * beta)
    scale = 1.0 / (top - 1.0)

    def total(parts):
        value = (parts[0] + parts[1]) + (parts[2] + parts[3])
        return jnp.sum(jnp.sum(value, axis=0, keepdims=True), axis=1, keepdims=True)

    def advance(state):
        low, high, low_known, high_known, middle, _ = state
        level = jnp.exp(2.0 * beta * middle)
        sums, slopes = [zero] * 4, [zero] * 4
        for index, row in enumerate(range(0, columns, 8)):
            raised = raised_ref[row : row + 8, :]
            below = raised + level
            part = pl.reciprocal(below, approx=True)
            part = part * (2.0 - below * part)
            share = (raised - 1.0) * part
            sums[index % 4] = sums[index % 4] + share
            slopes[index % 4] = slopes[index % 4] + share * part
        volume, slope = total(sums), total(slopes)
        whole = (top + level) * scale
        excess = volume * whole - fluid_share * cells
        slope = (2.0 * beta * level) * (volume * scale - whole * slope)
        above = excess > 0.0
        low, low_known = jnp.where(above, middle, low), jnp.where(above, 1.0, low_known)
        high, high_known = jnp.where(above, high, middle), jnp.where(above, high_known, 1.0)
        guess = middle - excess / slope
        taken = (guess >= low) & (guess <= high)
        other = jnp.where(
            (guess > high) & (high_known == 0.0),
            high,
            jnp.where((guess < low) & (low_known == 0.0), low, 0.5 * (low + high)),
        )
        change = jnp.where(taken, jnp.abs(guess - middle), 2.0**16 * (high - low))
        return low, high, low_known, high_known, jnp.where(taken, guess, other), change

    def going(carry):
        step, state = carry
        return (step < 64) & (jnp.max(state[5]) > CLOSE)

    state = advance(advance((zero, one, zero, zero, 0.5 * one, zero)))
    _, state = lax.while_loop(going, lambda carry: (carry[0] + 1, advance(carry[1])), (2, state))
    return jnp.clip(state[4], 0.5**31, 1.0)


def level_kernel(rows, splits, size, step_ref, copies_ref, share_ref, filtered_ref, raised_ref):
    layers = copies_ref.shape[2]
    planes = LANES // rows
    columns = size * LANES
    masks = plane_masks(rows)
    zero = jnp.zeros((8, LANES), jnp.float32)
    beta = exponent(step_ref)
    filtered_ref[0:8, :] = zero
    filtered_ref[columns + 8 : columns + 16, :] = zero
    for block in range(size):
        plane = gather_plane(
            lambda z, part: copies_ref[(z // layers) * splits + part, block, z % layers], planes, splits
        )
        filtered_ref[8 + block * LANES : 8 + (block + 1) * LANES, :] = plane.T
    for row in range(8, columns + 8, 8):
        value = plane_smooth(filtered_ref[row : row + 8, :], rows, masks)
        filtered_ref[row : row + 8, :] = value
        raised_ref[row - 8 : row, :] = jnp.exp(2.0 * beta * value)
    eta = volume_root(raised_ref, columns, beta)
    place = lax.axis_index("gx") * copies_ref.shape[0] + block_here(copies_ref.shape[0] // splits, splits)
    level = jnp.exp(2.0 * beta * eta)
    top = jnp.exp(2.0 * beta)
    whole = (top + level) / (top - 1.0)
    strength = alpha_most * penalty_shape
    for block in range(4):
        at = slice(8 * block, 8 * block + 8)
        start = pl.multiple_of(place * 16 + 8 * block, 8)
        raised = jnp.exp(2.0 * beta * filtered_ref[pl.ds(start, 8), :])
        part = 1.0 / (raised + level)
        density_hat = ((raised - 1.0) * part) * whole
        share_ref[0, at, :] = (penalty_shape + density_hat) / (
            penalty_shape + strength + (1.0 - strength) * density_hat
        )
        slope = 2.0 * beta * (raised * part) * ((level + 1.0) * part) * whole
        factor = -strength * (1.0 + penalty_shape) / (
            (penalty_shape + density_hat) * (penalty_shape + density_hat)
        )
        share_ref[1, at, :] = slope * factor


def flow(rho, speed):
    square = 1.0 - 1.5 * (speed[0] * speed[0] + speed[1] * speed[1] + speed[2] * speed[2])
    comps = [lattice_weights[0] * rho * square]
    weighted = {1.0 / 18.0: rho * (1.0 / 18.0), 1.0 / 36.0: rho * (1.0 / 36.0)}
    for i in range(1, 19, 2):
        along = along_of(speed, i)
        weight = weighted[lattice_weights[i]]
        even = weight * (square + 4.5 * along * along)
        odd = weight * (3.0 * along)
        comps += [even + odd, even - odd]
    return comps


def along_of(speed, i):
    total = None
    for axis in range(3):
        sign = int(velocities[i][axis])
        if sign:
            if total is None:
                total = speed[axis] if sign > 0 else -speed[axis]
            else:
                total = total + speed[axis] if sign > 0 else total - speed[axis]
    return total


def add_along(totals, value, i):
    for axis in range(3):
        sign = int(velocities[i][axis])
        if sign:
            if totals[axis] is None:
                totals[axis] = value if sign > 0 else -value
            else:
                totals[axis] = totals[axis] + value if sign > 0 else totals[axis] - value


def inlet_value(i):
    along = float(velocities[i][0]) * inlet_speed
    return lattice_weights[i] * (1.0 + 3.0 * along + 4.5 * along * along - 1.5 * inlet_speed * inlet_speed)


def flow_kernel(
    rows, splits, size, share_ref, body_ref, near_ref, far_ref, packed_ref,
    cotangent_ref, even_ref, odd_ref, kept_ref, grad_ref, smooth_ref, output_ref,
):
    devices = packed_ref.shape[0]
    planes = LANES // rows
    layers = planes * splits // devices
    masks = plane_masks(rows)
    zero = jnp.zeros((8, LANES), jnp.float32)
    me = block_here(devices // splits, splits)
    place = lax.axis_index("gx") * devices + me
    last = size * devices - 1

    def inside(value, block):
        if block == 0:
            return jnp.where(place > 0, value, 0.0)
        if block == 3:
            return jnp.where(place < last, value, 0.0)
        return value

    even = lax.rem(me, 2) == 0

    def outer(start, count):
        near, far = near_ref[start : start + count, :], far_ref[start : start + count, :]
        return jnp.where(even, far, near), jnp.where(even, near, far)

    def initial(i, row):
        if row == 0:
            return outer(8 * i, 8)[0]
        if row == 24:
            return outer(8 * i, 8)[1]
        return body_ref[i, row - 8 : row, :]

    for ref in (even_ref, odd_ref, cotangent_ref):
        for i in range(19):
            ref[i, 0:8, :] = zero
            ref[i, 40:48, :] = zero
    for i in range(19):
        start = 8 * 21 + NEAR * i
        cotangent_ref[i, 8:16, :] = zero
        cotangent_ref[i, 16 - NEAR : 16, :] = outer(start, NEAR)[0]
        cotangent_ref[i, 16:32, :] = body_ref[21 + i]
        cotangent_ref[i, 32:40, :] = zero
        cotangent_ref[i, 32 : 32 + NEAR, :] = outer(start, NEAR)[1]

    def arrived(ref, i, row):
        cz, cy, cx = (int(c) for c in velocities[i])
        return plane_shift(ref[i, row + 8 - cx : row + 16 - cx, :], cz, cy, rows, masks)

    buffers = (even_ref, odd_ref)
    for step in range(STEPS):
        source, target = buffers[(step + 1) % 2], buffers[step % 2]
        for block in range(4):
            row = 8 * block
            at = slice(row, row + 8)
            if step == 0:
                popul = [initial(i, row) for i in range(19)]
            else:
                popul = [arrived(source, i, row) for i in range(19)]
            wall = initial(19, row) > 0.0
            inlet = initial(20, row) > 0.0
            rho = popul[0]
            momentum = [None, None, None]
            for i in range(1, 19, 2):
                rho = rho + (popul[i] + popul[i + 1])
                add_along(momentum, popul[i] - popul[i + 1], i)
            scale = share_ref[0, at, :] / rho
            speed = [value * scale for value in momentum]
            kept_ref[step, 0, at, :] = rho
            for axis in range(3):
                kept_ref[step, 1 + axis, at, :] = speed[axis]
            settled = flow(relax_rate * rho, speed)
            for i in range(19):
                post = (1.0 - relax_rate) * popul[i] + settled[i]
                post = jnp.where(wall, popul[opposite[i]], jnp.where(inlet, inlet_value(i), post))
                target[i, row + 8 : row + 16, :] = inside(post, block)
    def put(index, row, value):
        group, slot = divmod(index, 8)
        for slot in (slot,) if group < 2 else (slot, slot + 4):
            start = group * LANES + 16 * lax.rem(slot + me, 8) + row
            output_ref[pl.ds(pl.multiple_of(start, 8), 8), :] = value

    source = buffers[(STEPS - 1) % 2]
    for i in range(19):
        for row in (8, 16):
            put(i, row - 8, arrived(source, i, row))

    for step in reversed(range(STEPS)):
        source = cotangent_ref if step == STEPS - 1 else buffers[step % 2]
        target = buffers[(step + 1) % 2]
        for block in range(4):
            row = 8 * block
            at = slice(row, row + 8)
            back = []
            for i in range(19):
                cz, cy, cx = (int(c) for c in velocities[i])
                value = source[i, row + 8 + cx : row + 16 + cx, :]
                back.append(plane_shift(value, -cz, -cy, rows, masks))
            wall = initial(19, row) > 0.0
            inlet = initial(20, row) > 0.0
            rho = kept_ref[step, 0, at, :]
            speed = [kept_ref[step, 1 + axis, at, :] for axis in range(3)]
            square = speed[0] * speed[0] + speed[1] * speed[1] + speed[2] * speed[2]
            share = share_ref[0, at, :]
            faces, edges = None, None
            first, second = [None, None, None], [None, None, None]
            for i in range(1, 19, 2):
                both, apart = back[i] + back[i + 1], back[i] - back[i + 1]
                if i < 7:
                    faces = both if faces is None else faces + both
                    both, apart = 2.0 * both, 2.0 * apart
                else:
                    edges = both if edges is None else edges + both
                add_along(first, apart, i)
                add_along(second, along_of(speed, i) * both, i)
            mean = lattice_weights[0] * back[0] + (1.0 / 18.0) * faces + (1.0 / 36.0) * edges
            first = [value * (3.0 / 36.0) for value in first]
            second = [value * (9.0 / 36.0) for value in second]
            twice = speed[0] * second[0] + speed[1] * second[1] + speed[2] * second[2]
            once = speed[0] * first[0] + speed[1] * first[1] + speed[2] * first[2]
            drag = once + twice - 3.0 * square * mean
            term = jnp.where(wall | inlet, 0.0, -relax_rate * (rho * share * drag))
            grad_ref[at, :] = term if step == STEPS - 1 else grad_ref[at, :] + term
            if step == 0:
                continue
            rest = relax_rate * (mean * (1.0 + 1.5 * square) - 0.5 * twice)
            push = [
                (relax_rate * share) * (first[axis] + second[axis] - 3.0 * mean * speed[axis]) for axis in range(3)
            ]
            for i in range(19):
                if i == 0:
                    post = (1.0 - relax_rate) * back[0] + rest
                else:
                    way = along_of(push, i if i % 2 else i - 1)
                    post = (1.0 - relax_rate) * back[i] + (rest + way if i % 2 else rest - way)
                post = jnp.where(wall, back[opposite[i]], jnp.where(inlet, 0.0, post))
                target[i, row + 8 : row + 16, :] = inside(post, block)

    smooth_ref[0:8, :] = zero
    smooth_ref[40:48, :] = zero
    for block in range(4):
        at = slice(8 * block, 8 * block + 8)
        value = inside(grad_ref[at, :] * share_ref[1, at, :], block)
        smooth_ref[8 * block + 8 : 8 * block + 16, :] = plane_smooth(value, rows, masks)
    for row in (8, 16):
        value = 0.5 * smooth_ref[row + 8 : row + 16, :] + 0.25 * (
            smooth_ref[row + 7 : row + 15, :] + smooth_ref[row + 9 : row + 17, :]
        )
        put(19, row - 8, value)
    second = lax.rem(lane_index() // 16 + 8 - me, 8) >= 4
    for group in range(3):
        plane = output_ref[group * LANES : (group + 1) * LANES, :].T
        for device in range(devices):
            tiles = []
            for layer in range(layers):
                at = (((device // splits) * layers + layer) * splits + device % splits) * 8
                tiles.append(plane[at : at + 8, :])
            if group < 2:
                for layer in range(layers):
                    packed_ref[device, group * layers + layer] = tiles[layer]
            else:
                packed_ref[device, group * layers] = jnp.where(second, tiles[1], tiles[0])


def result_kernel(splits, packed_ref, populations_ref, grad_ref):
    devices = [device_at(index, 8 // splits, splits) for index in range(8)]
    for tile in range(packed_ref.shape[1]):
        values = mixed([packed_ref[device, tile] for device in devices])
        for slot in range(8):
            value = rolled(values[-slot % 8], -16 * slot)
            if tile < 4:
                populations_ref[tile // 2 * 8 + slot, tile % 2] = value
            elif slot % 4 < 3:
                populations_ref[16 + slot % 4, slot // 4] = value
            else:
                grad_ref[slot // 4] = value


def call(kernel, outs, name, operands, spaces, scratch=(), room=32):
    vmem = pl.BlockSpec(memory_space=pltpu.VMEM)
    shapes = tuple(jax.ShapeDtypeStruct(shape, jnp.float32) for shape in outs)
    many = len(outs) > 1
    return pl.pallas_call(
        kernel,
        out_shape=shapes if many else shapes[0],
        in_specs=[pl.BlockSpec(memory_space=space) for space in spaces],
        out_specs=(vmem,) * len(outs) if many else vmem,
        scratch_shapes=list(scratch),
        compiler_params=pltpu.CompilerParams(vmem_limit_bytes=room * 2**20),
        name=name,
    )(*operands)


def body_by_columns(design, populations, cotangent, wall_mask, inlet_mask, beta_step):
    grp, splits, size = (lax.axis_size(axis) for axis in ("grp", "gy", "gx"))
    layers, height, width = design.shape
    rows, plane = height * splits, grp * splits
    tile = (layers, 8, LANES)
    vmem, real = pltpu.VMEM, jnp.float32
    design, packed = call(
        functools.partial(pack_kernel, splits),
        (tile, (plane, FIELDS // 8, *tile)),
        "pack",
        (design, populations, cotangent, wall_mask, inlet_mask),
        [pl.ANY] * 5,
        [vmem((38, *tile), real), vmem((2, *tile), jnp.int32), pltpu.SemaphoreType.DMA((5,))],
        60,
    )
    packed = lax.all_to_all(packed, ("grp", "gy"), 0, 0)
    designs = [design] * size
    for turn in reversed(range(1, size)):
        designs[turn] = lax.ppermute(design, "gx", [((i + turn) % size, i) for i in range(size)])
    copies = call(
        functools.partial(spread_kernel, size),
        ((plane, size, *tile),),
        "spread",
        [designs[turn] for turn in turns_of(size)],
        [vmem] * size,
        [vmem((size, *tile), real)],
    )
    outer = (-(-OUTER // 8) * 8, LANES)
    body, near, far = call(
        functools.partial(arrange_kernel, splits),
        ((FIELDS, 16, LANES), outer, outer),
        "arrange",
        (packed,),
        [vmem],
    )
    copies = lax.all_to_all(copies, ("grp", "gy"), 0, 0)
    path = [on_path(index, grp, splits) for index in range(plane)]
    order = [(path if gx % 2 == 0 else path[::-1])[index] * size + gx for gx in range(size) for index in range(plane)]
    line = ("grp", "gy", "gx")

    def exchange(value, start):
        pairs = [order[b : b + 2] for b in range(start, size * plane - 1, 2)]
        return lax.ppermute(value, line, [pair for i, j in pairs for pair in ((i, j), (j, i))])

    far, near = exchange(far, 1), exchange(near, 0)
    columns = size * LANES
    share = call(
        functools.partial(level_kernel, rows, splits, size),
        ((2, 32, LANES),),
        "level",
        (beta_step.reshape(1), copies),
        [pltpu.SMEM, vmem],
        [vmem((columns + 16, LANES), real), vmem((columns, LANES), real)],
    )
    shapes = [
        (19, 48, LANES),
        (19, 48, LANES),
        (19, 48, LANES),
        (STEPS, 4, 32, LANES),
        (32, LANES),
        (48, LANES),
        (3 * LANES, LANES),
    ]
    packed = call(
        functools.partial(flow_kernel, rows, splits, size),
        ((plane, 5, 8, LANES),),
        "flow",
        (share, body, near, far),
        [vmem] * 4,
        [vmem(shape, real) for shape in shapes],
    )
    packed = lax.all_to_all(packed, ("grp", "gy"), 0, 0)
    return call(functools.partial(result_kernel, splits), (populations.shape, design.shape), "result", (packed,), [vmem])


def body(design, populations, cotangent, wall_mask, inlet_mask, beta_step):
    grp, splits = lax.axis_size("grp"), lax.axis_size("gy")
    layers, height, width = design.shape
    fits = height == 8 and width == LANES and layers * grp * height * splits == LANES
    whole = body_by_columns if fits and grp * splits * 16 == LANES else body_by_blocks
    return whole(design, populations, cotangent, wall_mask, inlet_mask, beta_step)


def solution(mesh):
    placed = (
        P("grp", "gy", "gx"),
        P(None, "grp", "gy", "gx"),
        P(None, "grp", "gy", "gx"),
        P("grp", "gy", "gx"),
        P("grp", "gy", "gx"),
        P(),
    )
    return jax.shard_map(
        body,
        mesh=mesh,
        in_specs=placed,
        out_specs=(P(None, "grp", "gy", "gx"), P("grp", "gy", "gx")),
        check_vma=False,
    )
```

```python
import functools

import jax
import jax.numpy as jnp
import numpy as np
from jax import lax
from jax.experimental import pallas as pl
from jax.experimental.pallas import tpu as pltpu
from jax.sharding import PartitionSpec as P

STEPS = 4
BISECT = 30


velocities = np.array(
    [
        [0, 0, 0],
        [1, 0, 0],
        [-1, 0, 0],
        [0, 1, 0],
        [0, -1, 0],
        [0, 0, 1],
        [0, 0, -1],
        [1, 1, 0],
        [-1, -1, 0],
        [1, -1, 0],
        [-1, 1, 0],
        [1, 0, 1],
        [-1, 0, -1],
        [1, 0, -1],
        [-1, 0, 1],
        [0, 1, 1],
        [0, -1, -1],
        [0, 1, -1],
        [0, -1, 1],
    ]
)
opposite = [0, 2, 1, 4, 3, 6, 5, 8, 7, 10, 9, 12, 11, 14, 13, 16, 15, 18, 17]
lattice_weights = [1.0 / 3.0] + [1.0 / 18.0] * 6 + [1.0 / 36.0] * 12
relax_rate = 0.8
inlet_speed = 0.05
alpha_most = 8.0
penalty_shape = 0.1
fluid_share = 0.4


def extended(value, sides, width):
    for axis, dim in sides:
        size, length = (lax.axis_size(axis), value.shape[dim])
        up = [(i, (i + 1) % size) for i in range(size - 1)]
        down = [(j, i) for i, j in up]
        last = lax.slice_in_dim(value, length - width, length, axis=dim)
        leading = lax.slice_in_dim(value, 0, width, axis=dim)
        before = lax.ppermute(last, axis, up)
        after = lax.ppermute(leading, axis, down)
        value = jnp.concatenate([before, value, after], axis=dim)
    return value


def equilibrium(density, speed_z, speed_y, speed_x):
    square = speed_z * speed_z + speed_y * speed_y + speed_x * speed_x
    comps = []
    for i in range(19):
        along = (
            float(velocities[i][0]) * speed_z
            + float(velocities[i][1]) * speed_y
            + float(velocities[i][2]) * speed_x
        )
        comps.append(
            lattice_weights[i] * density * (1.0 + 3.0 * along + 4.5 * along * along - 1.5 * square)
        )
    return jnp.stack(comps)


def moment(popul, axis):
    total = jnp.zeros(popul.shape[1:], popul.dtype)
    for i in range(1, 19):
        if velocities[i][axis] != 0:
            total = total + float(velocities[i][axis]) * popul[i]
    return total


def collide(popul, alpha, wall_mask, inlet_mask):
    density = jnp.sum(popul, axis=0)
    scale = density * (1.0 + alpha)
    feq = equilibrium(
        density, moment(popul, 0) / scale, moment(popul, 1) / scale, moment(popul, 2) / scale
    )
    post = popul + relax_rate * (feq - popul)
    bounce = jnp.stack([popul[opposite[i]] for i in range(19)])
    inlet_values = []
    for i in range(19):
        along = float(velocities[i][0]) * inlet_speed
        inlet_values.append(
            lattice_weights[i]
            * (1.0 + 3.0 * along + 4.5 * along * along - 1.5 * inlet_speed * inlet_speed)
        )
    inlet_feq = jnp.stack([jnp.full(popul.shape[1:], value, popul.dtype) for value in inlet_values])
    return jnp.where(wall_mask[None] > 0, bounce, jnp.where(inlet_mask[None] > 0, inlet_feq, post))


def pick(padded, sign):
    depth, rows, cols = (padded.shape[1] - 2, padded.shape[2] - 2, padded.shape[3] - 2)
    outputs = []
    for i in range(19):
        start_z = 1 - sign * int(velocities[i][0])
        start_y = 1 - sign * int(velocities[i][1])
        start_x = 1 - sign * int(velocities[i][2])
        outputs.append(
            padded[i, start_z : start_z + depth, start_y : start_y + rows, start_x : start_x + cols]
        )
    return jnp.stack(outputs)


def shift_all(popul, sign):
    padded = extended(popul, (("grp", 1), ("gy", 2), ("gx", 3)), 1)
    return pick(padded, sign)


def smooth_field(field):
    padded = extended(field, (("grp", 0), ("gy", 1), ("gx", 2)), 1)
    along_z = 0.25 * padded[:-2] + 0.5 * padded[1:-1] + 0.25 * padded[2:]
    along_y = 0.25 * along_z[:, :-2] + 0.5 * along_z[:, 1:-1] + 0.25 * along_z[:, 2:]
    return 0.25 * along_y[:, :, :-2] + 0.5 * along_y[:, :, 1:-1] + 0.25 * along_y[:, :, 2:]


def project(filtered, thresh, beta):
    denom = jnp.tanh(beta * thresh) + jnp.tanh(beta * (1.0 - thresh))
    return (jnp.tanh(beta * thresh) + jnp.tanh(beta * (filtered - thresh))) / denom


def threshold_kernel(cells, beta_ref, filtered_ref, eta_ref, raised_ref):
    beta = jnp.full((8, 128), beta_ref[0], jnp.float32)
    raised_ref[...] = jnp.exp(2.0 * beta_ref[0] * filtered_ref[...])
    top = jnp.exp(2.0 * beta)
    rows = filtered_ref.shape[0]
    span = min(rows, 512)

    def halve(step, ends):
        low, high = ends
        middle = 0.5 * (low + high)
        level = jnp.exp(2.0 * beta * middle)

        def part(index, total):
            for row in range(0, span, 8):
                raised = raised_ref[pl.ds(pl.multiple_of(index * span + row, 8), 8), :]
                total = total + (raised - 1.0) / (raised + level)
            return total

        total = lax.fori_loop(0, rows // span, part, jnp.zeros((8, 128), jnp.float32))
        volume = jnp.sum(jnp.sum(total, axis=0, keepdims=True), axis=1, keepdims=True)
        above = volume * ((top + level) / (top - 1.0)) > fluid_share * cells
        return jnp.where(above, middle, low), jnp.where(above, high, middle)

    low, high = lax.fori_loop(
        0, BISECT, halve, (jnp.zeros((8, 128), jnp.float32), jnp.ones((8, 128), jnp.float32))
    )
    eta_ref[...] = 0.5 * (low + high)


def threshold(filtered, beta, cells):
    eta = pl.pallas_call(
        functools.partial(threshold_kernel, cells),
        out_shape=jax.ShapeDtypeStruct((8, 128), jnp.float32),
        in_specs=[
            pl.BlockSpec(memory_space=pltpu.SMEM),
            pl.BlockSpec(memory_space=pltpu.VMEM),
        ],
        out_specs=pl.BlockSpec(memory_space=pltpu.VMEM),
        scratch_shapes=[pltpu.VMEM(filtered.shape, jnp.float32)],
        compiler_params=pltpu.CompilerParams(vmem_limit_bytes=40 * 2**20),
        name="threshold",
    )(beta.reshape(1), filtered)
    return eta[0, 0]


def body_by_blocks(design, populations, cotangent, wall_mask, inlet_mask, beta_step):
    beta = jnp.exp2(beta_step.astype(jnp.float32) / 16.0)
    filtered = smooth_field(design)
    cells = design.size * lax.axis_size("grp") * lax.axis_size("gy") * lax.axis_size("gx")
    devices = lax.axis_size("grp") * lax.axis_size("gy") * lax.axis_size("gx")
    copies = jnp.broadcast_to(filtered, (devices, *filtered.shape))
    everywhere = lax.all_to_all(copies, ("grp", "gy", "gx"), 0, 0)
    eta = threshold(everywhere.reshape(-1, filtered.shape[-1]), beta, cells)
    density_hat = project(filtered, eta, beta)
    alpha = alpha_most * penalty_shape * (1.0 - density_hat) / (penalty_shape + density_hat)
    states = []
    popul = populations
    for step in range(STEPS):
        states.append(popul)
        popul = shift_all(collide(popul, alpha, wall_mask, inlet_mask), 1)
    adjoint = cotangent
    alpha_grad = jnp.zeros_like(alpha)
    for step in reversed(range(STEPS)):
        back = shift_all(adjoint, -1)
        unused, pullback = jax.vjp(
            lambda p, a: collide(p, a, wall_mask, inlet_mask), states[step], alpha
        )
        adjoint, term = pullback(back)
        alpha_grad = alpha_grad + term
    denom = jnp.tanh(beta * eta) + jnp.tanh(beta * (1.0 - eta))
    slope = beta * (1.0 - jnp.tanh(beta * (filtered - eta)) ** 2) / denom
    factor = (
        -alpha_most * penalty_shape * (1.0 + penalty_shape) / (penalty_shape + density_hat) ** 2
    )
    design_grad = smooth_field(alpha_grad * factor * slope)
    return (popul, design_grad)


LANES = 128
AROUND = ((1, 0), (-1, 0), (0, 1), (0, -1), (1, 1), (-1, -1), (1, -1), (-1, 1))
FIELDS = 40
NEAR = STEPS + 1
OUTER = 8 * 21 + NEAR * 19
CLOSE = 2.0**-14


def rolled(value, amount):
    amount = amount % LANES
    return value if amount == 0 else pltpu.roll(value, amount, 1)


def lane_index():
    return lax.broadcasted_iota(jnp.int32, (8, LANES), 1)


def on_path(index, grp, splits):
    part, step = index // grp, index % grp
    return (step if part % 2 == 0 else grp - 1 - step) * splits + part


def device_at(index, grp, splits):
    odd = lax.rem(lax.axis_index("gx"), 2)
    return jnp.where(odd == 0, on_path(index, grp, splits), on_path(grp * splits - 1 - index, grp, splits))


def block_here(grp, splits):
    step, part = lax.axis_index("grp"), lax.axis_index("gy")
    index = part * grp + jnp.where(lax.rem(part, 2) == 0, step, grp - 1 - step)
    return jnp.where(lax.rem(lax.axis_index("gx"), 2) == 0, index, grp * splits - 1 - index)


def mixed(values):
    place = lane_index() // 16
    for half in (4, 2, 1):
        upper = (place & half) != 0
        values = [jnp.where(upper, values[(index + half) % 8], values[index]) for index in range(8)]
    return values


def pack_kernel(
    splits, design_ref, populations_ref, cotangent_ref, wall_ref, inlet_ref, design_out_ref, packed_ref,
    fields_ref, masks_ref, sems,
):
    moves = [
        pltpu.make_async_copy(populations_ref, fields_ref.at[0:19], sems.at[0]),
        pltpu.make_async_copy(cotangent_ref, fields_ref.at[19:38], sems.at[1]),
        pltpu.make_async_copy(wall_ref, masks_ref.at[0], sems.at[2]),
        pltpu.make_async_copy(inlet_ref, masks_ref.at[1], sems.at[3]),
        pltpu.make_async_copy(design_ref, design_out_ref, sems.at[4]),
    ]
    for move in moves:
        move.start()
    for move in moves:
        move.wait()
    devices = [device_at(index, 8 // splits, splits) for index in range(8)]
    for layer in range(masks_ref.shape[1]):
        for group in range(FIELDS // 8):
            values = []
            for slot in range(8):
                index = group * 8 + slot
                if index in (19, 20):
                    value = masks_ref[index - 19, layer].astype(jnp.float32)
                else:
                    value = fields_ref[index if index < 19 else index - 2, layer]
                values.append(rolled(value, 16 * slot))
            values = mixed(values)
            for index in range(8):
                packed_ref[devices[index], group, layer] = values[-index % 8]


def arrange_kernel(splits, packed_ref, body_ref, near_ref, far_ref):
    layers = packed_ref.shape[2]
    planes = packed_ref.shape[0] // splits * layers
    me = block_here(packed_ref.shape[0] // splits, splits)
    for group in range(FIELDS // 8):
        plane = gather_plane(
            lambda z, part: packed_ref[(z // layers) * splits + part, group, z % layers], planes, splits
        ).T
        for slot in range(8):
            index = group * 8 + lax.rem(slot + 8 - me, 8)
            body_ref[index] = plane[16 * slot : 16 * slot + 16, :]
    even = lax.rem(me, 2) == 0

    def send(start, first, last):
        near_ref[start : start + first.shape[0], :] = jnp.where(even, last, first)
        far_ref[start : start + first.shape[0], :] = jnp.where(even, first, last)

    for index in range(FIELDS):
        if index < 21:
            send(8 * index, body_ref[index, 0:8, :], body_ref[index, 8:16, :])
        else:
            start = 8 * 21 + NEAR * (index - 21)
            send(start, body_ref[index, 0:NEAR, :], body_ref[index, 16 - NEAR : 16, :])
    for ref in (near_ref, far_ref):
        ref[OUTER:, :] = jnp.zeros((ref.shape[0] - OUTER, LANES), jnp.float32)


def turns_of(size):
    return sorted(range(size), key=lambda turn: (turn != 0, turn != size // 2, turn))


def spread_kernel(size, *refs):
    design_refs, (copies_ref, design_ref) = refs[:size], refs[size:]
    here = lax.axis_index("gx")
    for turn, ref in zip(turns_of(size), design_refs):
        design_ref[here ^ turn] = ref[...]
    lanes = lane_index()
    zero = jnp.zeros((8, LANES), jnp.float32)
    for layer in range(copies_ref.shape[2]):
        tiles = [zero] + [design_ref[index, layer] for index in range(size)] + [zero]
        ahead = [rolled(tile, 1) for tile in tiles]
        behind = [rolled(tile, -1) for tile in tiles]
        for index in range(1, size + 1):
            value = 0.5 * tiles[index] + 0.25 * (
                jnp.where(lanes == 0, ahead[index - 1], ahead[index])
                + jnp.where(lanes == LANES - 1, behind[index + 1], behind[index])
            )
            for device in range(copies_ref.shape[0]):
                copies_ref[device, index - 1, layer] = value


def exponent(step_ref):
    steps = jnp.full((8, LANES), step_ref[0], jnp.int32).astype(jnp.float32)
    return jnp.exp2(steps / 16.0)


def plane_masks(rows):
    lanes = lane_index()
    depth, place_z, place_y = LANES // rows, lanes // rows, lanes % rows
    masks = {}
    for cz, cy in AROUND:
        inside = None
        for shift, place, count in ((cz, place_z, depth), (cy, place_y, rows)):
            if shift:
                here = (place >= 1) if shift > 0 else (place < count - 1)
                inside = here if inside is None else inside & here
        masks[cz, cy] = inside
    return masks


def plane_shift(value, cz, cy, rows, masks):
    if cz == 0 and cy == 0:
        return value
    return jnp.where(masks[cz, cy], rolled(value, cz * rows + cy), 0.0)


def plane_smooth(value, rows, masks):
    for cz, cy in ((1, 0), (0, 1)):
        value = 0.5 * value + 0.25 * (
            plane_shift(value, cz, cy, rows, masks) + plane_shift(value, -cz, -cy, rows, masks)
        )
    return value


def gather_plane(read, planes, splits):
    blocks = []
    for z in range(planes):
        for part in range(splits):
            blocks.append(read(z, part))
    return jnp.concatenate(blocks, axis=0)


def volume_root(raised_ref, columns, beta):
    zero = jnp.zeros((8, LANES), jnp.float32)
    one = jnp.ones((8, LANES), jnp.float32)
    cells = columns * LANES
    top = jnp.exp(2.0 * beta)
    scale = 1.0 / (top - 1.0)

    def total(parts):
        value = (parts[0] + parts[1]) + (parts[2] + parts[3])
        return jnp.sum(jnp.sum(value, axis=0, keepdims=True), axis=1, keepdims=True)

    def advance(state):
        low, high, low_known, high_known, middle, _ = state
        level = jnp.exp(2.0 * beta * middle)
        sums, slopes = [zero] * 4, [zero] * 4
        for index, row in enumerate(range(0, columns, 8)):
            raised = raised_ref[row : row + 8, :]
            below = raised + level
            part = pl.reciprocal(below, approx=True)
            part = part * (2.0 - below * part)
            share = (raised - 1.0) * part
            sums[index % 4] = sums[index % 4] + share
            slopes[index % 4] = slopes[index % 4] + share * part
        volume, slope = total(sums), total(slopes)
        whole = (top + level) * scale
        excess = volume * whole - fluid_share * cells
        slope = (2.0 * beta * level) * (volume * scale - whole * slope)
        above = excess > 0.0
        low, low_known = jnp.where(above, middle, low), jnp.where(above, 1.0, low_known)
        high, high_known = jnp.where(above, high, middle), jnp.where(above, high_known, 1.0)
        guess = middle - excess / slope
        taken = (guess >= low) & (guess <= high)
        other = jnp.where(
            (guess > high) & (high_known == 0.0),
            high,
            jnp.where((guess < low) & (low_known == 0.0), low, 0.5 * (low + high)),
        )
        change = jnp.where(taken, jnp.abs(guess - middle), 2.0**16 * (high - low))
        return low, high, low_known, high_known, jnp.where(taken, guess, other), change

    def going(carry):
        step, state = carry
        return (step < 64) & (jnp.max(state[5]) > CLOSE)

    state = advance(advance((zero, one, zero, zero, 0.5 * one, zero)))
    _, state = lax.while_loop(going, lambda carry: (carry[0] + 1, advance(carry[1])), (2, state))
    return jnp.clip(state[4], 0.5**31, 1.0)


def level_kernel(rows, splits, size, step_ref, copies_ref, share_ref, filtered_ref, raised_ref):
    layers = copies_ref.shape[2]
    planes = LANES // rows
    columns = size * LANES
    masks = plane_masks(rows)
    zero = jnp.zeros((8, LANES), jnp.float32)
    beta = exponent(step_ref)
    filtered_ref[0:8, :] = zero
    filtered_ref[columns + 8 : columns + 16, :] = zero
    for block in range(size):
        plane = gather_plane(
            lambda z, part: copies_ref[(z // layers) * splits + part, block, z % layers], planes, splits
        )
        filtered_ref[8 + block * LANES : 8 + (block + 1) * LANES, :] = plane.T
    for row in range(8, columns + 8, 8):
        value = plane_smooth(filtered_ref[row : row + 8, :], rows, masks)
        filtered_ref[row : row + 8, :] = value
        raised_ref[row - 8 : row, :] = jnp.exp(2.0 * beta * value)
    eta = volume_root(raised_ref, columns, beta)
    place = lax.axis_index("gx") * copies_ref.shape[0] + block_here(copies_ref.shape[0] // splits, splits)
    level = jnp.exp(2.0 * beta * eta)
    top = jnp.exp(2.0 * beta)
    whole = (top + level) / (top - 1.0)
    strength = alpha_most * penalty_shape
    for block in range(4):
        at = slice(8 * block, 8 * block + 8)
        start = pl.multiple_of(place * 16 + 8 * block, 8)
        raised = jnp.exp(2.0 * beta * filtered_ref[pl.ds(start, 8), :])
        part = 1.0 / (raised + level)
        density_hat = ((raised - 1.0) * part) * whole
        share_ref[0, at, :] = (penalty_shape + density_hat) / (
            penalty_shape + strength + (1.0 - strength) * density_hat
        )
        slope = 2.0 * beta * (raised * part) * ((level + 1.0) * part) * whole
        factor = -strength * (1.0 + penalty_shape) / (
            (penalty_shape + density_hat) * (penalty_shape + density_hat)
        )
        share_ref[1, at, :] = slope * factor


def flow(rho, speed):
    square = 1.0 - 1.5 * (speed[0] * speed[0] + speed[1] * speed[1] + speed[2] * speed[2])
    comps = [lattice_weights[0] * rho * square]
    weighted = {1.0 / 18.0: rho * (1.0 / 18.0), 1.0 / 36.0: rho * (1.0 / 36.0)}
    for i in range(1, 19, 2):
        along = along_of(speed, i)
        weight = weighted[lattice_weights[i]]
        even = weight * (square + 4.5 * along * along)
        odd = weight * (3.0 * along)
        comps += [even + odd, even - odd]
    return comps


def along_of(speed, i):
    total = None
    for axis in range(3):
        sign = int(velocities[i][axis])
        if sign:
            if total is None:
                total = speed[axis] if sign > 0 else -speed[axis]
            else:
                total = total + speed[axis] if sign > 0 else total - speed[axis]
    return total


def add_along(totals, value, i):
    for axis in range(3):
        sign = int(velocities[i][axis])
        if sign:
            if totals[axis] is None:
                totals[axis] = value if sign > 0 else -value
            else:
                totals[axis] = totals[axis] + value if sign > 0 else totals[axis] - value


def inlet_value(i):
    along = float(velocities[i][0]) * inlet_speed
    return lattice_weights[i] * (1.0 + 3.0 * along + 4.5 * along * along - 1.5 * inlet_speed * inlet_speed)


def flow_kernel(
    rows, splits, size, share_ref, body_ref, near_ref, far_ref, packed_ref,
    cotangent_ref, even_ref, odd_ref, kept_ref, grad_ref, smooth_ref, output_ref,
):
    devices = packed_ref.shape[0]
    planes = LANES // rows
    layers = planes * splits // devices
    masks = plane_masks(rows)
    zero = jnp.zeros((8, LANES), jnp.float32)
    me = block_here(devices // splits, splits)
    place = lax.axis_index("gx") * devices + me
    last = size * devices - 1

    def inside(value, block):
        if block == 0:
            return jnp.where(place > 0, value, 0.0)
        if block == 3:
            return jnp.where(place < last, value, 0.0)
        return value

    even = lax.rem(me, 2) == 0

    def outer(start, count):
        near, far = near_ref[start : start + count, :], far_ref[start : start + count, :]
        return jnp.where(even, far, near), jnp.where(even, near, far)

    def initial(i, row):
        if row == 0:
            return outer(8 * i, 8)[0]
        if row == 24:
            return outer(8 * i, 8)[1]
        return body_ref[i, row - 8 : row, :]

    for ref in (even_ref, odd_ref, cotangent_ref):
        for i in range(19):
            ref[i, 0:8, :] = zero
            ref[i, 40:48, :] = zero
    for i in range(19):
        start = 8 * 21 + NEAR * i
        cotangent_ref[i, 8:16, :] = zero
        cotangent_ref[i, 16 - NEAR : 16, :] = outer(start, NEAR)[0]
        cotangent_ref[i, 16:32, :] = body_ref[21 + i]
        cotangent_ref[i, 32:40, :] = zero
        cotangent_ref[i, 32 : 32 + NEAR, :] = outer(start, NEAR)[1]

    def arrived(ref, i, row):
        cz, cy, cx = (int(c) for c in velocities[i])
        return plane_shift(ref[i, row + 8 - cx : row + 16 - cx, :], cz, cy, rows, masks)

    buffers = (even_ref, odd_ref)
    for step in range(STEPS):
        source, target = buffers[(step + 1) % 2], buffers[step % 2]
        for block in range(4):
            row = 8 * block
            at = slice(row, row + 8)
            if step == 0:
                popul = [initial(i, row) for i in range(19)]
            else:
                popul = [arrived(source, i, row) for i in range(19)]
            wall = initial(19, row) > 0.0
            inlet = initial(20, row) > 0.0
            rho = popul[0]
            momentum = [None, None, None]
            for i in range(1, 19, 2):
                rho = rho + (popul[i] + popul[i + 1])
                add_along(momentum, popul[i] - popul[i + 1], i)
            scale = share_ref[0, at, :] / rho
            speed = [value * scale for value in momentum]
            kept_ref[step, 0, at, :] = rho
            for axis in range(3):
                kept_ref[step, 1 + axis, at, :] = speed[axis]
            settled = flow(relax_rate * rho, speed)
            for i in range(19):
                post = (1.0 - relax_rate) * popul[i] + settled[i]
                post = jnp.where(wall, popul[opposite[i]], jnp.where(inlet, inlet_value(i), post))
                target[i, row + 8 : row + 16, :] = inside(post, block)
    def put(index, row, value):
        group, slot = divmod(index, 8)
        for slot in (slot,) if group < 2 else (slot, slot + 4):
            start = group * LANES + 16 * lax.rem(slot + me, 8) + row
            output_ref[pl.ds(pl.multiple_of(start, 8), 8), :] = value

    source = buffers[(STEPS - 1) % 2]
    for i in range(19):
        for row in (8, 16):
            put(i, row - 8, arrived(source, i, row))

    for step in reversed(range(STEPS)):
        source = cotangent_ref if step == STEPS - 1 else buffers[step % 2]
        target = buffers[(step + 1) % 2]
        for block in range(4):
            row = 8 * block
            at = slice(row, row + 8)
            back = []
            for i in range(19):
                cz, cy, cx = (int(c) for c in velocities[i])
                value = source[i, row + 8 + cx : row + 16 + cx, :]
                back.append(plane_shift(value, -cz, -cy, rows, masks))
            wall = initial(19, row) > 0.0
            inlet = initial(20, row) > 0.0
            rho = kept_ref[step, 0, at, :]
            speed = [kept_ref[step, 1 + axis, at, :] for axis in range(3)]
            square = speed[0] * speed[0] + speed[1] * speed[1] + speed[2] * speed[2]
            share = share_ref[0, at, :]
            faces, edges = None, None
            first, second = [None, None, None], [None, None, None]
            for i in range(1, 19, 2):
                both, apart = back[i] + back[i + 1], back[i] - back[i + 1]
                if i < 7:
                    faces = both if faces is None else faces + both
                    both, apart = 2.0 * both, 2.0 * apart
                else:
                    edges = both if edges is None else edges + both
                add_along(first, apart, i)
                add_along(second, along_of(speed, i) * both, i)
            mean = lattice_weights[0] * back[0] + (1.0 / 18.0) * faces + (1.0 / 36.0) * edges
            first = [value * (3.0 / 36.0) for value in first]
            second = [value * (9.0 / 36.0) for value in second]
            twice = speed[0] * second[0] + speed[1] * second[1] + speed[2] * second[2]
            once = speed[0] * first[0] + speed[1] * first[1] + speed[2] * first[2]
            drag = once + twice - 3.0 * square * mean
            term = jnp.where(wall | inlet, 0.0, -relax_rate * (rho * share * drag))
            grad_ref[at, :] = term if step == STEPS - 1 else grad_ref[at, :] + term
            if step == 0:
                continue
            rest = relax_rate * (mean * (1.0 + 1.5 * square) - 0.5 * twice)
            push = [
                (relax_rate * share) * (first[axis] + second[axis] - 3.0 * mean * speed[axis]) for axis in range(3)
            ]
            for i in range(19):
                if i == 0:
                    post = (1.0 - relax_rate) * back[0] + rest
                else:
                    way = along_of(push, i if i % 2 else i - 1)
                    post = (1.0 - relax_rate) * back[i] + (rest + way if i % 2 else rest - way)
                post = jnp.where(wall, back[opposite[i]], jnp.where(inlet, 0.0, post))
                target[i, row + 8 : row + 16, :] = inside(post, block)

    smooth_ref[0:8, :] = zero
    smooth_ref[40:48, :] = zero
    for block in range(4):
        at = slice(8 * block, 8 * block + 8)
        value = inside(grad_ref[at, :] * share_ref[1, at, :], block)
        smooth_ref[8 * block + 8 : 8 * block + 16, :] = plane_smooth(value, rows, masks)
    for row in (8, 16):
        value = 0.5 * smooth_ref[row + 8 : row + 16, :] + 0.25 * (
            smooth_ref[row + 7 : row + 15, :] + smooth_ref[row + 9 : row + 17, :]
        )
        put(19, row - 8, value)
    second = lax.rem(lane_index() // 16 + 8 - me, 8) >= 4
    for group in range(3):
        plane = output_ref[group * LANES : (group + 1) * LANES, :].T
        for device in range(devices):
            tiles = []
            for layer in range(layers):
                at = (((device // splits) * layers + layer) * splits + device % splits) * 8
                tiles.append(plane[at : at + 8, :])
            if group < 2:
                for layer in range(layers):
                    packed_ref[device, group * layers + layer] = tiles[layer]
            else:
                packed_ref[device, group * layers] = jnp.where(second, tiles[1], tiles[0])


def result_kernel(splits, packed_ref, populations_ref, grad_ref):
    devices = [device_at(index, 8 // splits, splits) for index in range(8)]
    for tile in range(packed_ref.shape[1]):
        values = mixed([packed_ref[device, tile] for device in devices])
        for slot in range(8):
            value = rolled(values[-slot % 8], -16 * slot)
            if tile < 4:
                populations_ref[tile // 2 * 8 + slot, tile % 2] = value
            elif slot % 4 < 3:
                populations_ref[16 + slot % 4, slot // 4] = value
            else:
                grad_ref[slot // 4] = value


def call(kernel, outs, name, operands, spaces, scratch=(), room=32):
    vmem = pl.BlockSpec(memory_space=pltpu.VMEM)
    shapes = tuple(jax.ShapeDtypeStruct(shape, jnp.float32) for shape in outs)
    many = len(outs) > 1
    return pl.pallas_call(
        kernel,
        out_shape=shapes if many else shapes[0],
        in_specs=[pl.BlockSpec(memory_space=space) for space in spaces],
        out_specs=(vmem,) * len(outs) if many else vmem,
        scratch_shapes=list(scratch),
        compiler_params=pltpu.CompilerParams(vmem_limit_bytes=room * 2**20),
        name=name,
    )(*operands)


def body_by_columns(design, populations, cotangent, wall_mask, inlet_mask, beta_step):
    grp, splits, size = (lax.axis_size(axis) for axis in ("grp", "gy", "gx"))
    layers, height, width = design.shape
    rows, plane = height * splits, grp * splits
    tile = (layers, 8, LANES)
    vmem, real = pltpu.VMEM, jnp.float32
    design, packed = call(
        functools.partial(pack_kernel, splits),
        (tile, (plane, FIELDS // 8, *tile)),
        "pack",
        (design, populations, cotangent, wall_mask, inlet_mask),
        [pl.ANY] * 5,
        [vmem((38, *tile), real), vmem((2, *tile), jnp.int32), pltpu.SemaphoreType.DMA((5,))],
        60,
    )
    packed = lax.all_to_all(packed, ("grp", "gy"), 0, 0)
    designs = [design] * size
    for turn in reversed(range(1, size)):
        designs[turn] = lax.ppermute(design, "gx", [(i, i ^ turn) for i in range(size)])
    copies = call(
        functools.partial(spread_kernel, size),
        ((plane, size, *tile),),
        "spread",
        [designs[turn] for turn in turns_of(size)],
        [vmem] * size,
        [vmem((size, *tile), real)],
    )
    outer = (-(-OUTER // 8) * 8, LANES)
    body, near, far = call(
        functools.partial(arrange_kernel, splits),
        ((FIELDS, 16, LANES), outer, outer),
        "arrange",
        (packed,),
        [vmem],
    )
    copies = lax.all_to_all(copies, ("grp", "gy"), 0, 0)
    path = [on_path(index, grp, splits) for index in range(plane)]
    order = [(path if gx % 2 == 0 else path[::-1])[index] * size + gx for gx in range(size) for index in range(plane)]
    line = ("grp", "gy", "gx")

    def exchange(value, start):
        pairs = [order[b : b + 2] for b in range(start, size * plane - 1, 2)]
        return lax.ppermute(value, line, [pair for i, j in pairs for pair in ((i, j), (j, i))])

    far, near = exchange(far, 1), exchange(near, 0)
    columns = size * LANES
    share = call(
        functools.partial(level_kernel, rows, splits, size),
        ((2, 32, LANES),),
        "level",
        (beta_step.reshape(1), copies),
        [pltpu.SMEM, vmem],
        [vmem((columns + 16, LANES), real), vmem((columns, LANES), real)],
    )
    shapes = [
        (19, 48, LANES),
        (19, 48, LANES),
        (19, 48, LANES),
        (STEPS, 4, 32, LANES),
        (32, LANES),
        (48, LANES),
        (3 * LANES, LANES),
    ]
    packed = call(
        functools.partial(flow_kernel, rows, splits, size),
        ((plane, 5, 8, LANES),),
        "flow",
        (share, body, near, far),
        [vmem] * 4,
        [vmem(shape, real) for shape in shapes],
    )
    packed = lax.all_to_all(packed, ("grp", "gy"), 0, 0)
    return call(functools.partial(result_kernel, splits), (populations.shape, design.shape), "result", (packed,), [vmem])


def body(design, populations, cotangent, wall_mask, inlet_mask, beta_step):
    grp, splits = lax.axis_size("grp"), lax.axis_size("gy")
    layers, height, width = design.shape
    fits = height == 8 and width == LANES and layers * grp * height * splits == LANES
    size = lax.axis_size("gx")
    fits = fits and grp * splits * 16 == LANES and size & (size - 1) == 0
    whole = body_by_columns if fits else body_by_blocks
    return whole(design, populations, cotangent, wall_mask, inlet_mask, beta_step)


def solution(mesh):
    placed = (
        P("grp", "gy", "gx"),
        P(None, "grp", "gy", "gx"),
        P(None, "grp", "gy", "gx"),
        P("grp", "gy", "gx"),
        P("grp", "gy", "gx"),
        P(),
    )
    return jax.shard_map(
        body,
        mesh=mesh,
        in_specs=placed,
        out_specs=(P(None, "grp", "gy", "gx"), P("grp", "gy", "gx")),
        check_vma=False,
    )
```

```python
import functools

import jax
import jax.numpy as jnp
import numpy as np
from jax import lax
from jax.experimental import pallas as pl
from jax.experimental.pallas import tpu as pltpu
from jax.sharding import PartitionSpec as P

STEPS = 4
BISECT = 30


velocities = np.array(
    [
        [0, 0, 0],
        [1, 0, 0],
        [-1, 0, 0],
        [0, 1, 0],
        [0, -1, 0],
        [0, 0, 1],
        [0, 0, -1],
        [1, 1, 0],
        [-1, -1, 0],
        [1, -1, 0],
        [-1, 1, 0],
        [1, 0, 1],
        [-1, 0, -1],
        [1, 0, -1],
        [-1, 0, 1],
        [0, 1, 1],
        [0, -1, -1],
        [0, 1, -1],
        [0, -1, 1],
    ]
)
opposite = [0, 2, 1, 4, 3, 6, 5, 8, 7, 10, 9, 12, 11, 14, 13, 16, 15, 18, 17]
lattice_weights = [1.0 / 3.0] + [1.0 / 18.0] * 6 + [1.0 / 36.0] * 12
relax_rate = 0.8
inlet_speed = 0.05
alpha_most = 8.0
penalty_shape = 0.1
fluid_share = 0.4


def extended(value, sides, width):
    for axis, dim in sides:
        size, length = (lax.axis_size(axis), value.shape[dim])
        up = [(i, (i + 1) % size) for i in range(size - 1)]
        down = [(j, i) for i, j in up]
        last = lax.slice_in_dim(value, length - width, length, axis=dim)
        leading = lax.slice_in_dim(value, 0, width, axis=dim)
        before = lax.ppermute(last, axis, up)
        after = lax.ppermute(leading, axis, down)
        value = jnp.concatenate([before, value, after], axis=dim)
    return value


def equilibrium(density, speed_z, speed_y, speed_x):
    square = speed_z * speed_z + speed_y * speed_y + speed_x * speed_x
    comps = []
    for i in range(19):
        along = (
            float(velocities[i][0]) * speed_z
            + float(velocities[i][1]) * speed_y
            + float(velocities[i][2]) * speed_x
        )
        comps.append(
            lattice_weights[i] * density * (1.0 + 3.0 * along + 4.5 * along * along - 1.5 * square)
        )
    return jnp.stack(comps)


def moment(popul, axis):
    total = jnp.zeros(popul.shape[1:], popul.dtype)
    for i in range(1, 19):
        if velocities[i][axis] != 0:
            total = total + float(velocities[i][axis]) * popul[i]
    return total


def collide(popul, alpha, wall_mask, inlet_mask):
    density = jnp.sum(popul, axis=0)
    scale = density * (1.0 + alpha)
    feq = equilibrium(
        density, moment(popul, 0) / scale, moment(popul, 1) / scale, moment(popul, 2) / scale
    )
    post = popul + relax_rate * (feq - popul)
    bounce = jnp.stack([popul[opposite[i]] for i in range(19)])
    inlet_values = []
    for i in range(19):
        along = float(velocities[i][0]) * inlet_speed
        inlet_values.append(
            lattice_weights[i]
            * (1.0 + 3.0 * along + 4.5 * along * along - 1.5 * inlet_speed * inlet_speed)
        )
    inlet_feq = jnp.stack([jnp.full(popul.shape[1:], value, popul.dtype) for value in inlet_values])
    return jnp.where(wall_mask[None] > 0, bounce, jnp.where(inlet_mask[None] > 0, inlet_feq, post))


def pick(padded, sign):
    depth, rows, cols = (padded.shape[1] - 2, padded.shape[2] - 2, padded.shape[3] - 2)
    outputs = []
    for i in range(19):
        start_z = 1 - sign * int(velocities[i][0])
        start_y = 1 - sign * int(velocities[i][1])
        start_x = 1 - sign * int(velocities[i][2])
        outputs.append(
            padded[i, start_z : start_z + depth, start_y : start_y + rows, start_x : start_x + cols]
        )
    return jnp.stack(outputs)


def shift_all(popul, sign):
    padded = extended(popul, (("grp", 1), ("gy", 2), ("gx", 3)), 1)
    return pick(padded, sign)


def smooth_field(field):
    padded = extended(field, (("grp", 0), ("gy", 1), ("gx", 2)), 1)
    along_z = 0.25 * padded[:-2] + 0.5 * padded[1:-1] + 0.25 * padded[2:]
    along_y = 0.25 * along_z[:, :-2] + 0.5 * along_z[:, 1:-1] + 0.25 * along_z[:, 2:]
    return 0.25 * along_y[:, :, :-2] + 0.5 * along_y[:, :, 1:-1] + 0.25 * along_y[:, :, 2:]


def project(filtered, thresh, beta):
    denom = jnp.tanh(beta * thresh) + jnp.tanh(beta * (1.0 - thresh))
    return (jnp.tanh(beta * thresh) + jnp.tanh(beta * (filtered - thresh))) / denom


def threshold_kernel(cells, beta_ref, filtered_ref, eta_ref, raised_ref):
    beta = jnp.full((8, 128), beta_ref[0], jnp.float32)
    raised_ref[...] = jnp.exp(2.0 * beta_ref[0] * filtered_ref[...])
    top = jnp.exp(2.0 * beta)
    rows = filtered_ref.shape[0]
    span = min(rows, 512)

    def halve(step, ends):
        low, high = ends
        middle = 0.5 * (low + high)
        level = jnp.exp(2.0 * beta * middle)

        def part(index, total):
            for row in range(0, span, 8):
                raised = raised_ref[pl.ds(pl.multiple_of(index * span + row, 8), 8), :]
                total = total + (raised - 1.0) / (raised + level)
            return total

        total = lax.fori_loop(0, rows // span, part, jnp.zeros((8, 128), jnp.float32))
        volume = jnp.sum(jnp.sum(total, axis=0, keepdims=True), axis=1, keepdims=True)
        above = volume * ((top + level) / (top - 1.0)) > fluid_share * cells
        return jnp.where(above, middle, low), jnp.where(above, high, middle)

    low, high = lax.fori_loop(
        0, BISECT, halve, (jnp.zeros((8, 128), jnp.float32), jnp.ones((8, 128), jnp.float32))
    )
    eta_ref[...] = 0.5 * (low + high)


def threshold(filtered, beta, cells):
    eta = pl.pallas_call(
        functools.partial(threshold_kernel, cells),
        out_shape=jax.ShapeDtypeStruct((8, 128), jnp.float32),
        in_specs=[
            pl.BlockSpec(memory_space=pltpu.SMEM),
            pl.BlockSpec(memory_space=pltpu.VMEM),
        ],
        out_specs=pl.BlockSpec(memory_space=pltpu.VMEM),
        scratch_shapes=[pltpu.VMEM(filtered.shape, jnp.float32)],
        compiler_params=pltpu.CompilerParams(vmem_limit_bytes=40 * 2**20),
        name="threshold",
    )(beta.reshape(1), filtered)
    return eta[0, 0]


def body_by_blocks(design, populations, cotangent, wall_mask, inlet_mask, beta_step):
    beta = jnp.exp2(beta_step.astype(jnp.float32) / 16.0)
    filtered = smooth_field(design)
    cells = design.size * lax.axis_size("grp") * lax.axis_size("gy") * lax.axis_size("gx")
    devices = lax.axis_size("grp") * lax.axis_size("gy") * lax.axis_size("gx")
    copies = jnp.broadcast_to(filtered, (devices, *filtered.shape))
    everywhere = lax.all_to_all(copies, ("grp", "gy", "gx"), 0, 0)
    eta = threshold(everywhere.reshape(-1, filtered.shape[-1]), beta, cells)
    density_hat = project(filtered, eta, beta)
    alpha = alpha_most * penalty_shape * (1.0 - density_hat) / (penalty_shape + density_hat)
    states = []
    popul = populations
    for step in range(STEPS):
        states.append(popul)
        popul = shift_all(collide(popul, alpha, wall_mask, inlet_mask), 1)
    adjoint = cotangent
    alpha_grad = jnp.zeros_like(alpha)
    for step in reversed(range(STEPS)):
        back = shift_all(adjoint, -1)
        unused, pullback = jax.vjp(
            lambda p, a: collide(p, a, wall_mask, inlet_mask), states[step], alpha
        )
        adjoint, term = pullback(back)
        alpha_grad = alpha_grad + term
    denom = jnp.tanh(beta * eta) + jnp.tanh(beta * (1.0 - eta))
    slope = beta * (1.0 - jnp.tanh(beta * (filtered - eta)) ** 2) / denom
    factor = (
        -alpha_most * penalty_shape * (1.0 + penalty_shape) / (penalty_shape + density_hat) ** 2
    )
    design_grad = smooth_field(alpha_grad * factor * slope)
    return (popul, design_grad)


LANES = 128
AROUND = ((1, 0), (-1, 0), (0, 1), (0, -1), (1, 1), (-1, -1), (1, -1), (-1, 1))
FIELDS = 40
NEAR = STEPS + 1
OUTER = 8 * 21 + NEAR * 19
CLOSE = 2.0**-14


def rolled(value, amount):
    amount = amount % LANES
    return value if amount == 0 else pltpu.roll(value, amount, 1)


def lane_index():
    return lax.broadcasted_iota(jnp.int32, (8, LANES), 1)


def on_path(index, grp, splits):
    part, step = index // grp, index % grp
    return (step if part % 2 == 0 else grp - 1 - step) * splits + part


def device_at(index, grp, splits):
    odd = lax.rem(lax.axis_index("gx"), 2)
    return jnp.where(odd == 0, on_path(index, grp, splits), on_path(grp * splits - 1 - index, grp, splits))


def block_here(grp, splits):
    step, part = lax.axis_index("grp"), lax.axis_index("gy")
    index = part * grp + jnp.where(lax.rem(part, 2) == 0, step, grp - 1 - step)
    return jnp.where(lax.rem(lax.axis_index("gx"), 2) == 0, index, grp * splits - 1 - index)


def mixed(values):
    place = lane_index() // 16
    for half in (4, 2, 1):
        upper = (place & half) != 0
        values = [jnp.where(upper, values[(index + half) % 8], values[index]) for index in range(8)]
    return values


def pack_kernel(
    splits, design_ref, populations_ref, cotangent_ref, wall_ref, inlet_ref, design_out_ref, packed_ref,
    fields_ref, masks_ref, sems,
):
    moves = [
        pltpu.make_async_copy(populations_ref, fields_ref.at[0:19], sems.at[0]),
        pltpu.make_async_copy(cotangent_ref, fields_ref.at[19:38], sems.at[1]),
        pltpu.make_async_copy(wall_ref, masks_ref.at[0], sems.at[2]),
        pltpu.make_async_copy(inlet_ref, masks_ref.at[1], sems.at[3]),
        pltpu.make_async_copy(design_ref, design_out_ref, sems.at[4]),
    ]
    for move in moves:
        move.start()
    for move in moves:
        move.wait()
    devices = [device_at(index, 8 // splits, splits) for index in range(8)]
    for layer in range(masks_ref.shape[1]):
        for group in range(FIELDS // 8):
            values = []
            for slot in range(8):
                index = group * 8 + slot
                if index in (19, 20):
                    value = masks_ref[index - 19, layer].astype(jnp.float32)
                else:
                    value = fields_ref[index if index < 19 else index - 2, layer]
                values.append(rolled(value, 16 * slot))
            values = mixed(values)
            for index in range(8):
                packed_ref[devices[index], group, layer] = values[-index % 8]


def arrange_kernel(splits, packed_ref, body_ref, near_ref, far_ref):
    layers = packed_ref.shape[2]
    planes = packed_ref.shape[0] // splits * layers
    me = block_here(packed_ref.shape[0] // splits, splits)
    for group in range(FIELDS // 8):
        plane = gather_plane(
            lambda z, part: packed_ref[(z // layers) * splits + part, group, z % layers], planes, splits
        ).T
        for slot in range(8):
            index = group * 8 + lax.rem(slot + 8 - me, 8)
            body_ref[index] = plane[16 * slot : 16 * slot + 16, :]
    even = lax.rem(me, 2) == 0

    def send(start, first, last):
        near_ref[start : start + first.shape[0], :] = jnp.where(even, last, first)
        far_ref[start : start + first.shape[0], :] = jnp.where(even, first, last)

    for index in range(FIELDS):
        if index < 21:
            send(8 * index, body_ref[index, 0:8, :], body_ref[index, 8:16, :])
        else:
            start = 8 * 21 + NEAR * (index - 21)
            send(start, body_ref[index, 0:NEAR, :], body_ref[index, 16 - NEAR : 16, :])
    for ref in (near_ref, far_ref):
        ref[OUTER:, :] = jnp.zeros((ref.shape[0] - OUTER, LANES), jnp.float32)


def turns_of(size):
    return sorted(range(size), key=lambda turn: (turn != 0, turn != size // 2, turn))


def spread_kernel(size, *refs):
    design_refs, (copies_ref, design_ref) = refs[:size], refs[size:]
    here = lax.axis_index("gx")
    for turn, ref in zip(turns_of(size), design_refs):
        design_ref[here ^ turn] = ref[...]
    lanes = lane_index()
    zero = jnp.zeros((8, LANES), jnp.float32)
    for layer in range(copies_ref.shape[2]):
        tiles = [zero] + [design_ref[index, layer] for index in range(size)] + [zero]
        ahead = [rolled(tile, 1) for tile in tiles]
        behind = [rolled(tile, -1) for tile in tiles]
        for index in range(1, size + 1):
            value = 0.5 * tiles[index] + 0.25 * (
                jnp.where(lanes == 0, ahead[index - 1], ahead[index])
                + jnp.where(lanes == LANES - 1, behind[index + 1], behind[index])
            )
            for device in range(copies_ref.shape[0]):
                copies_ref[device, index - 1, layer] = value


def exponent(step_ref):
    steps = jnp.full((8, LANES), step_ref[0], jnp.int32).astype(jnp.float32)
    return jnp.exp2(steps / 16.0)


def plane_masks(rows):
    lanes = lane_index()
    depth, place_z, place_y = LANES // rows, lanes // rows, lanes % rows
    masks = {}
    for cz, cy in AROUND:
        inside = None
        for shift, place, count in ((cz, place_z, depth), (cy, place_y, rows)):
            if shift:
                here = (place >= 1) if shift > 0 else (place < count - 1)
                inside = here if inside is None else inside & here
        masks[cz, cy] = inside
    return masks


def plane_shift(value, cz, cy, rows, masks):
    if cz == 0 and cy == 0:
        return value
    return jnp.where(masks[cz, cy], rolled(value, cz * rows + cy), 0.0)


def plane_smooth(value, rows, masks):
    for cz, cy in ((1, 0), (0, 1)):
        value = 0.5 * value + 0.25 * (
            plane_shift(value, cz, cy, rows, masks) + plane_shift(value, -cz, -cy, rows, masks)
        )
    return value


def gather_plane(read, planes, splits):
    blocks = []
    for z in range(planes):
        for part in range(splits):
            blocks.append(read(z, part))
    return jnp.concatenate(blocks, axis=0)


def volume_root(raised_ref, columns, beta):
    zero = jnp.zeros((8, LANES), jnp.float32)
    one = jnp.ones((8, LANES), jnp.float32)
    cells = columns * LANES
    top = jnp.exp(2.0 * beta)
    scale = 1.0 / (top - 1.0)

    def total(parts):
        value = (parts[0] + parts[1]) + (parts[2] + parts[3])
        return jnp.sum(jnp.sum(value, axis=0, keepdims=True), axis=1, keepdims=True)

    def advance(state):
        low, high, low_known, high_known, middle, _ = state
        level = jnp.exp(2.0 * beta * middle)
        sums, slopes = [zero] * 4, [zero] * 4
        for index, row in enumerate(range(0, columns, 8)):
            raised = raised_ref[row : row + 8, :]
            below = raised + level
            part = pl.reciprocal(below, approx=True)
            part = part * (2.0 - below * part)
            share = (raised - 1.0) * part
            sums[index % 4] = sums[index % 4] + share
            slopes[index % 4] = slopes[index % 4] + share * part
        volume, slope = total(sums), total(slopes)
        whole = (top + level) * scale
        excess = volume * whole - fluid_share * cells
        slope = (2.0 * beta * level) * (volume * scale - whole * slope)
        above = excess > 0.0
        low, low_known = jnp.where(above, middle, low), jnp.where(above, 1.0, low_known)
        high, high_known = jnp.where(above, high, middle), jnp.where(above, high_known, 1.0)
        guess = middle - excess / slope
        taken = (guess >= low) & (guess <= high)
        other = jnp.where(
            (guess > high) & (high_known == 0.0),
            high,
            jnp.where((guess < low) & (low_known == 0.0), low, 0.5 * (low + high)),
        )
        change = jnp.where(taken, jnp.abs(guess - middle), 2.0**16 * (high - low))
        return low, high, low_known, high_known, jnp.where(taken, guess, other), change

    def going(carry):
        step, state = carry
        return (step < 64) & (jnp.max(state[5]) > CLOSE)

    state = advance(advance((zero, one, zero, zero, 0.5 * one, zero)))
    _, state = lax.while_loop(going, lambda carry: (carry[0] + 1, advance(carry[1])), (2, state))
    return jnp.clip(state[4], 0.5**31, 1.0)


def level_kernel(rows, splits, size, step_ref, copies_ref, share_ref, filtered_ref, raised_ref):
    layers = copies_ref.shape[2]
    planes = LANES // rows
    columns = size * LANES
    masks = plane_masks(rows)
    zero = jnp.zeros((8, LANES), jnp.float32)
    beta = exponent(step_ref)
    filtered_ref[0:8, :] = zero
    filtered_ref[columns + 8 : columns + 16, :] = zero
    for block in range(size):
        plane = gather_plane(
            lambda z, part: copies_ref[(z // layers) * splits + part, block, z % layers], planes, splits
        )
        filtered_ref[8 + block * LANES : 8 + (block + 1) * LANES, :] = plane.T
    for row in range(8, columns + 8, 8):
        value = plane_smooth(filtered_ref[row : row + 8, :], rows, masks)
        filtered_ref[row : row + 8, :] = value
        raised_ref[row - 8 : row, :] = jnp.exp(2.0 * beta * value)
    eta = volume_root(raised_ref, columns, beta)
    place = lax.axis_index("gx") * copies_ref.shape[0] + block_here(copies_ref.shape[0] // splits, splits)
    level = jnp.exp(2.0 * beta * eta)
    top = jnp.exp(2.0 * beta)
    whole = (top + level) / (top - 1.0)
    strength = alpha_most * penalty_shape
    for block in range(4):
        at = slice(8 * block, 8 * block + 8)
        start = pl.multiple_of(place * 16 + 8 * block, 8)
        raised = jnp.exp(2.0 * beta * filtered_ref[pl.ds(start, 8), :])
        part = 1.0 / (raised + level)
        density_hat = ((raised - 1.0) * part) * whole
        share_ref[0, at, :] = (penalty_shape + density_hat) / (
            penalty_shape + strength + (1.0 - strength) * density_hat
        )
        slope = 2.0 * beta * (raised * part) * ((level + 1.0) * part) * whole
        factor = -strength * (1.0 + penalty_shape) / (
            (penalty_shape + density_hat) * (penalty_shape + density_hat)
        )
        share_ref[1, at, :] = slope * factor


def flow(rho, speed):
    square = 1.0 - 1.5 * (speed[0] * speed[0] + speed[1] * speed[1] + speed[2] * speed[2])
    comps = [lattice_weights[0] * rho * square]
    weighted = {1.0 / 18.0: rho * (1.0 / 18.0), 1.0 / 36.0: rho * (1.0 / 36.0)}
    for i in range(1, 19, 2):
        along = along_of(speed, i)
        weight = weighted[lattice_weights[i]]
        even = weight * (square + 4.5 * along * along)
        odd = weight * (3.0 * along)
        comps += [even + odd, even - odd]
    return comps


def along_of(speed, i):
    total = None
    for axis in range(3):
        sign = int(velocities[i][axis])
        if sign:
            if total is None:
                total = speed[axis] if sign > 0 else -speed[axis]
            else:
                total = total + speed[axis] if sign > 0 else total - speed[axis]
    return total


def add_along(totals, value, i):
    for axis in range(3):
        sign = int(velocities[i][axis])
        if sign:
            if totals[axis] is None:
                totals[axis] = value if sign > 0 else -value
            else:
                totals[axis] = totals[axis] + value if sign > 0 else totals[axis] - value


def inlet_value(i):
    along = float(velocities[i][0]) * inlet_speed
    return lattice_weights[i] * (1.0 + 3.0 * along + 4.5 * along * along - 1.5 * inlet_speed * inlet_speed)


def flow_kernel(
    rows, splits, size, share_ref, body_ref, far_ref, near_ref, packed_ref,
    cotangent_ref, even_ref, odd_ref, kept_ref, grad_ref, smooth_ref, output_ref,
):
    devices = packed_ref.shape[0]
    planes = LANES // rows
    layers = planes * splits // devices
    masks = plane_masks(rows)
    zero = jnp.zeros((8, LANES), jnp.float32)
    me = block_here(devices // splits, splits)
    place = lax.axis_index("gx") * devices + me
    last = size * devices - 1

    def inside(value, block):
        if block == 0:
            return jnp.where(place > 0, value, 0.0)
        if block == 3:
            return jnp.where(place < last, value, 0.0)
        return value

    even = lax.rem(me, 2) == 0

    def outer(start, count):
        near, far = near_ref[start : start + count, :], far_ref[start : start + count, :]
        return jnp.where(even, far, near), jnp.where(even, near, far)

    def initial(i, row):
        if row == 0:
            return outer(8 * i, 8)[0]
        if row == 24:
            return outer(8 * i, 8)[1]
        return body_ref[i, row - 8 : row, :]

    for ref in (even_ref, odd_ref, cotangent_ref):
        for i in range(19):
            ref[i, 0:8, :] = zero
            ref[i, 40:48, :] = zero
    for i in range(19):
        start = 8 * 21 + NEAR * i
        cotangent_ref[i, 8:16, :] = zero
        cotangent_ref[i, 16 - NEAR : 16, :] = outer(start, NEAR)[0]
        cotangent_ref[i, 16:32, :] = body_ref[21 + i]
        cotangent_ref[i, 32:40, :] = zero
        cotangent_ref[i, 32 : 32 + NEAR, :] = outer(start, NEAR)[1]

    def arrived(ref, i, row):
        cz, cy, cx = (int(c) for c in velocities[i])
        return plane_shift(ref[i, row + 8 - cx : row + 16 - cx, :], cz, cy, rows, masks)

    buffers = (even_ref, odd_ref)
    for step in range(STEPS):
        source, target = buffers[(step + 1) % 2], buffers[step % 2]
        for block in range(4):
            row = 8 * block
            at = slice(row, row + 8)
            if step == 0:
                popul = [initial(i, row) for i in range(19)]
            else:
                popul = [arrived(source, i, row) for i in range(19)]
            wall = initial(19, row) > 0.0
            inlet = initial(20, row) > 0.0
            rho = popul[0]
            momentum = [None, None, None]
            for i in range(1, 19, 2):
                rho = rho + (popul[i] + popul[i + 1])
                add_along(momentum, popul[i] - popul[i + 1], i)
            scale = share_ref[0, at, :] / rho
            speed = [value * scale for value in momentum]
            kept_ref[step, 0, at, :] = rho
            for axis in range(3):
                kept_ref[step, 1 + axis, at, :] = speed[axis]
            settled = flow(relax_rate * rho, speed)
            for i in range(19):
                post = (1.0 - relax_rate) * popul[i] + settled[i]
                post = jnp.where(wall, popul[opposite[i]], jnp.where(inlet, inlet_value(i), post))
                target[i, row + 8 : row + 16, :] = inside(post, block)
    def put(index, row, value):
        group, slot = divmod(index, 8)
        for slot in (slot,) if group < 2 else (slot, slot + 4):
            start = group * LANES + 16 * lax.rem(slot + me, 8) + row
            output_ref[pl.ds(pl.multiple_of(start, 8), 8), :] = value

    source = buffers[(STEPS - 1) % 2]
    for i in range(19):
        for row in (8, 16):
            put(i, row - 8, arrived(source, i, row))

    for step in reversed(range(STEPS)):
        source = cotangent_ref if step == STEPS - 1 else buffers[step % 2]
        target = buffers[(step + 1) % 2]
        for block in range(4):
            row = 8 * block
            at = slice(row, row + 8)
            back = []
            for i in range(19):
                cz, cy, cx = (int(c) for c in velocities[i])
                value = source[i, row + 8 + cx : row + 16 + cx, :]
                back.append(plane_shift(value, -cz, -cy, rows, masks))
            wall = initial(19, row) > 0.0
            inlet = initial(20, row) > 0.0
            rho = kept_ref[step, 0, at, :]
            speed = [kept_ref[step, 1 + axis, at, :] for axis in range(3)]
            square = speed[0] * speed[0] + speed[1] * speed[1] + speed[2] * speed[2]
            share = share_ref[0, at, :]
            faces, edges = None, None
            first, second = [None, None, None], [None, None, None]
            for i in range(1, 19, 2):
                both, apart = back[i] + back[i + 1], back[i] - back[i + 1]
                if i < 7:
                    faces = both if faces is None else faces + both
                    both, apart = 2.0 * both, 2.0 * apart
                else:
                    edges = both if edges is None else edges + both
                add_along(first, apart, i)
                add_along(second, along_of(speed, i) * both, i)
            mean = lattice_weights[0] * back[0] + (1.0 / 18.0) * faces + (1.0 / 36.0) * edges
            first = [value * (3.0 / 36.0) for value in first]
            second = [value * (9.0 / 36.0) for value in second]
            twice = speed[0] * second[0] + speed[1] * second[1] + speed[2] * second[2]
            once = speed[0] * first[0] + speed[1] * first[1] + speed[2] * first[2]
            drag = once + twice - 3.0 * square * mean
            term = jnp.where(wall | inlet, 0.0, -relax_rate * (rho * share * drag))
            grad_ref[at, :] = term if step == STEPS - 1 else grad_ref[at, :] + term
            if step == 0:
                continue
            rest = relax_rate * (mean * (1.0 + 1.5 * square) - 0.5 * twice)
            push = [
                (relax_rate * share) * (first[axis] + second[axis] - 3.0 * mean * speed[axis]) for axis in range(3)
            ]
            for i in range(19):
                if i == 0:
                    post = (1.0 - relax_rate) * back[0] + rest
                else:
                    way = along_of(push, i if i % 2 else i - 1)
                    post = (1.0 - relax_rate) * back[i] + (rest + way if i % 2 else rest - way)
                post = jnp.where(wall, back[opposite[i]], jnp.where(inlet, 0.0, post))
                target[i, row + 8 : row + 16, :] = inside(post, block)

    smooth_ref[0:8, :] = zero
    smooth_ref[40:48, :] = zero
    for block in range(4):
        at = slice(8 * block, 8 * block + 8)
        value = inside(grad_ref[at, :] * share_ref[1, at, :], block)
        smooth_ref[8 * block + 8 : 8 * block + 16, :] = plane_smooth(value, rows, masks)
    for row in (8, 16):
        value = 0.5 * smooth_ref[row + 8 : row + 16, :] + 0.25 * (
            smooth_ref[row + 7 : row + 15, :] + smooth_ref[row + 9 : row + 17, :]
        )
        put(19, row - 8, value)
    second = lax.rem(lane_index() // 16 + 8 - me, 8) >= 4
    for group in range(3):
        plane = output_ref[group * LANES : (group + 1) * LANES, :].T
        for device in range(devices):
            tiles = []
            for layer in range(layers):
                at = (((device // splits) * layers + layer) * splits + device % splits) * 8
                tiles.append(plane[at : at + 8, :])
            if group < 2:
                for layer in range(layers):
                    packed_ref[device, group * layers + layer] = tiles[layer]
            else:
                packed_ref[device, group * layers] = jnp.where(second, tiles[1], tiles[0])


def result_kernel(splits, packed_ref, populations_ref, grad_ref):
    devices = [device_at(index, 8 // splits, splits) for index in range(8)]
    for tile in range(packed_ref.shape[1]):
        values = mixed([packed_ref[device, tile] for device in devices])
        for slot in range(8):
            value = rolled(values[-slot % 8], -16 * slot)
            if tile < 4:
                populations_ref[tile // 2 * 8 + slot, tile % 2] = value
            elif slot % 4 < 3:
                populations_ref[16 + slot % 4, slot // 4] = value
            else:
                grad_ref[slot // 4] = value


def call(kernel, outs, name, operands, spaces, scratch=(), room=32):
    vmem = pl.BlockSpec(memory_space=pltpu.VMEM)
    shapes = tuple(jax.ShapeDtypeStruct(shape, jnp.float32) for shape in outs)
    many = len(outs) > 1
    return pl.pallas_call(
        kernel,
        out_shape=shapes if many else shapes[0],
        in_specs=[pl.BlockSpec(memory_space=space) for space in spaces],
        out_specs=(vmem,) * len(outs) if many else vmem,
        scratch_shapes=list(scratch),
        compiler_params=pltpu.CompilerParams(vmem_limit_bytes=room * 2**20),
        name=name,
    )(*operands)


def body_by_columns(design, populations, cotangent, wall_mask, inlet_mask, beta_step):
    grp, splits, size = (lax.axis_size(axis) for axis in ("grp", "gy", "gx"))
    layers, height, width = design.shape
    rows, plane = height * splits, grp * splits
    tile = (layers, 8, LANES)
    vmem, real = pltpu.VMEM, jnp.float32
    design, packed = call(
        functools.partial(pack_kernel, splits),
        (tile, (plane, FIELDS // 8, *tile)),
        "pack",
        (design, populations, cotangent, wall_mask, inlet_mask),
        [pl.ANY] * 5,
        [vmem((38, *tile), real), vmem((2, *tile), jnp.int32), pltpu.SemaphoreType.DMA((5,))],
        60,
    )
    packed = lax.all_to_all(packed, ("grp", "gy"), 0, 0)
    designs = [design] * size
    for turn in reversed(range(1, size)):
        designs[turn] = lax.ppermute(design, "gx", [(i, i ^ turn) for i in range(size)])
    copies = call(
        functools.partial(spread_kernel, size),
        ((plane, size, *tile),),
        "spread",
        [designs[turn] for turn in turns_of(size)],
        [vmem] * size,
        [vmem((size, *tile), real)],
    )
    outer = (-(-OUTER // 8) * 8, LANES)
    body, near, far = call(
        functools.partial(arrange_kernel, splits),
        ((FIELDS, 16, LANES), outer, outer),
        "arrange",
        (packed,),
        [vmem],
    )
    copies = lax.all_to_all(copies, ("grp", "gy"), 0, 0)
    path = [on_path(index, grp, splits) for index in range(plane)]
    order = [(path if gx % 2 == 0 else path[::-1])[index] * size + gx for gx in range(size) for index in range(plane)]
    line = ("grp", "gy", "gx")

    def exchange(value, start):
        pairs = [order[b : b + 2] for b in range(start, size * plane - 1, 2)]
        return lax.ppermute(value, line, [pair for i, j in pairs for pair in ((i, j), (j, i))])

    near, far = exchange(near, 0), exchange(far, 1)
    columns = size * LANES
    share = call(
        functools.partial(level_kernel, rows, splits, size),
        ((2, 32, LANES),),
        "level",
        (beta_step.reshape(1), copies),
        [pltpu.SMEM, vmem],
        [vmem((columns + 16, LANES), real), vmem((columns, LANES), real)],
    )
    shapes = [
        (19, 48, LANES),
        (19, 48, LANES),
        (19, 48, LANES),
        (STEPS, 4, 32, LANES),
        (32, LANES),
        (48, LANES),
        (3 * LANES, LANES),
    ]
    packed = call(
        functools.partial(flow_kernel, rows, splits, size),
        ((plane, 5, 8, LANES),),
        "flow",
        (share, body, far, near),
        [vmem] * 4,
        [vmem(shape, real) for shape in shapes],
    )
    packed = lax.all_to_all(packed, ("grp", "gy"), 0, 0)
    return call(functools.partial(result_kernel, splits), (populations.shape, design.shape), "result", (packed,), [vmem])


def body(design, populations, cotangent, wall_mask, inlet_mask, beta_step):
    grp, splits = lax.axis_size("grp"), lax.axis_size("gy")
    layers, height, width = design.shape
    fits = height == 8 and width == LANES and layers * grp * height * splits == LANES
    size = lax.axis_size("gx")
    fits = fits and grp * splits * 16 == LANES and size & (size - 1) == 0
    whole = body_by_columns if fits else body_by_blocks
    return whole(design, populations, cotangent, wall_mask, inlet_mask, beta_step)


def solution(mesh):
    placed = (
        P("grp", "gy", "gx"),
        P(None, "grp", "gy", "gx"),
        P(None, "grp", "gy", "gx"),
        P("grp", "gy", "gx"),
        P("grp", "gy", "gx"),
        P(),
    )
    return jax.shard_map(
        body,
        mesh=mesh,
        in_specs=placed,
        out_specs=(P(None, "grp", "gy", "gx"), P("grp", "gy", "gx")),
        check_vma=False,
    )
```
